128 devices in a mesh: section: 2 (over z_hi), dp: 16 (over y, z_lo, core), tensor: 4 (over x).
Axes of the slice: x: 4, y: 4, z: 4 (z_hi: 2, z_lo: 2; z = z_hi * 2 + z_lo), core: 2. Of those that a mesh axis runs over, the one named last changes fastest.
Arguments:
- block_input: bfloat16 [2, 4096, 2048], P(None, ('dp', 'tensor')), may hold values from -6 to 6
- cotangent: bfloat16 [2, 4096, 2048], P(None, ('dp', 'tensor')), may hold values from -6 to 6
- doc_lengths: int32 [2, 6], replicated, may hold values from 1 to 4091, as said below
- bank_choice: int32 [2], replicated, may hold values from 0 to 7
- first_gain: bfloat16 [2, 2048], P('section'), may hold values from 0.5 to 1.5
- first_shift: bfloat16 [2, 2048], P('section'), may hold values from -1 to 1
- query_weight: bfloat16 [2, 2048, 2048], P('section', 'dp', 'tensor'), may hold values from -0.125 to 0.125
- query_bias: bfloat16 [2, 2048], P('section', 'tensor'), may hold values from -1 to 1
- keyval_weight: bfloat16 [2, 2048, 256], P('section', 'dp'), may hold values from -0.125 to 0.125
- value_bias: bfloat16 [2, 128], P('section'), may hold values from -2.5 to 2.5
- output_weight: bfloat16 [2, 2048, 2048], P('section', 'tensor', 'dp'), may hold values from -1 to 1
- output_bias: bfloat16 [2, 2048], P('section'), may hold values from -1 to 1
- second_gain: bfloat16 [2, 2048], P('section'), may hold values from 0.5 to 1.5
- second_shift: bfloat16 [2, 2048], P('section'), may hold values from -1 to 1
- upward_weight: bfloat16 [2, 2048, 8192], P('section', 'dp', 'tensor'), may hold values from -0.125 to 0.125
- upward_bias: bfloat16 [2, 8192], P('section', 'tensor'), may hold values from -2.5 to 2.5
- downward_weight: bfloat16 [2, 8192, 2048], P('section', 'tensor', 'dp'), may hold values from -0.0625 to 0.0625
- downward_bias: bfloat16 [2, 2048], P('section'), may hold values from -1 to 1
- query_shrink: bfloat16 [2, 8, 2048, 16], P('section'), may hold values from -0.125 to 0.125
- query_expand: bfloat16 [2, 8, 16, 2048], P('section', None, None, 'tensor'), may hold values from -0.75 to 0.75
- keyval_shrink: bfloat16 [2, 8, 2048, 16], P('section'), may hold values from -0.125 to 0.125
- keyval_expand: bfloat16 [2, 8, 16, 256], P('section'), may hold values from -0.75 to 0.75
- output_shrink: bfloat16 [2, 8, 2048, 16], P('section', None, 'tensor'), may hold values from -1 to 1
- output_expand: bfloat16 [2, 8, 16, 2048], P('section'), may hold values from -0.75 to 0.75
- upward_shrink: bfloat16 [2, 8, 2048, 16], P('section'), may hold values from -0.125 to 0.125
- upward_expand: bfloat16 [2, 8, 16, 8192], P('section', None, None, 'tensor'), may hold values from -0.75 to 0.75
- downward_shrink: bfloat16 [2, 8, 8192, 16], P('section', None, 'tensor'), may hold values from -0.0625 to 0.0625
- downward_expand: bfloat16 [2, 8, 16, 2048], P('section'), may hold values from -0.75 to 0.75
Outputs:
- section_outputs: bfloat16 [2, 2, 4096, 2048], P('section', None, ('dp', 'tensor'))
- input_grads: float32 [2, 2, 4096, 2048], P('section', None, ('dp', 'tensor'))
- query_shrink_grad: float32 [2, 8, 2048, 16], P('section')
- query_expand_grad: float32 [2, 8, 16, 2048], P('section', None, None, 'tensor')
- keyval_shrink_grad: float32 [2, 8, 2048, 16], P('section')
- keyval_expand_grad: float32 [2, 8, 16, 256], P('section')
- output_shrink_grad: float32 [2, 8, 2048, 16], P('section', None, 'tensor')
- output_expand_grad: float32 [2, 8, 16, 2048], P('section')
- upward_shrink_grad: float32 [2, 8, 2048, 16], P('section')
- upward_expand_grad: float32 [2, 8, 16, 8192], P('section', None, None, 'tensor')
- downward_shrink_grad: float32 [2, 8, 8192, 16], P('section', None, 'tensor')
- downward_expand_grad: float32 [2, 8, 16, 2048], P('section')
The draws below stay inside these ranges and needn't reach their ends.
Inputs may be any that keep to these rules, and one draw needn't show every extreme that they name: `doc_lengths`: row i holds, in order, the lengths of the 6 documents packed into sequence i; every row sums to 4096.
All inputs are finite; a program needn't handle non-finite values.
Results may differ from the reference program's by a relative error of at most 0.025.
Values may be sent and summed in bfloat16 or wider, within the bound.
No kernel may reach another device: no remote copies, remote signals or barrier semaphores. Data moves between devices by JAX's collectives and lax.ppermute only.
A program may use at most 192 MiB of HBM per device.

```python
import math
import jax
import jax.numpy as jnp
from jax import lax

D = 2048
HEADS = 16
HD = 128
FF = 8192
R = 16
BANKS = 8
SEQ_LEN = 4096
WINDOW = 1024
NDOC = 6
MICRO = 2
SECTIONS = 2
GROUPS = 1
SEQS = 2
TOK_MB = 4096


def draw_doc_lengths(key, part):
    key = jax.random.fold_in(key, 7)
    cut_key, pick_key = jax.random.split(key)

    def regular(row_key):
        cut_points = jnp.sort(jax.random.permutation(row_key, SEQ_LEN - 1)[:NDOC - 1] + 1).astype(jnp.int32)
        bounds = jnp.concatenate([jnp.zeros((1,), jnp.int32), cut_points, jnp.full((1,), SEQ_LEN, jnp.int32)])
        return bounds[1:] - bounds[:-1]
    regular_rows = jax.vmap(regular)(jax.random.split(cut_key, SEQS))
    longest = jnp.concatenate([jnp.full((1,), SEQ_LEN - NDOC + 1, jnp.int32), jnp.ones((NDOC - 1,), jnp.int32)])
    picked = jax.random.randint(pick_key, (GROUPS,), 0, MICRO)
    sequence = jnp.arange(SEQS)
    is_long = sequence // GROUPS == picked[sequence % GROUPS]
    return jnp.where(is_long[:, None], longest[None, :], regular_rows).astype(jnp.int32)


def levels(own_key, dims, cuts, smallest, top_value):
    def one(dim, parts):
        heights = jax.random.uniform(jax.random.fold_in(jax.random.fold_in(own_key, 6), dim), (parts,), jnp.float32, smallest / len(cuts), top_value / len(cuts))
        return jnp.repeat(jnp.exp(heights), dims[dim] // parts).reshape((-1,) + (1,) * (len(dims) - dim - 1))

    level = one(*cuts[0])
    for cut in cuts[1:]:
        level = level * one(*cut)
    return level


def noise(own_key, shape, deviation, reach, shards=(), kind=jnp.bfloat16):
    level = levels(own_key, shape, shards, -0.22, 0.18) if shards else 1.0
    entries = jax.random.normal(own_key, shape, jnp.float32) * deviation * level
    return jnp.minimum(jnp.maximum(entries, -reach), reach).astype(kind)


def setup_inputs(seed: int = 0) -> dict:
    seeds = jax.random.split(jax.random.key(seed), 29)
    return {
        "block_input": noise(seeds[0], (MICRO, TOK_MB, D), 1.0, 6.0, ((1, 64),)),
        "cotangent": noise(seeds[1], (MICRO, TOK_MB, D), 1.0, 6.0, ((1, 64),)),
        "doc_lengths": draw_doc_lengths(jax.random.fold_in(seeds[28], 71), 0),
        "bank_choice": jax.random.randint(seeds[3], (SEQS,), 0, BANKS).astype(jnp.int32),
        "first_gain": jnp.clip(1.0 + 0.1 * jax.random.normal(seeds[4], (SECTIONS, D), jnp.float32), 0.5, 1.5).astype(jnp.bfloat16),
        "first_shift": noise(seeds[5], (SECTIONS, D), 0.2, 1.0, ((0, 2),)),
        "query_weight": noise(seeds[6], (SECTIONS, D, D), D ** -0.5, 0.125, ((0, 2), (1, 16), (2, 4))),
        "query_bias": noise(seeds[7], (SECTIONS, D), 0.2, 1.0, ((0, 2), (1, 4))),
        "keyval_weight": noise(seeds[8], (SECTIONS, D, 2 * HD), D ** -0.5, 0.125, ((0, 2), (1, 16))),
        "value_bias": noise(seeds[9], (SECTIONS, HD), 0.5, 2.5, ((0, 2),)),
        "output_weight": noise(seeds[10], (SECTIONS, D, D), (D // 64) ** -0.5, 1.0, ((0, 2), (1, 4), (2, 16))),
        "output_bias": noise(seeds[11], (SECTIONS, D), 0.2, 1.0, ((0, 2),)),
        "second_gain": jnp.clip(1.0 + 0.1 * jax.random.normal(seeds[12], (SECTIONS, D), jnp.float32), 0.5, 1.5).astype(jnp.bfloat16),
        "second_shift": noise(seeds[13], (SECTIONS, D), 0.2, 1.0, ((0, 2),)),
        "upward_weight": noise(seeds[14], (SECTIONS, D, FF), D ** -0.5, 0.125, ((0, 2), (1, 16), (2, 4))),
        "upward_bias": noise(seeds[15], (SECTIONS, FF), 0.5, 2.5, ((0, 2), (1, 4))),
        "downward_weight": noise(seeds[16], (SECTIONS, FF, D), FF ** -0.5, 0.0625, ((0, 2), (1, 4), (2, 16))),
        "downward_bias": noise(seeds[17], (SECTIONS, D), 0.2, 1.0, ((0, 2),)),
        "query_shrink": noise(seeds[18], (SECTIONS, BANKS, D, R), D ** -0.5, 0.125, ((0, 2),)),
        "query_expand": noise(seeds[19], (SECTIONS, BANKS, R, D), (4 * R) ** -0.5, 0.75, ((0, 2), (3, 4))),
        "keyval_shrink": noise(seeds[20], (SECTIONS, BANKS, D, R), D ** -0.5, 0.125, ((0, 2),)),
        "keyval_expand": noise(seeds[21], (SECTIONS, BANKS, R, 2 * HD), (4 * R) ** -0.5, 0.75, ((0, 2),)),
        "output_shrink": noise(seeds[22], (SECTIONS, BANKS, D, R), (D // 64) ** -0.5, 1.0, ((0, 2), (2, 4))),
        "output_expand": noise(seeds[23], (SECTIONS, BANKS, R, D), (4 * R) ** -0.5, 0.75, ((0, 2),)),
        "upward_shrink": noise(seeds[24], (SECTIONS, BANKS, D, R), D ** -0.5, 0.125, ((0, 2),)),
        "upward_expand": noise(seeds[25], (SECTIONS, BANKS, R, FF), (4 * R) ** -0.5, 0.75, ((0, 2), (3, 4))),
        "downward_shrink": noise(seeds[26], (SECTIONS, BANKS, FF, R), FF ** -0.5, 0.0625, ((0, 2), (2, 4))),
        "downward_expand": noise(seeds[27], (SECTIONS, BANKS, R, D), (4 * R) ** -0.5, 0.75, ((0, 2),)),
    }


epsilon = 1e-05
masked_score = -1e+30

@jax.custom_vjp
def low(v):
    return lax.optimization_barrier(v.astype(jnp.bfloat16)).astype(jnp.float32)

@jax.custom_vjp
def low_back(v):
    return v

def low_keep(v):
    return (low(v), None)

def low_pass(kept, grad):
    return (grad,)

def back_keep(v):
    return (v, None)

def back_low(kept, grad):
    return (low(grad),)
low.defvjp(low_keep, low_pass)
low_back.defvjp(back_keep, back_low)

def matmul(left, right):
    return jnp.dot(left, right, precision=lax.Precision.HIGHEST)

def layer_norm(value, gain, shift):
    centred = value - lax.optimization_barrier(jnp.mean(value, axis=-1, keepdims=True))
    variance = lax.optimization_barrier(jnp.mean(centred * centred, axis=-1, keepdims=True))
    return centred * lax.rsqrt(variance + epsilon) * gain + shift

def document_ids(lengths, positions):
    doc_ends = jnp.cumsum(lengths)
    return lax.optimization_barrier(jnp.sum((positions[:, None] >= doc_ends[None, :]).astype(jnp.int32), axis=1))

def attend(queries, keyval, documents):
    length = queries.shape[0]
    block_rows = min(512, length)
    keys_only = keyval[:, :HD]
    values_only = keyval[:, HD:]
    positions = jnp.arange(length, dtype=jnp.int32)
    score_scale = 1.0 / math.sqrt(HD)

    def one_block(start):
        query_rows = lax.dynamic_slice_in_dim(queries, start, block_rows, 0).reshape(block_rows, HEADS, HD)
        query_place = lax.dynamic_slice_in_dim(positions, start, block_rows, 0)
        query_doc = lax.dynamic_slice_in_dim(documents, start, block_rows, 0)
        scores = low_back(jnp.einsum('qhd,kd->qhk', query_rows, keys_only, precision=lax.Precision.HIGHEST) * score_scale)
        distance = query_place[:, None] - positions[None, :]
        allowed = (distance >= 0) & (distance < WINDOW) & (query_doc[:, None] == documents[None, :])
        scores = jnp.where(allowed[:, None, :], scores, masked_score)
        row_top = lax.optimization_barrier(jnp.max(scores, axis=-1, keepdims=True))
        lifted = jnp.exp(scores - row_top)
        probabilities = low(lifted / lax.optimization_barrier(jnp.sum(lifted, axis=-1, keepdims=True)))
        mixed_heads = jnp.einsum('qhk,kd->qhd', probabilities, values_only, precision=lax.Precision.HIGHEST)
        return mixed_heads.reshape(block_rows, HEADS * HD)
    starts = (jnp.arange(length // block_rows) * block_rows).astype(jnp.int32)
    return lax.map(jax.checkpoint(one_block), starts).reshape(length, HEADS * HD)

def block_layer(hidden, frozen, adapters, documents):
    first_gain, first_shift, query_weight, query_bias, keyval_weight, value_bias, output_weight, output_bias, second_gain, second_shift, upward_weight, upward_bias, downward_weight, downward_bias = frozen
    query_shrink, query_expand, keyval_shrink, keyval_expand, output_shrink, output_expand, upward_shrink, upward_expand, downward_shrink, downward_expand = adapters
    normed = low(layer_norm(hidden, first_gain, first_shift))
    queries = low(low_back(matmul(normed, query_weight) + query_bias + matmul(matmul(normed, query_shrink), query_expand)))
    keyval_bias = jnp.concatenate([jnp.zeros_like(value_bias), value_bias])
    keyval = low(low_back(matmul(normed, keyval_weight) + keyval_bias + matmul(matmul(normed, keyval_shrink), keyval_expand)))
    mixed_heads = low(low_back(attend(queries, keyval, documents)))
    attended = low_back(matmul(mixed_heads, output_weight) + output_bias + matmul(matmul(mixed_heads, output_shrink), output_expand))
    middle = hidden + attended
    second = low(layer_norm(middle, second_gain, second_shift))
    upward = low_back(matmul(second, upward_weight) + upward_bias + matmul(matmul(second, upward_shrink), upward_expand))
    activated = low(jax.nn.gelu(upward, approximate=True))
    downward = low_back(matmul(activated, downward_weight) + downward_bias + matmul(matmul(activated, downward_shrink), downward_expand))
    return middle + downward

def run_section(hidden_all, frozen, adapters_all, bank_choice, documents_all):

    def one_sequence(item):
        hidden, bank_index, documents = item
        chosen = tuple((jnp.take(table, bank_index, axis=0) for table in adapters_all))
        return block_layer(hidden, frozen, chosen, documents)
    return lax.map(one_sequence, (hidden_all, bank_choice, documents_all))

def reference(block_input, cotangent, doc_lengths, bank_choice, first_gain, first_shift, query_weight, query_bias, keyval_weight, value_bias, output_weight, output_bias, second_gain, second_shift, upward_weight, upward_bias, downward_weight, downward_bias, query_shrink, query_expand, keyval_shrink, keyval_expand, output_shrink, output_expand, upward_shrink, upward_expand, downward_shrink, downward_expand):
    frozen_all = (first_gain, first_shift, query_weight, query_bias, keyval_weight, value_bias, output_weight, output_bias, second_gain, second_shift, upward_weight, upward_bias, downward_weight, downward_bias)
    adapter_all = (query_shrink, query_expand, keyval_shrink, keyval_expand, output_shrink, output_expand, upward_shrink, upward_expand, downward_shrink, downward_expand)
    positions = jnp.arange(SEQ_LEN, dtype=jnp.int32)
    documents_all = jax.vmap(lambda lengths: document_ids(lengths, positions))(doc_lengths)
    frozen_zero = tuple((table[0].astype(jnp.float32) for table in frozen_all))
    frozen_one = tuple((table[1].astype(jnp.float32) for table in frozen_all))
    adapt_zero = tuple((table[0].astype(jnp.float32) for table in adapter_all))
    adapt_one = tuple((table[1].astype(jnp.float32) for table in adapter_all))
    start_rows = block_input.astype(jnp.float32).reshape(SEQS, SEQ_LEN, D)

    def section_zero(hidden_all, adapters):
        return run_section(hidden_all, frozen_zero, adapters, bank_choice, documents_all)

    def section_one(hidden_all, adapters):
        return run_section(hidden_all, frozen_one, adapters, bank_choice, documents_all)
    middle_out, back_zero = jax.vjp(section_zero, start_rows, adapt_zero)
    passed = low(middle_out)
    final_out, back_one = jax.vjp(section_one, passed, adapt_one)
    grad_passed, grads_one = back_one(cotangent.astype(jnp.float32).reshape(SEQS, SEQ_LEN, D))
    grad_start, grads_zero = back_zero(grad_passed)
    out_shape = (MICRO, TOK_MB, D)
    section_outputs = jnp.stack([passed.reshape(out_shape), final_out.reshape(out_shape)]).astype(jnp.bfloat16)
    input_grads = jnp.stack([grad_start.reshape(out_shape), grad_passed.reshape(out_shape)])
    stacked = [jnp.stack([grad_zero, grad_one]) for grad_zero, grad_one in zip(grads_zero, grads_one)]
    return (section_outputs, input_grads, stacked[0], stacked[1], stacked[2], stacked[3], stacked[4], stacked[5], stacked[6], stacked[7], stacked[8], stacked[9])
```

```python
import math

import jax
import jax.numpy as jnp
from jax import lax
from jax.experimental import pallas as pl
from jax.experimental.pallas import tpu as pltpu
from jax.sharding import PartitionSpec as P

WINDOW = 1024
epsilon = 1e-05
masked_score = -1e30
bf16 = jnp.bfloat16
f32 = jnp.float32


def plain(left, right):
    return jnp.dot(left, right, preferred_element_type=f32)


def against(left, right):
    return lax.dot_general(left, right, (((1,), (1,)), ((), ())), preferred_element_type=f32)


def across(left, right):
    return lax.dot_general(left, right, (((0,), (0,)), ((), ())), preferred_element_type=f32)


def around(block, axis, distance):
    size = lax.axis_size(axis)
    return lax.ppermute(block, axis, [(i, (i + distance) % size) for i in range(size)])


def along(block, axis, distance):
    size = lax.axis_size(axis)
    route = [(i, i + distance) for i in range(size) if 0 <= i + distance < size]
    return lax.ppermute(block, axis, route)


def flipped(block, axis, bit):
    size = lax.axis_size(axis)
    return lax.ppermute(block, axis, [(i, i ^ bit) for i in range(size)])


def pick(table, index, size=1):
    return lax.dynamic_slice_in_dim(table, index, size, 0)


def norm_parts(value):
    centred = value - jnp.mean(value, axis=-1, keepdims=True)
    spread = lax.rsqrt(jnp.mean(centred * centred, axis=-1, keepdims=True) + epsilon)
    return centred * spread, spread


def norm_back(unit, spread, scaled):
    inner = jnp.mean(scaled * unit, axis=-1, keepdims=True)
    return spread * (scaled - jnp.mean(scaled, axis=-1, keepdims=True) - unit * inner)


def gelu_parts(value):
    rate = math.sqrt(2.0 / math.pi)
    square = value * value
    bend = jnp.tanh(rate * (value + 0.044715 * value * square))
    rising = 0.5 * (1.0 + bend)
    slope = rising + 0.5 * value * (1.0 - bend * bend) * (rate * (1.0 + 3 * 0.044715 * square))
    return value * rising, slope


def attend_kernel(scale, query_ref, keyval_ref, bias_ref, prob_ref, mixed_ref):
    head = query_ref.shape[1]
    scores = against(query_ref[...], keyval_ref[:, :head]) * scale + bias_ref[...].astype(f32)
    top = jnp.max(scores, axis=-1, keepdims=True)
    lifted = jnp.exp(scores - top)
    total = jnp.sum(lifted, axis=-1, keepdims=True)
    probs = (lifted * (1.0 / total)).astype(bf16)
    prob_ref[0] = probs
    mixed_ref[...] = plain(probs, keyval_ref[:, head:]).astype(bf16)


def attend(queries, key_block, bias, head):
    rows, width = queries.shape
    keys = key_block.shape[0]
    heads = width // head
    whole = lambda shape: pl.BlockSpec(shape, lambda h: (0, 0))
    column = pl.BlockSpec((rows, head), lambda h: (0, h))
    return pl.pallas_call(
        lambda *refs: attend_kernel(1.0 / math.sqrt(head), *refs),
        grid=(heads,),
        in_specs=[column, whole((keys, 2 * head)), whole((rows, keys))],
        out_specs=[pl.BlockSpec((1, rows, keys), lambda h: (h, 0, 0)), column],
        out_shape=[
            jax.ShapeDtypeStruct((heads, rows, keys), bf16),
            jax.ShapeDtypeStruct((rows, width), bf16),
        ],
        compiler_params=pltpu.CompilerParams(vmem_limit_bytes=40 * 2**20),
        name="attend",
    )(queries, key_block, bias)


def attend_back_kernel(
    scale, grad_ref, prob_ref, query_ref, mixed_ref, keyval_ref, dq_ref, dkv_ref, key_sum, value_sum
):
    step = pl.program_id(0)
    head = query_ref.shape[1]
    grad = grad_ref[...]
    probs = prob_ref[0]
    delta = jnp.sum(grad.astype(f32) * mixed_ref[...].astype(f32), axis=-1, keepdims=True)
    grad_probs = against(grad, keyval_ref[:, head:])
    grad_scores = (probs.astype(f32) * (grad_probs - delta)).astype(bf16)
    dq_ref[...] = (plain(grad_scores, keyval_ref[:, :head]) * scale).astype(bf16)
    keys = across(grad_scores, query_ref[...])
    values = across(probs, grad)

    @pl.when(step == 0)
    def _():
        key_sum[...] = keys
        value_sum[...] = values

    @pl.when(step > 0)
    def _():
        key_sum[...] += keys
        value_sum[...] += values

    @pl.when(step == pl.num_programs(0) - 1)
    def _():
        dkv_ref[:, :head] = (key_sum[...] * scale).astype(bf16)
        dkv_ref[:, head:] = value_sum[...].astype(bf16)


def attend_back(grad_mixed, probs, queries, mixed, key_block, head):
    rows, width = queries.shape
    keys = key_block.shape[0]
    heads = width // head
    column = pl.BlockSpec((rows, head), lambda h: (0, h))
    whole = pl.BlockSpec((keys, 2 * head), lambda h: (0, 0))
    return pl.pallas_call(
        lambda *refs: attend_back_kernel(1.0 / math.sqrt(head), *refs),
        grid=(heads,),
        in_specs=[
            column,
            pl.BlockSpec((1, rows, keys), lambda h: (h, 0, 0)),
            column,
            column,
            whole,
        ],
        out_specs=[column, whole],
        out_shape=[
            jax.ShapeDtypeStruct((rows, width), bf16),
            jax.ShapeDtypeStruct((keys, 2 * head), bf16),
        ],
        scratch_shapes=[pltpu.VMEM((keys, head), f32), pltpu.VMEM((keys, head), f32)],
        compiler_params=pltpu.CompilerParams(vmem_limit_bytes=40 * 2**20),
        name="attend_back",
    )(grad_mixed, probs, queries, mixed, key_block)


def per_device(
    block_input,
    cotangent,
    doc_lengths,
    bank_choice,
    first_gain,
    first_shift,
    query_weight,
    query_bias,
    keyval_weight,
    value_bias,
    output_weight,
    output_bias,
    second_gain,
    second_shift,
    upward_weight,
    upward_bias,
    downward_weight,
    downward_bias,
    query_shrink,
    query_expand,
    keyval_shrink,
    keyval_expand,
    output_shrink,
    output_expand,
    upward_shrink,
    upward_expand,
    downward_shrink,
    downward_expand,
):
    section = lax.axis_index("section")
    data = lax.axis_index("dp")
    tensor = lax.axis_index("tensor")
    low_section = section == 0
    width = block_input.shape[2]
    rows = block_input.shape[1]
    ranks = lax.axis_size("tensor")
    span = rows * ranks
    head = value_bias.shape[1]
    local_q = query_bias.shape[1]
    local_f = upward_bias.shape[1]
    rank = query_expand.shape[2]
    banks = query_expand.shape[1]
    reach = WINDOW // span
    sides = [(0, 1), (1, 0)]

    def swap(value):
        return lax.ppermute(value, "section", sides)

    def by_layer(own, other):
        return jnp.where(low_section, own, other), jnp.where(low_section, other, own)

    def spread(block):
        parts = [block] + [around(block, "tensor", -j) for j in range(1, ranks)]
        return jnp.concatenate(parts, axis=0)

    def reduce_rows(partial):
        low = partial.astype(bf16)
        total = partial[:rows]
        for j in range(1, ranks):
            total = total + around(low[j * rows : (j + 1) * rows], "tensor", j).astype(f32)
        return total

    def chosen(table, bank, transpose):
        block = lax.dynamic_index_in_dim(table[0], bank, 0, keepdims=False)
        return block.T if transpose else block

    def early_pack(bank):
        return jnp.concatenate(
            [
                chosen(query_shrink, bank, True),
                chosen(keyval_shrink, bank, True),
                chosen(query_expand, bank, False),
                chosen(keyval_expand, bank, False),
            ],
            axis=1,
        )

    def late_pack(bank):
        return jnp.concatenate(
            [
                chosen(output_shrink, bank, True),
                chosen(output_expand, bank, False),
                chosen(upward_shrink, bank, True),
                chosen(upward_expand, bank, False),
                chosen(downward_shrink, bank, True),
                chosen(downward_expand, bank, False),
            ],
            axis=1,
        )

    own_bank = lax.dynamic_index_in_dim(bank_choice, section, 0, keepdims=False)
    other_bank = lax.dynamic_index_in_dim(bank_choice, 1 - section, 0, keepdims=False)

    vectors = jnp.concatenate(
        [
            first_gain,
            first_shift,
            query_bias,
            jnp.zeros_like(value_bias),
            value_bias,
            output_bias,
            second_gain,
            second_shift,
            upward_bias,
            downward_bias,
        ],
        axis=1,
    )
    vector_sizes = [width, width, local_q, 2 * head, width, width, width, local_f, width]

    shard_qkv = jnp.concatenate([query_weight[0], keyval_weight[0]], axis=1)
    shard_rest = jnp.concatenate(
        [output_weight[0].T, upward_weight[0], downward_weight[0].T], axis=1
    )
    qkv_layers = by_layer(shard_qkv, swap(shard_qkv))
    vector_layers = by_layer(vectors, swap(vectors))
    early_layers = by_layer(early_pack(own_bank), swap(early_pack(other_bank)))
    rest_layers = by_layer(shard_rest, swap(shard_rest))
    late_layers = by_layer(late_pack(own_bank), swap(late_pack(other_bank)))

    def gather(shard):
        return lax.all_gather(shard, "dp", axis=0, tiled=True)

    first = gather(qkv_layers[0])
    second_shard = jnp.concatenate(
        [rest_layers[0], qkv_layers[1], rest_layers[1][:, :local_q]], axis=1
    )
    first, second_shard = lax.optimization_barrier((first, second_shard))
    middle_all = gather(second_shard)
    third_shard = rest_layers[1][:, local_q:]
    middle_all, third_shard = lax.optimization_barrier((middle_all, third_shard))
    last_all = gather(third_shard)

    def split(table, sizes):
        cuts = [0]
        for size in sizes:
            cuts.append(cuts[-1] + size)
        return [table[:, a:b] for a, b in zip(cuts[:-1], cuts[1:])]

    wide = local_q + 2 * head
    out_zero, up_zero, down_zero, qkv_one, out_one = split(
        middle_all, [local_q, local_f, local_f, wide, local_q]
    )
    up_one, down_one = split(last_all, [local_f, local_f])
    weights = [
        (first, out_zero, up_zero, down_zero),
        (qkv_one, out_one, up_one, down_one),
    ]
    small = [
        [part.astype(f32) for part in split(vector_layers[layer], vector_sizes)]
        for layer in range(2)
    ]
    adapters = [
        split(early_layers[layer], [width, width, local_q, 2 * head])
        + split(late_layers[layer], [local_q, width, width, local_f, local_f, width])
        for layer in range(2)
    ]

    place = (
        ((tensor + jnp.arange(ranks, dtype=jnp.int32)) % ranks)[:, None] * rows
        + jnp.arange(rows, dtype=jnp.int32)[None, :]
    ).reshape(-1)
    query_place = data * span + place
    key_place = jnp.concatenate([(data - back) * span + place for back in range(reach, -1, -1)])
    lengths = lax.dynamic_index_in_dim(doc_lengths, section, 0, keepdims=False)
    ends = jnp.cumsum(lengths)
    query_doc = jnp.sum((query_place[:, None] >= ends[None, :]).astype(jnp.int32), axis=1)
    key_doc = jnp.sum((key_place[:, None] >= ends[None, :]).astype(jnp.int32), axis=1)
    distance = query_place[:, None] - key_place[None, :]
    allowed = (
        (key_place[None, :] >= 0)
        & (distance >= 0)
        & (distance < WINDOW)
        & (query_doc[:, None] == key_doc[None, :])
    )
    bias = jnp.where(allowed, 0.0, masked_score).astype(bf16)

    def forward(layer, hidden):
        qkv_w, out_w, up_w, down_w = weights[layer]
        gain1, shift1, q_bias, kv_bias, out_bias, gain2, shift2, up_bias, down_bias = small[layer]
        sq, skv, eq, ekv, so, eo, su, eu, sd, ed = adapters[layer]
        unit1, rsd1 = norm_parts(hidden)
        normed = spread((unit1 * gain1 + shift1).astype(bf16))
        low_q = against(normed, sq).astype(bf16)
        low_kv = against(normed, skv).astype(bf16)
        both = plain(normed, qkv_w)
        keyval = (both[:, local_q:] + kv_bias + plain(low_kv, ekv)).astype(bf16)
        pieces = [along(keyval, "dp", back) for back in range(reach, 0, -1)] + [keyval]
        queries = (both[:, :local_q] + q_bias + plain(low_q, eq)).astype(bf16)
        key_block = jnp.concatenate(pieces, axis=0)
        probs, mixed = attend(queries, key_block, bias, head)
        low_o = against(mixed, so).astype(bf16)
        attended = reduce_rows(against(mixed, out_w) + plain(low_o, eo))
        middle = hidden + (attended + out_bias)
        unit2, rsd2 = norm_parts(middle)
        second = spread((unit2 * gain2 + shift2).astype(bf16))
        low_u = against(second, su).astype(bf16)
        upward = plain(second, up_w) + up_bias + plain(low_u, eu)
        active, slope = gelu_parts(upward)
        active = active.astype(bf16)
        slope = slope.astype(bf16)
        low_d = against(active, sd).astype(bf16)
        result = middle + (reduce_rows(against(active, down_w) + plain(low_d, ed)) + down_bias)
        kept = (
            unit1,
            rsd1,
            normed,
            low_q,
            low_kv,
            queries,
            key_block,
            probs,
            mixed,
            low_o,
            unit2,
            rsd2,
            second,
            low_u,
            active,
            slope,
            low_d,
        )
        return result, kept

    def tiles(block):
        return block.reshape(rank, -1, 128).transpose(1, 0, 2)

    def flat(block):
        return block.transpose(1, 0, 2).reshape(rank, -1)

    def reduce_grads(shared, owned):
        pile = jnp.concatenate([tiles(part) for part in shared], axis=0).astype(bf16)
        lack = -pile.shape[0] % ranks
        if lack:
            pile = jnp.concatenate([pile, jnp.zeros((lack,) + pile.shape[1:], bf16)], axis=0)
        each = pile.shape[0] // ranks
        total = pick(pile, tensor * each, each).astype(f32)
        for j in range(1, ranks):
            block = pick(pile, ((tensor + j) % ranks) * each, each)
            total = total + around(block, "tensor", j).astype(f32)
        pile = jnp.concatenate([total] + [tiles(part) for part in owned], axis=0).astype(bf16)
        if pile.shape[0] % 2:
            pile = jnp.concatenate([pile, jnp.zeros((1,) + pile.shape[1:], bf16)], axis=0)
        half = pile.shape[0] // 2
        core = data % 2
        got = flipped(pick(pile, (1 - core) * half, half), "dp", 1)
        mine = (pick(pile, core * half, half).astype(f32) + got.astype(f32)).astype(bf16)
        got = flipped(mine, "dp", 2)
        mine = (mine.astype(f32) + got.astype(f32)).astype(bf16)
        parts = jnp.stack([mine] + [around(mine, "dp", 4 * k) for k in range(1, 4)])
        turn = data // 4
        total = sum(
            lax.dynamic_index_in_dim(parts, (turn - r) % 4, 0, keepdims=False).astype(f32)
            for r in range(4)
        )
        return total.astype(bf16)

    def spread_grads(mine, shared_sizes, owned_sizes):
        shared_count = sum(shared_sizes) // 128
        each = -(-shared_count // ranks)
        owned_count = sum(owned_sizes) // 128
        core = data % 2
        other = flipped(mine, "dp", 1)
        lower = jnp.where(core == 0, mine, other)
        upper = jnp.where(core == 0, other, mine)
        pile = jnp.concatenate([lower, upper], axis=1)
        own = pile[:, :each]
        parts = jnp.stack([own] + [around(own, "tensor", k) for k in range(1, ranks)])
        ordered = jnp.concatenate(
            [
                lax.dynamic_index_in_dim(parts, (tensor - r) % ranks, 0, keepdims=False)
                for r in range(ranks)
            ],
            axis=1,
        )
        results = []
        begin = 0
        for size in shared_sizes:
            count = size // 128
            results.append([flat(ordered[m, begin : begin + count]) for m in range(2)])
            begin += count
        begin = each
        owned = []
        for size in owned_sizes:
            count = size // 128
            owned.append([flat(pile[m, begin : begin + count]) for m in range(2)])
            begin += count
        return results, owned

    def backward_feed(layer, kept, grad):
        up_w, down_w = weights[layer][2:]
        gain2 = small[layer][5]
        so, eo, su, eu, sd, ed = adapters[layer][4:]
        unit2, rsd2, second, low_u, active, slope, low_d = kept[10:]
        branch = spread(grad.astype(bf16))
        inner_d = against(branch, ed).astype(bf16)
        grad_up = ((plain(branch, down_w) + plain(inner_d, sd)) * slope.astype(f32)).astype(bf16)
        inner_u = against(grad_up, eu).astype(bf16)
        grad_second = reduce_rows(against(grad_up, up_w) + plain(inner_u, su))
        grad_middle = grad + norm_back(unit2, rsd2, grad_second * gain2)
        shared = [across(inner_u, second), across(low_d, branch)]
        owned = [across(low_u, grad_up), across(inner_d, active)]
        return grad_middle, shared, owned

    def backward_attend(layer, kept, grad_middle):
        qkv_w, out_w = weights[layer][:2]
        gain1 = small[layer][0]
        sq, skv, eq, ekv, so, eo = adapters[layer][:6]
        unit1, rsd1, normed, low_q, low_kv, queries, key_block, probs, mixed, low_o = kept[:10]
        branch = spread(grad_middle.astype(bf16))
        inner_o = against(branch, eo).astype(bf16)
        grad_mixed = (plain(branch, out_w) + plain(inner_o, so)).astype(bf16)
        grad_q, grad_block = attend_back(grad_mixed, probs, queries, mixed, key_block, head)
        own = grad_block[reach * span :].astype(f32)
        for back in range(1, reach + 1):
            begin = (reach - back) * span
            own = own + along(grad_block[begin : begin + span], "dp", -back).astype(f32)
        grad_kv = own.astype(bf16)
        inner_q = against(grad_q, eq).astype(bf16)
        inner_kv = against(grad_kv, ekv).astype(bf16)
        grad_normed = (
            against(grad_q, qkv_w[:, :local_q])
            + plain(inner_q, sq)
            + against(grad_kv, qkv_w[:, local_q:])
            + plain(inner_kv, skv)
        )
        grad_hidden = grad_middle + norm_back(unit1, rsd1, reduce_rows(grad_normed) * gain1)
        out_grads = ([across(low_o, branch)], [across(inner_o, mixed)])
        shared = [across(inner_q, normed), across(inner_kv, normed), across(low_kv, grad_kv)]
        owned = [across(low_q, grad_q)]
        return grad_hidden, out_grads, (shared, owned)

    def to_upper(value):
        return lax.ppermute(value, "section", [(0, 1)])

    def to_lower(value):
        return lax.ppermute(value, "section", [(1, 0)])

    fresh = lax.dynamic_index_in_dim(block_input, section, 0, keepdims=False).astype(f32)
    result_zero, kept_zero = forward(0, fresh)
    passed = result_zero.astype(bf16)
    result_one, kept_one = forward(1, passed.astype(f32))
    final = result_one.astype(bf16)

    given = lax.dynamic_index_in_dim(cotangent, section, 0, keepdims=False).astype(f32)
    grad_middle_one, feed_shared, feed_owned = backward_feed(1, kept_one, given)
    grad_one, out_one_grads, qkv_one_grads = backward_attend(1, kept_one, grad_middle_one)
    late_one = reduce_grads(feed_shared + out_one_grads[0], feed_owned + out_one_grads[1])
    early_one = reduce_grads(*qkv_one_grads)
    grad_middle_zero, feed_shared, feed_owned = backward_feed(0, kept_zero, grad_one)
    grad_zero, out_zero_grads, qkv_zero_grads = backward_attend(0, kept_zero, grad_middle_zero)
    late_zero = reduce_grads(feed_shared + out_zero_grads[0], feed_owned + out_zero_grads[1])
    early_zero = reduce_grads(*qkv_zero_grads)

    def both_micros(zero, one):
        received = jnp.where(low_section, to_lower(zero), to_upper(one))
        own = jnp.where(low_section, zero, one)
        return jnp.where(
            low_section, jnp.stack([own, received]), jnp.stack([received, own])
        )

    section_outputs = both_micros(passed, final)
    received = jnp.where(
        low_section, to_lower(grad_zero.astype(bf16)), to_upper(grad_one.astype(bf16))
    ).astype(f32)
    own = jnp.where(low_section, grad_zero, grad_one)
    input_grads = jnp.where(
        low_section, jnp.stack([own, received]), jnp.stack([received, own])
    )

    late_shared, late_owned = spread_grads(
        both_micros(late_zero, late_one), [width, width, width], [local_f, local_f, local_q]
    )
    early_shared, early_owned = spread_grads(
        both_micros(early_zero, early_one), [width, width, 2 * head], [local_q]
    )
    onehot = (bank_choice[:, None] == jnp.arange(banks)[None, :]).astype(f32)

    def placed(pair, transpose):
        out = sum(
            onehot[m][:, None, None] * pair[m].astype(f32)[None] for m in range(2)
        )
        return (out.transpose(0, 2, 1) if transpose else out)[None]

    up_shrink_grad, down_expand_grad, out_expand_grad = late_shared
    up_expand_grad, down_shrink_grad, out_shrink_grad = late_owned
    q_shrink_grad, kv_shrink_grad, kv_expand_grad = early_shared
    (q_expand_grad,) = early_owned
    return (
        section_outputs[None],
        input_grads[None],
        placed(q_shrink_grad, True),
        placed(q_expand_grad, False),
        placed(kv_shrink_grad, True),
        placed(kv_expand_grad, False),
        placed(out_shrink_grad, True),
        placed(out_expand_grad, False),
        placed(up_shrink_grad, True),
        placed(up_expand_grad, False),
        placed(down_shrink_grad, True),
        placed(down_expand_grad, False),
    )


def solution(mesh):
    return jax.shard_map(
        per_device,
        mesh=mesh,
        in_specs=(
            P(None, ("dp", "tensor"), None),
            P(None, ("dp", "tensor"), None),
            P(),
            P(),
            P("section", None),
            P("section", None),
            P("section", "dp", "tensor"),
            P("section", "tensor"),
            P("section", "dp", None),
            P("section", None),
            P("section", "tensor", "dp"),
            P("section", None),
            P("section", None),
            P("section", None),
            P("section", "dp", "tensor"),
            P("section", "tensor"),
            P("section", "tensor", "dp"),
            P("section", None),
            P("section", None, None, None),
            P("section", None, None, "tensor"),
            P("section", None, None, None),
            P("section", None, None, None),
            P("section", None, "tensor", None),
            P("section", None, None, None),
            P("section", None, None, None),
            P("section", None, None, "tensor"),
            P("section", None, "tensor", None),
            P("section", None, None, None),
        ),
        out_specs=(
            P("section", None, ("dp", "tensor"), None),
            P("section", None, ("dp", "tensor"), None),
            P("section", None, None, None),
            P("section", None, None, "tensor"),
            P("section", None, None, None),
            P("section", None, None, None),
            P("section", None, "tensor", None),
            P("section", None, None, None),
            P("section", None, None, None),
            P("section", None, None, "tensor"),
            P("section", None, "tensor", None),
            P("section", None, None, None),
        ),
        check_vma=False,
    )
```

```python
import math

import jax
import jax.numpy as jnp
from jax import lax
from jax.experimental import pallas as pl
from jax.experimental.pallas import tpu as pltpu
from jax.sharding import PartitionSpec as P

WINDOW = 1024
epsilon = 1e-05
masked_score = -1e30
bf16 = jnp.bfloat16
f32 = jnp.float32


def plain(left, right):
    return jnp.dot(left, right, preferred_element_type=f32)


def against(left, right):
    return lax.dot_general(left, right, (((1,), (1,)), ((), ())), preferred_element_type=f32)


def across(left, right):
    return lax.dot_general(left, right, (((0,), (0,)), ((), ())), preferred_element_type=f32)


def around(block, axis, distance):
    size = lax.axis_size(axis)
    return lax.ppermute(block, axis, [(i, (i + distance) % size) for i in range(size)])


def along(block, axis, distance):
    size = lax.axis_size(axis)
    route = [(i, i + distance) for i in range(size) if 0 <= i + distance < size]
    return lax.ppermute(block, axis, route)


def flipped(block, axis, bit):
    size = lax.axis_size(axis)
    return lax.ppermute(block, axis, [(i, i ^ bit) for i in range(size)])


def pick(table, index, size=1):
    return lax.dynamic_slice_in_dim(table, index, size, 0)


def norm_parts(value):
    centred = value - jnp.mean(value, axis=-1, keepdims=True)
    spread = lax.rsqrt(jnp.mean(centred * centred, axis=-1, keepdims=True) + epsilon)
    return centred * spread, spread


def norm_back(unit, spread, scaled):
    inner = jnp.mean(scaled * unit, axis=-1, keepdims=True)
    return spread * (scaled - jnp.mean(scaled, axis=-1, keepdims=True) - unit * inner)


def gelu_parts(value):
    rate = math.sqrt(2.0 / math.pi)
    square = value * value
    bend = jnp.tanh(rate * (value + 0.044715 * value * square))
    rising = 0.5 * (1.0 + bend)
    slope = rising + 0.5 * value * (1.0 - bend * bend) * (rate * (1.0 + 3 * 0.044715 * square))
    return value * rising, slope


def attend_kernel(scale, query_ref, keyval_ref, bias_ref, prob_ref, mixed_ref):
    head = query_ref.shape[1]
    scores = against(query_ref[...], keyval_ref[:, :head]) * scale + bias_ref[...].astype(f32)
    top = jnp.max(scores, axis=-1, keepdims=True)
    lifted = jnp.exp(scores - top)
    total = jnp.sum(lifted, axis=-1, keepdims=True)
    probs = lifted * (1.0 / total)
    prob_ref[0] = probs
    mixed_ref[...] = plain(probs.astype(bf16), keyval_ref[:, head:]).astype(bf16)


def attend(queries, key_block, bias, head):
    rows, width = queries.shape
    keys = key_block.shape[0]
    heads = width // head
    whole = lambda shape: pl.BlockSpec(shape, lambda h: (0, 0))
    column = pl.BlockSpec((rows, head), lambda h: (0, h))
    return pl.pallas_call(
        lambda *refs: attend_kernel(1.0 / math.sqrt(head), *refs),
        grid=(heads,),
        in_specs=[column, whole((keys, 2 * head)), whole((rows, keys))],
        out_specs=[pl.BlockSpec((1, rows, keys), lambda h: (h, 0, 0)), column],
        out_shape=[
            jax.ShapeDtypeStruct((heads, rows, keys), f32),
            jax.ShapeDtypeStruct((rows, width), bf16),
        ],
        compiler_params=pltpu.CompilerParams(vmem_limit_bytes=40 * 2**20),
        name="attend",
    )(queries, key_block, bias)


def attend_back_kernel(
    scale, grad_ref, prob_ref, query_ref, keyval_ref, dq_ref, dkv_ref, key_sum, value_sum
):
    step = pl.program_id(0)
    head = query_ref.shape[1]
    grad = grad_ref[...]
    probs = prob_ref[0]
    grad_probs = against(grad, keyval_ref[:, head:])
    delta = jnp.sum(grad_probs * probs, axis=-1, keepdims=True)
    grad_scores = (probs * (grad_probs - delta)).astype(bf16)
    dq_ref[...] = (plain(grad_scores, keyval_ref[:, :head]) * scale).astype(bf16)
    keys = across(grad_scores, query_ref[...])
    values = across(probs.astype(bf16), grad)

    @pl.when(step == 0)
    def _():
        key_sum[...] = keys
        value_sum[...] = values

    @pl.when(step > 0)
    def _():
        key_sum[...] += keys
        value_sum[...] += values

    @pl.when(step == pl.num_programs(0) - 1)
    def _():
        dkv_ref[:, :head] = (key_sum[...] * scale).astype(bf16)
        dkv_ref[:, head:] = value_sum[...].astype(bf16)


def attend_back(grad_mixed, probs, queries, key_block, head):
    rows, width = queries.shape
    keys = key_block.shape[0]
    heads = width // head
    column = pl.BlockSpec((rows, head), lambda h: (0, h))
    whole = pl.BlockSpec((keys, 2 * head), lambda h: (0, 0))
    return pl.pallas_call(
        lambda *refs: attend_back_kernel(1.0 / math.sqrt(head), *refs),
        grid=(heads,),
        in_specs=[
            column,
            pl.BlockSpec((1, rows, keys), lambda h: (h, 0, 0)),
            column,
            whole,
        ],
        out_specs=[column, whole],
        out_shape=[
            jax.ShapeDtypeStruct((rows, width), bf16),
            jax.ShapeDtypeStruct((keys, 2 * head), bf16),
        ],
        scratch_shapes=[pltpu.VMEM((keys, head), f32), pltpu.VMEM((keys, head), f32)],
        compiler_params=pltpu.CompilerParams(vmem_limit_bytes=40 * 2**20),
        name="attend_back",
    )(grad_mixed, probs, queries, key_block)


def weight_copies(table_ref, up_buf, down_buf, sems):
    count, width, tile = up_buf.shape
    each = count // 2
    copies = []
    for j in range(count):
        rows = pl.ds(j // each * width, width)
        begin = j % each * tile
        for k, buf in enumerate((up_buf, down_buf)):
            columns = pl.ds(begin + k * each * tile, tile)
            copies.append(
                pltpu.make_async_copy(table_ref.at[rows, columns], buf.at[j], sems.at[k, j])
            )
    return copies


def feed_kernel(
    second_ref, table_ref, bias_ref, eu_ref, sd_ref, su_ref, ed_ref,
    active_ref, slope_ref, low_u_ref, low_d_ref, out_ref, up_buf, down_buf, total, sems,
):
    count, width, tile = up_buf.shape
    copies = weight_copies(table_ref, up_buf, down_buf, sems)
    for copy in copies:
        copy.start()
    second = second_ref[...]
    low_u = against(second, su_ref[...]).astype(bf16)
    low_u_ref[...] = low_u
    low = 0.0
    for j in range(count):
        columns = pl.ds(j * tile, tile)
        copies[2 * j].wait()
        upward = plain(second, up_buf[j]) + plain(low_u, eu_ref[:, columns]) + bias_ref[:, columns]
        active, slope = gelu_parts(upward)
        active = active.astype(bf16)
        active_ref[:, columns] = active
        slope_ref[:, columns] = slope.astype(bf16)
        low = low + against(active, sd_ref[:, columns])
        copies[2 * j + 1].wait()
        part = against(active, down_buf[j])
        if j == 0:
            total[...] = part
        elif j < count - 1:
            total[...] += part
    low_d = low.astype(bf16)
    low_d_ref[...] = low_d
    out_ref[...] = (total[...] + part + plain(low_d, ed_ref[...])).astype(bf16)


def feed_scratch(rows, width, hidden, tile):
    return [
        pltpu.VMEM((hidden // tile, width, tile), bf16),
        pltpu.VMEM((hidden // tile, width, tile), bf16),
        pltpu.VMEM((rows, width), f32),
        pltpu.SemaphoreType.DMA((2, hidden // tile)),
    ]


def feed(second, table, bias, eu, sd, su, ed):
    rows, width = second.shape
    rank, hidden = eu.shape
    held = pl.BlockSpec(memory_space=pltpu.VMEM)
    return pl.pallas_call(
        feed_kernel,
        in_specs=[held, pl.BlockSpec(memory_space=pl.ANY)] + [held] * 5,
        out_specs=[held] * 5,
        out_shape=[
            jax.ShapeDtypeStruct((rows, hidden), bf16),
            jax.ShapeDtypeStruct((rows, hidden), bf16),
            jax.ShapeDtypeStruct((rows, rank), bf16),
            jax.ShapeDtypeStruct((rows, rank), bf16),
            jax.ShapeDtypeStruct((rows, width), bf16),
        ],
        scratch_shapes=feed_scratch(rows, width, hidden, 512),
        compiler_params=pltpu.CompilerParams(vmem_limit_bytes=40 * 2**20),
        cost_estimate=pl.CostEstimate(
            flops=4 * rows * width * hidden,
            bytes_accessed=4 * width * hidden + 8 * rows * hidden,
            transcendentals=rows * hidden,
        ),
        name="feed",
    )(second, table, bias, eu, sd, su, ed)


def feed_back_kernel(
    branch_ref, table_ref, slope_ref, eu_ref, sd_ref, su_ref, ed_ref,
    grad_up_ref, inner_d_ref, inner_u_ref, out_ref, up_buf, down_buf, total, sems,
):
    count, width, tile = up_buf.shape
    copies = weight_copies(table_ref, up_buf, down_buf, sems)
    for j in range(count):
        copies[2 * j + 1].start()
        copies[2 * j].start()
    branch = branch_ref[...]
    inner_d = against(branch, ed_ref[...]).astype(bf16)
    inner_d_ref[...] = inner_d
    inner = 0.0
    for j in range(count):
        columns = pl.ds(j * tile, tile)
        copies[2 * j + 1].wait()
        grad = plain(branch, down_buf[j]) + plain(inner_d, sd_ref[:, columns])
        grad = (grad * slope_ref[:, columns].astype(f32)).astype(bf16)
        grad_up_ref[:, columns] = grad
        inner = inner + against(grad, eu_ref[:, columns])
        copies[2 * j].wait()
        part = against(grad, up_buf[j])
        if j == 0:
            total[...] = part
        elif j < count - 1:
            total[...] += part
    inner_u = inner.astype(bf16)
    inner_u_ref[...] = inner_u
    out_ref[...] = (total[...] + part + plain(inner_u, su_ref[...])).astype(bf16)


def feed_back(branch, table, slope, eu, sd, su, ed):
    rows, width = branch.shape
    rank, hidden = eu.shape
    held = pl.BlockSpec(memory_space=pltpu.VMEM)
    return pl.pallas_call(
        feed_back_kernel,
        in_specs=[held, pl.BlockSpec(memory_space=pl.ANY)] + [held] * 5,
        out_specs=[held] * 4,
        out_shape=[
            jax.ShapeDtypeStruct((rows, hidden), bf16),
            jax.ShapeDtypeStruct((rows, rank), bf16),
            jax.ShapeDtypeStruct((rows, rank), bf16),
            jax.ShapeDtypeStruct((rows, width), bf16),
        ],
        scratch_shapes=feed_scratch(rows, width, hidden, 512),
        compiler_params=pltpu.CompilerParams(vmem_limit_bytes=40 * 2**20),
        cost_estimate=pl.CostEstimate(
            flops=4 * rows * width * hidden,
            bytes_accessed=4 * width * hidden + 4 * rows * hidden,
            transcendentals=0,
        ),
        name="feed_back",
    )(branch, table, slope, eu, sd, su, ed)


def place_kernel(rank_ref, mine_ref, other_ref, out_ref):
    core = rank_ref[0] % 2
    out_ref[0, pl.ds(core, 1)] = mine_ref[...]
    out_ref[0, pl.ds(1 - core, 1)] = other_ref[...]


def by_rank(rank, mine, other):
    chips, rows, columns = mine.shape
    block = pl.BlockSpec((1, rows, columns), lambda i, r: (i, 0, 0))
    return pl.pallas_call(
        place_kernel,
        grid_spec=pltpu.PrefetchScalarGridSpec(
            num_scalar_prefetch=1,
            grid=(chips,),
            in_specs=[block, block],
            out_specs=pl.BlockSpec((1, 2, rows, columns), lambda i, r: (i ^ (r[0] // 2), 0, 0, 0)),
        ),
        out_shape=jax.ShapeDtypeStruct((chips, 2, rows, columns), bf16),
        name="place",
    )(rank.reshape(1).astype(jnp.int32), mine, other)


def per_device(
    block_input,
    cotangent,
    doc_lengths,
    bank_choice,
    first_gain,
    first_shift,
    query_weight,
    query_bias,
    keyval_weight,
    value_bias,
    output_weight,
    output_bias,
    second_gain,
    second_shift,
    upward_weight,
    upward_bias,
    downward_weight,
    downward_bias,
    query_shrink,
    query_expand,
    keyval_shrink,
    keyval_expand,
    output_shrink,
    output_expand,
    upward_shrink,
    upward_expand,
    downward_shrink,
    downward_expand,
):
    section = lax.axis_index("section")
    data = lax.axis_index("dp")
    tensor = lax.axis_index("tensor")
    low_section = section == 0
    width = block_input.shape[2]
    rows = block_input.shape[1]
    ranks = lax.axis_size("tensor")
    span = rows * ranks
    head = value_bias.shape[1]
    local_q = query_bias.shape[1]
    local_f = upward_bias.shape[1]
    rank = query_expand.shape[2]
    banks = query_expand.shape[1]
    reach = WINDOW // span
    sides = [(0, 1), (1, 0)]

    def swap(value):
        return lax.ppermute(value, "section", sides)

    def by_layer(own, other):
        return jnp.where(low_section, own, other), jnp.where(low_section, other, own)

    def spread(block):
        parts = [block] + [around(block, "tensor", -j) for j in range(1, ranks)]
        return jnp.concatenate(parts, axis=0)

    def reduce_rows(partial):
        low = partial.astype(bf16)
        total = partial[:rows].astype(f32)
        for j in range(1, ranks):
            total = total + around(low[j * rows : (j + 1) * rows], "tensor", j).astype(f32)
        return total

    def chosen(table, bank, transpose):
        block = lax.dynamic_index_in_dim(table[0], bank, 0, keepdims=False)
        return block.T if transpose else block

    def early_pack(bank):
        return jnp.concatenate(
            [
                chosen(query_shrink, bank, True),
                chosen(keyval_shrink, bank, True),
                chosen(query_expand, bank, False),
                chosen(keyval_expand, bank, False),
            ],
            axis=1,
        )

    def late_pack(bank):
        return jnp.concatenate(
            [
                chosen(output_shrink, bank, True),
                chosen(output_expand, bank, False),
                chosen(upward_shrink, bank, True),
                chosen(upward_expand, bank, False),
                chosen(downward_shrink, bank, True),
                chosen(downward_expand, bank, False),
            ],
            axis=1,
        )

    own_bank = lax.dynamic_index_in_dim(bank_choice, section, 0, keepdims=False)
    other_bank = lax.dynamic_index_in_dim(bank_choice, 1 - section, 0, keepdims=False)

    vectors = jnp.concatenate(
        [
            first_gain,
            first_shift,
            query_bias,
            jnp.zeros_like(value_bias),
            value_bias,
            output_bias,
            second_gain,
            second_shift,
            upward_bias,
            downward_bias,
        ],
        axis=1,
    )
    vector_sizes = [width, width, local_q, 2 * head, width, width, width, local_f, width]

    both = ("section", "dp")
    shard_early = jnp.concatenate(
        [query_weight[0], keyval_weight[0], output_weight[0].T], axis=1
    )

    def mask_flip(block, mask):
        return lax.ppermute(block, both, [(i, i ^ mask) for i in range(2 * lax.axis_size("dp"))])

    pair_near = jnp.stack([shard_early, mask_flip(shard_early, 2)])
    pair_far = jnp.stack([mask_flip(shard_early, 16), mask_flip(shard_early, 18)])

    def early_table(pair):
        quad = jnp.concatenate([pair] + [mask_flip(pair, 4 * k) for k in range(1, 4)], axis=0)
        table = by_rank(data, quad, mask_flip(quad, 1))
        return table.reshape(width, -1)

    early_tables = [early_table(pair) for pair in by_layer(pair_near, pair_far)]
    vector_layers = by_layer(vectors, swap(vectors))
    early_layers = by_layer(early_pack(own_bank), swap(early_pack(other_bank)))
    late_layers = by_layer(late_pack(own_bank), swap(late_pack(other_bank)))
    half = local_f // 2
    shard_up = upward_weight[0]
    shard_down = downward_weight[0].T
    halves = [
        jnp.concatenate(
            [shard_up[:, h * half : (h + 1) * half], shard_down[:, h * half : (h + 1) * half]],
            axis=1,
        )
        for h in range(2)
    ]
    keep = jnp.where(low_section, halves[0], halves[1])
    gained = swap(jnp.where(low_section, halves[1], halves[0]))
    feed_zero, feed_one = by_layer(keep, gained)
    feed_zero = lax.all_gather(feed_zero, both, axis=0, tiled=True)
    feed_one = lax.all_gather(feed_one, both, axis=0, tiled=True)

    def split(table, sizes):
        cuts = [0]
        for size in sizes:
            cuts.append(cuts[-1] + size)
        return [table[:, a:b] for a, b in zip(cuts[:-1], cuts[1:])]

    wide = local_q + 2 * head
    weights = [
        split(early_tables[layer], [wide, local_q]) + [table]
        for layer, table in enumerate([feed_zero, feed_one])
    ]
    small = [
        [part.astype(f32) for part in split(vector_layers[layer], vector_sizes)]
        for layer in range(2)
    ]
    adapters = [
        split(early_layers[layer], [width, width, local_q, 2 * head])
        + split(late_layers[layer], [local_q, width, width, local_f, local_f, width])
        for layer in range(2)
    ]

    place = (
        ((tensor + jnp.arange(ranks, dtype=jnp.int32)) % ranks)[:, None] * rows
        + jnp.arange(rows, dtype=jnp.int32)[None, :]
    ).reshape(-1)
    query_place = data * span + place
    key_place = jnp.concatenate([(data - back) * span + place for back in range(reach, -1, -1)])
    lengths = lax.dynamic_index_in_dim(doc_lengths, section, 0, keepdims=False)
    ends = jnp.cumsum(lengths)
    query_doc = jnp.sum((query_place[:, None] >= ends[None, :]).astype(jnp.int32), axis=1)
    key_doc = jnp.sum((key_place[:, None] >= ends[None, :]).astype(jnp.int32), axis=1)
    distance = query_place[:, None] - key_place[None, :]
    allowed = (
        (key_place[None, :] >= 0)
        & (distance >= 0)
        & (distance < WINDOW)
        & (query_doc[:, None] == key_doc[None, :])
    )
    bias = jnp.where(allowed, 0.0, masked_score).astype(bf16)

    def forward(layer, hidden):
        qkv_w, out_w, feed_w = weights[layer]
        gain1, shift1, q_bias, kv_bias, out_bias, gain2, shift2, up_bias, down_bias = small[layer]
        sq, skv, eq, ekv, so, eo, su, eu, sd, ed = adapters[layer]
        unit1, rsd1 = norm_parts(hidden)
        normed = spread((unit1 * gain1 + shift1).astype(bf16))
        low_q = against(normed, sq).astype(bf16)
        low_kv = against(normed, skv).astype(bf16)
        both = plain(normed, qkv_w)
        keyval = (both[:, local_q:] + kv_bias + plain(low_kv, ekv)).astype(bf16)
        pieces = [along(keyval, "dp", back) for back in range(reach, 0, -1)] + [keyval]
        queries = (both[:, :local_q] + q_bias + plain(low_q, eq)).astype(bf16)
        key_block = jnp.concatenate(pieces, axis=0)
        probs, mixed = attend(queries, key_block, bias, head)
        low_o = against(mixed, so).astype(bf16)
        attended = reduce_rows(against(mixed, out_w) + plain(low_o, eo))
        middle = hidden + (attended + out_bias)
        unit2, rsd2 = norm_parts(middle)
        second = spread((unit2 * gain2 + shift2).astype(bf16))
        active, slope, low_u, low_d, partial = feed(second, feed_w, up_bias, eu, sd, su, ed)
        result = middle + (reduce_rows(partial) + down_bias)
        kept = (
            unit1,
            rsd1,
            normed,
            low_q,
            low_kv,
            queries,
            key_block,
            probs,
            mixed,
            low_o,
            unit2,
            rsd2,
            second,
            low_u,
            active,
            slope,
            low_d,
        )
        return result, kept

    def tiles(block):
        return block.reshape(rank, -1, 128).transpose(1, 0, 2)

    def flat(block):
        return block.transpose(1, 0, 2).reshape(rank, -1)

    def reduce_grads(shared, owned):
        pile = jnp.concatenate([tiles(part) for part in shared], axis=0).astype(bf16)
        lack = -pile.shape[0] % ranks
        if lack:
            pile = jnp.concatenate([pile, jnp.zeros((lack,) + pile.shape[1:], bf16)], axis=0)
        each = pile.shape[0] // ranks
        total = pick(pile, tensor * each, each).astype(f32)
        for j in range(1, ranks):
            block = pick(pile, ((tensor + j) % ranks) * each, each)
            total = total + around(block, "tensor", j).astype(f32)
        pile = jnp.concatenate([total] + [tiles(part) for part in owned], axis=0).astype(bf16)
        if pile.shape[0] % 2:
            pile = jnp.concatenate([pile, jnp.zeros((1,) + pile.shape[1:], bf16)], axis=0)
        half = pile.shape[0] // 2
        core = data % 2
        got = flipped(pick(pile, (1 - core) * half, half), "dp", 1)
        mine = (pick(pile, core * half, half).astype(f32) + got.astype(f32)).astype(bf16)
        got = flipped(mine, "dp", 2)
        mine = (mine.astype(f32) + got.astype(f32)).astype(bf16)
        parts = jnp.stack([mine] + [around(mine, "dp", 4 * k) for k in range(1, 4)])
        turn = data // 4
        total = sum(
            lax.dynamic_index_in_dim(parts, (turn - r) % 4, 0, keepdims=False).astype(f32)
            for r in range(4)
        )
        return total.astype(bf16)

    def to_upper(value):
        return lax.ppermute(value, "section", [(0, 1)])

    def to_lower(value):
        return lax.ppermute(value, "section", [(1, 0)])

    def offloaded_grads(shared, owned):
        pile = jnp.concatenate([tiles(part) for part in shared], axis=0).astype(bf16)
        lack = -pile.shape[0] % ranks
        pile = jnp.concatenate([pile, jnp.zeros((lack,) + pile.shape[1:], bf16)], axis=0)
        mine = lax.psum_scatter(pile, "tensor", scatter_dimension=0, tiled=True)
        pile = jnp.concatenate([mine] + [tiles(part).astype(bf16) for part in owned], axis=0)
        lack = -pile.shape[0] % lax.axis_size("dp")
        pile = jnp.concatenate([pile, jnp.zeros((lack,) + pile.shape[1:], bf16)], axis=0)
        mine = lax.psum_scatter(pile, "dp", scatter_dimension=0, tiled=True)
        pair = jnp.stack([to_upper(mine), mine], axis=1)
        pile = lax.all_gather(pair, "dp", axis=0, tiled=True)
        shared_sizes = [part.shape[1] for part in shared]
        each = -(-(sum(shared_sizes) // 128) // ranks)
        ordered = lax.all_gather(pile[:each], "tensor", axis=0, tiled=True)
        results, begin = [], 0
        for size in shared_sizes:
            count = size // 128
            results.append([flat(ordered[begin : begin + count, m]) for m in range(2)])
            begin += count
        begin, others = each, []
        for part in owned:
            count = part.shape[1] // 128
            others.append([flat(pile[begin : begin + count, m]) for m in range(2)])
            begin += count
        return results + others

    def spread_grads(mine, shared_sizes, owned_sizes):
        shared_count = sum(shared_sizes) // 128
        each = -(-shared_count // ranks)
        owned_count = sum(owned_sizes) // 128
        core = data % 2
        other = flipped(mine, "dp", 1)
        lower = jnp.where(core == 0, mine, other)
        upper = jnp.where(core == 0, other, mine)
        pile = jnp.concatenate([lower, upper], axis=1)
        own = pile[:, :each]
        parts = jnp.stack([own] + [around(own, "tensor", k) for k in range(1, ranks)])
        ordered = jnp.concatenate(
            [
                lax.dynamic_index_in_dim(parts, (tensor - r) % ranks, 0, keepdims=False)
                for r in range(ranks)
            ],
            axis=1,
        )
        results = []
        begin = 0
        for size in shared_sizes:
            count = size // 128
            results.append([flat(ordered[m, begin : begin + count]) for m in range(2)])
            begin += count
        begin = each
        owned = []
        for size in owned_sizes:
            count = size // 128
            owned.append([flat(pile[m, begin : begin + count]) for m in range(2)])
            begin += count
        return results, owned

    def backward_feed(layer, kept, grad):
        feed_w = weights[layer][2]
        gain2 = small[layer][5]
        su, eu, sd, ed = adapters[layer][6:]
        unit2, rsd2, second, low_u, active, slope, low_d = kept[10:]
        branch = spread(grad.astype(bf16))
        grad_up, inner_d, inner_u, partial = feed_back(branch, feed_w, slope, eu, sd, su, ed)
        grad_second = reduce_rows(partial)
        grad_middle = grad + norm_back(unit2, rsd2, grad_second * gain2)
        shared = [across(inner_u, second), across(low_d, branch)]
        owned = [across(low_u, grad_up), across(inner_d, active)]
        return grad_middle, shared, owned

    def backward_attend(layer, kept, grad_middle):
        qkv_w, out_w = weights[layer][:2]
        gain1 = small[layer][0]
        sq, skv, eq, ekv, so, eo = adapters[layer][:6]
        unit1, rsd1, normed, low_q, low_kv, queries, key_block, probs, mixed, low_o = kept[:10]
        branch = spread(grad_middle.astype(bf16))
        inner_o = against(branch, eo).astype(bf16)
        grad_mixed = (plain(branch, out_w) + plain(inner_o, so)).astype(bf16)
        grad_q, grad_block = attend_back(grad_mixed, probs, queries, key_block, head)
        own = grad_block[reach * span :].astype(f32)
        for back in range(1, reach + 1):
            begin = (reach - back) * span
            own = own + along(grad_block[begin : begin + span], "dp", -back).astype(f32)
        grad_kv = own.astype(bf16)
        inner_q = against(grad_q, eq).astype(bf16)
        inner_kv = against(grad_kv, ekv).astype(bf16)
        grad_normed = (
            against(grad_q, qkv_w[:, :local_q])
            + plain(inner_q, sq)
            + against(grad_kv, qkv_w[:, local_q:])
            + plain(inner_kv, skv)
        )
        grad_hidden = grad_middle + norm_back(unit1, rsd1, reduce_rows(grad_normed) * gain1)
        out_grads = ([across(low_o, branch)], [across(inner_o, mixed)])
        shared = [across(inner_q, normed), across(inner_kv, normed), across(low_kv, grad_kv)]
        owned = [across(low_q, grad_q)]
        return grad_hidden, out_grads, (shared, owned)

    fresh = lax.dynamic_index_in_dim(block_input, section, 0, keepdims=False).astype(f32)
    result_zero, kept_zero = forward(0, fresh)
    passed = result_zero.astype(bf16)
    result_one, kept_one = forward(1, passed.astype(f32))
    final = result_one.astype(bf16)

    given = lax.dynamic_index_in_dim(cotangent, section, 0, keepdims=False).astype(f32)
    grad_middle_one, feed_shared, feed_owned = backward_feed(1, kept_one, given)
    grad_one, out_one_grads, qkv_one_grads = backward_attend(1, kept_one, grad_middle_one)
    grads_one = offloaded_grads(
        feed_shared + out_one_grads[0] + qkv_one_grads[0],
        feed_owned + out_one_grads[1] + qkv_one_grads[1],
    )
    grad_middle_zero, feed_shared, feed_owned = backward_feed(0, kept_zero, grad_one)
    grad_zero, out_zero_grads, qkv_zero_grads = backward_attend(0, kept_zero, grad_middle_zero)
    shared = feed_shared + out_zero_grads[0] + qkv_zero_grads[0]
    owned = feed_owned + out_zero_grads[1] + qkv_zero_grads[1]
    mine = reduce_grads(shared, owned)
    grads_zero = spread_grads(
        jnp.stack([mine, to_lower(mine)]),
        [part.shape[1] for part in shared],
        [part.shape[1] for part in owned],
    )
    grads_zero = grads_zero[0] + grads_zero[1]

    def both_micros(zero, one):
        received = jnp.where(low_section, to_lower(zero), to_upper(one))
        own = jnp.where(low_section, zero, one)
        return jnp.where(
            low_section, jnp.stack([own, received]), jnp.stack([received, own])
        )

    section_outputs = both_micros(passed, final)
    received = jnp.where(
        low_section, to_lower(grad_zero.astype(bf16)), to_upper(grad_one.astype(bf16))
    ).astype(f32)
    own = jnp.where(low_section, grad_zero, grad_one)
    input_grads = jnp.where(
        low_section, jnp.stack([own, received]), jnp.stack([received, own])
    )

    onehot = (bank_choice[:, None] == jnp.arange(banks)[None, :]).astype(f32)

    def placed(pair, transpose):
        out = sum(
            onehot[m][:, None, None] * pair[m].astype(f32)[None] for m in range(2)
        )
        return (out.transpose(0, 2, 1) if transpose else out)[None]

    (
        up_shrink_grad,
        down_expand_grad,
        out_expand_grad,
        q_shrink_grad,
        kv_shrink_grad,
        kv_expand_grad,
        up_expand_grad,
        down_shrink_grad,
        out_shrink_grad,
        q_expand_grad,
    ) = [
        [jnp.where(low_section, zero[m], one[m]) for m in range(2)]
        for zero, one in zip(grads_zero, grads_one)
    ]
    return (
        section_outputs[None],
        input_grads[None],
        placed(q_shrink_grad, True),
        placed(q_expand_grad, False),
        placed(kv_shrink_grad, True),
        placed(kv_expand_grad, False),
        placed(out_shrink_grad, True),
        placed(out_expand_grad, False),
        placed(up_shrink_grad, True),
        placed(up_expand_grad, False),
        placed(down_shrink_grad, True),
        placed(down_expand_grad, False),
    )


def solution(mesh):
    return jax.shard_map(
        per_device,
        mesh=mesh,
        in_specs=(
            P(None, ("dp", "tensor"), None),
            P(None, ("dp", "tensor"), None),
            P(),
            P(),
            P("section", None),
            P("section", None),
            P("section", "dp", "tensor"),
            P("section", "tensor"),
            P("section", "dp", None),
            P("section", None),
            P("section", "tensor", "dp"),
            P("section", None),
            P("section", None),
            P("section", None),
            P("section", "dp", "tensor"),
            P("section", "tensor"),
            P("section", "tensor", "dp"),
            P("section", None),
            P("section", None, None, None),
            P("section", None, None, "tensor"),
            P("section", None, None, None),
            P("section", None, None, None),
            P("section", None, "tensor", None),
            P("section", None, None, None),
            P("section", None, None, None),
            P("section", None, None, "tensor"),
            P("section", None, "tensor", None),
            P("section", None, None, None),
        ),
        out_specs=(
            P("section", None, ("dp", "tensor"), None),
            P("section", None, ("dp", "tensor"), None),
            P("section", None, None, None),
            P("section", None, None, "tensor"),
            P("section", None, None, None),
            P("section", None, None, None),
            P("section", None, "tensor", None),
            P("section", None, None, None),
            P("section", None, None, None),
            P("section", None, None, "tensor"),
            P("section", None, "tensor", None),
            P("section", None, None, None),
        ),
        check_vma=False,
    )
```

```python
import math

import jax
import jax.numpy as jnp
from jax import lax
from jax.experimental import pallas as pl
from jax.experimental.pallas import tpu as pltpu
from jax.sharding import PartitionSpec as P

WINDOW = 1024
epsilon = 1e-05
masked_score = -1e30
bf16 = jnp.bfloat16
f32 = jnp.float32


def plain(left, right):
    return jnp.dot(left, right, preferred_element_type=f32)


def against(left, right):
    return lax.dot_general(left, right, (((1,), (1,)), ((), ())), preferred_element_type=f32)


def across(left, right):
    return lax.dot_general(left, right, (((0,), (0,)), ((), ())), preferred_element_type=f32)


def around(block, axis, distance):
    size = lax.axis_size(axis)
    return lax.ppermute(block, axis, [(i, (i + distance) % size) for i in range(size)])


def along(block, axis, distance):
    size = lax.axis_size(axis)
    route = [(i, i + distance) for i in range(size) if 0 <= i + distance < size]
    return lax.ppermute(block, axis, route)


def flipped(block, axis, bit):
    size = lax.axis_size(axis)
    return lax.ppermute(block, axis, [(i, i ^ bit) for i in range(size)])


def pick(table, index, size=1):
    return lax.dynamic_slice_in_dim(table, index, size, 0)


def norm_parts(value):
    centred = value - jnp.mean(value, axis=-1, keepdims=True)
    spread = lax.rsqrt(jnp.mean(centred * centred, axis=-1, keepdims=True) + epsilon)
    return centred * spread, spread


def norm_back(unit, spread, scaled):
    inner = jnp.mean(scaled * unit, axis=-1, keepdims=True)
    return spread * (scaled - jnp.mean(scaled, axis=-1, keepdims=True) - unit * inner)


def gelu_parts(value):
    rate = math.sqrt(2.0 / math.pi)
    square = value * value
    bend = jnp.tanh(rate * (value + 0.044715 * value * square))
    rising = 0.5 * (1.0 + bend)
    slope = rising + 0.5 * value * (1.0 - bend * bend) * (rate * (1.0 + 3 * 0.044715 * square))
    return value * rising, slope


def attend_kernel(scale, query_ref, keyval_ref, bias_ref, prob_ref, mixed_ref):
    head = query_ref.shape[1]
    scores = against(query_ref[...], keyval_ref[:, :head]) * scale + bias_ref[...].astype(f32)
    top = jnp.max(scores, axis=-1, keepdims=True)
    lifted = jnp.exp(scores - top)
    total = jnp.sum(lifted, axis=-1, keepdims=True)
    probs = lifted * (1.0 / total)
    prob_ref[0] = probs
    mixed_ref[...] = plain(probs.astype(bf16), keyval_ref[:, head:]).astype(bf16)


def attend(queries, key_block, bias, head):
    rows, width = queries.shape
    keys = key_block.shape[0]
    heads = width // head
    whole = lambda shape: pl.BlockSpec(shape, lambda h: (0, 0))
    column = pl.BlockSpec((rows, head), lambda h: (0, h))
    return pl.pallas_call(
        lambda *refs: attend_kernel(1.0 / math.sqrt(head), *refs),
        grid=(heads,),
        in_specs=[column, whole((keys, 2 * head)), whole((rows, keys))],
        out_specs=[pl.BlockSpec((1, rows, keys), lambda h: (h, 0, 0)), column],
        out_shape=[
            jax.ShapeDtypeStruct((heads, rows, keys), f32),
            jax.ShapeDtypeStruct((rows, width), bf16),
        ],
        compiler_params=pltpu.CompilerParams(vmem_limit_bytes=40 * 2**20),
        name="attend",
    )(queries, key_block, bias)


def attend_back_kernel(
    scale, grad_ref, prob_ref, query_ref, keyval_ref, dq_ref, dkv_ref, key_sum, value_sum
):
    step = pl.program_id(0)
    head = query_ref.shape[1]
    grad = grad_ref[...]
    probs = prob_ref[0]
    grad_probs = against(grad, keyval_ref[:, head:])
    delta = jnp.sum(grad_probs * probs, axis=-1, keepdims=True)
    grad_scores = (probs * (grad_probs - delta)).astype(bf16)
    dq_ref[...] = (plain(grad_scores, keyval_ref[:, :head]) * scale).astype(bf16)
    keys = across(grad_scores, query_ref[...])
    values = across(probs.astype(bf16), grad)

    @pl.when(step == 0)
    def _():
        key_sum[...] = keys
        value_sum[...] = values

    @pl.when(step > 0)
    def _():
        key_sum[...] += keys
        value_sum[...] += values

    @pl.when(step == pl.num_programs(0) - 1)
    def _():
        dkv_ref[:, :head] = (key_sum[...] * scale).astype(bf16)
        dkv_ref[:, head:] = value_sum[...].astype(bf16)


def attend_back(grad_mixed, probs, queries, key_block, head):
    rows, width = queries.shape
    keys = key_block.shape[0]
    heads = width // head
    column = pl.BlockSpec((rows, head), lambda h: (0, h))
    whole = pl.BlockSpec((keys, 2 * head), lambda h: (0, 0))
    return pl.pallas_call(
        lambda *refs: attend_back_kernel(1.0 / math.sqrt(head), *refs),
        grid=(heads,),
        in_specs=[
            column,
            pl.BlockSpec((1, rows, keys), lambda h: (h, 0, 0)),
            column,
            whole,
        ],
        out_specs=[column, whole],
        out_shape=[
            jax.ShapeDtypeStruct((rows, width), bf16),
            jax.ShapeDtypeStruct((keys, 2 * head), bf16),
        ],
        scratch_shapes=[pltpu.VMEM((keys, head), f32), pltpu.VMEM((keys, head), f32)],
        compiler_params=pltpu.CompilerParams(vmem_limit_bytes=40 * 2**20),
        name="attend_back",
    )(grad_mixed, probs, queries, key_block)


def weight_tile(table_ref, hidden, tile, j, second):
    width = table_ref.shape[0] // 2
    half = hidden // 2
    row = j * tile // half * width
    column = j * tile % half + second * half
    return table_ref[row : row + width, column : column + tile]


def feed_kernel(
    tile, second_ref, table_ref, bias_ref, eu_ref, sd_ref, su_ref, ed_ref,
    active_ref, slope_ref, low_u_ref, low_d_ref, out_ref, total,
):
    hidden = eu_ref.shape[1]
    count = hidden // tile
    second = second_ref[...]
    low_u = against(second, su_ref[...]).astype(bf16)
    low_u_ref[...] = low_u
    low = 0.0
    for j in range(count):
        columns = pl.ds(j * tile, tile)
        upward = plain(second, weight_tile(table_ref, hidden, tile, j, 0))
        upward = upward + plain(low_u, eu_ref[:, columns]) + bias_ref[:, columns]
        active, slope = gelu_parts(upward)
        active = active.astype(bf16)
        active_ref[:, columns] = active
        slope_ref[:, columns] = slope.astype(bf16)
        low = low + against(active, sd_ref[:, columns])
        part = against(active, weight_tile(table_ref, hidden, tile, j, 1))
        if j == 0:
            total[...] = part
        elif j < count - 1:
            total[...] += part
    low_d = low.astype(bf16)
    low_d_ref[...] = low_d
    out_ref[...] = (total[...] + part + plain(low_d, ed_ref[...])).astype(bf16)


def feed_limit(table):
    return table.size * 2 + 12 * 2**20


def feed(second, table, bias, eu, sd, su, ed):
    rows, width = second.shape
    rank, hidden = eu.shape
    held = pl.BlockSpec(memory_space=pltpu.VMEM)
    return pl.pallas_call(
        lambda *refs: feed_kernel(512, *refs),
        in_specs=[held] * 7,
        out_specs=[held] * 5,
        out_shape=[
            jax.ShapeDtypeStruct((rows, hidden), bf16),
            jax.ShapeDtypeStruct((rows, hidden), bf16),
            jax.ShapeDtypeStruct((rows, rank), bf16),
            jax.ShapeDtypeStruct((rows, rank), bf16),
            jax.ShapeDtypeStruct((rows, width), bf16),
        ],
        scratch_shapes=[pltpu.VMEM((rows, width), f32)],
        compiler_params=pltpu.CompilerParams(vmem_limit_bytes=feed_limit(table)),
        cost_estimate=pl.CostEstimate(
            flops=4 * rows * width * hidden,
            bytes_accessed=4 * width * hidden + 8 * rows * hidden,
            transcendentals=rows * hidden,
        ),
        name="feed",
    )(second, table, bias, eu, sd, su, ed)


def feed_back_kernel(
    tile, branch_ref, table_ref, slope_ref, eu_ref, sd_ref, su_ref, ed_ref,
    grad_up_ref, inner_d_ref, inner_u_ref, out_ref, total,
):
    hidden = eu_ref.shape[1]
    count = hidden // tile
    branch = branch_ref[...]
    inner_d = against(branch, ed_ref[...]).astype(bf16)
    inner_d_ref[...] = inner_d
    inner = 0.0
    for j in range(count):
        columns = pl.ds(j * tile, tile)
        grad = plain(branch, weight_tile(table_ref, hidden, tile, j, 1))
        grad = grad + plain(inner_d, sd_ref[:, columns])
        grad = (grad * slope_ref[:, columns].astype(f32)).astype(bf16)
        grad_up_ref[:, columns] = grad
        inner = inner + against(grad, eu_ref[:, columns])
        part = against(grad, weight_tile(table_ref, hidden, tile, j, 0))
        if j == 0:
            total[...] = part
        elif j < count - 1:
            total[...] += part
    inner_u = inner.astype(bf16)
    inner_u_ref[...] = inner_u
    out_ref[...] = (total[...] + part + plain(inner_u, su_ref[...])).astype(bf16)


def feed_back(branch, table, slope, eu, sd, su, ed):
    rows, width = branch.shape
    rank, hidden = eu.shape
    held = pl.BlockSpec(memory_space=pltpu.VMEM)
    return pl.pallas_call(
        lambda *refs: feed_back_kernel(512, *refs),
        in_specs=[held] * 7,
        out_specs=[held] * 4,
        out_shape=[
            jax.ShapeDtypeStruct((rows, hidden), bf16),
            jax.ShapeDtypeStruct((rows, rank), bf16),
            jax.ShapeDtypeStruct((rows, rank), bf16),
            jax.ShapeDtypeStruct((rows, width), bf16),
        ],
        scratch_shapes=[pltpu.VMEM((rows, width), f32)],
        compiler_params=pltpu.CompilerParams(vmem_limit_bytes=feed_limit(table)),
        cost_estimate=pl.CostEstimate(
            flops=4 * rows * width * hidden,
            bytes_accessed=4 * width * hidden + 4 * rows * hidden,
            transcendentals=0,
        ),
        name="feed_back",
    )(branch, table, slope, eu, sd, su, ed)


def per_device(
    block_input,
    cotangent,
    doc_lengths,
    bank_choice,
    first_gain,
    first_shift,
    query_weight,
    query_bias,
    keyval_weight,
    value_bias,
    output_weight,
    output_bias,
    second_gain,
    second_shift,
    upward_weight,
    upward_bias,
    downward_weight,
    downward_bias,
    query_shrink,
    query_expand,
    keyval_shrink,
    keyval_expand,
    output_shrink,
    output_expand,
    upward_shrink,
    upward_expand,
    downward_shrink,
    downward_expand,
):
    section = lax.axis_index("section")
    data = lax.axis_index("dp")
    tensor = lax.axis_index("tensor")
    low_section = section == 0
    width = block_input.shape[2]
    rows = block_input.shape[1]
    ranks = lax.axis_size("tensor")
    span = rows * ranks
    head = value_bias.shape[1]
    local_q = query_bias.shape[1]
    local_f = upward_bias.shape[1]
    rank = query_expand.shape[2]
    banks = query_expand.shape[1]
    reach = WINDOW // span
    sides = [(0, 1), (1, 0)]

    def swap(value):
        return lax.ppermute(value, "section", sides)

    def by_layer(own, other):
        return jnp.where(low_section, own, other), jnp.where(low_section, other, own)

    def spread(block):
        parts = [block] + [around(block, "tensor", -j) for j in range(1, ranks)]
        return jnp.concatenate(parts, axis=0)

    def reduce_rows(partial):
        low = partial.astype(bf16)
        total = partial[:rows].astype(f32)
        for j in range(1, ranks):
            total = total + around(low[j * rows : (j + 1) * rows], "tensor", j).astype(f32)
        return total

    def chosen(table, bank, transpose):
        block = lax.dynamic_index_in_dim(table[0], bank, 0, keepdims=False)
        return block.T if transpose else block

    def early_pack(bank):
        return jnp.concatenate(
            [
                chosen(query_shrink, bank, True),
                chosen(keyval_shrink, bank, True),
                chosen(query_expand, bank, False),
                chosen(keyval_expand, bank, False),
            ],
            axis=1,
        )

    def late_pack(bank):
        return jnp.concatenate(
            [
                chosen(output_shrink, bank, True),
                chosen(output_expand, bank, False),
                chosen(upward_shrink, bank, True),
                chosen(upward_expand, bank, False),
                chosen(downward_shrink, bank, True),
                chosen(downward_expand, bank, False),
            ],
            axis=1,
        )

    own_bank = lax.dynamic_index_in_dim(bank_choice, section, 0, keepdims=False)
    other_bank = lax.dynamic_index_in_dim(bank_choice, 1 - section, 0, keepdims=False)

    vectors = jnp.concatenate(
        [
            first_gain,
            first_shift,
            query_bias,
            jnp.zeros_like(value_bias),
            value_bias,
            output_bias,
            second_gain,
            second_shift,
            upward_bias,
            downward_bias,
        ],
        axis=1,
    )
    vector_sizes = [width, width, local_q, 2 * head, width, width, width, local_f, width]

    both = ("section", "dp")

    def gather(shard, axes):
        return lax.all_gather(shard, axes, axis=0, tiled=True)

    def halves(shard):
        cut = shard.shape[1] // 2
        return shard[:, :cut], shard[:, cut:]

    shard_early = jnp.concatenate(
        [query_weight[0], keyval_weight[0], output_weight[0].T], axis=1
    )
    early_zero = gather(jnp.where(low_section, shard_early, swap(shard_early)), "dp")
    vector_layers = by_layer(vectors, swap(vectors))
    early_layers = by_layer(early_pack(own_bank), swap(early_pack(other_bank)))
    late_layers = by_layer(late_pack(own_bank), swap(late_pack(other_bank)))
    up_halves = halves(upward_weight[0])
    down_halves = halves(downward_weight[0].T)
    early_halves = halves(shard_early)
    side = [
        jnp.concatenate([up_halves[h], down_halves[h], early_halves[h]], axis=1) for h in range(2)
    ]
    keep = jnp.where(low_section, side[0], side[1])
    gained = swap(jnp.where(low_section, side[1], side[0]))
    side_zero, side_one = by_layer(keep, gained)
    feed_zero = gather(
        jnp.concatenate([side_zero[:, :local_f], side_one[:, local_f:]], axis=1), both
    )
    feed_one = gather(side_one[:, :local_f], both)
    early_one = jnp.concatenate([feed_zero[:width, local_f:], feed_zero[width:, local_f:]], axis=1)

    def split(table, sizes):
        cuts = [0]
        for size in sizes:
            cuts.append(cuts[-1] + size)
        return [table[:, a:b] for a, b in zip(cuts[:-1], cuts[1:])]

    wide = local_q + 2 * head
    weights = [
        split(early, [wide, local_q]) + [table]
        for early, table in [(early_zero, feed_zero), (early_one, feed_one)]
    ]
    small = [
        [part.astype(f32) for part in split(vector_layers[layer], vector_sizes)]
        for layer in range(2)
    ]
    adapters = [
        split(early_layers[layer], [width, width, local_q, 2 * head])
        + split(late_layers[layer], [local_q, width, width, local_f, local_f, width])
        for layer in range(2)
    ]

    place = (
        ((tensor + jnp.arange(ranks, dtype=jnp.int32)) % ranks)[:, None] * rows
        + jnp.arange(rows, dtype=jnp.int32)[None, :]
    ).reshape(-1)
    query_place = data * span + place
    key_place = jnp.concatenate([(data - back) * span + place for back in range(reach, -1, -1)])
    lengths = lax.dynamic_index_in_dim(doc_lengths, section, 0, keepdims=False)
    ends = jnp.cumsum(lengths)
    query_doc = jnp.sum((query_place[:, None] >= ends[None, :]).astype(jnp.int32), axis=1)
    key_doc = jnp.sum((key_place[:, None] >= ends[None, :]).astype(jnp.int32), axis=1)
    distance = query_place[:, None] - key_place[None, :]
    allowed = (
        (key_place[None, :] >= 0)
        & (distance >= 0)
        & (distance < WINDOW)
        & (query_doc[:, None] == key_doc[None, :])
    )
    bias = jnp.where(allowed, 0.0, masked_score).astype(bf16)

    def forward(layer, hidden):
        qkv_w, out_w, feed_w = weights[layer]
        gain1, shift1, q_bias, kv_bias, out_bias, gain2, shift2, up_bias, down_bias = small[layer]
        sq, skv, eq, ekv, so, eo, su, eu, sd, ed = adapters[layer]
        unit1, rsd1 = norm_parts(hidden)
        normed = spread((unit1 * gain1 + shift1).astype(bf16))
        low_q = against(normed, sq).astype(bf16)
        low_kv = against(normed, skv).astype(bf16)
        both = plain(normed, qkv_w)
        keyval = (both[:, local_q:] + kv_bias + plain(low_kv, ekv)).astype(bf16)
        pieces = [along(keyval, "dp", back) for back in range(reach, 0, -1)] + [keyval]
        queries = (both[:, :local_q] + q_bias + plain(low_q, eq)).astype(bf16)
        key_block = jnp.concatenate(pieces, axis=0)
        probs, mixed = attend(queries, key_block, bias, head)
        low_o = against(mixed, so).astype(bf16)
        attended = reduce_rows(against(mixed, out_w) + plain(low_o, eo))
        middle = hidden + (attended + out_bias)
        unit2, rsd2 = norm_parts(middle)
        second = spread((unit2 * gain2 + shift2).astype(bf16))
        active, slope, low_u, low_d, partial = feed(second, feed_w, up_bias, eu, sd, su, ed)
        result = middle + (reduce_rows(partial) + down_bias)
        kept = (
            unit1,
            rsd1,
            normed,
            low_q,
            low_kv,
            queries,
            key_block,
            probs,
            mixed,
            low_o,
            unit2,
            rsd2,
            second,
            low_u,
            active,
            slope,
            low_d,
        )
        return result, kept

    def tiles(block):
        return block.reshape(rank, -1, 128).transpose(1, 0, 2)

    def flat(block):
        return block.transpose(1, 0, 2).reshape(rank, -1)

    chips = lax.axis_size("dp") // 4
    turn, plane, core = data // 4, data // 2 % 2, data % 2

    def padded(pile, multiple):
        lack = -pile.shape[0] % multiple
        if not lack:
            return pile
        return jnp.concatenate([pile, jnp.zeros((lack,) + pile.shape[1:], pile.dtype)], axis=0)

    def piled(shared):
        return padded(jnp.concatenate([tiles(part) for part in shared], axis=0).astype(bf16), ranks)

    def owned_pile(mine, owned):
        pile = jnp.concatenate([mine] + [tiles(part) for part in owned], axis=0).astype(bf16)
        return padded(pile, lax.axis_size("dp"))

    def at(block, index, axis):
        return lax.dynamic_index_in_dim(block, index, axis, keepdims=False)

    def offloaded_grads(shared, owned):
        mine = lax.psum_scatter(piled(shared), "tensor", scatter_dimension=0, tiled=True)
        return lax.psum_scatter(owned_pile(mine, owned), "dp", scatter_dimension=0, tiled=True)

    def scattered_grads(shared, owned):
        pile = piled(shared)
        each = pile.shape[0] // ranks
        mine = pick(pile, tensor * each, each).astype(f32)
        for j in range(1, ranks):
            block = pick(pile, ((tensor + j) % ranks) * each, each)
            mine = mine + around(block, "tensor", j).astype(f32)
        pile = owned_pile(mine, owned)
        pile = pile.reshape((chips, 2, 2, -1) + pile.shape[1:])
        got = flipped(at(pile, 1 - core, 2), "dp", 1)
        pile = (at(pile, core, 2).astype(f32) + got.astype(f32)).astype(bf16)
        got = flipped(at(pile, 1 - plane, 1), "dp", 2)
        pile = (at(pile, plane, 1).astype(f32) + got.astype(f32)).astype(bf16)
        mine = at(pile, turn, 0).astype(f32)
        for k in range(1, chips):
            mine = mine + flipped(at(pile, turn ^ k, 0), "dp", 4 * k).astype(f32)
        return mine.astype(bf16)

    def spread_grads(pair, shared_sizes, owned_sizes):
        parts = jnp.stack([pair] + [flipped(pair, "dp", 4 * k) for k in range(1, chips)])
        parts = jnp.stack([at(parts, turn ^ k, 0) for k in range(chips)])
        other = flipped(parts, "dp", 2)
        parts = jnp.stack(
            [jnp.where(plane == 0, parts, other), jnp.where(plane == 0, other, parts)], axis=1
        )
        other = flipped(parts, "dp", 1)
        parts = jnp.stack(
            [jnp.where(core == 0, parts, other), jnp.where(core == 0, other, parts)], axis=2
        )
        pile = jnp.moveaxis(parts, 3, 0).reshape((2, -1) + parts.shape[5:])
        each = -(-(sum(shared_sizes) // 128) // ranks)
        own = pile[:, :each]
        parts = jnp.stack([own] + [around(own, "tensor", k) for k in range(1, ranks)])
        ordered = jnp.concatenate([at(parts, (tensor - r) % ranks, 0) for r in range(ranks)], axis=1)
        results = []
        for whole, begin, sizes in [(ordered, 0, shared_sizes), (pile, each, owned_sizes)]:
            for size in sizes:
                count = size // 128
                results.append([flat(whole[m, begin : begin + count]) for m in range(2)])
                begin += count
        return results

    def backward_feed(layer, kept, grad):
        feed_w = weights[layer][2]
        gain2 = small[layer][5]
        su, eu, sd, ed = adapters[layer][6:]
        unit2, rsd2, second, low_u, active, slope, low_d = kept[10:]
        branch = spread(grad.astype(bf16))
        grad_up, inner_d, inner_u, partial = feed_back(branch, feed_w, slope, eu, sd, su, ed)
        grad_second = reduce_rows(partial)
        grad_middle = grad + norm_back(unit2, rsd2, grad_second * gain2)
        shared = [across(inner_u, second), across(low_d, branch)]
        owned = [across(low_u, grad_up), across(inner_d, active)]
        return grad_middle, shared, owned

    def backward_attend(layer, kept, grad_middle):
        qkv_w, out_w = weights[layer][:2]
        gain1 = small[layer][0]
        sq, skv, eq, ekv, so, eo = adapters[layer][:6]
        unit1, rsd1, normed, low_q, low_kv, queries, key_block, probs, mixed, low_o = kept[:10]
        branch = spread(grad_middle.astype(bf16))
        inner_o = against(branch, eo).astype(bf16)
        grad_mixed = (plain(branch, out_w) + plain(inner_o, so)).astype(bf16)
        grad_q, grad_block = attend_back(grad_mixed, probs, queries, key_block, head)
        own = grad_block[reach * span :].astype(f32)
        for back in range(1, reach + 1):
            begin = (reach - back) * span
            own = own + along(grad_block[begin : begin + span], "dp", -back).astype(f32)
        grad_kv = own.astype(bf16)
        inner_q = against(grad_q, eq).astype(bf16)
        inner_kv = against(grad_kv, ekv).astype(bf16)
        grad_normed = (
            against(grad_q, qkv_w[:, :local_q])
            + plain(inner_q, sq)
            + against(grad_kv, qkv_w[:, local_q:])
            + plain(inner_kv, skv)
        )
        grad_hidden = grad_middle + norm_back(unit1, rsd1, reduce_rows(grad_normed) * gain1)
        out_grads = ([across(low_o, branch)], [across(inner_o, mixed)])
        shared = [across(inner_q, normed), across(inner_kv, normed), across(low_kv, grad_kv)]
        owned = [across(low_q, grad_q)]
        return grad_hidden, out_grads, (shared, owned)

    fresh = lax.dynamic_index_in_dim(block_input, section, 0, keepdims=False).astype(f32)
    result_zero, kept_zero = forward(0, fresh)
    passed = result_zero.astype(bf16)
    result_one, kept_one = forward(1, passed.astype(f32))
    final = result_one.astype(bf16)

    given = lax.dynamic_index_in_dim(cotangent, section, 0, keepdims=False).astype(f32)
    grad_middle_one, feed_shared, feed_owned = backward_feed(1, kept_one, given)
    grad_one, out_one_grads, qkv_one_grads = backward_attend(1, kept_one, grad_middle_one)
    mine_one = offloaded_grads(
        feed_shared + out_one_grads[0] + qkv_one_grads[0],
        feed_owned + out_one_grads[1] + qkv_one_grads[1],
    )
    grad_middle_zero, feed_shared, feed_owned = backward_feed(0, kept_zero, grad_one)
    grad_zero, out_zero_grads, qkv_zero_grads = backward_attend(0, kept_zero, grad_middle_zero)
    shared = feed_shared + out_zero_grads[0] + qkv_zero_grads[0]
    owned = feed_owned + out_zero_grads[1] + qkv_zero_grads[1]
    mine_zero = scattered_grads(shared, owned)
    received = swap(jnp.where(low_section, mine_one, mine_zero))
    pair = jnp.where(
        low_section, jnp.stack([mine_zero, received]), jnp.stack([received, mine_one])
    )
    grads = spread_grads(
        pair, [part.shape[1] for part in shared], [part.shape[1] for part in owned]
    )

    def to_upper(value):
        return lax.ppermute(value, "section", [(0, 1)])

    def to_lower(value):
        return lax.ppermute(value, "section", [(1, 0)])

    def both_micros(zero, one):
        received = jnp.where(low_section, to_lower(zero), to_upper(one))
        own = jnp.where(low_section, zero, one)
        return jnp.where(
            low_section, jnp.stack([own, received]), jnp.stack([received, own])
        )

    section_outputs = both_micros(passed, final)
    received = jnp.where(
        low_section, to_lower(grad_zero.astype(bf16)), to_upper(grad_one.astype(bf16))
    ).astype(f32)
    own = jnp.where(low_section, grad_zero, grad_one)
    input_grads = jnp.where(
        low_section, jnp.stack([own, received]), jnp.stack([received, own])
    )

    onehot = (bank_choice[:, None] == jnp.arange(banks)[None, :]).astype(f32)

    def placed(pair, transpose):
        out = sum(
            onehot[m][:, None, None] * pair[m].astype(f32)[None] for m in range(2)
        )
        return (out.transpose(0, 2, 1) if transpose else out)[None]

    (
        up_shrink_grad,
        down_expand_grad,
        out_expand_grad,
        q_shrink_grad,
        kv_shrink_grad,
        kv_expand_grad,
        up_expand_grad,
        down_shrink_grad,
        out_shrink_grad,
        q_expand_grad,
    ) = grads
    return (
        section_outputs[None],
        input_grads[None],
        placed(q_shrink_grad, True),
        placed(q_expand_grad, False),
        placed(kv_shrink_grad, True),
        placed(kv_expand_grad, False),
        placed(out_shrink_grad, True),
        placed(out_expand_grad, False),
        placed(up_shrink_grad, True),
        placed(up_expand_grad, False),
        placed(down_shrink_grad, True),
        placed(down_expand_grad, False),
    )


def solution(mesh):
    return jax.shard_map(
        per_device,
        mesh=mesh,
        in_specs=(
            P(None, ("dp", "tensor"), None),
            P(None, ("dp", "tensor"), None),
            P(),
            P(),
            P("section", None),
            P("section", None),
            P("section", "dp", "tensor"),
            P("section", "tensor"),
            P("section", "dp", None),
            P("section", None),
            P("section", "tensor", "dp"),
            P("section", None),
            P("section", None),
            P("section", None),
            P("section", "dp", "tensor"),
            P("section", "tensor"),
            P("section", "tensor", "dp"),
            P("section", None),
            P("section", None, None, None),
            P("section", None, None, "tensor"),
            P("section", None, None, None),
            P("section", None, None, None),
            P("section", None, "tensor", None),
            P("section", None, None, None),
            P("section", None, None, None),
            P("section", None, None, "tensor"),
            P("section", None, "tensor", None),
            P("section", None, None, None),
        ),
        out_specs=(
            P("section", None, ("dp", "tensor"), None),
            P("section", None, ("dp", "tensor"), None),
            P("section", None, None, None),
            P("section", None, None, "tensor"),
            P("section", None, None, None),
            P("section", None, None, None),
            P("section", None, "tensor", None),
            P("section", None, None, None),
            P("section", None, None, None),
            P("section", None, None, "tensor"),
            P("section", None, "tensor", None),
            P("section", None, None, None),
        ),
        check_vma=False,
    )
```

```python
import math

import jax
import jax.numpy as jnp
from jax import lax
from jax.experimental import pallas as pl
from jax.experimental.pallas import tpu as pltpu
from jax.sharding import PartitionSpec as P

WINDOW = 1024
epsilon = 1e-05
masked_score = -1e30
bf16 = jnp.bfloat16
f32 = jnp.float32


def plain(left, right):
    return jnp.dot(left, right, preferred_element_type=f32)


def against(left, right):
    return lax.dot_general(left, right, (((1,), (1,)), ((), ())), preferred_element_type=f32)


def across(left, right):
    return lax.dot_general(left, right, (((0,), (0,)), ((), ())), preferred_element_type=f32)


def around(block, axis, distance):
    size = lax.axis_size(axis)
    return lax.ppermute(block, axis, [(i, (i + distance) % size) for i in range(size)])


def along(block, axis, distance):
    size = lax.axis_size(axis)
    route = [(i, i + distance) for i in range(size) if 0 <= i + distance < size]
    return lax.ppermute(block, axis, route)


def flipped(block, axis, bit):
    size = lax.axis_size(axis)
    return lax.ppermute(block, axis, [(i, i ^ bit) for i in range(size)])


def pick(table, index, size=1):
    return lax.dynamic_slice_in_dim(table, index, size, 0)


def norm_parts(value):
    centred = value - jnp.mean(value, axis=-1, keepdims=True)
    spread = lax.rsqrt(jnp.mean(centred * centred, axis=-1, keepdims=True) + epsilon)
    return centred * spread, spread


def norm_back(unit, spread, scaled):
    inner = jnp.mean(scaled * unit, axis=-1, keepdims=True)
    return spread * (scaled - jnp.mean(scaled, axis=-1, keepdims=True) - unit * inner)


def gelu_parts(value):
    rate = math.sqrt(2.0 / math.pi)
    square = value * value
    bend = jnp.tanh(rate * (value + 0.044715 * value * square))
    rising = 0.5 * (1.0 + bend)
    slope = rising + 0.5 * value * (1.0 - bend * bend) * (rate * (1.0 + 3 * 0.044715 * square))
    return value * rising, slope


def attend_kernel(
    head, query_ref, keyval_ref, bias_ref, out_ref, so_ref, eo_ref,
    prob_ref, mixed_ref, low_ref, part_ref,
):
    scale = 1.0 / math.sqrt(head)
    bias = bias_ref[...].astype(f32)
    for h in range(query_ref.shape[1] // head):
        columns = pl.ds(h * head, head)
        scores = against(query_ref[:, columns], keyval_ref[:, :head]) * scale + bias
        lifted = jnp.exp(scores - jnp.max(scores, axis=-1, keepdims=True))
        probs = lifted * (1.0 / jnp.sum(lifted, axis=-1, keepdims=True))
        prob_ref[h] = probs
        mixed_ref[:, columns] = plain(probs.astype(bf16), keyval_ref[:, head:]).astype(bf16)
    mixed = mixed_ref[...]
    low = against(mixed, so_ref[...]).astype(bf16)
    low_ref[...] = low
    part_ref[...] = (against(mixed, out_ref[...]) + plain(low, eo_ref[...])).astype(bf16)


def attend(queries, key_block, bias, out_w, so, eo, head):
    rows, width = queries.shape
    keys = key_block.shape[0]
    heads = width // head
    rank = so.shape[0]
    model = out_w.shape[0]
    held = pl.BlockSpec(memory_space=pltpu.VMEM)
    return pl.pallas_call(
        lambda *refs: attend_kernel(head, *refs),
        in_specs=[held] * 6,
        out_specs=[held] * 4,
        out_shape=[
            jax.ShapeDtypeStruct((heads, rows, keys), f32),
            jax.ShapeDtypeStruct((rows, width), bf16),
            jax.ShapeDtypeStruct((rows, rank), bf16),
            jax.ShapeDtypeStruct((rows, model), bf16),
        ],
        compiler_params=pltpu.CompilerParams(vmem_limit_bytes=32 * 2**20),
        cost_estimate=pl.CostEstimate(
            flops=2 * rows * width * (2 * keys + model),
            bytes_accessed=4 * heads * rows * keys,
            transcendentals=heads * rows * keys,
        ),
        name="attend",
    )(queries, key_block, bias, out_w, so, eo)


def attend_back_kernel(
    head, branch_ref, out_ref, so_ref, eo_ref, prob_ref, query_ref, keyval_ref, qw_ref, eq_ref, sq_ref,
    dq_ref, dkv_ref, inner_o_ref, inner_q_ref, part_ref, key_sum, value_sum,
):
    scale = 1.0 / math.sqrt(head)
    branch = branch_ref[...]
    inner_o = against(branch, eo_ref[...]).astype(bf16)
    inner_o_ref[...] = inner_o
    grad_mixed = (plain(branch, out_ref[...]) + plain(inner_o, so_ref[...])).astype(bf16)
    for h in range(query_ref.shape[1] // head):
        columns = pl.ds(h * head, head)
        grad = grad_mixed[:, h * head : (h + 1) * head]
        probs = prob_ref[h]
        grad_probs = against(grad, keyval_ref[:, head:])
        delta = jnp.sum(grad_probs * probs, axis=-1, keepdims=True)
        grad_scores = (probs * (grad_probs - delta)).astype(bf16)
        dq_ref[:, columns] = (plain(grad_scores, keyval_ref[:, :head]) * scale).astype(bf16)
        keys = across(grad_scores, query_ref[:, columns])
        values = across(probs.astype(bf16), grad)
        if h == 0:
            key_sum[...] = keys
            value_sum[...] = values
        else:
            key_sum[...] += keys
            value_sum[...] += values
    dkv_ref[:, :head] = (key_sum[...] * scale).astype(bf16)
    dkv_ref[:, head:] = value_sum[...].astype(bf16)
    grad_q = dq_ref[...]
    inner_q = against(grad_q, eq_ref[...]).astype(bf16)
    inner_q_ref[...] = inner_q
    part_ref[...] = against(grad_q, qw_ref[...]) + plain(inner_q, sq_ref[...])


def attend_back(branch, out_w, so, eo, probs, queries, key_block, query_w, eq, sq, head):
    rows, width = queries.shape
    keys = key_block.shape[0]
    heads = width // head
    rank, model = eo.shape
    held = pl.BlockSpec(memory_space=pltpu.VMEM)
    return pl.pallas_call(
        lambda *refs: attend_back_kernel(head, *refs),
        in_specs=[held] * 10,
        out_specs=[held] * 5,
        out_shape=[
            jax.ShapeDtypeStruct((rows, width), bf16),
            jax.ShapeDtypeStruct((keys, 2 * head), bf16),
            jax.ShapeDtypeStruct((rows, rank), bf16),
            jax.ShapeDtypeStruct((rows, rank), bf16),
            jax.ShapeDtypeStruct((rows, model), f32),
        ],
        scratch_shapes=[pltpu.VMEM((keys, head), f32), pltpu.VMEM((keys, head), f32)],
        compiler_params=pltpu.CompilerParams(vmem_limit_bytes=32 * 2**20),
        cost_estimate=pl.CostEstimate(
            flops=2 * rows * width * (4 * keys + 2 * model),
            bytes_accessed=4 * heads * rows * keys + 8 * model * width,
            transcendentals=0,
        ),
        name="attend_back",
    )(branch, out_w, so, eo, probs, queries, key_block, query_w, eq, sq)


def weight_tile(table_ref, hidden, tile, j, second):
    half = hidden // 2
    column = j * tile % half + second * half
    return [
        table_ref[chunk, j * tile // half, :, column : column + tile]
        for chunk in range(table_ref.shape[0])
    ]


def plain_chunks(left, tables):
    rows = tables[0].shape[0]
    return sum(plain(left[:, i * rows : (i + 1) * rows], t) for i, t in enumerate(tables))


def add_against(total, left, tables, first):
    rows = tables[0].shape[0]
    for i, table in enumerate(tables):
        columns = pl.ds(i * rows, rows)
        if first:
            total[:, columns] = against(left, table)
        else:
            total[:, columns] += against(left, table)


def feed_kernel(
    tile, second_ref, table_ref, bias_ref, eu_ref, sd_ref, su_ref, ed_ref,
    active_ref, slope_ref, low_u_ref, low_d_ref, out_ref, total,
):
    hidden = eu_ref.shape[1]
    count = hidden // tile
    second = second_ref[...]
    low_u = against(second, su_ref[...]).astype(bf16)
    low_u_ref[...] = low_u
    low = 0.0
    for j in range(count):
        columns = pl.ds(j * tile, tile)
        upward = plain_chunks(second, weight_tile(table_ref, hidden, tile, j, 0))
        upward = upward + plain(low_u, eu_ref[:, columns]) + bias_ref[:, columns]
        active, slope = gelu_parts(upward)
        active = active.astype(bf16)
        active_ref[:, columns] = active
        slope_ref[:, columns] = slope.astype(bf16)
        low = low + against(active, sd_ref[:, columns])
        add_against(total, active, weight_tile(table_ref, hidden, tile, j, 1), j == 0)
    low_d = low.astype(bf16)
    low_d_ref[...] = low_d
    out_ref[...] = (total[...] + plain(low_d, ed_ref[...])).astype(bf16)


def feed_limit(table):
    return table.size * 2 + 12 * 2**20


def feed(second, table, bias, eu, sd, su, ed):
    rows, width = second.shape
    rank, hidden = eu.shape
    held = pl.BlockSpec(memory_space=pltpu.VMEM)
    return pl.pallas_call(
        lambda *refs: feed_kernel(512, *refs),
        in_specs=[held] * 7,
        out_specs=[held] * 5,
        out_shape=[
            jax.ShapeDtypeStruct((rows, hidden), bf16),
            jax.ShapeDtypeStruct((rows, hidden), bf16),
            jax.ShapeDtypeStruct((rows, rank), bf16),
            jax.ShapeDtypeStruct((rows, rank), bf16),
            jax.ShapeDtypeStruct((rows, width), bf16),
        ],
        scratch_shapes=[pltpu.VMEM((rows, width), f32)],
        compiler_params=pltpu.CompilerParams(vmem_limit_bytes=feed_limit(table)),
        cost_estimate=pl.CostEstimate(
            flops=4 * rows * width * hidden,
            bytes_accessed=4 * width * hidden + 8 * rows * hidden,
            transcendentals=rows * hidden,
        ),
        name="feed",
    )(second, table, bias, eu, sd, su, ed)


def feed_back_kernel(
    tile, branch_ref, table_ref, slope_ref, eu_ref, sd_ref, su_ref, ed_ref,
    grad_up_ref, inner_d_ref, inner_u_ref, out_ref, total,
):
    hidden = eu_ref.shape[1]
    count = hidden // tile
    branch = branch_ref[...]
    inner_d = against(branch, ed_ref[...]).astype(bf16)
    inner_d_ref[...] = inner_d
    inner = 0.0
    for j in range(count):
        columns = pl.ds(j * tile, tile)
        grad = plain_chunks(branch, weight_tile(table_ref, hidden, tile, j, 1))
        grad = grad + plain(inner_d, sd_ref[:, columns])
        grad = (grad * slope_ref[:, columns].astype(f32)).astype(bf16)
        grad_up_ref[:, columns] = grad
        inner = inner + against(grad, eu_ref[:, columns])
        add_against(total, grad, weight_tile(table_ref, hidden, tile, j, 0), j == 0)
    inner_u = inner.astype(bf16)
    inner_u_ref[...] = inner_u
    out_ref[...] = (total[...] + plain(inner_u, su_ref[...])).astype(bf16)


def feed_back(branch, table, slope, eu, sd, su, ed):
    rows, width = branch.shape
    rank, hidden = eu.shape
    held = pl.BlockSpec(memory_space=pltpu.VMEM)
    return pl.pallas_call(
        lambda *refs: feed_back_kernel(512, *refs),
        in_specs=[held] * 7,
        out_specs=[held] * 4,
        out_shape=[
            jax.ShapeDtypeStruct((rows, hidden), bf16),
            jax.ShapeDtypeStruct((rows, rank), bf16),
            jax.ShapeDtypeStruct((rows, rank), bf16),
            jax.ShapeDtypeStruct((rows, width), bf16),
        ],
        scratch_shapes=[pltpu.VMEM((rows, width), f32)],
        compiler_params=pltpu.CompilerParams(vmem_limit_bytes=feed_limit(table)),
        cost_estimate=pl.CostEstimate(
            flops=4 * rows * width * hidden,
            bytes_accessed=4 * width * hidden + 4 * rows * hidden,
            transcendentals=0,
        ),
        name="feed_back",
    )(branch, table, slope, eu, sd, su, ed)


def per_device(
    block_input,
    cotangent,
    doc_lengths,
    bank_choice,
    first_gain,
    first_shift,
    query_weight,
    query_bias,
    keyval_weight,
    value_bias,
    output_weight,
    output_bias,
    second_gain,
    second_shift,
    upward_weight,
    upward_bias,
    downward_weight,
    downward_bias,
    query_shrink,
    query_expand,
    keyval_shrink,
    keyval_expand,
    output_shrink,
    output_expand,
    upward_shrink,
    upward_expand,
    downward_shrink,
    downward_expand,
):
    section = lax.axis_index("section")
    data = lax.axis_index("dp")
    tensor = lax.axis_index("tensor")
    low_section = section == 0
    width = block_input.shape[2]
    rows = block_input.shape[1]
    ranks = lax.axis_size("tensor")
    span = rows * ranks
    head = value_bias.shape[1]
    local_q = query_bias.shape[1]
    local_f = upward_bias.shape[1]
    rank = query_expand.shape[2]
    banks = query_expand.shape[1]
    reach = WINDOW // span
    sides = [(0, 1), (1, 0)]

    def swap(value):
        return lax.ppermute(value, "section", sides)

    def by_layer(own, other):
        return jnp.where(low_section, own, other), jnp.where(low_section, other, own)

    def spread(block):
        parts = [block] + [around(block, "tensor", -j) for j in range(1, ranks)]
        return jnp.concatenate(parts, axis=0)

    def reduce_rows(partial):
        low = partial.astype(bf16)
        total = partial[:rows].astype(f32)
        for j in range(1, ranks):
            total = total + around(low[j * rows : (j + 1) * rows], "tensor", j).astype(f32)
        return total

    def chosen(table, bank, transpose):
        block = lax.dynamic_index_in_dim(table[0], bank, 0, keepdims=False)
        return block.T if transpose else block

    def early_pack(bank):
        return jnp.concatenate(
            [
                chosen(query_shrink, bank, True),
                chosen(keyval_shrink, bank, True),
                chosen(query_expand, bank, False),
                chosen(keyval_expand, bank, False),
            ],
            axis=1,
        )

    def late_pack(bank):
        return jnp.concatenate(
            [
                chosen(output_shrink, bank, True),
                chosen(output_expand, bank, False),
                chosen(upward_shrink, bank, True),
                chosen(upward_expand, bank, False),
                chosen(downward_shrink, bank, True),
                chosen(downward_expand, bank, False),
            ],
            axis=1,
        )

    own_bank = lax.dynamic_index_in_dim(bank_choice, section, 0, keepdims=False)
    other_bank = lax.dynamic_index_in_dim(bank_choice, 1 - section, 0, keepdims=False)

    vectors = jnp.concatenate(
        [
            first_gain,
            first_shift,
            query_bias,
            jnp.zeros_like(value_bias),
            value_bias,
            output_bias,
            second_gain,
            second_shift,
            upward_bias,
            downward_bias,
        ],
        axis=1,
    )
    vector_sizes = [width, width, local_q, 2 * head, width, width, width, local_f, width]

    both = ("section", "dp")
    chips = lax.axis_size("dp") // 4
    order = [
        side * 4 * chips + chip * 4 + near
        for chip in range(chips)
        for side in range(2)
        for near in range(4)
    ]

    def gather(shard):
        table = lax.all_gather(shard, both, axis=0, tiled=True, axis_index_groups=[order])
        return table.reshape(chips, 2, -1, shard.shape[1])

    def halves(shard):
        cut = shard.shape[1] // 2
        return shard[:, :cut], shard[:, cut:]

    early_all = gather(
        jnp.concatenate([query_weight[0], keyval_weight[0], output_weight[0].T], axis=1)
    )
    vector_layers = by_layer(vectors, swap(vectors))
    early_layers = by_layer(early_pack(own_bank), swap(early_pack(other_bank)))
    late_layers = by_layer(late_pack(own_bank), swap(late_pack(other_bank)))
    up_halves = halves(upward_weight[0])
    down_halves = halves(downward_weight[0].T)
    side = [jnp.concatenate([up_halves[h], down_halves[h]], axis=1) for h in range(2)]
    keep = jnp.where(low_section, side[0], side[1])
    gained = swap(jnp.where(low_section, side[1], side[0]))
    feed_zero, feed_one = [gather(table) for table in by_layer(keep, gained)]

    def split(table, sizes):
        cuts = [0]
        for size in sizes:
            cuts.append(cuts[-1] + size)
        return [table[:, a:b] for a, b in zip(cuts[:-1], cuts[1:])]

    wide = local_q + 2 * head
    weights = [
        (
            early_all[:, layer, :, :local_q].reshape(width, -1),
            early_all[:, layer, :, local_q:wide].reshape(width, -1),
            early_all[:, layer, :, wide:].reshape(width, -1),
            table,
        )
        for layer, table in enumerate([feed_zero, feed_one])
    ]
    small = [
        [part.astype(f32) for part in split(vector_layers[layer], vector_sizes)]
        for layer in range(2)
    ]
    adapters = [
        split(early_layers[layer], [width, width, local_q, 2 * head])
        + split(late_layers[layer], [local_q, width, width, local_f, local_f, width])
        for layer in range(2)
    ]

    place = (
        ((tensor + jnp.arange(ranks, dtype=jnp.int32)) % ranks)[:, None] * rows
        + jnp.arange(rows, dtype=jnp.int32)[None, :]
    ).reshape(-1)
    query_place = data * span + place
    key_place = jnp.concatenate([(data - back) * span + place for back in range(reach, -1, -1)])
    lengths = lax.dynamic_index_in_dim(doc_lengths, section, 0, keepdims=False)
    ends = jnp.cumsum(lengths)
    query_doc = jnp.sum((query_place[:, None] >= ends[None, :]).astype(jnp.int32), axis=1)
    key_doc = jnp.sum((key_place[:, None] >= ends[None, :]).astype(jnp.int32), axis=1)
    distance = query_place[:, None] - key_place[None, :]
    allowed = (
        (key_place[None, :] >= 0)
        & (distance >= 0)
        & (distance < WINDOW)
        & (query_doc[:, None] == key_doc[None, :])
    )
    bias = jnp.where(allowed, 0.0, masked_score).astype(bf16)

    def forward(layer, hidden):
        query_w, keyval_w, out_w, feed_w = weights[layer]
        gain1, shift1, q_bias, kv_bias, out_bias, gain2, shift2, up_bias, down_bias = small[layer]
        sq, skv, eq, ekv, so, eo, su, eu, sd, ed = adapters[layer]
        unit1, rsd1 = norm_parts(hidden)
        normed = spread((unit1 * gain1 + shift1).astype(bf16))
        low_q = against(normed, sq).astype(bf16)
        low_kv = against(normed, skv).astype(bf16)
        keyval = (plain(normed, keyval_w) + kv_bias + plain(low_kv, ekv)).astype(bf16)
        pieces = [along(keyval, "dp", back) for back in range(reach, 0, -1)] + [keyval]
        queries = (plain(normed, query_w) + q_bias + plain(low_q, eq)).astype(bf16)
        key_block = jnp.concatenate(pieces, axis=0)
        probs, mixed, low_o, partial = attend(queries, key_block, bias, out_w, so, eo, head)
        attended = reduce_rows(partial)
        middle = hidden + (attended + out_bias)
        unit2, rsd2 = norm_parts(middle)
        second = spread((unit2 * gain2 + shift2).astype(bf16))
        active, slope, low_u, low_d, partial = feed(second, feed_w, up_bias, eu, sd, su, ed)
        result = middle + (reduce_rows(partial) + down_bias)
        kept = (
            unit1,
            rsd1,
            normed,
            low_q,
            low_kv,
            queries,
            key_block,
            probs,
            mixed,
            low_o,
            unit2,
            rsd2,
            second,
            low_u,
            active,
            slope,
            low_d,
        )
        return result, kept

    def tiles(block):
        return block.reshape(rank, -1, 128).transpose(1, 0, 2)

    def flat(block):
        return block.transpose(1, 0, 2).reshape(rank, -1)

    turn, near = data // 4, data % 4

    def padded(pile, multiple):
        lack = -pile.shape[0] % multiple
        if not lack:
            return pile
        return jnp.concatenate([pile, jnp.zeros((lack,) + pile.shape[1:], pile.dtype)], axis=0)

    def piled(shared):
        return padded(jnp.concatenate([tiles(part) for part in shared], axis=0).astype(bf16), ranks)

    def owned_pile(mine, owned):
        pile = jnp.concatenate([mine] + [tiles(part) for part in owned], axis=0).astype(bf16)
        return padded(pile, lax.axis_size("dp"))

    def at(block, index, axis):
        return lax.dynamic_index_in_dim(block, index, axis, keepdims=False)

    def offloaded_grads(shared, owned):
        mine = lax.psum_scatter(piled(shared), "tensor", scatter_dimension=0, tiled=True)
        return lax.psum_scatter(owned_pile(mine, owned), "dp", scatter_dimension=0, tiled=True)

    def scattered_grads(shared, owned):
        pile = piled(shared)
        each = pile.shape[0] // ranks
        mine = pick(pile, tensor * each, each).astype(f32)
        for j in range(1, ranks):
            block = pick(pile, ((tensor + j) % ranks) * each, each)
            mine = mine + around(block, "tensor", j).astype(f32)
        pile = owned_pile(mine, owned)
        pile = pile.reshape((chips, 4, -1) + pile.shape[1:])
        mine = at(pile, near, 1).astype(f32)
        for k in range(1, 4):
            mine = mine + flipped(at(pile, near ^ k, 1), "dp", k).astype(f32)
        pile = mine.astype(bf16)
        mine = at(pile, turn, 0).astype(f32)
        for k in range(1, chips):
            mine = mine + flipped(at(pile, turn ^ k, 0), "dp", 4 * k).astype(f32)
        return mine.astype(bf16)

    def crossed(block, mask):
        return lax.ppermute(block, both, [(i, i ^ mask) for i in range(8 * chips)])

    def spread_grads(zero, one, shared_sizes, owned_sizes):
        own = jnp.where(low_section, zero, one)
        away = jnp.where(low_section, one, zero)
        dp_size = 4 * chips
        home = jnp.stack([own, flipped(own, "dp", 2)])
        guest = jnp.stack([crossed(away, dp_size), crossed(away, dp_size + 2)])
        home, guest = [
            jnp.where(near // 2 == 0, block, block[::-1]) for block in (home, guest)
        ]
        pair = jnp.where(
            low_section, jnp.stack([home, guest], axis=1), jnp.stack([guest, home], axis=1)
        )
        parts = jnp.stack([pair] + [flipped(pair, "dp", 4 * k) for k in range(1, chips)])
        parts = jnp.stack([at(parts, turn ^ k, 0) for k in range(chips)])
        other = flipped(parts, "dp", 1)
        core = near % 2
        parts = jnp.stack(
            [jnp.where(core == 0, parts, other), jnp.where(core == 0, other, parts)], axis=2
        )
        pile = jnp.moveaxis(parts, 3, 0).reshape((2, -1) + parts.shape[5:])
        each = -(-(sum(shared_sizes) // 128) // ranks)
        own = pile[:, :each]
        parts = jnp.stack([own] + [around(own, "tensor", k) for k in range(1, ranks)])
        ordered = jnp.concatenate([at(parts, (tensor - r) % ranks, 0) for r in range(ranks)], axis=1)
        results = []
        for whole, begin, sizes in [(ordered, 0, shared_sizes), (pile, each, owned_sizes)]:
            for size in sizes:
                count = size // 128
                results.append([flat(whole[m, begin : begin + count]) for m in range(2)])
                begin += count
        return results

    def backward_feed(layer, kept, grad):
        feed_w = weights[layer][3]
        gain2 = small[layer][5]
        su, eu, sd, ed = adapters[layer][6:]
        unit2, rsd2, second, low_u, active, slope, low_d = kept[10:]
        branch = spread(grad.astype(bf16))
        grad_up, inner_d, inner_u, partial = feed_back(branch, feed_w, slope, eu, sd, su, ed)
        grad_second = reduce_rows(partial)
        grad_middle = grad + norm_back(unit2, rsd2, grad_second * gain2)
        shared = [across(inner_u, second), across(low_d, branch)]
        owned = [across(low_u, grad_up), across(inner_d, active)]
        return grad_middle, shared, owned

    def backward_attend(layer, kept, grad_middle):
        query_w, keyval_w, out_w = weights[layer][:3]
        gain1 = small[layer][0]
        sq, skv, eq, ekv, so, eo = adapters[layer][:6]
        unit1, rsd1, normed, low_q, low_kv, queries, key_block, probs, mixed, low_o = kept[:10]
        branch = spread(grad_middle.astype(bf16))
        grad_q, grad_block, inner_o, inner_q, partial = attend_back(
            branch, out_w, so, eo, probs, queries, key_block, query_w, eq, sq, head
        )
        own = grad_block[reach * span :].astype(f32)
        for back in range(1, reach + 1):
            begin = (reach - back) * span
            own = own + along(grad_block[begin : begin + span], "dp", -back).astype(f32)
        grad_kv = own.astype(bf16)
        inner_kv = against(grad_kv, ekv).astype(bf16)
        grad_normed = partial + against(grad_kv, keyval_w) + plain(inner_kv, skv)
        grad_hidden = grad_middle + norm_back(unit1, rsd1, reduce_rows(grad_normed) * gain1)
        out_grads = ([across(low_o, branch)], [across(inner_o, mixed)])
        shared = [across(inner_q, normed), across(inner_kv, normed), across(low_kv, grad_kv)]
        owned = [across(low_q, grad_q)]
        return grad_hidden, out_grads, (shared, owned)

    fresh = lax.dynamic_index_in_dim(block_input, section, 0, keepdims=False).astype(f32)
    result_zero, kept_zero = forward(0, fresh)
    passed = result_zero.astype(bf16)
    result_one, kept_one = forward(1, passed.astype(f32))
    final = result_one.astype(bf16)

    given = lax.dynamic_index_in_dim(cotangent, section, 0, keepdims=False).astype(f32)
    grad_middle_one, feed_shared, feed_owned = backward_feed(1, kept_one, given)
    grad_one, out_one_grads, qkv_one_grads = backward_attend(1, kept_one, grad_middle_one)
    mine_one = offloaded_grads(
        feed_shared + out_one_grads[0] + qkv_one_grads[0],
        feed_owned + out_one_grads[1] + qkv_one_grads[1],
    )
    grad_middle_zero, feed_shared, feed_owned = backward_feed(0, kept_zero, grad_one)
    grad_zero, out_zero_grads, qkv_zero_grads = backward_attend(0, kept_zero, grad_middle_zero)
    shared = feed_shared + out_zero_grads[0] + qkv_zero_grads[0]
    owned = feed_owned + out_zero_grads[1] + qkv_zero_grads[1]
    mine_zero = scattered_grads(shared, owned)
    grads = spread_grads(
        mine_zero,
        mine_one,
        [part.shape[1] for part in shared],
        [part.shape[1] for part in owned],
    )

    def both_micros(zero, one, kind):
        own = jnp.where(low_section, zero, one)
        received = swap(jnp.where(low_section, one, zero).astype(bf16)).astype(kind)
        return jnp.where(low_section, jnp.stack([own, received]), jnp.stack([received, own]))

    passed, final, _ = lax.optimization_barrier((passed, final, grad_middle_zero))
    section_outputs = both_micros(passed, final, bf16)
    input_grads = both_micros(grad_zero, grad_one, f32)
    onehot = (bank_choice[:, None] == jnp.arange(banks)[None, :]).astype(f32)

    def placed(pair, transpose):
        out = sum(
            onehot[m][:, None, None] * pair[m].astype(f32)[None] for m in range(2)
        )
        return (out.transpose(0, 2, 1) if transpose else out)[None]

    (
        up_shrink_grad,
        down_expand_grad,
        out_expand_grad,
        q_shrink_grad,
        kv_shrink_grad,
        kv_expand_grad,
        up_expand_grad,
        down_shrink_grad,
        out_shrink_grad,
        q_expand_grad,
    ) = grads
    return (
        section_outputs[None],
        input_grads[None],
        placed(q_shrink_grad, True),
        placed(q_expand_grad, False),
        placed(kv_shrink_grad, True),
        placed(kv_expand_grad, False),
        placed(out_shrink_grad, True),
        placed(out_expand_grad, False),
        placed(up_shrink_grad, True),
        placed(up_expand_grad, False),
        placed(down_shrink_grad, True),
        placed(down_expand_grad, False),
    )


def solution(mesh):
    return jax.shard_map(
        per_device,
        mesh=mesh,
        in_specs=(
            P(None, ("dp", "tensor"), None),
            P(None, ("dp", "tensor"), None),
            P(),
            P(),
            P("section", None),
            P("section", None),
            P("section", "dp", "tensor"),
            P("section", "tensor"),
            P("section", "dp", None),
            P("section", None),
            P("section", "tensor", "dp"),
            P("section", None),
            P("section", None),
            P("section", None),
            P("section", "dp", "tensor"),
            P("section", "tensor"),
            P("section", "tensor", "dp"),
            P("section", None),
            P("section", None, None, None),
            P("section", None, None, "tensor"),
            P("section", None, None, None),
            P("section", None, None, None),
            P("section", None, "tensor", None),
            P("section", None, None, None),
            P("section", None, None, None),
            P("section", None, None, "tensor"),
            P("section", None, "tensor", None),
            P("section", None, None, None),
        ),
        out_specs=(
            P("section", None, ("dp", "tensor"), None),
            P("section", None, ("dp", "tensor"), None),
            P("section", None, None, None),
            P("section", None, None, "tensor"),
            P("section", None, None, None),
            P("section", None, None, None),
            P("section", None, "tensor", None),
            P("section", None, None, None),
            P("section", None, None, None),
            P("section", None, None, "tensor"),
            P("section", None, "tensor", None),
            P("section", None, None, None),
        ),
        check_vma=False,
    )
```

```python
import math

import jax
import jax.numpy as jnp
from jax import lax
from jax.experimental import pallas as pl
from jax.experimental.layout import Layout, with_layout_constraint
from jax.experimental.pallas import tpu as pltpu
from jax.sharding import PartitionSpec as P

WINDOW = 1024
epsilon = 1e-05
masked_score = -1e30
bf16 = jnp.bfloat16
f32 = jnp.float32


def plain(left, right):
    return jnp.dot(left, right, preferred_element_type=f32)


def against(left, right):
    return lax.dot_general(left, right, (((1,), (1,)), ((), ())), preferred_element_type=f32)


def across(left, right):
    return lax.dot_general(left, right, (((0,), (0,)), ((), ())), preferred_element_type=f32)


def around(block, axis, distance):
    size = lax.axis_size(axis)
    return lax.ppermute(block, axis, [(i, (i + distance) % size) for i in range(size)])


def along(block, axis, distance):
    size = lax.axis_size(axis)
    route = [(i, i + distance) for i in range(size) if 0 <= i + distance < size]
    return lax.ppermute(block, axis, route)


def flipped(block, axis, bit):
    size = lax.axis_size(axis)
    return lax.ppermute(block, axis, [(i, i ^ bit) for i in range(size)])


def pick(table, index, size=1):
    return lax.dynamic_slice_in_dim(table, index, size, 0)


def norm_parts(value):
    centred = value - jnp.mean(value, axis=-1, keepdims=True)
    spread = lax.rsqrt(jnp.mean(centred * centred, axis=-1, keepdims=True) + epsilon)
    return centred * spread, spread


def norm_back(unit, spread, scaled):
    inner = jnp.mean(scaled * unit, axis=-1, keepdims=True)
    return spread * (scaled - jnp.mean(scaled, axis=-1, keepdims=True) - unit * inner)


def gelu_parts(value):
    rate = math.sqrt(2.0 / math.pi)
    square = value * value
    bend = jnp.tanh(rate * (value + 0.044715 * value * square))
    rising = 0.5 * (1.0 + bend)
    slope = rising + 0.5 * value * (1.0 - bend * bend) * (rate * (1.0 + 3 * 0.044715 * square))
    return value * rising, slope


def side_blocks(query_ref, group, head):
    begin = group * 4 * head
    return jnp.concatenate(
        [query_ref[:, begin + h * head : begin + (h + 1) * head] for h in range(4)], axis=0
    )


def put_blocks(out_ref, value, group, head):
    rows = value.shape[0] // 4
    for h in range(4):
        begin = (group * 4 + h) * head
        out_ref[:, begin : begin + head] = value[h * rows : (h + 1) * rows]


def table_copies(table_ref, buf, sem, layer, begin):
    ranks, chunks, _, width = buf.shape
    return [
        pltpu.make_async_copy(
            table_ref.at[x, y, layer, :, pl.ds(begin, width)], buf.at[x, y], sem.at[x, y]
        )
        for x in range(ranks)
        for y in range(chunks)
    ]


def query_kernel(layer, normed_ref, table_ref, bias_ref, eq_ref, sq_ref, out_ref, low_ref, buf, sem):
    ranks, chunks, rows, width = buf.shape
    copies = table_copies(table_ref, buf, sem, layer, 0)
    for copy in copies:
        copy.start()
    normed = normed_ref[...]
    low = against(normed, sq_ref[...]).astype(bf16)
    low_ref[...] = low
    for x in range(ranks):
        columns = pl.ds(x * width, width)
        total = bias_ref[:, columns] + plain(low, eq_ref[:, columns])
        for y in range(chunks):
            copies[x * chunks + y].wait()
            total = total + plain(normed[:, y * rows : (y + 1) * rows], buf[x, y])
        out_ref[:, columns] = total.astype(bf16)


def table_scratch(table, width):
    ranks, chunks, _, rows, _ = table.shape
    return [
        pltpu.VMEM((ranks, chunks, rows, width), bf16),
        pltpu.SemaphoreType.DMA((ranks, chunks)),
    ]


held = pl.BlockSpec(memory_space=pltpu.VMEM)
remote = pl.BlockSpec(memory_space=pl.ANY)


def project_queries(layer, normed, table, bias, eq, sq):
    rows, model = normed.shape
    rank = sq.shape[0]
    width = model // table.shape[0]
    return pl.pallas_call(
        lambda *refs: query_kernel(layer, *refs),
        in_specs=[held, remote, held, held, held],
        out_specs=[held] * 2,
        out_shape=[
            jax.ShapeDtypeStruct((rows, model), bf16),
            jax.ShapeDtypeStruct((rows, rank), bf16),
        ],
        scratch_shapes=table_scratch(table, width),
        compiler_params=pltpu.CompilerParams(vmem_limit_bytes=20 * 2**20),
        cost_estimate=pl.CostEstimate(
            flops=8 * rows * model * model, bytes_accessed=2 * model * model, transcendentals=0
        ),
        name="project_queries",
    )(normed, table, bias, eq, sq)


def attend_kernel(
    layer, head, query_ref, keyval_ref, bias_ref, table_ref, so_ref, eo_ref,
    prob_ref, mixed_ref, low_ref, out_ref, buf, sem,
):
    ranks, chunks, rows, width = buf.shape
    copies = table_copies(table_ref, buf, sem, layer, width)
    for copy in copies:
        copy.start()
    scale = 1.0 / math.sqrt(head)
    bias = jnp.concatenate([bias_ref[...].astype(f32)] * 4, axis=0)
    for g in range(prob_ref.shape[0]):
        queries = side_blocks(query_ref, g, head)
        scores = against(queries, keyval_ref[:, :head]) * scale + bias
        lifted = jnp.exp(scores - jnp.max(scores, axis=-1, keepdims=True))
        probs = lifted * (1.0 / jnp.sum(lifted, axis=-1, keepdims=True))
        prob_ref[g] = probs
        put_blocks(mixed_ref, plain(probs.astype(bf16), keyval_ref[:, head:]).astype(bf16), g, head)
    mixed = mixed_ref[...]
    low = against(mixed, so_ref[...]).astype(bf16)
    low_ref[...] = low
    for copy in copies:
        copy.wait()
    for y in range(chunks):
        columns = pl.ds(y * rows, rows)
        total = plain(low, eo_ref[:, columns])
        for x in range(ranks):
            total = total + against(mixed[:, x * width : (x + 1) * width], buf[x, y])
        out_ref[:, columns] = total


def attend(layer, queries, key_block, bias, table, so, eo, head):
    rows, model = queries.shape
    keys = key_block.shape[0]
    groups = model // head // 4
    rank = so.shape[0]
    return pl.pallas_call(
        lambda *refs: attend_kernel(layer, head, *refs),
        in_specs=[held, held, held, remote, held, held],
        out_specs=[held] * 4,
        out_shape=[
            jax.ShapeDtypeStruct((groups, 4 * rows, keys), f32),
            jax.ShapeDtypeStruct((rows, model), bf16),
            jax.ShapeDtypeStruct((rows, rank), bf16),
            jax.ShapeDtypeStruct((rows, model), f32),
        ],
        scratch_shapes=table_scratch(table, model // table.shape[0]),
        compiler_params=pltpu.CompilerParams(vmem_limit_bytes=36 * 2**20),
        cost_estimate=pl.CostEstimate(
            flops=4 * rows * model * (keys + 2 * model),
            bytes_accessed=2 * model * model,
            transcendentals=groups * 4 * rows * keys,
        ),
        name="attend",
    )(queries, key_block, bias, table, so, eo)


def attend_back_kernel(
    layer, head, branch_ref, table_ref, so_ref, eo_ref, prob_ref, query_ref, keyval_ref, eq_ref, sq_ref,
    dq_ref, dkv_ref, inner_o_ref, inner_q_ref, part_ref,
    out_buf, out_sem, query_buf, query_sem, mixed_buf, key_sum, value_sum,
):
    ranks, chunks, rows, width = out_buf.shape
    out_copies = table_copies(table_ref, out_buf, out_sem, layer, width)
    query_copies = table_copies(table_ref, query_buf, query_sem, layer, 0)
    for copy in out_copies + query_copies:
        copy.start()
    scale = 1.0 / math.sqrt(head)
    branch = branch_ref[...]
    inner_o = against(branch, eo_ref[...]).astype(bf16)
    inner_o_ref[...] = inner_o
    for g in range(prob_ref.shape[0]):
        columns = pl.ds(g * width, width)
        total = plain(inner_o, so_ref[:, columns])
        for y in range(chunks):
            out_copies[g * chunks + y].wait()
            total = total + plain(branch[:, y * rows : (y + 1) * rows], out_buf[g, y])
        mixed_buf[:, columns] = total.astype(bf16)
        grad = side_blocks(mixed_buf, g, head)
        probs = prob_ref[g]
        grad_probs = against(grad, keyval_ref[:, head:])
        delta = jnp.sum(grad_probs * probs, axis=-1, keepdims=True)
        grad_scores = (probs * (grad_probs - delta)).astype(bf16)
        put_blocks(dq_ref, (plain(grad_scores, keyval_ref[:, :head]) * scale).astype(bf16), g, head)
        keys = across(grad_scores, side_blocks(query_ref, g, head))
        values = across(probs.astype(bf16), grad)
        if g == 0:
            key_sum[...] = keys
            value_sum[...] = values
        else:
            key_sum[...] += keys
            value_sum[...] += values
    dkv_ref[:, :head] = (key_sum[...] * scale).astype(bf16)
    dkv_ref[:, head:] = value_sum[...].astype(bf16)
    grad_q = dq_ref[...]
    inner_q = against(grad_q, eq_ref[...]).astype(bf16)
    inner_q_ref[...] = inner_q
    for copy in query_copies:
        copy.wait()
    for y in range(chunks):
        columns = pl.ds(y * rows, rows)
        total = plain(inner_q, sq_ref[:, columns])
        for x in range(ranks):
            total = total + against(grad_q[:, x * width : (x + 1) * width], query_buf[x, y])
        part_ref[:, columns] = total


def attend_back(layer, branch, table, so, eo, probs, queries, key_block, eq, sq, head):
    rows, model = queries.shape
    keys = key_block.shape[0]
    groups = probs.shape[0]
    rank = so.shape[0]
    width = model // table.shape[0]
    return pl.pallas_call(
        lambda *refs: attend_back_kernel(layer, head, *refs),
        in_specs=[held, remote] + [held] * 7,
        out_specs=[held] * 5,
        out_shape=[
            jax.ShapeDtypeStruct((rows, model), bf16),
            jax.ShapeDtypeStruct((keys, 2 * head), bf16),
            jax.ShapeDtypeStruct((rows, rank), bf16),
            jax.ShapeDtypeStruct((rows, rank), bf16),
            jax.ShapeDtypeStruct((rows, model), f32),
        ],
        scratch_shapes=table_scratch(table, width)
        + table_scratch(table, width)
        + [
            pltpu.VMEM((rows, model), bf16),
            pltpu.VMEM((keys, head), f32),
            pltpu.VMEM((keys, head), f32),
        ],
        compiler_params=pltpu.CompilerParams(vmem_limit_bytes=44 * 2**20),
        cost_estimate=pl.CostEstimate(
            flops=8 * rows * model * (keys + 2 * model),
            bytes_accessed=4 * model * model + 4 * groups * 4 * rows * keys,
            transcendentals=0,
        ),
        name="attend_back",
    )(branch, table, so, eo, probs, queries, key_block, eq, sq)


def feed_copies(table_ref, buf, sems):
    _, count, chunks, rows, tile = buf.shape
    half = count // 2 * tile
    copies = []
    for j in range(count):
        pair = []
        for k in range(2):
            columns = pl.ds(j * tile % half + k * half, tile)
            pair.append(
                pltpu.make_async_copy(
                    table_ref.at[:, j * tile // half, :, columns], buf.at[k, j], sems.at[k, j]
                )
            )
        copies.append(pair)
    return copies


def plain_chunks(left, buf, k, j):
    rows = buf.shape[3]
    return sum(plain(left[:, i * rows : (i + 1) * rows], buf[k, j, i]) for i in range(buf.shape[2]))


def add_against(total, left, buf, k, j):
    rows = buf.shape[3]
    for i in range(buf.shape[2]):
        columns = pl.ds(i * rows, rows)
        if j == 0:
            total[:, columns] = against(left, buf[k, j, i])
        else:
            total[:, columns] += against(left, buf[k, j, i])


def feed_kernel(
    second_ref, table_ref, bias_ref, eu_ref, sd_ref, su_ref, ed_ref,
    active_ref, slope_ref, low_u_ref, low_d_ref, out_ref, buf, sems, total,
):
    _, count, _, _, tile = buf.shape
    copies = feed_copies(table_ref, buf, sems)
    for up, down in copies:
        up.start()
        down.start()
    second = second_ref[...]
    low_u = against(second, su_ref[...]).astype(bf16)
    low_u_ref[...] = low_u
    low = 0.0
    for j in range(count):
        columns = pl.ds(j * tile, tile)
        copies[j][0].wait()
        upward = plain_chunks(second, buf, 0, j)
        upward = upward + plain(low_u, eu_ref[:, columns]) + bias_ref[:, columns]
        active, slope = gelu_parts(upward)
        active = active.astype(bf16)
        active_ref[:, columns] = active
        slope_ref[:, columns] = slope.astype(bf16)
        low = low + against(active, sd_ref[:, columns])
        copies[j][1].wait()
        add_against(total, active, buf, 1, j)
    low_d = low.astype(bf16)
    low_d_ref[...] = low_d
    out_ref[...] = (total[...] + plain(low_d, ed_ref[...])).astype(bf16)


def feed_back_kernel(
    branch_ref, table_ref, slope_ref, eu_ref, sd_ref, su_ref, ed_ref,
    grad_up_ref, inner_d_ref, inner_u_ref, out_ref, buf, sems, total,
):
    _, count, _, _, tile = buf.shape
    copies = feed_copies(table_ref, buf, sems)
    for up, down in copies:
        down.start()
        up.start()
    branch = branch_ref[...]
    inner_d = against(branch, ed_ref[...]).astype(bf16)
    inner_d_ref[...] = inner_d
    inner = 0.0
    for j in range(count):
        columns = pl.ds(j * tile, tile)
        copies[j][1].wait()
        grad = plain_chunks(branch, buf, 1, j) + plain(inner_d, sd_ref[:, columns])
        grad = (grad * slope_ref[:, columns].astype(f32)).astype(bf16)
        grad_up_ref[:, columns] = grad
        inner = inner + against(grad, eu_ref[:, columns])
        copies[j][0].wait()
        add_against(total, grad, buf, 0, j)
    inner_u = inner.astype(bf16)
    inner_u_ref[...] = inner_u
    out_ref[...] = (total[...] + plain(inner_u, su_ref[...])).astype(bf16)


def feed_both_kernel(
    second_ref, branch_ref, table_ref, bias_ref, eu_ref, sd_ref, su_ref, ed_ref,
    active_ref, low_u_ref, low_d_ref, out_ref, grad_up_ref, inner_d_ref, inner_u_ref, back_ref,
    buf, sems, total, back_total,
):
    _, count, _, _, tile = buf.shape
    copies = feed_copies(table_ref, buf, sems)
    for up, down in copies:
        up.start()
        down.start()
    second = second_ref[...]
    branch = branch_ref[...]
    low_u = against(second, su_ref[...]).astype(bf16)
    low_u_ref[...] = low_u
    inner_d = against(branch, ed_ref[...]).astype(bf16)
    inner_d_ref[...] = inner_d
    low = 0.0
    inner = 0.0
    for j in range(count):
        columns = pl.ds(j * tile, tile)
        copies[j][0].wait()
        upward = plain_chunks(second, buf, 0, j)
        upward = upward + plain(low_u, eu_ref[:, columns]) + bias_ref[:, columns]
        active, slope = gelu_parts(upward)
        active = active.astype(bf16)
        active_ref[:, columns] = active
        low = low + against(active, sd_ref[:, columns])
        copies[j][1].wait()
        add_against(total, active, buf, 1, j)
        grad = plain_chunks(branch, buf, 1, j) + plain(inner_d, sd_ref[:, columns])
        grad = (grad * slope).astype(bf16)
        grad_up_ref[:, columns] = grad
        inner = inner + against(grad, eu_ref[:, columns])
        add_against(back_total, grad, buf, 0, j)
    inner_u = inner.astype(bf16)
    inner_u_ref[...] = inner_u
    back_ref[...] = (back_total[...] + plain(inner_u, su_ref[...])).astype(bf16)
    low_d = low.astype(bf16)
    low_d_ref[...] = low_d
    out_ref[...] = (total[...] + plain(low_d, ed_ref[...])).astype(bf16)


def feed_call(kernel, name, inputs, outputs, hidden, totals):
    table = [value for value in inputs if value.ndim == 4][0]
    rows, model = inputs[0].shape
    tile = 512
    chunks = table.shape[0]
    return pl.pallas_call(
        kernel,
        in_specs=[remote if value.ndim == 4 else held for value in inputs],
        out_specs=[held] * len(outputs),
        out_shape=[jax.ShapeDtypeStruct((rows, width), bf16) for width in outputs],
        scratch_shapes=[
            pltpu.VMEM((2, hidden // tile, chunks, model // chunks, tile), bf16),
            pltpu.SemaphoreType.DMA((2, hidden // tile)),
        ]
        + [pltpu.VMEM((rows, model), f32)] * totals,
        compiler_params=pltpu.CompilerParams(vmem_limit_bytes=44 * 2**20),
        cost_estimate=pl.CostEstimate(
            flops=4 * totals * rows * model * hidden,
            bytes_accessed=4 * model * hidden,
            transcendentals=rows * hidden,
        ),
        name=name,
    )(*inputs)


def per_device(
    block_input,
    cotangent,
    doc_lengths,
    bank_choice,
    first_gain,
    first_shift,
    query_weight,
    query_bias,
    keyval_weight,
    value_bias,
    output_weight,
    output_bias,
    second_gain,
    second_shift,
    upward_weight,
    upward_bias,
    downward_weight,
    downward_bias,
    query_shrink,
    query_expand,
    keyval_shrink,
    keyval_expand,
    output_shrink,
    output_expand,
    upward_shrink,
    upward_expand,
    downward_shrink,
    downward_expand,
):
    section = lax.axis_index("section")
    data = lax.axis_index("dp")
    tensor = lax.axis_index("tensor")
    low_section = section == 0
    width = block_input.shape[2]
    rows = block_input.shape[1]
    ranks = lax.axis_size("tensor")
    span = rows * ranks
    head = value_bias.shape[1]
    local_q = query_bias.shape[1]
    local_f = upward_bias.shape[1]
    rank = query_expand.shape[2]
    banks = query_expand.shape[1]
    reach = WINDOW // span
    sides = [(0, 1), (1, 0)]

    def swap(value):
        return lax.ppermute(value, "section", sides)

    def by_layer(own, other):
        return jnp.where(low_section, own, other), jnp.where(low_section, other, own)

    def spread(block):
        parts = [block] + [around(block, "tensor", -j) for j in range(1, ranks)]
        return jnp.concatenate(parts, axis=0)

    def reduce_rows(partial):
        low = partial.astype(bf16)
        total = partial[:rows].astype(f32)
        for j in range(1, ranks):
            total = total + around(low[j * rows : (j + 1) * rows], "tensor", j).astype(f32)
        return total

    own_bank = lax.dynamic_index_in_dim(bank_choice, section, 0, keepdims=False)
    other_bank = lax.dynamic_index_in_dim(bank_choice, 1 - section, 0, keepdims=False)

    chips = lax.axis_size("dp") // 4
    both = ("section", "dp")
    every = ("section", "dp", "tensor")
    order = [
        side * 4 * chips + chip * 4 + near
        for chip in range(chips)
        for side in range(2)
        for near in range(4)
    ]
    order_all = [place * ranks + x for x in range(ranks) for place in order]

    def row_major(block):
        return with_layout_constraint(block, Layout(major_to_minor=(0, 1)))

    def gather(shard):
        table = lax.all_gather(row_major(shard), both, axis=0, tiled=True, axis_index_groups=[order])
        return row_major(table).reshape(chips, 2, -1, shard.shape[1])

    def gather_all(shard):
        table = lax.all_gather(
            row_major(shard), every, axis=0, tiled=True, axis_index_groups=[order_all]
        )
        return row_major(table).reshape(ranks, chips, 2, -1, shard.shape[1])

    def halves(shard):
        cut = shard.shape[1] // 2
        return shard[:, :cut], shard[:, cut:]

    keyval_half = jnp.where(tensor % 2 == 0, keyval_weight[0][:, :head], keyval_weight[0][:, head:])
    early_all = gather_all(
        jnp.concatenate([query_weight[0], row_major(output_weight[0].T), keyval_half], axis=1)
    )
    keyval_ws = [
        jnp.concatenate(
            [early_all[x, :, layer, :, 2 * local_q :].reshape(width, head) for x in range(2)], axis=1
        )
        for layer in range(2)
    ]

    vectors = jnp.concatenate(
        [
            first_gain,
            first_shift,
            jnp.zeros_like(value_bias),
            value_bias,
            output_bias,
            second_gain,
            second_shift,
            upward_bias,
            downward_bias,
        ],
        axis=1,
    )
    vector_sizes = [width, width, 2 * head, width, width, width, local_f, width]
    vector_layers = by_layer(vectors, swap(vectors))

    def chosen(table, bank, transpose):
        block = lax.dynamic_index_in_dim(table[0], bank, 0, keepdims=False)
        return block.T if transpose else block

    def pack(bank, parts):
        return jnp.concatenate([chosen(table, bank, flip) for table, flip in parts], axis=1)

    def exchanged(parts):
        return by_layer(pack(own_bank, parts), swap(pack(other_bank, parts)))

    def cut_pack(parts):
        own = jnp.concatenate([pack(own_bank, parts), query_rows], axis=1)
        other = jnp.concatenate([pack(other_bank, parts), query_rows], axis=1)
        return by_layer(own, swap(other))

    query_rows = jnp.broadcast_to(query_bias, (rank, local_q))
    cut_layers = jnp.stack(cut_pack([(query_expand, False), (output_shrink, True)]))
    cut_parts = jnp.stack(
        [cut_layers] + [around(cut_layers, "tensor", j) for j in range(1, ranks)]
    )
    cut_whole = jnp.stack(
        [
            lax.dynamic_index_in_dim(cut_parts, (tensor - r) % ranks, 0, keepdims=False)
            for r in range(ranks)
        ],
        axis=2,
    ).reshape(2, rank, ranks, 3, local_q)
    eq_all, so_all, query_bias_all = [
        cut_whole[:, :, :, k].reshape(2, rank, ranks * local_q) for k in range(3)
    ]
    early_layers = exchanged([(query_shrink, True), (keyval_shrink, True), (keyval_expand, False)])
    late_layers = exchanged(
        [
            (output_expand, False),
            (upward_shrink, True),
            (upward_expand, False),
            (downward_shrink, True),
            (downward_expand, False),
        ]
    )

    up_halves = halves(upward_weight[0])
    down_halves = halves(row_major(downward_weight[0].T))
    side = [jnp.concatenate([up_halves[h], down_halves[h]], axis=1) for h in range(2)]
    keep = jnp.where(low_section, side[0], side[1])
    gained = swap(jnp.where(low_section, side[1], side[0]))
    feed_tables = [gather(table) for table in by_layer(keep, gained)]

    def split(table, sizes):
        cuts = [0]
        for size in sizes:
            cuts.append(cuts[-1] + size)
        return [table[:, a:b] for a, b in zip(cuts[:-1], cuts[1:])]

    small = [
        [part.astype(f32) for part in split(vector_layers[layer], vector_sizes)]
        for layer in range(2)
    ]
    adapters = [
        split(early_layers[layer], [width, width, 2 * head])
        + split(late_layers[layer], [width, width, local_f, local_f, width])
        for layer in range(2)
    ]

    inside = jnp.arange(rows, dtype=jnp.int32)
    query_place = data * span + tensor * rows + inside
    key_place = jnp.concatenate(
        [
            (data - back) * span + (tensor + j) % ranks * rows + inside
            for j in range(ranks)
            for back in range(reach, -1, -1)
        ]
    )
    lengths = lax.dynamic_index_in_dim(doc_lengths, section, 0, keepdims=False)
    ends = jnp.cumsum(lengths)
    query_doc = jnp.sum((query_place[:, None] >= ends[None, :]).astype(jnp.int32), axis=1)
    key_doc = jnp.sum((key_place[:, None] >= ends[None, :]).astype(jnp.int32), axis=1)
    distance = query_place[:, None] - key_place[None, :]
    allowed = (
        (key_place[None, :] >= 0)
        & (distance >= 0)
        & (distance < WINDOW)
        & (query_doc[:, None] == key_doc[None, :])
    )
    bias = jnp.where(allowed, 0.0, masked_score).astype(bf16)

    def forward_attend(layer, hidden):
        gain1, shift1, kv_bias, out_bias = small[layer][:4]
        sq, skv, ekv, eo = adapters[layer][:4]
        unit1, rsd1 = norm_parts(hidden)
        normed = (unit1 * gain1 + shift1).astype(bf16)
        low_kv = against(normed, skv).astype(bf16)
        keyval = (plain(normed, keyval_ws[layer]) + kv_bias + plain(low_kv, ekv)).astype(bf16)
        pieces = [along(keyval, "dp", back) for back in range(reach, 0, -1)] + [keyval]
        key_block = spread(jnp.concatenate(pieces, axis=0))
        queries, low_q = project_queries(
            layer, normed, early_all, query_bias_all[layer, :1].astype(f32), eq_all[layer], sq
        )
        probs, mixed, low_o, attended = attend(
            layer, queries, key_block, bias, early_all, so_all[layer], eo, head
        )
        middle = hidden + (attended + out_bias)
        return middle, (unit1, rsd1, normed, low_q, low_kv, queries, key_block, probs, mixed, low_o)

    def feed_inputs(layer, middle):
        gain2, shift2, up_bias = small[layer][4:7]
        unit2, rsd2 = norm_parts(middle)
        second = spread((unit2 * gain2 + shift2).astype(bf16))
        return unit2, rsd2, second, up_bias

    def feed_result(layer, middle, partial):
        return middle + (reduce_rows(partial) + small[layer][7])

    def tiles(block):
        return block.reshape(rank, -1, 128).transpose(1, 0, 2)

    def flat(block):
        return block.transpose(1, 0, 2).reshape(rank, -1)

    turn, near = data // 4, data % 4

    def padded(pile, multiple):
        lack = -pile.shape[0] % multiple
        if not lack:
            return pile
        return jnp.concatenate([pile, jnp.zeros((lack,) + pile.shape[1:], pile.dtype)], axis=0)

    def piled(shared, quartered):
        pile = padded(jnp.concatenate([tiles(part) for part in shared], axis=0), ranks)
        return jnp.concatenate(
            [block.reshape((ranks, -1) + block.shape[1:]) for block in [pile] + [tiles(part) for part in quartered]],
            axis=1,
        ).astype(bf16)

    def owned_pile(mine, owned):
        pile = jnp.concatenate([mine] + [tiles(part) for part in owned], axis=0).astype(bf16)
        return padded(pile, lax.axis_size("dp"))

    def at(block, index, axis):
        return lax.dynamic_index_in_dim(block, index, axis, keepdims=False)

    def offloaded_grads(shared, quartered, owned):
        pile = piled(shared, quartered)
        mine = lax.psum_scatter(
            pile.reshape((-1,) + pile.shape[2:]), "tensor", scatter_dimension=0, tiled=True
        )
        return lax.psum_scatter(owned_pile(mine, owned), "dp", scatter_dimension=0, tiled=True)

    def scattered_grads(shared, quartered, owned):
        pile = piled(shared, quartered)
        mine = at(pile, tensor, 0).astype(f32)
        for j in range(1, ranks):
            mine = mine + around(at(pile, (tensor + j) % ranks, 0), "tensor", j).astype(f32)
        pile = owned_pile(mine, owned)
        pile = pile.reshape((chips, 4, -1) + pile.shape[1:])
        mine = at(pile, near, 1).astype(f32)
        for k in range(1, 4):
            mine = mine + flipped(at(pile, near ^ k, 1), "dp", k).astype(f32)
        pile = mine.astype(bf16)
        mine = at(pile, turn, 0).astype(f32)
        for k in range(1, chips):
            mine = mine + flipped(at(pile, turn ^ k, 0), "dp", 4 * k).astype(f32)
        return mine.astype(bf16)

    def crossed(block, mask):
        return lax.ppermute(block, both, [(i, i ^ mask) for i in range(8 * chips)])

    def spread_grads(zero, one, shared, quartered, owned):
        own = jnp.where(low_section, zero, one)
        away = jnp.where(low_section, one, zero)
        dp_size = 4 * chips
        home = jnp.stack([own, flipped(own, "dp", 2)])
        guest = jnp.stack([crossed(away, dp_size), crossed(away, dp_size + 2)])
        home, guest = [
            jnp.where(near // 2 == 0, block, block[::-1]) for block in (home, guest)
        ]
        pair = jnp.where(
            low_section, jnp.stack([home, guest], axis=1), jnp.stack([guest, home], axis=1)
        )
        parts = jnp.stack([pair] + [flipped(pair, "dp", 4 * k) for k in range(1, chips)])
        parts = jnp.stack([at(parts, turn ^ k, 0) for k in range(chips)])
        other = flipped(parts, "dp", 1)
        core = near % 2
        parts = jnp.stack(
            [jnp.where(core == 0, parts, other), jnp.where(core == 0, other, parts)], axis=2
        )
        pile = jnp.moveaxis(parts, 3, 0).reshape((2, -1) + parts.shape[5:])
        shared_sizes = [part.shape[1] // 128 for part in shared]
        quarter_sizes = [part.shape[1] // 128 // ranks for part in quartered]
        owned_sizes = [part.shape[1] // 128 for part in owned]
        each = -(-sum(shared_sizes) // ranks)
        own = pile[:, :each]
        parts = jnp.stack([own] + [around(own, "tensor", k) for k in range(1, ranks)])
        ordered = jnp.concatenate([at(parts, (tensor - r) % ranks, 0) for r in range(ranks)], axis=1)
        results = []
        for whole, begin, sizes in [
            (ordered, 0, shared_sizes),
            (pile, each, quarter_sizes + owned_sizes),
        ]:
            for count in sizes:
                results.append([flat(whole[m, begin : begin + count]) for m in range(2)])
                begin += count
        return results

    def feed_grads(layer, grad, unit2, rsd2, partial):
        return grad + norm_back(unit2, rsd2, reduce_rows(partial) * small[layer][4])

    def feed_adapters(second, branch, low_u, low_d, inner_u, inner_d, active, grad_up):
        shared = [across(inner_u, second), across(low_d, branch)]
        owned = [across(low_u, grad_up), across(inner_d, active)]
        return shared, owned

    def backward_attend(layer, kept, grad_middle):
        gain1 = small[layer][0]
        sq, skv, ekv, eo = adapters[layer][:4]
        unit1, rsd1, normed, low_q, low_kv, queries, key_block, probs, mixed, low_o = kept
        branch = grad_middle.astype(bf16)
        grad_q, grad_block, inner_o, inner_q, partial = attend_back(
            layer, branch, early_all, so_all[layer], eo, probs, queries, key_block,
            eq_all[layer], sq, head,
        )
        count = (reach + 1) * rows
        blocks = grad_block[:count].astype(f32)
        for j in range(1, ranks):
            part = grad_block[j * count : (j + 1) * count]
            blocks = blocks + around(part, "tensor", j).astype(f32)
        own = blocks[reach * rows :]
        for back in range(1, reach + 1):
            begin = (reach - back) * rows
            own = own + along(blocks[begin : begin + rows].astype(bf16), "dp", -back).astype(f32)
        grad_kv = own.astype(bf16)
        inner_kv = against(grad_kv, ekv).astype(bf16)
        grad_normed = partial + against(grad_kv, keyval_ws[layer]) + plain(inner_kv, skv)
        grad_hidden = grad_middle + norm_back(unit1, rsd1, grad_normed * gain1)
        shared = [
            across(low_o, branch),
            across(inner_q, normed),
            across(inner_kv, normed),
            across(low_kv, grad_kv),
        ]
        quartered = [across(low_q, grad_q), across(inner_o, mixed)]
        return grad_hidden, shared, quartered

    fresh = lax.dynamic_index_in_dim(block_input, section, 0, keepdims=False).astype(f32)
    given = lax.dynamic_index_in_dim(cotangent, section, 0, keepdims=False).astype(f32)

    middle_zero, kept_zero = forward_attend(0, fresh)
    unit_zero, rsd_zero, second_zero, up_bias = feed_inputs(0, middle_zero)
    su, eu, sd, ed = adapters[0][4:]
    active_zero, slope_zero, low_u_zero, low_d_zero, partial = feed_call(
        feed_kernel,
        "feed",
        (second_zero, feed_tables[0], up_bias, eu, sd, su, ed),
        (local_f, local_f, rank, rank, width),
        local_f,
        1,
    )
    passed = feed_result(0, middle_zero, partial).astype(bf16)

    middle_one, kept_one = forward_attend(1, passed.astype(f32))
    unit_one, rsd_one, second_one, up_bias = feed_inputs(1, middle_one)
    su, eu, sd, ed = adapters[1][4:]
    branch_one = spread(given.astype(bf16))
    active, low_u, low_d, partial, grad_up, inner_d, inner_u, partial_back = feed_call(
        feed_both_kernel,
        "feed_both",
        (second_one, branch_one, feed_tables[1], up_bias, eu, sd, su, ed),
        (local_f, rank, rank, width, local_f, rank, rank, width),
        local_f,
        2,
    )
    shared, owned = feed_adapters(
        second_one, branch_one, low_u, low_d, inner_u, inner_d, active, grad_up
    )
    grad_middle = feed_grads(1, given, unit_one, rsd_one, partial_back)
    grad_one, more, quartered = backward_attend(1, kept_one, grad_middle)
    mine_one = offloaded_grads(shared + more, quartered, owned)

    su, eu, sd, ed = adapters[0][4:]
    branch_zero = spread(grad_one.astype(bf16))
    grad_up, inner_d, inner_u, partial_back = feed_call(
        feed_back_kernel,
        "feed_back",
        (branch_zero, feed_tables[0], slope_zero, eu, sd, su, ed),
        (local_f, rank, rank, width),
        local_f,
        1,
    )
    shared, owned = feed_adapters(
        second_zero, branch_zero, low_u_zero, low_d_zero, inner_u, inner_d, active_zero, grad_up
    )
    grad_middle_zero = feed_grads(0, grad_one, unit_zero, rsd_zero, partial_back)
    partial, _ = lax.optimization_barrier((partial, grad_middle_zero))
    final = feed_result(1, middle_one, partial).astype(bf16)
    grad_zero, more, quartered = backward_attend(0, kept_zero, grad_middle_zero)
    shared = shared + more
    mine_zero = scattered_grads(shared, quartered, owned)
    grads = spread_grads(mine_zero, mine_one, shared, quartered, owned)

    def both_micros(zero, one, kind):
        own = jnp.where(low_section, zero, one)
        received = swap(jnp.where(low_section, one, zero).astype(bf16)).astype(kind)
        return jnp.where(low_section, jnp.stack([own, received]), jnp.stack([received, own]))

    section_outputs = both_micros(passed, final, bf16)
    input_grads = both_micros(grad_zero, grad_one, f32)
    onehot = (bank_choice[:, None] == jnp.arange(banks)[None, :]).astype(f32)

    def placed(pair, transpose):
        out = sum(
            onehot[m][:, None, None] * pair[m].astype(f32)[None] for m in range(2)
        )
        return (out.transpose(0, 2, 1) if transpose else out)[None]

    (
        up_shrink_grad,
        down_expand_grad,
        out_expand_grad,
        q_shrink_grad,
        kv_shrink_grad,
        kv_expand_grad,
        q_expand_grad,
        out_shrink_grad,
        up_expand_grad,
        down_shrink_grad,
    ) = grads
    return (
        section_outputs[None],
        input_grads[None],
        placed(q_shrink_grad, True),
        placed(q_expand_grad, False),
        placed(kv_shrink_grad, True),
        placed(kv_expand_grad, False),
        placed(out_shrink_grad, True),
        placed(out_expand_grad, False),
        placed(up_shrink_grad, True),
        placed(up_expand_grad, False),
        placed(down_shrink_grad, True),
        placed(down_expand_grad, False),
    )


def solution(mesh):
    return jax.shard_map(
        per_device,
        mesh=mesh,
        in_specs=(
            P(None, ("dp", "tensor"), None),
            P(None, ("dp", "tensor"), None),
            P(),
            P(),
            P("section", None),
            P("section", None),
            P("section", "dp", "tensor"),
            P("section", "tensor"),
            P("section", "dp", None),
            P("section", None),
            P("section", "tensor", "dp"),
            P("section", None),
            P("section", None),
            P("section", None),
            P("section", "dp", "tensor"),
            P("section", "tensor"),
            P("section", "tensor", "dp"),
            P("section", None),
            P("section", None, None, None),
            P("section", None, None, "tensor"),
            P("section", None, None, None),
            P("section", None, None, None),
            P("section", None, "tensor", None),
            P("section", None, None, None),
            P("section", None, None, None),
            P("section", None, None, "tensor"),
            P("section", None, "tensor", None),
            P("section", None, None, None),
        ),
        out_specs=(
            P("section", None, ("dp", "tensor"), None),
            P("section", None, ("dp", "tensor"), None),
            P("section", None, None, None),
            P("section", None, None, "tensor"),
            P("section", None, None, None),
            P("section", None, None, None),
            P("section", None, "tensor", None),
            P("section", None, None, None),
            P("section", None, None, None),
            P("section", None, None, "tensor"),
            P("section", None, "tensor", None),
            P("section", None, None, None),
        ),
        check_vma=False,
    )
```

```python
import math

import jax
import jax.numpy as jnp
from jax import lax
from jax.experimental import pallas as pl
from jax.experimental.layout import Layout, with_layout_constraint
from jax.experimental.pallas import tpu as pltpu
from jax.sharding import PartitionSpec as P

WINDOW = 1024
epsilon = 1e-05
masked_score = -1e30
bf16 = jnp.bfloat16
f32 = jnp.float32


def plain(left, right):
    return jnp.dot(left, right, preferred_element_type=f32)


def against(left, right):
    return lax.dot_general(left, right, (((1,), (1,)), ((), ())), preferred_element_type=f32)


def across(left, right):
    return lax.dot_general(left, right, (((0,), (0,)), ((), ())), preferred_element_type=f32)


def around(block, axis, distance):
    size = lax.axis_size(axis)
    return lax.ppermute(block, axis, [(i, (i + distance) % size) for i in range(size)])


def along(block, axis, distance):
    size = lax.axis_size(axis)
    route = [(i, i + distance) for i in range(size) if 0 <= i + distance < size]
    return lax.ppermute(block, axis, route)


def flipped(block, axis, bit):
    size = lax.axis_size(axis)
    return lax.ppermute(block, axis, [(i, i ^ bit) for i in range(size)])


def pick(table, index, size=1):
    return lax.dynamic_slice_in_dim(table, index, size, 0)


def norm_parts(value):
    centred = value - jnp.mean(value, axis=-1, keepdims=True)
    spread = lax.rsqrt(jnp.mean(centred * centred, axis=-1, keepdims=True) + epsilon)
    return centred * spread, spread


def norm_back(unit, spread, scaled):
    inner = jnp.mean(scaled * unit, axis=-1, keepdims=True)
    return spread * (scaled - jnp.mean(scaled, axis=-1, keepdims=True) - unit * inner)


def gelu_parts(value):
    rate = math.sqrt(2.0 / math.pi)
    square = value * value
    bend = jnp.tanh(rate * (value + 0.044715 * value * square))
    rising = 0.5 * (1.0 + bend)
    slope = rising + 0.5 * value * (1.0 - bend * bend) * (rate * (1.0 + 3 * 0.044715 * square))
    return value * rising, slope


def side_blocks(query_ref, group, head):
    begin = group * 4 * head
    return jnp.concatenate(
        [query_ref[:, begin + h * head : begin + (h + 1) * head] for h in range(4)], axis=0
    )


def put_blocks(out_ref, value, group, head):
    rows = value.shape[0] // 4
    for h in range(4):
        begin = (group * 4 + h) * head
        out_ref[:, begin : begin + head] = value[h * rows : (h + 1) * rows]


def table_copies(table_ref, buf, sem, layer, begin):
    ranks, chunks, _, width = buf.shape
    return [
        pltpu.make_async_copy(
            table_ref.at[x, y, layer, :, pl.ds(begin, width)], buf.at[x, y], sem.at[x, y]
        )
        for x in range(ranks)
        for y in range(chunks)
    ]


def query_kernel(layer, normed_ref, table_ref, bias_ref, eq_ref, sq_ref, out_ref, low_ref, buf, sem):
    ranks, chunks, rows, width = buf.shape
    copies = table_copies(table_ref, buf, sem, layer, 0)
    for copy in copies:
        copy.start()
    normed = normed_ref[...]
    low = against(normed, sq_ref[...]).astype(bf16)
    low_ref[...] = low
    for x in range(ranks):
        columns = pl.ds(x * width, width)
        total = bias_ref[:, columns] + plain(low, eq_ref[:, columns])
        for y in range(chunks):
            copies[x * chunks + y].wait()
            total = total + plain(normed[:, y * rows : (y + 1) * rows], buf[x, y])
        out_ref[:, columns] = total.astype(bf16)


def table_scratch(table, width):
    ranks, chunks, _, rows, _ = table.shape
    return [
        pltpu.VMEM((ranks, chunks, rows, width), bf16),
        pltpu.SemaphoreType.DMA((ranks, chunks)),
    ]


held = pl.BlockSpec(memory_space=pltpu.VMEM)
remote = pl.BlockSpec(memory_space=pl.ANY)


def project_queries(layer, normed, table, bias, eq, sq):
    rows, model = normed.shape
    rank = sq.shape[0]
    width = model // table.shape[0]
    return pl.pallas_call(
        lambda *refs: query_kernel(layer, *refs),
        in_specs=[held, remote, held, held, held],
        out_specs=[held] * 2,
        out_shape=[
            jax.ShapeDtypeStruct((rows, model), bf16),
            jax.ShapeDtypeStruct((rows, rank), bf16),
        ],
        scratch_shapes=table_scratch(table, width),
        compiler_params=pltpu.CompilerParams(vmem_limit_bytes=20 * 2**20),
        cost_estimate=pl.CostEstimate(
            flops=8 * rows * model * model, bytes_accessed=2 * model * model, transcendentals=0
        ),
        name="project_queries",
    )(normed, table, bias, eq, sq)


def attend_kernel(
    layer, head, query_ref, keyval_ref, bias_ref, table_ref, so_ref, eo_ref,
    prob_ref, mixed_ref, low_ref, out_ref, buf, sem, prob_buf, prob_sem,
):
    ranks, chunks, rows, width = buf.shape
    copies = table_copies(table_ref, buf, sem, layer, width)
    for copy in copies:
        copy.start()
    scale = 1.0 / math.sqrt(head)
    bias = jnp.concatenate([bias_ref[...].astype(f32)] * 4, axis=0)
    prob_copies = [
        pltpu.make_async_copy(prob_buf.at[g], prob_ref.at[g], prob_sem.at[g])
        for g in range(prob_buf.shape[0])
    ]
    for g, prob_copy in enumerate(prob_copies):
        queries = side_blocks(query_ref, g, head)
        scores = against(queries, keyval_ref[:, :head]) * scale + bias
        lifted = jnp.exp(scores - jnp.max(scores, axis=-1, keepdims=True))
        probs = lifted * (1.0 / jnp.sum(lifted, axis=-1, keepdims=True))
        prob_buf[g] = probs
        prob_copy.start()
        put_blocks(mixed_ref, plain(probs.astype(bf16), keyval_ref[:, head:]).astype(bf16), g, head)
    mixed = mixed_ref[...]
    low = against(mixed, so_ref[...]).astype(bf16)
    low_ref[...] = low
    for copy in copies:
        copy.wait()
    for y in range(chunks):
        columns = pl.ds(y * rows, rows)
        total = plain(low, eo_ref[:, columns])
        for x in range(ranks):
            total = total + against(mixed[:, x * width : (x + 1) * width], buf[x, y])
        out_ref[:, columns] = total
    for prob_copy in prob_copies:
        prob_copy.wait()


def attend(layer, queries, key_block, bias, table, so, eo, head):
    rows, model = queries.shape
    keys = key_block.shape[0]
    groups = model // head // 4
    rank = so.shape[0]
    return pl.pallas_call(
        lambda *refs: attend_kernel(layer, head, *refs),
        in_specs=[held, held, held, remote, held, held],
        out_specs=[remote] + [held] * 3,
        out_shape=[
            jax.ShapeDtypeStruct((groups, 4 * rows, keys), f32),
            jax.ShapeDtypeStruct((rows, model), bf16),
            jax.ShapeDtypeStruct((rows, rank), bf16),
            jax.ShapeDtypeStruct((rows, model), f32),
        ],
        scratch_shapes=table_scratch(table, model // table.shape[0])
        + [pltpu.VMEM((groups, 4 * rows, keys), f32), pltpu.SemaphoreType.DMA((groups,))],
        compiler_params=pltpu.CompilerParams(vmem_limit_bytes=36 * 2**20),
        cost_estimate=pl.CostEstimate(
            flops=4 * rows * model * (keys + 2 * model),
            bytes_accessed=2 * model * model,
            transcendentals=groups * 4 * rows * keys,
        ),
        name="attend",
    )(queries, key_block, bias, table, so, eo)


def attend_back_kernel(
    layer, head, branch_ref, table_ref, so_ref, eo_ref, prob_ref, query_ref, keyval_ref, eq_ref, sq_ref,
    dq_ref, dkv_ref, inner_o_ref, inner_q_ref, part_ref,
    out_buf, out_sem, query_buf, query_sem, prob_buf, prob_sem, mixed_buf, key_sum, value_sum,
):
    ranks, chunks, rows, width = out_buf.shape
    out_copies = table_copies(table_ref, out_buf, out_sem, layer, width)
    query_copies = table_copies(table_ref, query_buf, query_sem, layer, 0)
    prob_copies = [
        pltpu.make_async_copy(prob_ref.at[g], prob_buf.at[g], prob_sem.at[g])
        for g in range(prob_buf.shape[0])
    ]
    for g, prob_copy in enumerate(prob_copies):
        for copy in out_copies[g * chunks : (g + 1) * chunks] + [prob_copy]:
            copy.start()
    for copy in query_copies:
        copy.start()
    scale = 1.0 / math.sqrt(head)
    branch = branch_ref[...]
    inner_o = against(branch, eo_ref[...]).astype(bf16)
    inner_o_ref[...] = inner_o
    for g, prob_copy in enumerate(prob_copies):
        columns = pl.ds(g * width, width)
        total = plain(inner_o, so_ref[:, columns])
        for y in range(chunks):
            out_copies[g * chunks + y].wait()
            total = total + plain(branch[:, y * rows : (y + 1) * rows], out_buf[g, y])
        mixed_buf[:, columns] = total.astype(bf16)
        grad = side_blocks(mixed_buf, g, head)
        prob_copy.wait()
        probs = prob_buf[g]
        grad_probs = against(grad, keyval_ref[:, head:])
        delta = jnp.sum(grad_probs * probs, axis=-1, keepdims=True)
        grad_scores = (probs * (grad_probs - delta)).astype(bf16)
        put_blocks(dq_ref, (plain(grad_scores, keyval_ref[:, :head]) * scale).astype(bf16), g, head)
        keys = across(grad_scores, side_blocks(query_ref, g, head))
        values = across(probs.astype(bf16), grad)
        if g == 0:
            key_sum[...] = keys
            value_sum[...] = values
        else:
            key_sum[...] += keys
            value_sum[...] += values
    dkv_ref[:, :head] = (key_sum[...] * scale).astype(bf16)
    dkv_ref[:, head:] = value_sum[...].astype(bf16)
    grad_q = dq_ref[...]
    inner_q = against(grad_q, eq_ref[...]).astype(bf16)
    inner_q_ref[...] = inner_q
    for copy in query_copies:
        copy.wait()
    for y in range(chunks):
        columns = pl.ds(y * rows, rows)
        total = plain(inner_q, sq_ref[:, columns])
        for x in range(ranks):
            total = total + against(grad_q[:, x * width : (x + 1) * width], query_buf[x, y])
        part_ref[:, columns] = total


def attend_back(layer, branch, table, so, eo, probs, queries, key_block, eq, sq, head):
    rows, model = queries.shape
    keys = key_block.shape[0]
    groups = probs.shape[0]
    rank = so.shape[0]
    width = model // table.shape[0]
    return pl.pallas_call(
        lambda *refs: attend_back_kernel(layer, head, *refs),
        in_specs=[held, remote, held, held, remote] + [held] * 4,
        out_specs=[held] * 5,
        out_shape=[
            jax.ShapeDtypeStruct((rows, model), bf16),
            jax.ShapeDtypeStruct((keys, 2 * head), bf16),
            jax.ShapeDtypeStruct((rows, rank), bf16),
            jax.ShapeDtypeStruct((rows, rank), bf16),
            jax.ShapeDtypeStruct((rows, model), f32),
        ],
        scratch_shapes=table_scratch(table, width)
        + table_scratch(table, width)
        + [
            pltpu.VMEM((groups, 4 * rows, keys), f32),
            pltpu.SemaphoreType.DMA((groups,)),
            pltpu.VMEM((rows, model), bf16),
            pltpu.VMEM((keys, head), f32),
            pltpu.VMEM((keys, head), f32),
        ],
        compiler_params=pltpu.CompilerParams(vmem_limit_bytes=44 * 2**20),
        cost_estimate=pl.CostEstimate(
            flops=8 * rows * model * (keys + 2 * model),
            bytes_accessed=4 * model * model + 4 * groups * 4 * rows * keys,
            transcendentals=0,
        ),
        name="attend_back",
    )(branch, table, so, eo, probs, queries, key_block, eq, sq)


def feed_copies(table_ref, buf, sems):
    _, count, chunks, rows, tile = buf.shape
    half = count // 2 * tile
    copies = []
    for j in range(count):
        pair = []
        for k in range(2):
            columns = pl.ds(j * tile % half + k * half, tile)
            pair.append(
                pltpu.make_async_copy(
                    table_ref.at[:, j * tile // half, :, columns], buf.at[k, j], sems.at[k, j]
                )
            )
        copies.append(pair)
    return copies


def plain_chunks(left, buf, k, j):
    rows = buf.shape[3]
    return sum(plain(left[:, i * rows : (i + 1) * rows], buf[k, j, i]) for i in range(buf.shape[2]))


def add_against(total, left, buf, k, j):
    rows = buf.shape[3]
    for i in range(buf.shape[2]):
        columns = pl.ds(i * rows, rows)
        if j == 0:
            total[:, columns] = against(left, buf[k, j, i])
        else:
            total[:, columns] += against(left, buf[k, j, i])


def feed_kernel(
    second_ref, table_ref, bias_ref, eu_ref, sd_ref, su_ref, ed_ref,
    active_ref, slope_ref, low_u_ref, low_d_ref, out_ref, buf, sems, total,
):
    _, count, _, _, tile = buf.shape
    copies = feed_copies(table_ref, buf, sems)
    for up, down in copies:
        up.start()
        down.start()
    second = second_ref[...]
    low_u = against(second, su_ref[...]).astype(bf16)
    low_u_ref[...] = low_u
    low = 0.0
    for j in range(count):
        columns = pl.ds(j * tile, tile)
        copies[j][0].wait()
        upward = plain_chunks(second, buf, 0, j)
        upward = upward + plain(low_u, eu_ref[:, columns]) + bias_ref[:, columns]
        active, slope = gelu_parts(upward)
        active = active.astype(bf16)
        active_ref[:, columns] = active
        slope_ref[:, columns] = slope.astype(bf16)
        low = low + against(active, sd_ref[:, columns])
        copies[j][1].wait()
        add_against(total, active, buf, 1, j)
    low_d = low.astype(bf16)
    low_d_ref[...] = low_d
    out_ref[...] = (total[...] + plain(low_d, ed_ref[...])).astype(bf16)


def feed_back_kernel(
    branch_ref, table_ref, slope_ref, eu_ref, sd_ref, su_ref, ed_ref,
    grad_up_ref, inner_d_ref, inner_u_ref, out_ref, buf, sems, total,
):
    _, count, _, _, tile = buf.shape
    copies = feed_copies(table_ref, buf, sems)
    for up, down in copies:
        down.start()
        up.start()
    branch = branch_ref[...]
    inner_d = against(branch, ed_ref[...]).astype(bf16)
    inner_d_ref[...] = inner_d
    inner = 0.0
    for j in range(count):
        columns = pl.ds(j * tile, tile)
        copies[j][1].wait()
        grad = plain_chunks(branch, buf, 1, j) + plain(inner_d, sd_ref[:, columns])
        grad = (grad * slope_ref[:, columns].astype(f32)).astype(bf16)
        grad_up_ref[:, columns] = grad
        inner = inner + against(grad, eu_ref[:, columns])
        copies[j][0].wait()
        add_against(total, grad, buf, 0, j)
    inner_u = inner.astype(bf16)
    inner_u_ref[...] = inner_u
    out_ref[...] = (total[...] + plain(inner_u, su_ref[...])).astype(bf16)


def feed_both_kernel(
    second_ref, branch_ref, table_ref, bias_ref, eu_ref, sd_ref, su_ref, ed_ref,
    active_ref, low_u_ref, low_d_ref, out_ref, grad_up_ref, inner_d_ref, inner_u_ref, back_ref,
    buf, sems, total, back_total,
):
    _, count, _, _, tile = buf.shape
    copies = feed_copies(table_ref, buf, sems)
    for up, down in copies:
        up.start()
        down.start()
    second = second_ref[...]
    branch = branch_ref[...]
    low_u = against(second, su_ref[...]).astype(bf16)
    low_u_ref[...] = low_u
    inner_d = against(branch, ed_ref[...]).astype(bf16)
    inner_d_ref[...] = inner_d
    low = 0.0
    inner = 0.0
    for j in range(count):
        columns = pl.ds(j * tile, tile)
        copies[j][0].wait()
        upward = plain_chunks(second, buf, 0, j)
        upward = upward + plain(low_u, eu_ref[:, columns]) + bias_ref[:, columns]
        active, slope = gelu_parts(upward)
        active = active.astype(bf16)
        active_ref[:, columns] = active
        low = low + against(active, sd_ref[:, columns])
        copies[j][1].wait()
        add_against(total, active, buf, 1, j)
        grad = plain_chunks(branch, buf, 1, j) + plain(inner_d, sd_ref[:, columns])
        grad = (grad * slope).astype(bf16)
        grad_up_ref[:, columns] = grad
        inner = inner + against(grad, eu_ref[:, columns])
        add_against(back_total, grad, buf, 0, j)
    inner_u = inner.astype(bf16)
    inner_u_ref[...] = inner_u
    back_ref[...] = (back_total[...] + plain(inner_u, su_ref[...])).astype(bf16)
    low_d = low.astype(bf16)
    low_d_ref[...] = low_d
    out_ref[...] = (total[...] + plain(low_d, ed_ref[...])).astype(bf16)


def feed_call(kernel, name, inputs, outputs, hidden, totals):
    table = [value for value in inputs if value.ndim == 4][0]
    rows, model = inputs[0].shape
    tile = 512
    chunks = table.shape[0]
    return pl.pallas_call(
        kernel,
        in_specs=[remote if value.ndim == 4 else held for value in inputs],
        out_specs=[held] * len(outputs),
        out_shape=[jax.ShapeDtypeStruct((rows, width), bf16) for width in outputs],
        scratch_shapes=[
            pltpu.VMEM((2, hidden // tile, chunks, model // chunks, tile), bf16),
            pltpu.SemaphoreType.DMA((2, hidden // tile)),
        ]
        + [pltpu.VMEM((rows, model), f32)] * totals,
        compiler_params=pltpu.CompilerParams(vmem_limit_bytes=44 * 2**20),
        cost_estimate=pl.CostEstimate(
            flops=4 * totals * rows * model * hidden,
            bytes_accessed=4 * model * hidden,
            transcendentals=rows * hidden,
        ),
        name=name,
    )(*inputs)


def per_device(
    block_input,
    cotangent,
    doc_lengths,
    bank_choice,
    first_gain,
    first_shift,
    query_weight,
    query_bias,
    keyval_weight,
    value_bias,
    output_weight,
    output_bias,
    second_gain,
    second_shift,
    upward_weight,
    upward_bias,
    downward_weight,
    downward_bias,
    query_shrink,
    query_expand,
    keyval_shrink,
    keyval_expand,
    output_shrink,
    output_expand,
    upward_shrink,
    upward_expand,
    downward_shrink,
    downward_expand,
):
    section = lax.axis_index("section")
    data = lax.axis_index("dp")
    tensor = lax.axis_index("tensor")
    low_section = section == 0
    width = block_input.shape[2]
    rows = block_input.shape[1]
    ranks = lax.axis_size("tensor")
    span = rows * ranks
    head = value_bias.shape[1]
    local_q = query_bias.shape[1]
    local_f = upward_bias.shape[1]
    rank = query_expand.shape[2]
    banks = query_expand.shape[1]
    reach = WINDOW // span
    sides = [(0, 1), (1, 0)]

    def swap(value):
        return lax.ppermute(value, "section", sides)

    def by_layer(own, other):
        return jnp.where(low_section, own, other), jnp.where(low_section, other, own)

    def spread(block):
        parts = [block] + [around(block, "tensor", -j) for j in range(1, ranks)]
        return jnp.concatenate(parts, axis=0)

    def reduce_rows(partial):
        low = partial.astype(bf16)
        total = partial[:rows].astype(f32)
        for j in range(1, ranks):
            total = total + around(low[j * rows : (j + 1) * rows], "tensor", j).astype(f32)
        return total

    own_bank = lax.dynamic_index_in_dim(bank_choice, section, 0, keepdims=False)
    other_bank = lax.dynamic_index_in_dim(bank_choice, 1 - section, 0, keepdims=False)

    chips = lax.axis_size("dp") // 4
    both = ("section", "dp")
    every = ("section", "dp", "tensor")
    order = [
        side * 4 * chips + chip * 4 + near
        for chip in range(chips)
        for side in range(2)
        for near in range(4)
    ]
    order_all = [place * ranks + x for x in range(ranks) for place in order]

    def row_major(block):
        return with_layout_constraint(block, Layout(major_to_minor=(0, 1)))

    def gather(shard):
        table = lax.all_gather(row_major(shard), both, axis=0, tiled=True, axis_index_groups=[order])
        return row_major(table).reshape(chips, 2, -1, shard.shape[1])

    def gather_all(shard):
        table = lax.all_gather(
            row_major(shard), every, axis=0, tiled=True, axis_index_groups=[order_all]
        )
        return row_major(table).reshape(ranks, chips, 2, -1, shard.shape[1])

    def halves(shard):
        cut = shard.shape[1] // 2
        return shard[:, :cut], shard[:, cut:]

    keyval_half = jnp.where(tensor % 2 == 0, keyval_weight[0][:, :head], keyval_weight[0][:, head:])
    early_all = gather_all(
        jnp.concatenate([query_weight[0], row_major(output_weight[0].T), keyval_half], axis=1)
    )
    keyval_ws = [
        jnp.concatenate(
            [early_all[x, :, layer, :, 2 * local_q :].reshape(width, head) for x in range(2)], axis=1
        )
        for layer in range(2)
    ]

    vectors = jnp.concatenate(
        [
            first_gain,
            first_shift,
            jnp.zeros_like(value_bias),
            value_bias,
            output_bias,
            second_gain,
            second_shift,
            upward_bias,
            downward_bias,
        ],
        axis=1,
    )
    vector_sizes = [width, width, 2 * head, width, width, width, local_f, width]
    vector_layers = by_layer(vectors, swap(vectors))

    def chosen(table, bank, transpose):
        block = lax.dynamic_index_in_dim(table[0], bank, 0, keepdims=False)
        return block.T if transpose else block

    def pack(bank, parts):
        return jnp.concatenate([chosen(table, bank, flip) for table, flip in parts], axis=1)

    def exchanged(parts):
        return by_layer(pack(own_bank, parts), swap(pack(other_bank, parts)))

    def cut_pack(parts):
        own = jnp.concatenate([pack(own_bank, parts), query_rows], axis=1)
        other = jnp.concatenate([pack(other_bank, parts), query_rows], axis=1)
        return by_layer(own, swap(other))

    query_rows = jnp.broadcast_to(query_bias, (rank, local_q))
    cut_layers = jnp.stack(cut_pack([(query_expand, False), (output_shrink, True)]))
    cut_parts = jnp.stack(
        [cut_layers] + [around(cut_layers, "tensor", j) for j in range(1, ranks)]
    )
    cut_whole = jnp.stack(
        [
            lax.dynamic_index_in_dim(cut_parts, (tensor - r) % ranks, 0, keepdims=False)
            for r in range(ranks)
        ],
        axis=2,
    ).reshape(2, rank, ranks, 3, local_q)
    eq_all, so_all, query_bias_all = [
        cut_whole[:, :, :, k].reshape(2, rank, ranks * local_q) for k in range(3)
    ]
    early_layers = exchanged([(query_shrink, True), (keyval_shrink, True), (keyval_expand, False)])
    late_layers = exchanged(
        [
            (output_expand, False),
            (upward_shrink, True),
            (upward_expand, False),
            (downward_shrink, True),
            (downward_expand, False),
        ]
    )

    up_halves = halves(upward_weight[0])
    down_halves = halves(row_major(downward_weight[0].T))
    side = [jnp.concatenate([up_halves[h], down_halves[h]], axis=1) for h in range(2)]
    keep = jnp.where(low_section, side[0], side[1])
    gained = swap(jnp.where(low_section, side[1], side[0]))
    feed_tables = [gather(table) for table in by_layer(keep, gained)]

    def split(table, sizes):
        cuts = [0]
        for size in sizes:
            cuts.append(cuts[-1] + size)
        return [table[:, a:b] for a, b in zip(cuts[:-1], cuts[1:])]

    small = [
        [part.astype(f32) for part in split(vector_layers[layer], vector_sizes)]
        for layer in range(2)
    ]
    adapters = [
        split(early_layers[layer], [width, width, 2 * head])
        + split(late_layers[layer], [width, width, local_f, local_f, width])
        for layer in range(2)
    ]

    inside = jnp.arange(rows, dtype=jnp.int32)
    query_place = data * span + tensor * rows + inside
    key_place = jnp.concatenate(
        [
            (data - back) * span + (tensor + j) % ranks * rows + inside
            for j in range(ranks)
            for back in range(reach, -1, -1)
        ]
    )
    lengths = lax.dynamic_index_in_dim(doc_lengths, section, 0, keepdims=False)
    ends = jnp.cumsum(lengths)
    query_doc = jnp.sum((query_place[:, None] >= ends[None, :]).astype(jnp.int32), axis=1)
    key_doc = jnp.sum((key_place[:, None] >= ends[None, :]).astype(jnp.int32), axis=1)
    distance = query_place[:, None] - key_place[None, :]
    allowed = (
        (key_place[None, :] >= 0)
        & (distance >= 0)
        & (distance < WINDOW)
        & (query_doc[:, None] == key_doc[None, :])
    )
    bias = jnp.where(allowed, 0.0, masked_score).astype(bf16)

    def forward_attend(layer, hidden):
        gain1, shift1, kv_bias, out_bias = small[layer][:4]
        sq, skv, ekv, eo = adapters[layer][:4]
        unit1, rsd1 = norm_parts(hidden)
        normed = (unit1 * gain1 + shift1).astype(bf16)
        low_kv = against(normed, skv).astype(bf16)
        keyval = (plain(normed, keyval_ws[layer]) + kv_bias + plain(low_kv, ekv)).astype(bf16)
        pieces = [along(keyval, "dp", back) for back in range(reach, 0, -1)] + [keyval]
        key_block = spread(jnp.concatenate(pieces, axis=0))
        queries, low_q = project_queries(
            layer, normed, early_all, query_bias_all[layer, :1].astype(f32), eq_all[layer], sq
        )
        probs, mixed, low_o, attended = attend(
            layer, queries, key_block, bias, early_all, so_all[layer], eo, head
        )
        middle = hidden + (attended + out_bias)
        return middle, (unit1, rsd1, normed, low_q, low_kv, queries, key_block, probs, mixed, low_o)

    def feed_inputs(layer, middle):
        gain2, shift2, up_bias = small[layer][4:7]
        unit2, rsd2 = norm_parts(middle)
        second = spread((unit2 * gain2 + shift2).astype(bf16))
        return unit2, rsd2, second, up_bias

    def feed_result(layer, middle, partial):
        return middle + (reduce_rows(partial) + small[layer][7])

    def tiles(block):
        return block.reshape(rank, -1, 128).transpose(1, 0, 2)

    def flat(block):
        return block.transpose(1, 0, 2).reshape(rank, -1)

    turn, near = data // 4, data % 4

    def padded(pile, multiple):
        lack = -pile.shape[0] % multiple
        if not lack:
            return pile
        return jnp.concatenate([pile, jnp.zeros((lack,) + pile.shape[1:], pile.dtype)], axis=0)

    def piled(shared, quartered):
        pile = padded(jnp.concatenate([tiles(part) for part in shared], axis=0), ranks)
        return jnp.concatenate(
            [block.reshape((ranks, -1) + block.shape[1:]) for block in [pile] + [tiles(part) for part in quartered]],
            axis=1,
        ).astype(bf16)

    def owned_pile(mine, owned):
        pile = jnp.concatenate([mine] + [tiles(part) for part in owned], axis=0).astype(bf16)
        return padded(pile, lax.axis_size("dp"))

    def at(block, index, axis):
        return lax.dynamic_index_in_dim(block, index, axis, keepdims=False)

    def scattered_grads(layers):
        pile = jnp.stack([piled(shared, quartered) for shared, quartered, _ in layers], axis=1)
        mine = at(pile, tensor, 0).astype(f32)
        for j in range(1, ranks):
            mine = mine + around(at(pile, (tensor + j) % ranks, 0), "tensor", j).astype(f32)
        pile = jnp.stack([owned_pile(mine[i], layers[i][2]) for i in range(2)])
        pile = pile.reshape((2, chips, 4, -1) + pile.shape[2:])
        mine = at(pile, near, 2).astype(f32)
        for k in range(1, 4):
            mine = mine + flipped(at(pile, near ^ k, 2), "dp", k).astype(f32)
        pile = mine.astype(bf16)
        mine = at(pile, turn, 1).astype(f32)
        for k in range(1, chips):
            mine = mine + flipped(at(pile, turn ^ k, 1), "dp", 4 * k).astype(f32)
        return mine.astype(bf16)

    def crossed(block, mask):
        return lax.ppermute(block, both, [(i, i ^ mask) for i in range(8 * chips)])

    def spread_grads(zero, one, shared, quartered, owned):
        own = jnp.where(low_section, zero, one)
        away = jnp.where(low_section, one, zero)
        dp_size = 4 * chips
        home = jnp.stack([own, flipped(own, "dp", 2)])
        guest = jnp.stack([crossed(away, dp_size), crossed(away, dp_size + 2)])
        home, guest = [
            jnp.where(near // 2 == 0, block, block[::-1]) for block in (home, guest)
        ]
        pair = jnp.where(
            low_section, jnp.stack([home, guest], axis=1), jnp.stack([guest, home], axis=1)
        )
        parts = jnp.stack([pair] + [flipped(pair, "dp", 4 * k) for k in range(1, chips)])
        parts = jnp.stack([at(parts, turn ^ k, 0) for k in range(chips)])
        other = flipped(parts, "dp", 1)
        core = near % 2
        parts = jnp.stack(
            [jnp.where(core == 0, parts, other), jnp.where(core == 0, other, parts)], axis=2
        )
        pile = jnp.moveaxis(parts, 3, 0).reshape((2, -1) + parts.shape[5:])
        shared_sizes = [part.shape[1] // 128 for part in shared]
        quarter_sizes = [part.shape[1] // 128 // ranks for part in quartered]
        owned_sizes = [part.shape[1] // 128 for part in owned]
        each = -(-sum(shared_sizes) // ranks)
        own = pile[:, :each]
        parts = jnp.stack([own] + [around(own, "tensor", k) for k in range(1, ranks)])
        ordered = jnp.concatenate([at(parts, (tensor - r) % ranks, 0) for r in range(ranks)], axis=1)
        results = []
        for whole, begin, sizes in [
            (ordered, 0, shared_sizes),
            (pile, each, quarter_sizes + owned_sizes),
        ]:
            for count in sizes:
                results.append([flat(whole[m, begin : begin + count]) for m in range(2)])
                begin += count
        return results

    def feed_grads(layer, grad, unit2, rsd2, partial):
        return grad + norm_back(unit2, rsd2, reduce_rows(partial) * small[layer][4])

    def feed_adapters(second, branch, low_u, low_d, inner_u, inner_d, active, grad_up):
        shared = [across(inner_u, second), across(low_d, branch)]
        owned = [across(low_u, grad_up), across(inner_d, active)]
        return shared, owned

    def backward_attend(layer, kept, grad_middle):
        gain1 = small[layer][0]
        sq, skv, ekv, eo = adapters[layer][:4]
        unit1, rsd1, normed, low_q, low_kv, queries, key_block, probs, mixed, low_o = kept
        branch = grad_middle.astype(bf16)
        grad_q, grad_block, inner_o, inner_q, partial = attend_back(
            layer, branch, early_all, so_all[layer], eo, probs, queries, key_block,
            eq_all[layer], sq, head,
        )
        count = (reach + 1) * rows
        blocks = grad_block[:count].astype(f32)
        for j in range(1, ranks):
            part = grad_block[j * count : (j + 1) * count]
            blocks = blocks + around(part, "tensor", j).astype(f32)
        own = blocks[reach * rows :]
        for back in range(1, reach + 1):
            begin = (reach - back) * rows
            own = own + along(blocks[begin : begin + rows].astype(bf16), "dp", -back).astype(f32)
        grad_kv = own.astype(bf16)
        inner_kv = against(grad_kv, ekv).astype(bf16)
        grad_normed = partial + against(grad_kv, keyval_ws[layer]) + plain(inner_kv, skv)
        grad_hidden = grad_middle + norm_back(unit1, rsd1, grad_normed * gain1)
        shared = [
            across(low_o, branch),
            across(inner_q, normed),
            across(inner_kv, normed),
            across(low_kv, grad_kv),
        ]
        quartered = [across(low_q, grad_q), across(inner_o, mixed)]
        return grad_hidden, shared, quartered

    fresh = lax.dynamic_index_in_dim(block_input, section, 0, keepdims=False).astype(f32)
    given = lax.dynamic_index_in_dim(cotangent, section, 0, keepdims=False).astype(f32)

    middle_zero, kept_zero = forward_attend(0, fresh)
    unit_zero, rsd_zero, second_zero, up_bias = feed_inputs(0, middle_zero)
    su, eu, sd, ed = adapters[0][4:]
    active_zero, slope_zero, low_u_zero, low_d_zero, partial = feed_call(
        feed_kernel,
        "feed",
        (second_zero, feed_tables[0], up_bias, eu, sd, su, ed),
        (local_f, local_f, rank, rank, width),
        local_f,
        1,
    )
    passed = feed_result(0, middle_zero, partial).astype(bf16)

    middle_one, kept_one = forward_attend(1, passed.astype(f32))
    unit_one, rsd_one, second_one, up_bias = feed_inputs(1, middle_one)
    su, eu, sd, ed = adapters[1][4:]
    branch_one = spread(given.astype(bf16))
    active, low_u, low_d, partial, grad_up, inner_d, inner_u, partial_back = feed_call(
        feed_both_kernel,
        "feed_both",
        (second_one, branch_one, feed_tables[1], up_bias, eu, sd, su, ed),
        (local_f, rank, rank, width, local_f, rank, rank, width),
        local_f,
        2,
    )
    shared, owned = feed_adapters(
        second_one, branch_one, low_u, low_d, inner_u, inner_d, active, grad_up
    )
    grad_middle = feed_grads(1, given, unit_one, rsd_one, partial_back)
    grad_one, more, quartered = backward_attend(1, kept_one, grad_middle)
    layer_one = (shared + more, quartered, owned)
    partial, _ = lax.optimization_barrier((partial, grad_middle))
    final = feed_result(1, middle_one, partial).astype(bf16)

    su, eu, sd, ed = adapters[0][4:]
    branch_zero = spread(grad_one.astype(bf16))
    grad_up, inner_d, inner_u, partial_back = feed_call(
        feed_back_kernel,
        "feed_back",
        (branch_zero, feed_tables[0], slope_zero, eu, sd, su, ed),
        (local_f, rank, rank, width),
        local_f,
        1,
    )
    shared, owned = feed_adapters(
        second_zero, branch_zero, low_u_zero, low_d_zero, inner_u, inner_d, active_zero, grad_up
    )
    grad_middle_zero = feed_grads(0, grad_one, unit_zero, rsd_zero, partial_back)
    grad_zero, more, quartered = backward_attend(0, kept_zero, grad_middle_zero)
    shared = shared + more
    mine = scattered_grads([(shared, quartered, owned), layer_one])
    grads = spread_grads(mine[0], mine[1], shared, quartered, owned)

    def both_micros(zero, one, kind):
        own = jnp.where(low_section, zero, one)
        received = swap(jnp.where(low_section, one, zero).astype(bf16)).astype(kind)
        return jnp.where(low_section, jnp.stack([own, received]), jnp.stack([received, own]))

    passed, final, _ = lax.optimization_barrier((passed, final, grad_middle_zero))
    section_outputs = both_micros(passed, final, bf16)
    input_grads = both_micros(grad_zero, grad_one, f32)
    onehot = (bank_choice[:, None] == jnp.arange(banks)[None, :]).astype(f32)

    def placed(pair, transpose):
        out = sum(
            onehot[m][:, None, None] * pair[m].astype(f32)[None] for m in range(2)
        )
        return (out.transpose(0, 2, 1) if transpose else out)[None]

    (
        up_shrink_grad,
        down_expand_grad,
        out_expand_grad,
        q_shrink_grad,
        kv_shrink_grad,
        kv_expand_grad,
        q_expand_grad,
        out_shrink_grad,
        up_expand_grad,
        down_shrink_grad,
    ) = grads
    return (
        section_outputs[None],
        input_grads[None],
        placed(q_shrink_grad, True),
        placed(q_expand_grad, False),
        placed(kv_shrink_grad, True),
        placed(kv_expand_grad, False),
        placed(out_shrink_grad, True),
        placed(out_expand_grad, False),
        placed(up_shrink_grad, True),
        placed(up_expand_grad, False),
        placed(down_shrink_grad, True),
        placed(down_expand_grad, False),
    )


def solution(mesh):
    return jax.shard_map(
        per_device,
        mesh=mesh,
        in_specs=(
            P(None, ("dp", "tensor"), None),
            P(None, ("dp", "tensor"), None),
            P(),
            P(),
            P("section", None),
            P("section", None),
            P("section", "dp", "tensor"),
            P("section", "tensor"),
            P("section", "dp", None),
            P("section", None),
            P("section", "tensor", "dp"),
            P("section", None),
            P("section", None),
            P("section", None),
            P("section", "dp", "tensor"),
            P("section", "tensor"),
            P("section", "tensor", "dp"),
            P("section", None),
            P("section", None, None, None),
            P("section", None, None, "tensor"),
            P("section", None, None, None),
            P("section", None, None, None),
            P("section", None, "tensor", None),
            P("section", None, None, None),
            P("section", None, None, None),
            P("section", None, None, "tensor"),
            P("section", None, "tensor", None),
            P("section", None, None, None),
        ),
        out_specs=(
            P("section", None, ("dp", "tensor"), None),
            P("section", None, ("dp", "tensor"), None),
            P("section", None, None, None),
            P("section", None, None, "tensor"),
            P("section", None, None, None),
            P("section", None, None, None),
            P("section", None, "tensor", None),
            P("section", None, None, None),
            P("section", None, None, None),
            P("section", None, None, "tensor"),
            P("section", None, "tensor", None),
            P("section", None, None, None),
        ),
        check_vma=False,
    )
```

```python
import math

import jax
import jax.numpy as jnp
from jax import lax
from jax.experimental import pallas as pl
from jax.experimental.layout import Layout, with_layout_constraint
from jax.experimental.pallas import tpu as pltpu
from jax.sharding import PartitionSpec as P

WINDOW = 1024
epsilon = 1e-05
masked_score = -1e30
bf16 = jnp.bfloat16
f32 = jnp.float32


def plain(left, right):
    return jnp.dot(left, right, preferred_element_type=f32)


def against(left, right):
    return lax.dot_general(left, right, (((1,), (1,)), ((), ())), preferred_element_type=f32)


def across(left, right):
    return lax.dot_general(left, right, (((0,), (0,)), ((), ())), preferred_element_type=f32)


def around(block, axis, distance):
    size = lax.axis_size(axis)
    return lax.ppermute(block, axis, [(i, (i + distance) % size) for i in range(size)])


def along(block, axis, distance):
    size = lax.axis_size(axis)
    route = [(i, i + distance) for i in range(size) if 0 <= i + distance < size]
    return lax.ppermute(block, axis, route)


def flipped(block, axis, bit):
    size = lax.axis_size(axis)
    return lax.ppermute(block, axis, [(i, i ^ bit) for i in range(size)])


def pick(table, index, size=1):
    return lax.dynamic_slice_in_dim(table, index, size, 0)


def norm_parts(value):
    centred = value - jnp.mean(value, axis=-1, keepdims=True)
    spread = lax.rsqrt(jnp.mean(centred * centred, axis=-1, keepdims=True) + epsilon)
    return centred * spread, spread


def norm_back(unit, spread, scaled):
    inner = jnp.mean(scaled * unit, axis=-1, keepdims=True)
    return spread * (scaled - jnp.mean(scaled, axis=-1, keepdims=True) - unit * inner)


def gelu_parts(value):
    rate = math.sqrt(2.0 / math.pi)
    square = value * value
    bend = jnp.tanh(rate * (value + 0.044715 * value * square))
    rising = 0.5 * (1.0 + bend)
    slope = rising + 0.5 * value * (1.0 - bend * bend) * (rate * (1.0 + 3 * 0.044715 * square))
    return value * rising, slope


def side_blocks(query_ref, group, head):
    begin = group * 4 * head
    return jnp.concatenate(
        [query_ref[:, begin + h * head : begin + (h + 1) * head] for h in range(4)], axis=0
    )


def put_blocks(out_ref, value, group, head):
    rows = value.shape[0] // 4
    for h in range(4):
        begin = (group * 4 + h) * head
        out_ref[:, begin : begin + head] = value[h * rows : (h + 1) * rows]


def table_copies(table_ref, buf, sem, layer, begin):
    ranks, chunks, _, width = buf.shape
    return [
        pltpu.make_async_copy(
            table_ref.at[x, y, layer, :, pl.ds(begin, width)], buf.at[x, y], sem.at[x, y]
        )
        for x in range(ranks)
        for y in range(chunks)
    ]


def query_kernel(layer, normed_ref, table_ref, bias_ref, eq_ref, sq_ref, out_ref, low_ref, buf, sem):
    ranks, chunks, rows, width = buf.shape
    copies = table_copies(table_ref, buf, sem, layer, 0)
    for copy in copies:
        copy.start()
    normed = normed_ref[...]
    low = against(normed, sq_ref[...]).astype(bf16)
    low_ref[...] = low
    for x in range(ranks):
        columns = pl.ds(x * width, width)
        total = bias_ref[:, columns] + plain(low, eq_ref[:, columns])
        for y in range(chunks):
            copies[x * chunks + y].wait()
            total = total + plain(normed[:, y * rows : (y + 1) * rows], buf[x, y])
        out_ref[:, columns] = total.astype(bf16)


def table_scratch(table, width):
    ranks, chunks, _, rows, _ = table.shape
    return [
        pltpu.VMEM((ranks, chunks, rows, width), bf16),
        pltpu.SemaphoreType.DMA((ranks, chunks)),
    ]


held = pl.BlockSpec(memory_space=pltpu.VMEM)
remote = pl.BlockSpec(memory_space=pltpu.HBM)


def project_queries(layer, normed, table, bias, eq, sq):
    rows, model = normed.shape
    rank = sq.shape[0]
    width = model // table.shape[0]
    return pl.pallas_call(
        lambda *refs: query_kernel(layer, *refs),
        in_specs=[held, remote, held, held, held],
        out_specs=[held] * 2,
        out_shape=[
            jax.ShapeDtypeStruct((rows, model), bf16),
            jax.ShapeDtypeStruct((rows, rank), bf16),
        ],
        scratch_shapes=table_scratch(table, width),
        compiler_params=pltpu.CompilerParams(vmem_limit_bytes=20 * 2**20),
        cost_estimate=pl.CostEstimate(
            flops=8 * rows * model * model, bytes_accessed=2 * model * model, transcendentals=0
        ),
        name="project_queries",
    )(normed, table, bias, eq, sq)


def attend_kernel(
    layer, head, query_ref, keyval_ref, bias_ref, table_ref, so_ref, eo_ref,
    prob_ref, mixed_ref, low_ref, out_ref, buf, sem, prob_buf, prob_sem,
):
    ranks, chunks, rows, width = buf.shape
    copies = table_copies(table_ref, buf, sem, layer, width)
    for copy in copies:
        copy.start()
    scale = 1.0 / math.sqrt(head)
    bias = jnp.concatenate([bias_ref[...].astype(f32)] * 4, axis=0)
    prob_copies = [
        pltpu.make_async_copy(prob_buf.at[g], prob_ref.at[g], prob_sem.at[g])
        for g in range(prob_buf.shape[0])
    ]
    for g, prob_copy in enumerate(prob_copies):
        queries = side_blocks(query_ref, g, head)
        scores = against(queries, keyval_ref[:, :head]) * scale + bias
        lifted = jnp.exp(scores - jnp.max(scores, axis=-1, keepdims=True))
        probs = (lifted * (1.0 / jnp.sum(lifted, axis=-1, keepdims=True))).astype(bf16)
        prob_buf[g] = probs
        prob_copy.start()
        put_blocks(mixed_ref, plain(probs, keyval_ref[:, head:]).astype(bf16), g, head)
    mixed = mixed_ref[...]
    low = against(mixed, so_ref[...]).astype(bf16)
    low_ref[...] = low
    for copy in copies:
        copy.wait()
    for y in range(chunks):
        columns = pl.ds(y * rows, rows)
        total = plain(low, eo_ref[:, columns])
        for x in range(ranks):
            total = total + against(mixed[:, x * width : (x + 1) * width], buf[x, y])
        out_ref[:, columns] = total
    for prob_copy in prob_copies:
        prob_copy.wait()


def attend(layer, queries, key_block, bias, table, so, eo, head):
    rows, model = queries.shape
    keys = key_block.shape[0]
    groups = model // head // 4
    rank = so.shape[0]
    return pl.pallas_call(
        lambda *refs: attend_kernel(layer, head, *refs),
        in_specs=[held, held, held, remote, held, held],
        out_specs=[remote] + [held] * 3,
        out_shape=[
            jax.ShapeDtypeStruct((groups, 4 * rows, keys), bf16),
            jax.ShapeDtypeStruct((rows, model), bf16),
            jax.ShapeDtypeStruct((rows, rank), bf16),
            jax.ShapeDtypeStruct((rows, model), f32),
        ],
        scratch_shapes=table_scratch(table, model // table.shape[0])
        + [pltpu.VMEM((groups, 4 * rows, keys), bf16), pltpu.SemaphoreType.DMA((groups,))],
        compiler_params=pltpu.CompilerParams(vmem_limit_bytes=36 * 2**20),
        cost_estimate=pl.CostEstimate(
            flops=4 * rows * model * (keys + 2 * model),
            bytes_accessed=2 * model * model,
            transcendentals=groups * 4 * rows * keys,
        ),
        name="attend",
    )(queries, key_block, bias, table, so, eo)


def attend_back_kernel(
    layer, head, branch_ref, table_ref, so_ref, eo_ref, prob_ref, query_ref, keyval_ref, eq_ref, sq_ref,
    dq_ref, dkv_ref, inner_o_ref, inner_q_ref, part_ref,
    out_buf, out_sem, query_buf, query_sem, prob_buf, prob_sem, mixed_buf, key_sum, value_sum,
):
    ranks, chunks, rows, width = out_buf.shape
    out_copies = table_copies(table_ref, out_buf, out_sem, layer, width)
    query_copies = table_copies(table_ref, query_buf, query_sem, layer, 0)
    prob_copies = [
        pltpu.make_async_copy(prob_ref.at[g], prob_buf.at[g], prob_sem.at[g])
        for g in range(prob_buf.shape[0])
    ]
    for g, prob_copy in enumerate(prob_copies):
        for copy in out_copies[g * chunks : (g + 1) * chunks] + [prob_copy]:
            copy.start()
    for copy in query_copies:
        copy.start()
    scale = 1.0 / math.sqrt(head)
    branch = branch_ref[...]
    inner_o = against(branch, eo_ref[...]).astype(bf16)
    inner_o_ref[...] = inner_o
    for g, prob_copy in enumerate(prob_copies):
        columns = pl.ds(g * width, width)
        total = plain(inner_o, so_ref[:, columns])
        for y in range(chunks):
            out_copies[g * chunks + y].wait()
            total = total + plain(branch[:, y * rows : (y + 1) * rows], out_buf[g, y])
        mixed_buf[:, columns] = total.astype(bf16)
        grad = side_blocks(mixed_buf, g, head)
        prob_copy.wait()
        low_probs = prob_buf[g]
        probs = low_probs.astype(f32)
        grad_probs = against(grad, keyval_ref[:, head:])
        delta = jnp.sum(grad_probs * probs, axis=-1, keepdims=True)
        delta = delta / jnp.sum(probs, axis=-1, keepdims=True)
        grad_scores = (probs * (grad_probs - delta)).astype(bf16)
        put_blocks(dq_ref, (plain(grad_scores, keyval_ref[:, :head]) * scale).astype(bf16), g, head)
        keys = across(grad_scores, side_blocks(query_ref, g, head))
        values = across(low_probs, grad)
        if g == 0:
            key_sum[...] = keys
            value_sum[...] = values
        else:
            key_sum[...] += keys
            value_sum[...] += values
    dkv_ref[:, :head] = (key_sum[...] * scale).astype(bf16)
    dkv_ref[:, head:] = value_sum[...].astype(bf16)
    grad_q = dq_ref[...]
    inner_q = against(grad_q, eq_ref[...]).astype(bf16)
    inner_q_ref[...] = inner_q
    for copy in query_copies:
        copy.wait()
    for y in range(chunks):
        columns = pl.ds(y * rows, rows)
        total = plain(inner_q, sq_ref[:, columns])
        for x in range(ranks):
            total = total + against(grad_q[:, x * width : (x + 1) * width], query_buf[x, y])
        part_ref[:, columns] = total


def attend_back(layer, branch, table, so, eo, probs, queries, key_block, eq, sq, head):
    rows, model = queries.shape
    keys = key_block.shape[0]
    groups = probs.shape[0]
    rank = so.shape[0]
    width = model // table.shape[0]
    return pl.pallas_call(
        lambda *refs: attend_back_kernel(layer, head, *refs),
        in_specs=[held, remote, held, held, remote] + [held] * 4,
        out_specs=[held] * 5,
        out_shape=[
            jax.ShapeDtypeStruct((rows, model), bf16),
            jax.ShapeDtypeStruct((keys, 2 * head), bf16),
            jax.ShapeDtypeStruct((rows, rank), bf16),
            jax.ShapeDtypeStruct((rows, rank), bf16),
            jax.ShapeDtypeStruct((rows, model), f32),
        ],
        scratch_shapes=table_scratch(table, width)
        + table_scratch(table, width)
        + [
            pltpu.VMEM((groups, 4 * rows, keys), bf16),
            pltpu.SemaphoreType.DMA((groups,)),
            pltpu.VMEM((rows, model), bf16),
            pltpu.VMEM((keys, head), f32),
            pltpu.VMEM((keys, head), f32),
        ],
        compiler_params=pltpu.CompilerParams(vmem_limit_bytes=44 * 2**20),
        cost_estimate=pl.CostEstimate(
            flops=8 * rows * model * (keys + 2 * model),
            bytes_accessed=4 * model * model + 4 * groups * 4 * rows * keys,
            transcendentals=0,
        ),
        name="attend_back",
    )(branch, table, so, eo, probs, queries, key_block, eq, sq)


def feed_copies(table_ref, buf, sems):
    _, count, chunks, rows, tile = buf.shape
    half = count // 2 * tile
    copies = []
    for j in range(count):
        pair = []
        for k in range(2):
            columns = pl.ds(j * tile % half + k * half, tile)
            pair.append(
                pltpu.make_async_copy(
                    table_ref.at[:, j * tile // half, :, columns], buf.at[k, j], sems.at[k, j]
                )
            )
        copies.append(pair)
    return copies


def plain_chunks(left, buf, k, j):
    rows = buf.shape[3]
    return sum(plain(left[:, i * rows : (i + 1) * rows], buf[k, j, i]) for i in range(buf.shape[2]))


def against_chunk(left_ref, buf, k, i):
    tile = buf.shape[4]
    return sum(
        against(left_ref[:, j * tile : (j + 1) * tile], buf[k, j, i]) for j in range(buf.shape[1])
    )


def gathered(part_refs, whole):
    rows = part_refs[0].shape[0]
    for j, part_ref in enumerate(part_refs):
        whole[j * rows : (j + 1) * rows] = part_ref[...]
    return whole[...]


def feed_kernel(
    part0, part1, part2, part3, table_ref, bias_ref, eu_ref, sd_ref, su_ref, ed_ref,
    active_ref, slope_ref, low_u_ref, low_d_ref, out_ref, buf, sems, whole,
):
    _, count, chunks, rows, tile = buf.shape
    copies = feed_copies(table_ref, buf, sems)
    for up, _ in copies:
        up.start()
    for _, down in copies:
        down.start()
    second = gathered((part0, part1, part2, part3), whole)
    low_u = against(second, su_ref[...]).astype(bf16)
    low_u_ref[...] = low_u
    for j in range(count):
        columns = pl.ds(j * tile, tile)
        copies[j][0].wait()
        upward = plain_chunks(second, buf, 0, j)
        upward = upward + plain(low_u, eu_ref[:, columns]) + bias_ref[:, columns]
        active, slope = gelu_parts(upward)
        active_ref[:, columns] = active.astype(bf16)
        slope_ref[:, columns] = slope.astype(bf16)
    low_d = against(active_ref[...], sd_ref[...]).astype(bf16)
    low_d_ref[...] = low_d
    for _, down in copies:
        down.wait()
    for i in range(chunks):
        columns = pl.ds(i * rows, rows)
        out_ref[:, columns] = (
            against_chunk(active_ref, buf, 1, i) + plain(low_d, ed_ref[:, columns])
        ).astype(bf16)


def feed_back_kernel(
    part0, part1, part2, part3, table_ref, slope_ref, eu_ref, sd_ref, su_ref, ed_ref,
    grad_up_ref, inner_d_ref, inner_u_ref, out_ref, buf, sems, whole,
):
    _, count, chunks, rows, tile = buf.shape
    copies = feed_copies(table_ref, buf, sems)
    for _, down in copies:
        down.start()
    for up, _ in copies:
        up.start()
    branch = gathered((part0, part1, part2, part3), whole)
    inner_d = against(branch, ed_ref[...]).astype(bf16)
    inner_d_ref[...] = inner_d
    for j in range(count):
        columns = pl.ds(j * tile, tile)
        copies[j][1].wait()
        grad = plain_chunks(branch, buf, 1, j) + plain(inner_d, sd_ref[:, columns])
        grad_up_ref[:, columns] = (grad * slope_ref[:, columns].astype(f32)).astype(bf16)
    inner_u = against(grad_up_ref[...], eu_ref[...]).astype(bf16)
    inner_u_ref[...] = inner_u
    for up, _ in copies:
        up.wait()
    for i in range(chunks):
        columns = pl.ds(i * rows, rows)
        out_ref[:, columns] = (
            against_chunk(grad_up_ref, buf, 0, i) + plain(inner_u, su_ref[:, columns])
        ).astype(bf16)


def feed_both_kernel(
    part0, part1, part2, part3, branch_ref, table_ref, bias_ref, eu_ref, sd_ref, su_ref, ed_ref,
    active_ref, low_u_ref, low_d_ref, out_ref, grad_up_ref, inner_d_ref, inner_u_ref, back_ref,
    buf, sems, whole,
):
    _, count, chunks, rows, tile = buf.shape
    copies = feed_copies(table_ref, buf, sems)
    for up, down in copies:
        up.start()
        down.start()
    second = gathered((part0, part1, part2, part3), whole)
    branch = branch_ref[...]
    low_u = against(second, su_ref[...]).astype(bf16)
    low_u_ref[...] = low_u
    inner_d = against(branch, ed_ref[...]).astype(bf16)
    inner_d_ref[...] = inner_d
    for j in range(count):
        columns = pl.ds(j * tile, tile)
        copies[j][0].wait()
        upward = plain_chunks(second, buf, 0, j)
        upward = upward + plain(low_u, eu_ref[:, columns]) + bias_ref[:, columns]
        active, slope = gelu_parts(upward)
        active_ref[:, columns] = active.astype(bf16)
        copies[j][1].wait()
        grad = plain_chunks(branch, buf, 1, j) + plain(inner_d, sd_ref[:, columns])
        grad_up_ref[:, columns] = (grad * slope).astype(bf16)
    inner_u = against(grad_up_ref[...], eu_ref[...]).astype(bf16)
    inner_u_ref[...] = inner_u
    low_d = against(active_ref[...], sd_ref[...]).astype(bf16)
    low_d_ref[...] = low_d
    for i in range(chunks):
        columns = pl.ds(i * rows, rows)
        back_ref[:, columns] = (
            against_chunk(grad_up_ref, buf, 0, i) + plain(inner_u, su_ref[:, columns])
        ).astype(bf16)
        out_ref[:, columns] = (
            against_chunk(active_ref, buf, 1, i) + plain(low_d, ed_ref[:, columns])
        ).astype(bf16)


def feed_call(kernel, name, parts, inputs, outputs, hidden, matmuls):
    inputs = tuple(parts) + inputs
    table = [value for value in inputs if value.ndim == 4][0]
    model = parts[0].shape[1]
    rows = sum(part.shape[0] for part in parts)
    tile = 512
    chunks = table.shape[0]
    return pl.pallas_call(
        kernel,
        in_specs=[remote if value.ndim == 4 else held for value in inputs],
        out_specs=[held] * len(outputs),
        out_shape=[jax.ShapeDtypeStruct((rows, width), bf16) for width in outputs],
        scratch_shapes=[
            pltpu.VMEM((2, hidden // tile, chunks, model // chunks, tile), bf16),
            pltpu.SemaphoreType.DMA((2, hidden // tile)),
            pltpu.VMEM((rows, model), bf16),
        ],
        compiler_params=pltpu.CompilerParams(vmem_limit_bytes=40 * 2**20),
        cost_estimate=pl.CostEstimate(
            flops=2 * matmuls * rows * model * hidden,
            bytes_accessed=4 * model * hidden,
            transcendentals=rows * hidden,
        ),
        name=name,
    )(*inputs)


def per_device(
    block_input,
    cotangent,
    doc_lengths,
    bank_choice,
    first_gain,
    first_shift,
    query_weight,
    query_bias,
    keyval_weight,
    value_bias,
    output_weight,
    output_bias,
    second_gain,
    second_shift,
    upward_weight,
    upward_bias,
    downward_weight,
    downward_bias,
    query_shrink,
    query_expand,
    keyval_shrink,
    keyval_expand,
    output_shrink,
    output_expand,
    upward_shrink,
    upward_expand,
    downward_shrink,
    downward_expand,
):
    section = lax.axis_index("section")
    data = lax.axis_index("dp")
    tensor = lax.axis_index("tensor")
    low_section = section == 0
    width = block_input.shape[2]
    rows = block_input.shape[1]
    ranks = lax.axis_size("tensor")
    span = rows * ranks
    head = value_bias.shape[1]
    local_q = query_bias.shape[1]
    local_f = upward_bias.shape[1]
    rank = query_expand.shape[2]
    banks = query_expand.shape[1]
    reach = WINDOW // span
    sides = [(0, 1), (1, 0)]

    def swap(value):
        return lax.ppermute(value, "section", sides)

    def by_layer(own, other):
        return jnp.where(low_section, own, other), jnp.where(low_section, other, own)

    def spread_parts(block):
        return [block] + [around(block, "tensor", -j) for j in range(1, ranks)]

    def spread(block):
        return jnp.concatenate(spread_parts(block), axis=0)

    def reduce_rows(partial):
        low = partial.astype(bf16)
        total = partial[:rows].astype(f32)
        for j in range(1, ranks):
            total = total + around(low[j * rows : (j + 1) * rows], "tensor", j).astype(f32)
        return total

    own_bank = lax.dynamic_index_in_dim(bank_choice, section, 0, keepdims=False)
    other_bank = lax.dynamic_index_in_dim(bank_choice, 1 - section, 0, keepdims=False)

    chips = lax.axis_size("dp") // 4
    both = ("section", "dp")
    every = ("section", "dp", "tensor")
    order = [
        side * 4 * chips + chip * 4 + near
        for chip in range(chips)
        for side in range(2)
        for near in range(4)
    ]
    order_all = [place * ranks + x for x in range(ranks) for place in order]

    def row_major(block):
        return with_layout_constraint(block, Layout(major_to_minor=(0, 1)))

    def gather(shard):
        table = lax.all_gather(row_major(shard), both, axis=0, tiled=True, axis_index_groups=[order])
        return row_major(table).reshape(chips, 2, -1, shard.shape[1])

    def gather_all(shard):
        table = lax.all_gather(
            row_major(shard), every, axis=0, tiled=True, axis_index_groups=[order_all]
        )
        return row_major(table).reshape(ranks, chips, 2, -1, shard.shape[1])

    def halves(shard):
        cut = shard.shape[1] // 2
        return shard[:, :cut], shard[:, cut:]

    keyval_half = jnp.where(tensor % 2 == 0, keyval_weight[0][:, :head], keyval_weight[0][:, head:])
    early_all = gather_all(
        jnp.concatenate([query_weight[0], row_major(output_weight[0].T), keyval_half], axis=1)
    )
    keyval_ws = [
        jnp.concatenate(
            [early_all[x, :, layer, :, 2 * local_q :].reshape(width, head) for x in range(2)], axis=1
        )
        for layer in range(2)
    ]

    vectors = jnp.concatenate(
        [
            first_gain,
            first_shift,
            jnp.zeros_like(value_bias),
            value_bias,
            output_bias,
            second_gain,
            second_shift,
            upward_bias,
            downward_bias,
        ],
        axis=1,
    )
    vector_sizes = [width, width, 2 * head, width, width, width, local_f, width]
    vector_layers = by_layer(vectors, swap(vectors))

    def chosen(table, bank, transpose):
        block = lax.dynamic_index_in_dim(table[0], bank, 0, keepdims=False)
        return block.T if transpose else block

    def pack(bank, parts):
        return jnp.concatenate([chosen(table, bank, flip) for table, flip in parts], axis=1)

    def exchanged(parts):
        return by_layer(pack(own_bank, parts), swap(pack(other_bank, parts)))

    def cut_pack(parts):
        own = jnp.concatenate([pack(own_bank, parts), query_rows], axis=1)
        other = jnp.concatenate([pack(other_bank, parts), query_rows], axis=1)
        return by_layer(own, swap(other))

    query_rows = jnp.broadcast_to(query_bias, (rank, local_q))
    cut_layers = jnp.stack(cut_pack([(query_expand, False), (output_shrink, True)]))
    cut_parts = jnp.stack(
        [cut_layers] + [around(cut_layers, "tensor", j) for j in range(1, ranks)]
    )
    cut_whole = jnp.stack(
        [
            lax.dynamic_index_in_dim(cut_parts, (tensor - r) % ranks, 0, keepdims=False)
            for r in range(ranks)
        ],
        axis=2,
    ).reshape(2, rank, ranks, 3, local_q)
    eq_all, so_all, query_bias_all = [
        cut_whole[:, :, :, k].reshape(2, rank, ranks * local_q) for k in range(3)
    ]
    early_layers = exchanged([(query_shrink, True), (keyval_shrink, True), (keyval_expand, False)])
    late_layers = exchanged(
        [
            (output_expand, False),
            (upward_shrink, True),
            (upward_expand, False),
            (downward_shrink, True),
            (downward_expand, False),
        ]
    )

    up_halves = halves(upward_weight[0])
    down_halves = halves(row_major(downward_weight[0].T))
    side = [jnp.concatenate([up_halves[h], down_halves[h]], axis=1) for h in range(2)]
    keep = jnp.where(low_section, side[0], side[1])
    gained = swap(jnp.where(low_section, side[1], side[0]))
    feed_tables = [gather(table) for table in by_layer(keep, gained)]

    def split(table, sizes):
        cuts = [0]
        for size in sizes:
            cuts.append(cuts[-1] + size)
        return [table[:, a:b] for a, b in zip(cuts[:-1], cuts[1:])]

    small = [
        [part.astype(f32) for part in split(vector_layers[layer], vector_sizes)]
        for layer in range(2)
    ]
    adapters = [
        split(early_layers[layer], [width, width, 2 * head])
        + split(late_layers[layer], [width, width, local_f, local_f, width])
        for layer in range(2)
    ]

    inside = jnp.arange(rows, dtype=jnp.int32)
    query_place = data * span + tensor * rows + inside
    key_place = jnp.concatenate(
        [
            (data - back) * span + (tensor + j) % ranks * rows + inside
            for j in range(ranks)
            for back in range(reach, -1, -1)
        ]
    )
    lengths = lax.dynamic_index_in_dim(doc_lengths, section, 0, keepdims=False)
    ends = jnp.cumsum(lengths)
    query_doc = jnp.sum((query_place[:, None] >= ends[None, :]).astype(jnp.int32), axis=1)
    key_doc = jnp.sum((key_place[:, None] >= ends[None, :]).astype(jnp.int32), axis=1)
    distance = query_place[:, None] - key_place[None, :]
    allowed = (
        (key_place[None, :] >= 0)
        & (distance >= 0)
        & (distance < WINDOW)
        & (query_doc[:, None] == key_doc[None, :])
    )
    bias = jnp.where(allowed, 0.0, masked_score).astype(bf16)

    def forward_attend(layer, hidden):
        gain1, shift1, kv_bias, out_bias = small[layer][:4]
        sq, skv, ekv, eo = adapters[layer][:4]
        unit1, rsd1 = norm_parts(hidden)
        normed = (unit1 * gain1 + shift1).astype(bf16)
        low_kv = against(normed, skv).astype(bf16)
        keyval = (plain(normed, keyval_ws[layer]) + kv_bias + plain(low_kv, ekv)).astype(bf16)
        pieces = [along(keyval, "dp", back) for back in range(reach, 0, -1)] + [keyval]
        key_block = spread(jnp.concatenate(pieces, axis=0))
        queries, low_q = project_queries(
            layer, normed, early_all, query_bias_all[layer, :1].astype(f32), eq_all[layer], sq
        )
        probs, mixed, low_o, attended = attend(
            layer, queries, key_block, bias, early_all, so_all[layer], eo, head
        )
        middle = hidden + (attended + out_bias)
        return middle, (unit1, rsd1, normed, low_q, low_kv, queries, key_block, probs, mixed, low_o)

    def feed_inputs(layer, middle):
        gain2, shift2, up_bias = small[layer][4:7]
        unit2, rsd2 = norm_parts(middle)
        second = spread_parts((unit2 * gain2 + shift2).astype(bf16))
        return unit2, rsd2, second, up_bias

    def feed_result(layer, middle, partial):
        return middle + (reduce_rows(partial) + small[layer][7])

    def tiles(block):
        return block.reshape(rank, -1, 128).transpose(1, 0, 2)

    def flat(block):
        return block.transpose(1, 0, 2).reshape(rank, -1)

    turn, near = data // 4, data % 4

    def padded(pile, multiple):
        lack = -pile.shape[0] % multiple
        if not lack:
            return pile
        return jnp.concatenate([pile, jnp.zeros((lack,) + pile.shape[1:], pile.dtype)], axis=0)

    def piled(shared, quartered):
        pile = padded(jnp.concatenate([tiles(part) for part in shared], axis=0), ranks)
        return jnp.concatenate(
            [block.reshape((ranks, -1) + block.shape[1:]) for block in [pile] + [tiles(part) for part in quartered]],
            axis=1,
        ).astype(bf16)

    def owned_pile(mine, owned):
        pile = jnp.concatenate([mine] + [tiles(part) for part in owned], axis=0).astype(bf16)
        return padded(pile, lax.axis_size("dp"))

    def at(block, index, axis):
        return lax.dynamic_index_in_dim(block, index, axis, keepdims=False)

    def scattered_grads(layers):
        pile = jnp.stack([piled(shared, quartered) for shared, quartered, _ in layers], axis=1)
        mine = at(pile, tensor, 0).astype(f32)
        for j in range(1, ranks):
            mine = mine + around(at(pile, (tensor + j) % ranks, 0), "tensor", j).astype(f32)
        pile = jnp.stack([owned_pile(mine[i], layers[i][2]) for i in range(2)])
        pile = pile.reshape((2, chips, 4, -1) + pile.shape[2:])
        mine = at(pile, near, 2).astype(f32)
        for k in range(1, 4):
            mine = mine + flipped(at(pile, near ^ k, 2), "dp", k).astype(f32)
        pile = mine.astype(bf16)
        mine = at(pile, turn, 1).astype(f32)
        for k in range(1, chips):
            mine = mine + flipped(at(pile, turn ^ k, 1), "dp", 4 * k).astype(f32)
        return mine.astype(bf16)

    def crossed(block, mask):
        return lax.ppermute(block, both, [(i, i ^ mask) for i in range(8 * chips)])

    def spread_grads(zero, one, shared, quartered, owned):
        own = jnp.where(low_section, zero, one)
        away = jnp.where(low_section, one, zero)
        dp_size = 4 * chips
        home = jnp.stack([own, flipped(own, "dp", 2)])
        guest = jnp.stack([crossed(away, dp_size), crossed(away, dp_size + 2)])
        home, guest = [
            jnp.where(near // 2 == 0, block, block[::-1]) for block in (home, guest)
        ]
        pair = jnp.where(
            low_section, jnp.stack([home, guest], axis=1), jnp.stack([guest, home], axis=1)
        )
        parts = jnp.stack([pair] + [flipped(pair, "dp", 4 * k) for k in range(1, chips)])
        parts = jnp.stack([at(parts, turn ^ k, 0) for k in range(chips)])
        other = flipped(parts, "dp", 1)
        core = near % 2
        parts = jnp.stack(
            [jnp.where(core == 0, parts, other), jnp.where(core == 0, other, parts)], axis=2
        )
        pile = jnp.moveaxis(parts, 3, 0).reshape((2, -1) + parts.shape[5:])
        shared_sizes = [part.shape[1] // 128 for part in shared]
        quarter_sizes = [part.shape[1] // 128 // ranks for part in quartered]
        owned_sizes = [part.shape[1] // 128 for part in owned]
        each = -(-sum(shared_sizes) // ranks)
        own = pile[:, :each]
        parts = jnp.stack([own] + [around(own, "tensor", k) for k in range(1, ranks)])
        ordered = jnp.concatenate([at(parts, (tensor - r) % ranks, 0) for r in range(ranks)], axis=1)
        results = []
        for whole, begin, sizes in [
            (ordered, 0, shared_sizes),
            (pile, each, quarter_sizes + owned_sizes),
        ]:
            for count in sizes:
                results.append([flat(whole[m, begin : begin + count]) for m in range(2)])
                begin += count
        return results

    def feed_grads(layer, grad, unit2, rsd2, partial):
        return grad + norm_back(unit2, rsd2, reduce_rows(partial) * small[layer][4])

    def feed_adapters(after, second, branch, *others):
        parts = (after, *second, branch) if not isinstance(branch, list) else (after, *second, *branch)
        _, *parts = lax.optimization_barrier(parts + others)
        second = jnp.concatenate(parts[:ranks], axis=0)
        parts = parts[ranks:]
        count = len(parts) - len(others)
        branch = jnp.concatenate(parts[:count], axis=0)
        low_u, low_d, inner_u, inner_d, active, grad_up = parts[count:]
        shared = [across(inner_u, second), across(low_d, branch)]
        owned = [across(low_u, grad_up), across(inner_d, active)]
        return shared, owned

    def backward_attend(layer, kept, grad_middle):
        gain1 = small[layer][0]
        sq, skv, ekv, eo = adapters[layer][:4]
        unit1, rsd1, normed, low_q, low_kv, queries, key_block, probs, mixed, low_o = kept
        branch = grad_middle.astype(bf16)
        grad_q, grad_block, inner_o, inner_q, partial = attend_back(
            layer, branch, early_all, so_all[layer], eo, probs, queries, key_block,
            eq_all[layer], sq, head,
        )
        count = (reach + 1) * rows
        blocks = grad_block[:count].astype(f32)
        for j in range(1, ranks):
            part = grad_block[j * count : (j + 1) * count]
            blocks = blocks + around(part, "tensor", j).astype(f32)
        own = blocks[reach * rows :]
        for back in range(1, reach + 1):
            begin = (reach - back) * rows
            own = own + along(blocks[begin : begin + rows].astype(bf16), "dp", -back).astype(f32)
        grad_kv = own.astype(bf16)
        inner_kv = against(grad_kv, ekv).astype(bf16)
        grad_normed = partial + against(grad_kv, keyval_ws[layer]) + plain(inner_kv, skv)
        grad_hidden = grad_middle + norm_back(unit1, rsd1, grad_normed * gain1)
        shared = [
            across(low_o, branch),
            across(inner_q, normed),
            across(inner_kv, normed),
            across(low_kv, grad_kv),
        ]
        quartered = [across(low_q, grad_q), across(inner_o, mixed)]
        return grad_hidden, shared, quartered

    fresh = lax.dynamic_index_in_dim(block_input, section, 0, keepdims=False).astype(f32)
    given = lax.dynamic_index_in_dim(cotangent, section, 0, keepdims=False).astype(f32)

    middle_zero, kept_zero = forward_attend(0, fresh)
    unit_zero, rsd_zero, second_zero, up_bias = feed_inputs(0, middle_zero)
    su, eu, sd, ed = adapters[0][4:]
    active_zero, slope_zero, low_u_zero, low_d_zero, partial = feed_call(
        feed_kernel,
        "feed",
        second_zero,
        (feed_tables[0], up_bias, eu, sd, su, ed),
        (local_f, local_f, rank, rank, width),
        local_f,
        2,
    )
    passed = feed_result(0, middle_zero, partial).astype(bf16)

    middle_one, kept_one = forward_attend(1, passed.astype(f32))
    unit_one, rsd_one, second_one, up_bias = feed_inputs(1, middle_one)
    su, eu, sd, ed = adapters[1][4:]
    branch_one = spread(given.astype(bf16))
    active, low_u, low_d, partial, grad_up, inner_d, inner_u, partial_back = feed_call(
        feed_both_kernel,
        "feed_both",
        second_one,
        (branch_one, feed_tables[1], up_bias, eu, sd, su, ed),
        (local_f, rank, rank, width, local_f, rank, rank, width),
        local_f,
        4,
    )
    grad_middle = feed_grads(1, given, unit_one, rsd_one, partial_back)
    shared, owned = feed_adapters(
        grad_middle, second_one, branch_one, low_u, low_d, inner_u, inner_d, active, grad_up
    )
    grad_one, more, quartered = backward_attend(1, kept_one, grad_middle)
    layer_one = (shared + more, quartered, owned)
    partial, _ = lax.optimization_barrier((partial, grad_middle))
    final = feed_result(1, middle_one, partial).astype(bf16)

    su, eu, sd, ed = adapters[0][4:]
    branch_zero = spread_parts(grad_one.astype(bf16))
    grad_up, inner_d, inner_u, partial_back = feed_call(
        feed_back_kernel,
        "feed_back",
        branch_zero,
        (feed_tables[0], slope_zero, eu, sd, su, ed),
        (local_f, rank, rank, width),
        local_f,
        2,
    )
    grad_middle_zero = feed_grads(0, grad_one, unit_zero, rsd_zero, partial_back)
    shared, owned = feed_adapters(
        grad_middle_zero,
        second_zero,
        branch_zero,
        low_u_zero,
        low_d_zero,
        inner_u,
        inner_d,
        active_zero,
        grad_up,
    )
    grad_zero, more, quartered = backward_attend(0, kept_zero, grad_middle_zero)
    shared = shared + more
    mine = scattered_grads([(shared, quartered, owned), layer_one])
    grads = spread_grads(mine[0], mine[1], shared, quartered, owned)

    def both_micros(zero, one, kind):
        own = jnp.where(low_section, zero, one)
        received = swap(jnp.where(low_section, one, zero).astype(bf16)).astype(kind)
        return jnp.where(low_section, jnp.stack([own, received]), jnp.stack([received, own]))

    passed, final, _ = lax.optimization_barrier((passed, final, grad_middle_zero))
    section_outputs = both_micros(passed, final, bf16)
    input_grads = both_micros(grad_zero, grad_one, f32)
    onehot = (bank_choice[:, None] == jnp.arange(banks)[None, :]).astype(f32)

    def placed(pair, transpose):
        out = sum(
            onehot[m][:, None, None] * pair[m].astype(f32)[None] for m in range(2)
        )
        return (out.transpose(0, 2, 1) if transpose else out)[None]

    (
        up_shrink_grad,
        down_expand_grad,
        out_expand_grad,
        q_shrink_grad,
        kv_shrink_grad,
        kv_expand_grad,
        q_expand_grad,
        out_shrink_grad,
        up_expand_grad,
        down_shrink_grad,
    ) = grads
    return (
        section_outputs[None],
        input_grads[None],
        placed(q_shrink_grad, True),
        placed(q_expand_grad, False),
        placed(kv_shrink_grad, True),
        placed(kv_expand_grad, False),
        placed(out_shrink_grad, True),
        placed(out_expand_grad, False),
        placed(up_shrink_grad, True),
        placed(up_expand_grad, False),
        placed(down_shrink_grad, True),
        placed(down_expand_grad, False),
    )


def solution(mesh):
    return jax.shard_map(
        per_device,
        mesh=mesh,
        in_specs=(
            P(None, ("dp", "tensor"), None),
            P(None, ("dp", "tensor"), None),
            P(),
            P(),
            P("section", None),
            P("section", None),
            P("section", "dp", "tensor"),
            P("section", "tensor"),
            P("section", "dp", None),
            P("section", None),
            P("section", "tensor", "dp"),
            P("section", None),
            P("section", None),
            P("section", None),
            P("section", "dp", "tensor"),
            P("section", "tensor"),
            P("section", "tensor", "dp"),
            P("section", None),
            P("section", None, None, None),
            P("section", None, None, "tensor"),
            P("section", None, None, None),
            P("section", None, None, None),
            P("section", None, "tensor", None),
            P("section", None, None, None),
            P("section", None, None, None),
            P("section", None, None, "tensor"),
            P("section", None, "tensor", None),
            P("section", None, None, None),
        ),
        out_specs=(
            P("section", None, ("dp", "tensor"), None),
            P("section", None, ("dp", "tensor"), None),
            P("section", None, None, None),
            P("section", None, None, "tensor"),
            P("section", None, None, None),
            P("section", None, None, None),
            P("section", None, "tensor", None),
            P("section", None, None, None),
            P("section", None, None, None),
            P("section", None, None, "tensor"),
            P("section", None, "tensor", None),
            P("section", None, None, None),
        ),
        check_vma=False,
    )
```

```python
import math

import jax
import jax.numpy as jnp
from jax import lax
from jax.experimental import pallas as pl
from jax.experimental.layout import Layout, with_layout_constraint
from jax.experimental.pallas import tpu as pltpu
from jax.sharding import PartitionSpec as P

WINDOW = 1024
epsilon = 1e-05
masked_score = -1e30
bf16 = jnp.bfloat16
f32 = jnp.float32


def plain(left, right):
    return jnp.dot(left, right, preferred_element_type=f32)


def against(left, right):
    return lax.dot_general(left, right, (((1,), (1,)), ((), ())), preferred_element_type=f32)


def across(left, right):
    return lax.dot_general(left, right, (((0,), (0,)), ((), ())), preferred_element_type=f32)


def around(block, axis, distance):
    size = lax.axis_size(axis)
    return lax.ppermute(block, axis, [(i, (i + distance) % size) for i in range(size)])


def along(block, axis, distance):
    size = lax.axis_size(axis)
    route = [(i, i + distance) for i in range(size) if 0 <= i + distance < size]
    return lax.ppermute(block, axis, route)


def flipped(block, axis, bit):
    size = lax.axis_size(axis)
    return lax.ppermute(block, axis, [(i, i ^ bit) for i in range(size)])


def pick(table, index, size=1):
    return lax.dynamic_slice_in_dim(table, index, size, 0)


def norm_parts(value):
    centred = value - jnp.mean(value, axis=-1, keepdims=True)
    spread = lax.rsqrt(jnp.mean(centred * centred, axis=-1, keepdims=True) + epsilon)
    return centred * spread, spread


def norm_back(unit, spread, scaled):
    inner = jnp.mean(scaled * unit, axis=-1, keepdims=True)
    return spread * (scaled - jnp.mean(scaled, axis=-1, keepdims=True) - unit * inner)


def gelu_parts(value):
    rate = math.sqrt(2.0 / math.pi)
    square = value * value
    bend = jnp.tanh(rate * (value + 0.044715 * value * square))
    rising = 0.5 * (1.0 + bend)
    slope = rising + 0.5 * value * (1.0 - bend * bend) * (rate * (1.0 + 3 * 0.044715 * square))
    return value * rising, slope


def side_blocks(query_ref, group, head):
    begin = group * 4 * head
    return jnp.concatenate(
        [query_ref[:, begin + h * head : begin + (h + 1) * head] for h in range(4)], axis=0
    )


def put_blocks(out_ref, value, group, head):
    rows = value.shape[0] // 4
    for h in range(4):
        begin = (group * 4 + h) * head
        out_ref[:, begin : begin + head] = value[h * rows : (h + 1) * rows]


def table_copies(table_ref, buf, sem, layer, begin):
    ranks, chunks, _, width = buf.shape
    return [
        pltpu.make_async_copy(
            table_ref.at[x, y, layer, :, pl.ds(begin, width)], buf.at[x, y], sem.at[x, y]
        )
        for x in range(ranks)
        for y in range(chunks)
    ]


def query_kernel(layer, normed_ref, table_ref, bias_ref, eq_ref, sq_ref, out_ref, low_ref, buf, sem):
    ranks, chunks, rows, width = buf.shape
    copies = table_copies(table_ref, buf, sem, layer, 0)
    for copy in copies:
        copy.start()
    normed = normed_ref[...]
    low = against(normed, sq_ref[...]).astype(bf16)
    low_ref[...] = low
    for x in range(ranks):
        columns = pl.ds(x * width, width)
        total = bias_ref[:, columns] + plain(low, eq_ref[:, columns])
        for y in range(chunks):
            copies[x * chunks + y].wait()
            total = total + plain(normed[:, y * rows : (y + 1) * rows], buf[x, y])
        out_ref[:, columns] = total.astype(bf16)


def table_scratch(table, width):
    ranks, chunks, _, rows, _ = table.shape
    return [
        pltpu.VMEM((ranks, chunks, rows, width), bf16),
        pltpu.SemaphoreType.DMA((ranks, chunks)),
    ]


held = pl.BlockSpec(memory_space=pltpu.VMEM)
remote = pl.BlockSpec(memory_space=pltpu.HBM)


def project_queries(layer, normed, table, bias, eq, sq):
    rows, model = normed.shape
    rank = sq.shape[0]
    width = model // table.shape[0]
    return pl.pallas_call(
        lambda *refs: query_kernel(layer, *refs),
        in_specs=[held, remote, held, held, held],
        out_specs=[held] * 2,
        out_shape=[
            jax.ShapeDtypeStruct((rows, model), bf16),
            jax.ShapeDtypeStruct((rows, rank), bf16),
        ],
        scratch_shapes=table_scratch(table, width),
        compiler_params=pltpu.CompilerParams(vmem_limit_bytes=12 * 2**20),
        cost_estimate=pl.CostEstimate(
            flops=8 * rows * model * model, bytes_accessed=2 * model * model, transcendentals=0
        ),
        name="project_queries",
    )(normed, table, bias, eq, sq)


def attend_kernel(
    layer, head, query_ref, keyval_ref, bias_ref, table_ref, so_ref, eo_ref,
    prob_ref, mixed_ref, low_ref, out_ref, buf, sem,
):
    ranks, chunks, rows, width = buf.shape
    copies = table_copies(table_ref, buf, sem, layer, width)
    for copy in copies:
        copy.start()
    scale = 1.0 / math.sqrt(head)
    bias = jnp.concatenate([bias_ref[...].astype(f32)] * 4, axis=0)
    for g in range(prob_ref.shape[0]):
        queries = side_blocks(query_ref, g, head)
        scores = against(queries, keyval_ref[:, :head]) * scale + bias
        lifted = jnp.exp(scores - jnp.max(scores, axis=-1, keepdims=True))
        probs = (lifted * (1.0 / jnp.sum(lifted, axis=-1, keepdims=True))).astype(bf16)
        prob_ref[g] = probs
        put_blocks(mixed_ref, plain(probs, keyval_ref[:, head:]).astype(bf16), g, head)
    mixed = mixed_ref[...]
    low = against(mixed, so_ref[...]).astype(bf16)
    low_ref[...] = low
    for copy in copies:
        copy.wait()
    for y in range(chunks):
        columns = pl.ds(y * rows, rows)
        total = plain(low, eo_ref[:, columns])
        for x in range(ranks):
            total = total + against(mixed[:, x * width : (x + 1) * width], buf[x, y])
        out_ref[:, columns] = total


def attend(layer, queries, key_block, bias, table, so, eo, head):
    rows, model = queries.shape
    keys = key_block.shape[0]
    groups = model // head // 4
    rank = so.shape[0]
    return pl.pallas_call(
        lambda *refs: attend_kernel(layer, head, *refs),
        in_specs=[held, held, held, remote, held, held],
        out_specs=[held] * 4,
        out_shape=[
            jax.ShapeDtypeStruct((groups, 4 * rows, keys), bf16),
            jax.ShapeDtypeStruct((rows, model), bf16),
            jax.ShapeDtypeStruct((rows, rank), bf16),
            jax.ShapeDtypeStruct((rows, model), f32),
        ],
        scratch_shapes=table_scratch(table, model // table.shape[0]),
        compiler_params=pltpu.CompilerParams(vmem_limit_bytes=20 * 2**20),
        cost_estimate=pl.CostEstimate(
            flops=4 * rows * model * (keys + 2 * model),
            bytes_accessed=2 * model * model,
            transcendentals=groups * 4 * rows * keys,
        ),
        name="attend",
    )(queries, key_block, bias, table, so, eo)


def attend_back_kernel(
    layer, head, branch_ref, table_ref, so_ref, eo_ref, prob_ref, query_ref, keyval_ref, eq_ref, sq_ref,
    dq_ref, dkv_ref, inner_o_ref, inner_q_ref, part_ref,
    out_buf, out_sem, query_buf, query_sem, mixed_buf, key_sum, value_sum,
):
    ranks, chunks, rows, width = out_buf.shape
    out_copies = table_copies(table_ref, out_buf, out_sem, layer, width)
    query_copies = table_copies(table_ref, query_buf, query_sem, layer, 0)
    for copy in out_copies + query_copies:
        copy.start()
    scale = 1.0 / math.sqrt(head)
    branch = branch_ref[...]
    inner_o = against(branch, eo_ref[...]).astype(bf16)
    inner_o_ref[...] = inner_o
    for g in range(prob_ref.shape[0]):
        columns = pl.ds(g * width, width)
        total = plain(inner_o, so_ref[:, columns])
        for y in range(chunks):
            out_copies[g * chunks + y].wait()
            total = total + plain(branch[:, y * rows : (y + 1) * rows], out_buf[g, y])
        mixed_buf[:, columns] = total.astype(bf16)
        grad = side_blocks(mixed_buf, g, head)
        low_probs = prob_ref[g]
        probs = low_probs.astype(f32)
        grad_probs = against(grad, keyval_ref[:, head:])
        delta = jnp.sum(grad_probs * probs, axis=-1, keepdims=True)
        delta = delta / jnp.sum(probs, axis=-1, keepdims=True)
        grad_scores = (probs * (grad_probs - delta)).astype(bf16)
        put_blocks(dq_ref, (plain(grad_scores, keyval_ref[:, :head]) * scale).astype(bf16), g, head)
        keys = across(grad_scores, side_blocks(query_ref, g, head))
        values = across(low_probs, grad)
        if g == 0:
            key_sum[...] = keys
            value_sum[...] = values
        else:
            key_sum[...] += keys
            value_sum[...] += values
    dkv_ref[:, :head] = (key_sum[...] * scale).astype(bf16)
    dkv_ref[:, head:] = value_sum[...].astype(bf16)
    grad_q = dq_ref[...]
    inner_q = against(grad_q, eq_ref[...]).astype(bf16)
    inner_q_ref[...] = inner_q
    for copy in query_copies:
        copy.wait()
    for y in range(chunks):
        columns = pl.ds(y * rows, rows)
        total = plain(inner_q, sq_ref[:, columns])
        for x in range(ranks):
            total = total + against(grad_q[:, x * width : (x + 1) * width], query_buf[x, y])
        part_ref[:, columns] = total


def attend_back(layer, branch, table, so, eo, probs, queries, key_block, eq, sq, head):
    rows, model = queries.shape
    keys = key_block.shape[0]
    groups = probs.shape[0]
    rank = so.shape[0]
    width = model // table.shape[0]
    return pl.pallas_call(
        lambda *refs: attend_back_kernel(layer, head, *refs),
        in_specs=[held, remote] + [held] * 7,
        out_specs=[held] * 5,
        out_shape=[
            jax.ShapeDtypeStruct((rows, model), bf16),
            jax.ShapeDtypeStruct((keys, 2 * head), bf16),
            jax.ShapeDtypeStruct((rows, rank), bf16),
            jax.ShapeDtypeStruct((rows, rank), bf16),
            jax.ShapeDtypeStruct((rows, model), f32),
        ],
        scratch_shapes=table_scratch(table, width)
        + table_scratch(table, width)
        + [
            pltpu.VMEM((rows, model), bf16),
            pltpu.VMEM((keys, head), f32),
            pltpu.VMEM((keys, head), f32),
        ],
        compiler_params=pltpu.CompilerParams(vmem_limit_bytes=30 * 2**20),
        cost_estimate=pl.CostEstimate(
            flops=8 * rows * model * (keys + 2 * model),
            bytes_accessed=4 * model * model + 4 * groups * 4 * rows * keys,
            transcendentals=0,
        ),
        name="attend_back",
    )(branch, table, so, eo, probs, queries, key_block, eq, sq)


def feed_copies(table_ref, buf, sems):
    _, count, chunks, rows, tile = buf.shape
    half = count // 2 * tile
    copies = []
    for j in range(count):
        pair = []
        for k in range(2):
            columns = pl.ds(j * tile % half + k * half, tile)
            pair.append(
                pltpu.make_async_copy(
                    table_ref.at[:, j * tile // half, :, columns], buf.at[k, j], sems.at[k, j]
                )
            )
        copies.append(pair)
    return copies


def plain_chunks(left, buf, k, j):
    rows = buf.shape[3]
    return sum(plain(left[:, i * rows : (i + 1) * rows], buf[k, j, i]) for i in range(buf.shape[2]))


def against_chunk(left_ref, buf, k, i):
    tile = buf.shape[4]
    return sum(
        against(left_ref[:, j * tile : (j + 1) * tile], buf[k, j, i]) for j in range(buf.shape[1])
    )


def gathered(part_refs, whole):
    rows = part_refs[0].shape[0]
    for j, part_ref in enumerate(part_refs):
        whole[j * rows : (j + 1) * rows] = part_ref[...]
    return whole[...]


def feed_pack(pack_ref, model, hidden):
    cuts = [model, 2 * model, 2 * model + hidden, 2 * model + 2 * hidden, 3 * model + 2 * hidden]
    return [pack_ref.at[:, a:b] for a, b in zip(cuts[:-1], cuts[1:])]


def feed_kernel(
    part0, part1, part2, part3, table_ref, bias_ref, pack_ref,
    active_ref, slope_ref, low_u_ref, low_d_ref, out_ref, buf, sems, whole,
):
    _, count, chunks, rows, tile = buf.shape
    su_ref, eu_ref, sd_ref, ed_ref = feed_pack(pack_ref, chunks * rows, count * tile)
    copies = feed_copies(table_ref, buf, sems)
    for up, _ in copies:
        up.start()
    for _, down in copies:
        down.start()
    second = gathered((part0, part1, part2, part3), whole)
    low_u = against(second, su_ref[...]).astype(bf16)
    low_u_ref[...] = low_u
    for j in range(count):
        columns = pl.ds(j * tile, tile)
        copies[j][0].wait()
        upward = plain_chunks(second, buf, 0, j)
        upward = upward + plain(low_u, eu_ref[:, columns]) + bias_ref[:, columns]
        active, slope = gelu_parts(upward)
        active_ref[:, columns] = active.astype(bf16)
        slope_ref[:, columns] = slope.astype(bf16)
    low_d = against(active_ref[...], sd_ref[...]).astype(bf16)
    low_d_ref[...] = low_d
    for _, down in copies:
        down.wait()
    for i in range(chunks):
        columns = pl.ds(i * rows, rows)
        out_ref[:, columns] = (
            against_chunk(active_ref, buf, 1, i) + plain(low_d, ed_ref[:, columns])
        ).astype(bf16)


def feed_back_kernel(
    part0, part1, part2, part3, table_ref, slope_ref, pack_ref,
    grad_up_ref, inner_d_ref, inner_u_ref, out_ref, buf, sems, whole,
):
    _, count, chunks, rows, tile = buf.shape
    su_ref, eu_ref, sd_ref, ed_ref = feed_pack(pack_ref, chunks * rows, count * tile)
    copies = feed_copies(table_ref, buf, sems)
    for _, down in copies:
        down.start()
    for up, _ in copies:
        up.start()
    branch = gathered((part0, part1, part2, part3), whole)
    inner_d = against(branch, ed_ref[...]).astype(bf16)
    inner_d_ref[...] = inner_d
    for j in range(count):
        columns = pl.ds(j * tile, tile)
        copies[j][1].wait()
        grad = plain_chunks(branch, buf, 1, j) + plain(inner_d, sd_ref[:, columns])
        grad_up_ref[:, columns] = (grad * slope_ref[:, columns].astype(f32)).astype(bf16)
    inner_u = against(grad_up_ref[...], eu_ref[...]).astype(bf16)
    inner_u_ref[...] = inner_u
    for up, _ in copies:
        up.wait()
    for i in range(chunks):
        columns = pl.ds(i * rows, rows)
        out_ref[:, columns] = (
            against_chunk(grad_up_ref, buf, 0, i) + plain(inner_u, su_ref[:, columns])
        ).astype(bf16)


def feed_both_kernel(
    part0, part1, part2, part3, branch_ref, table_ref, bias_ref, pack_ref,
    active_ref, low_u_ref, low_d_ref, out_ref, grad_up_ref, inner_d_ref, inner_u_ref, back_ref,
    buf, sems, whole,
):
    _, count, chunks, rows, tile = buf.shape
    su_ref, eu_ref, sd_ref, ed_ref = feed_pack(pack_ref, chunks * rows, count * tile)
    copies = feed_copies(table_ref, buf, sems)
    for up, down in copies:
        up.start()
        down.start()
    second = gathered((part0, part1, part2, part3), whole)
    branch = branch_ref[...]
    low_u = against(second, su_ref[...]).astype(bf16)
    low_u_ref[...] = low_u
    inner_d = against(branch, ed_ref[...]).astype(bf16)
    inner_d_ref[...] = inner_d
    for j in range(count):
        columns = pl.ds(j * tile, tile)
        copies[j][0].wait()
        upward = plain_chunks(second, buf, 0, j)
        upward = upward + plain(low_u, eu_ref[:, columns]) + bias_ref[:, columns]
        active, slope = gelu_parts(upward)
        active_ref[:, columns] = active.astype(bf16)
        copies[j][1].wait()
        grad = plain_chunks(branch, buf, 1, j) + plain(inner_d, sd_ref[:, columns])
        grad_up_ref[:, columns] = (grad * slope).astype(bf16)
    inner_u = against(grad_up_ref[...], eu_ref[...]).astype(bf16)
    inner_u_ref[...] = inner_u
    low_d = against(active_ref[...], sd_ref[...]).astype(bf16)
    low_d_ref[...] = low_d
    for i in range(chunks):
        columns = pl.ds(i * rows, rows)
        back_ref[:, columns] = (
            against_chunk(grad_up_ref, buf, 0, i) + plain(inner_u, su_ref[:, columns])
        ).astype(bf16)
        out_ref[:, columns] = (
            against_chunk(active_ref, buf, 1, i) + plain(low_d, ed_ref[:, columns])
        ).astype(bf16)


def feed_call(kernel, name, parts, inputs, outputs, hidden, matmuls):
    inputs = tuple(parts) + inputs
    table = [value for value in inputs if value.ndim == 4][0]
    model = parts[0].shape[1]
    rows = sum(part.shape[0] for part in parts)
    tile = 512
    chunks = table.shape[0]
    return pl.pallas_call(
        kernel,
        in_specs=[remote if value.ndim == 4 else held for value in inputs],
        out_specs=[held] * len(outputs),
        out_shape=[jax.ShapeDtypeStruct((rows, width), bf16) for width in outputs],
        scratch_shapes=[
            pltpu.VMEM((2, hidden // tile, chunks, model // chunks, tile), bf16),
            pltpu.SemaphoreType.DMA((2, hidden // tile)),
            pltpu.VMEM((rows, model), bf16),
        ],
        compiler_params=pltpu.CompilerParams(vmem_limit_bytes=26 * 2**20),
        cost_estimate=pl.CostEstimate(
            flops=2 * matmuls * rows * model * hidden,
            bytes_accessed=4 * model * hidden,
            transcendentals=rows * hidden,
        ),
        name=name,
    )(*inputs)


def per_device(
    block_input,
    cotangent,
    doc_lengths,
    bank_choice,
    first_gain,
    first_shift,
    query_weight,
    query_bias,
    keyval_weight,
    value_bias,
    output_weight,
    output_bias,
    second_gain,
    second_shift,
    upward_weight,
    upward_bias,
    downward_weight,
    downward_bias,
    query_shrink,
    query_expand,
    keyval_shrink,
    keyval_expand,
    output_shrink,
    output_expand,
    upward_shrink,
    upward_expand,
    downward_shrink,
    downward_expand,
):
    section = lax.axis_index("section")
    data = lax.axis_index("dp")
    tensor = lax.axis_index("tensor")
    low_section = section == 0
    width = block_input.shape[2]
    rows = block_input.shape[1]
    ranks = lax.axis_size("tensor")
    span = rows * ranks
    head = value_bias.shape[1]
    local_q = query_bias.shape[1]
    local_f = upward_bias.shape[1]
    rank = query_expand.shape[2]
    banks = query_expand.shape[1]
    reach = WINDOW // span
    sides = [(0, 1), (1, 0)]

    def swap(value):
        return lax.ppermute(value, "section", sides)

    def by_layer(own, other):
        return jnp.where(low_section, own, other), jnp.where(low_section, other, own)

    def spread_parts(block):
        return [block] + [around(block, "tensor", -j) for j in range(1, ranks)]

    def spread(block):
        return jnp.concatenate(spread_parts(block), axis=0)

    def reduce_rows(partial):
        low = partial.astype(bf16)
        total = partial[:rows].astype(f32)
        for j in range(1, ranks):
            total = total + around(low[j * rows : (j + 1) * rows], "tensor", j).astype(f32)
        return total

    own_bank = lax.dynamic_index_in_dim(bank_choice, section, 0, keepdims=False)
    other_bank = lax.dynamic_index_in_dim(bank_choice, 1 - section, 0, keepdims=False)

    chips = lax.axis_size("dp") // 4
    both = ("section", "dp")
    every = ("section", "dp", "tensor")
    order = [
        side * 4 * chips + chip * 4 + near
        for chip in range(chips)
        for side in range(2)
        for near in range(4)
    ]
    order_all = [place * ranks + x for x in range(ranks) for place in order]

    def row_major(block):
        return with_layout_constraint(block, Layout(major_to_minor=(0, 1)))

    def gather(shard):
        table = lax.all_gather(row_major(shard), both, axis=0, tiled=True, axis_index_groups=[order])
        return row_major(table).reshape(chips, 2, -1, shard.shape[1])

    def gather_all(shard):
        table = lax.all_gather(
            row_major(shard), every, axis=0, tiled=True, axis_index_groups=[order_all]
        )
        return row_major(table).reshape(ranks, chips, 2, -1, shard.shape[1])

    def halves(shard):
        cut = shard.shape[1] // 2
        return shard[:, :cut], shard[:, cut:]

    keyval_half = jnp.where(tensor % 2 == 0, keyval_weight[0][:, :head], keyval_weight[0][:, head:])
    early_all = gather_all(
        jnp.concatenate([query_weight[0], row_major(output_weight[0].T), keyval_half], axis=1)
    )
    keyval_ws = [
        jnp.concatenate(
            [early_all[x, :, layer, :, 2 * local_q :].reshape(width, head) for x in range(2)], axis=1
        )
        for layer in range(2)
    ]

    vectors = jnp.concatenate(
        [
            first_gain,
            first_shift,
            jnp.zeros_like(value_bias),
            value_bias,
            output_bias,
            second_gain,
            second_shift,
            upward_bias,
            downward_bias,
        ],
        axis=1,
    )
    vector_sizes = [width, width, 2 * head, width, width, width, local_f, width]
    vector_layers = by_layer(vectors, swap(vectors))

    def chosen(table, bank, transpose):
        block = lax.dynamic_index_in_dim(table[0], bank, 0, keepdims=False)
        return block.T if transpose else block

    def pack(bank, parts):
        return jnp.concatenate([chosen(table, bank, flip) for table, flip in parts], axis=1)

    def exchanged(parts):
        return by_layer(pack(own_bank, parts), swap(pack(other_bank, parts)))

    def cut_pack(parts):
        own = jnp.concatenate([pack(own_bank, parts), query_rows], axis=1)
        other = jnp.concatenate([pack(other_bank, parts), query_rows], axis=1)
        return by_layer(own, swap(other))

    query_rows = jnp.broadcast_to(query_bias, (rank, local_q))
    cut_layers = jnp.stack(cut_pack([(query_expand, False), (output_shrink, True)]))
    cut_parts = jnp.stack(
        [cut_layers] + [around(cut_layers, "tensor", j) for j in range(1, ranks)]
    )
    cut_whole = jnp.stack(
        [
            lax.dynamic_index_in_dim(cut_parts, (tensor - r) % ranks, 0, keepdims=False)
            for r in range(ranks)
        ],
        axis=2,
    ).reshape(2, rank, ranks, 3, local_q)
    eq_all, so_all, query_bias_all = [
        cut_whole[:, :, :, k].reshape(2, rank, ranks * local_q) for k in range(3)
    ]
    early_layers = exchanged([(query_shrink, True), (keyval_shrink, True), (keyval_expand, False)])
    late_layers = exchanged(
        [
            (output_expand, False),
            (upward_shrink, True),
            (upward_expand, False),
            (downward_shrink, True),
            (downward_expand, False),
        ]
    )

    up_halves = halves(upward_weight[0])
    down_halves = halves(row_major(downward_weight[0].T))
    side = [jnp.concatenate([up_halves[h], down_halves[h]], axis=1) for h in range(2)]
    keep = jnp.where(low_section, side[0], side[1])
    gained = swap(jnp.where(low_section, side[1], side[0]))
    feed_tables = [gather(table) for table in by_layer(keep, gained)]

    def split(table, sizes):
        cuts = [0]
        for size in sizes:
            cuts.append(cuts[-1] + size)
        return [table[:, a:b] for a, b in zip(cuts[:-1], cuts[1:])]

    small = [
        [part.astype(f32) for part in split(vector_layers[layer], vector_sizes)]
        for layer in range(2)
    ]
    adapters = [
        split(early_layers[layer], [width, width, 2 * head]) + [late_layers[layer][:, :width]]
        for layer in range(2)
    ]

    inside = jnp.arange(rows, dtype=jnp.int32)
    query_place = data * span + tensor * rows + inside
    key_place = jnp.concatenate(
        [
            (data - back) * span + (tensor + j) % ranks * rows + inside
            for j in range(ranks)
            for back in range(reach, -1, -1)
        ]
    )
    lengths = lax.dynamic_index_in_dim(doc_lengths, section, 0, keepdims=False)
    ends = jnp.cumsum(lengths)
    query_doc = jnp.sum((query_place[:, None] >= ends[None, :]).astype(jnp.int32), axis=1)
    key_doc = jnp.sum((key_place[:, None] >= ends[None, :]).astype(jnp.int32), axis=1)
    distance = query_place[:, None] - key_place[None, :]
    allowed = (
        (key_place[None, :] >= 0)
        & (distance >= 0)
        & (distance < WINDOW)
        & (query_doc[:, None] == key_doc[None, :])
    )
    bias = jnp.where(allowed, 0.0, masked_score).astype(bf16)

    def forward_attend(layer, hidden):
        gain1, shift1, kv_bias, out_bias = small[layer][:4]
        sq, skv, ekv, eo = adapters[layer]
        unit1, rsd1 = norm_parts(hidden)
        normed = (unit1 * gain1 + shift1).astype(bf16)
        low_kv = against(normed, skv).astype(bf16)
        keyval = (plain(normed, keyval_ws[layer]) + kv_bias + plain(low_kv, ekv)).astype(bf16)
        pieces = [along(keyval, "dp", back) for back in range(reach, 0, -1)] + [keyval]
        key_block = spread(jnp.concatenate(pieces, axis=0))
        queries, low_q = project_queries(
            layer, normed, early_all, query_bias_all[layer, :1].astype(f32), eq_all[layer], sq
        )
        probs, mixed, low_o, attended = attend(
            layer, queries, key_block, bias, early_all, so_all[layer], eo, head
        )
        middle = hidden + (attended + out_bias)
        return middle, (unit1, rsd1, normed, low_q, low_kv, queries, key_block, probs, mixed, low_o)

    def feed_inputs(layer, middle):
        gain2, shift2, up_bias = small[layer][4:7]
        unit2, rsd2 = norm_parts(middle)
        second = spread_parts((unit2 * gain2 + shift2).astype(bf16))
        return unit2, rsd2, second, up_bias

    def feed_result(layer, middle, partial):
        return middle + (reduce_rows(partial) + small[layer][7])

    def tiles(block):
        return block.reshape(rank, -1, 128).transpose(1, 0, 2)

    def flat(block):
        return block.transpose(1, 0, 2).reshape(rank, -1)

    turn, near = data // 4, data % 4

    def padded(pile, multiple):
        lack = -pile.shape[0] % multiple
        if not lack:
            return pile
        return jnp.concatenate([pile, jnp.zeros((lack,) + pile.shape[1:], pile.dtype)], axis=0)

    def piled(shared, quartered):
        pile = padded(jnp.concatenate([tiles(part) for part in shared], axis=0), ranks)
        return jnp.concatenate(
            [block.reshape((ranks, -1) + block.shape[1:]) for block in [pile] + [tiles(part) for part in quartered]],
            axis=1,
        ).astype(bf16)

    def owned_pile(mine, owned):
        pile = jnp.concatenate([mine] + [tiles(part) for part in owned], axis=0).astype(bf16)
        return padded(pile, lax.axis_size("dp"))

    def at(block, index, axis):
        return lax.dynamic_index_in_dim(block, index, axis, keepdims=False)

    def scattered_grads(layers):
        pile = jnp.stack([piled(shared, quartered) for shared, quartered, _ in layers], axis=1)
        mine = at(pile, tensor, 0).astype(f32)
        for j in range(1, ranks):
            mine = mine + around(at(pile, (tensor + j) % ranks, 0), "tensor", j).astype(f32)
        pile = jnp.stack([owned_pile(mine[i], layers[i][2]) for i in range(2)])
        pile = pile.reshape((2, chips, 4, -1) + pile.shape[2:])
        mine = at(pile, near, 2).astype(f32)
        for k in range(1, 4):
            mine = mine + flipped(at(pile, near ^ k, 2), "dp", k).astype(f32)
        pile = mine.astype(bf16)
        mine = at(pile, turn, 1).astype(f32)
        for k in range(1, chips):
            mine = mine + flipped(at(pile, turn ^ k, 1), "dp", 4 * k).astype(f32)
        return mine.astype(bf16)

    def crossed(block, mask):
        return lax.ppermute(block, both, [(i, i ^ mask) for i in range(8 * chips)])

    def spread_grads(zero, one, shared, quartered, owned):
        own = jnp.where(low_section, zero, one)
        away = jnp.where(low_section, one, zero)
        dp_size = 4 * chips
        home = jnp.stack([own, flipped(own, "dp", 2)])
        guest = jnp.stack([crossed(away, dp_size), crossed(away, dp_size + 2)])
        home, guest = [
            jnp.where(near // 2 == 0, block, block[::-1]) for block in (home, guest)
        ]
        pair = jnp.where(
            low_section, jnp.stack([home, guest], axis=1), jnp.stack([guest, home], axis=1)
        )
        parts = jnp.stack([pair] + [flipped(pair, "dp", 4 * k) for k in range(1, chips)])
        parts = jnp.stack([at(parts, turn ^ k, 0) for k in range(chips)])
        other = flipped(parts, "dp", 1)
        core = near % 2
        parts = jnp.stack(
            [jnp.where(core == 0, parts, other), jnp.where(core == 0, other, parts)], axis=2
        )
        pile = jnp.moveaxis(parts, 3, 0).reshape((2, -1) + parts.shape[5:])
        shared_sizes = [part.shape[1] // 128 for part in shared]
        quarter_sizes = [part.shape[1] // 128 // ranks for part in quartered]
        owned_sizes = [part.shape[1] // 128 for part in owned]
        each = -(-sum(shared_sizes) // ranks)
        own = pile[:, :each]
        parts = jnp.stack([own] + [around(own, "tensor", k) for k in range(1, ranks)])
        ordered = jnp.concatenate([at(parts, (tensor - r) % ranks, 0) for r in range(ranks)], axis=1)
        results = []
        for whole, begin, sizes in [
            (ordered, 0, shared_sizes),
            (pile, each, quarter_sizes + owned_sizes),
        ]:
            for count in sizes:
                results.append([flat(whole[m, begin : begin + count]) for m in range(2)])
                begin += count
        return results

    def feed_grads(layer, grad, unit2, rsd2, partial):
        return grad + norm_back(unit2, rsd2, reduce_rows(partial) * small[layer][4])

    def feed_adapters(after, second, branch, *others):
        parts = (after, *second, branch) if not isinstance(branch, list) else (after, *second, *branch)
        _, *parts = lax.optimization_barrier(parts + others)
        second = jnp.concatenate(parts[:ranks], axis=0)
        parts = parts[ranks:]
        count = len(parts) - len(others)
        branch = jnp.concatenate(parts[:count], axis=0)
        low_u, low_d, inner_u, inner_d, active, grad_up = parts[count:]
        shared = [across(inner_u, second), across(low_d, branch)]
        owned = [across(low_u, grad_up), across(inner_d, active)]
        return shared, owned

    def backward_attend(layer, kept, grad_middle):
        gain1 = small[layer][0]
        sq, skv, ekv, eo = adapters[layer]
        unit1, rsd1, normed, low_q, low_kv, queries, key_block, probs, mixed, low_o = kept
        branch = grad_middle.astype(bf16)
        grad_q, grad_block, inner_o, inner_q, partial = attend_back(
            layer, branch, early_all, so_all[layer], eo, probs, queries, key_block,
            eq_all[layer], sq, head,
        )
        count = (reach + 1) * rows
        blocks = grad_block[:count].astype(f32)
        for j in range(1, ranks):
            part = grad_block[j * count : (j + 1) * count]
            blocks = blocks + around(part, "tensor", j).astype(f32)
        own = blocks[reach * rows :]
        for back in range(1, reach + 1):
            begin = (reach - back) * rows
            own = own + along(blocks[begin : begin + rows].astype(bf16), "dp", -back).astype(f32)
        grad_kv = own.astype(bf16)
        inner_kv = against(grad_kv, ekv).astype(bf16)
        grad_normed = partial + against(grad_kv, keyval_ws[layer]) + plain(inner_kv, skv)
        grad_hidden = grad_middle + norm_back(unit1, rsd1, grad_normed * gain1)
        shared = [
            across(low_o, branch),
            across(inner_q, normed),
            across(inner_kv, normed),
            across(low_kv, grad_kv),
        ]
        quartered = [across(low_q, grad_q), across(inner_o, mixed)]
        return grad_hidden, shared, quartered

    fresh = lax.dynamic_index_in_dim(block_input, section, 0, keepdims=False).astype(f32)
    given = lax.dynamic_index_in_dim(cotangent, section, 0, keepdims=False).astype(f32)

    middle_zero, kept_zero = forward_attend(0, fresh)
    unit_zero, rsd_zero, second_zero, up_bias = feed_inputs(0, middle_zero)
    active_zero, slope_zero, low_u_zero, low_d_zero, partial = feed_call(
        feed_kernel,
        "feed",
        second_zero,
        (feed_tables[0], up_bias, late_layers[0]),
        (local_f, local_f, rank, rank, width),
        local_f,
        2,
    )
    passed = feed_result(0, middle_zero, partial).astype(bf16)

    middle_one, kept_one = forward_attend(1, passed.astype(f32))
    unit_one, rsd_one, second_one, up_bias = feed_inputs(1, middle_one)
    branch_one = spread(given.astype(bf16))
    active, low_u, low_d, partial, grad_up, inner_d, inner_u, partial_back = feed_call(
        feed_both_kernel,
        "feed_both",
        second_one,
        (branch_one, feed_tables[1], up_bias, late_layers[1]),
        (local_f, rank, rank, width, local_f, rank, rank, width),
        local_f,
        4,
    )
    grad_middle = feed_grads(1, given, unit_one, rsd_one, partial_back)
    shared, owned = feed_adapters(
        grad_middle, second_one, branch_one, low_u, low_d, inner_u, inner_d, active, grad_up
    )
    grad_one, more, quartered = backward_attend(1, kept_one, grad_middle)
    layer_one = (shared + more, quartered, owned)
    partial, _ = lax.optimization_barrier((partial, grad_middle))
    final = feed_result(1, middle_one, partial).astype(bf16)

    branch_zero = spread_parts(grad_one.astype(bf16))
    grad_up, inner_d, inner_u, partial_back = feed_call(
        feed_back_kernel,
        "feed_back",
        branch_zero,
        (feed_tables[0], slope_zero, late_layers[0]),
        (local_f, rank, rank, width),
        local_f,
        2,
    )
    grad_middle_zero = feed_grads(0, grad_one, unit_zero, rsd_zero, partial_back)
    shared, owned = feed_adapters(
        grad_middle_zero,
        second_zero,
        branch_zero,
        low_u_zero,
        low_d_zero,
        inner_u,
        inner_d,
        active_zero,
        grad_up,
    )
    grad_zero, more, quartered = backward_attend(0, kept_zero, grad_middle_zero)
    shared = shared + more
    mine = scattered_grads([(shared, quartered, owned), layer_one])
    grads = spread_grads(mine[0], mine[1], shared, quartered, owned)

    def both_micros(zero, one, kind):
        own = jnp.where(low_section, zero, one)
        received = swap(jnp.where(low_section, one, zero).astype(bf16)).astype(kind)
        return jnp.where(low_section, jnp.stack([own, received]), jnp.stack([received, own]))

    passed, final, _ = lax.optimization_barrier((passed, final, grad_middle_zero))
    section_outputs = both_micros(passed, final, bf16)
    input_grads = both_micros(grad_zero, grad_one, f32)
    onehot = (bank_choice[:, None] == jnp.arange(banks)[None, :]).astype(f32)

    def placed(pair, transpose):
        out = sum(
            onehot[m][:, None, None] * pair[m].astype(f32)[None] for m in range(2)
        )
        return (out.transpose(0, 2, 1) if transpose else out)[None]

    (
        up_shrink_grad,
        down_expand_grad,
        out_expand_grad,
        q_shrink_grad,
        kv_shrink_grad,
        kv_expand_grad,
        q_expand_grad,
        out_shrink_grad,
        up_expand_grad,
        down_shrink_grad,
    ) = grads
    return (
        section_outputs[None],
        input_grads[None],
        placed(q_shrink_grad, True),
        placed(q_expand_grad, False),
        placed(kv_shrink_grad, True),
        placed(kv_expand_grad, False),
        placed(out_shrink_grad, True),
        placed(out_expand_grad, False),
        placed(up_shrink_grad, True),
        placed(up_expand_grad, False),
        placed(down_shrink_grad, True),
        placed(down_expand_grad, False),
    )


def solution(mesh):
    return jax.shard_map(
        per_device,
        mesh=mesh,
        in_specs=(
            P(None, ("dp", "tensor"), None),
            P(None, ("dp", "tensor"), None),
            P(),
            P(),
            P("section", None),
            P("section", None),
            P("section", "dp", "tensor"),
            P("section", "tensor"),
            P("section", "dp", None),
            P("section", None),
            P("section", "tensor", "dp"),
            P("section", None),
            P("section", None),
            P("section", None),
            P("section", "dp", "tensor"),
            P("section", "tensor"),
            P("section", "tensor", "dp"),
            P("section", None),
            P("section", None, None, None),
            P("section", None, None, "tensor"),
            P("section", None, None, None),
            P("section", None, None, None),
            P("section", None, "tensor", None),
            P("section", None, None, None),
            P("section", None, None, None),
            P("section", None, None, "tensor"),
            P("section", None, "tensor", None),
            P("section", None, None, None),
        ),
        out_specs=(
            P("section", None, ("dp", "tensor"), None),
            P("section", None, ("dp", "tensor"), None),
            P("section", None, None, None),
            P("section", None, None, "tensor"),
            P("section", None, None, None),
            P("section", None, None, None),
            P("section", None, "tensor", None),
            P("section", None, None, None),
            P("section", None, None, None),
            P("section", None, None, "tensor"),
            P("section", None, "tensor", None),
            P("section", None, None, None),
        ),
        check_vma=False,
    )
```

```python
import math

import jax
import jax.numpy as jnp
from jax import lax
from jax.experimental import pallas as pl
from jax.experimental.layout import Layout, with_layout_constraint
from jax.experimental.pallas import tpu as pltpu
from jax.sharding import PartitionSpec as P

WINDOW = 1024
epsilon = 1e-05
masked_score = -1e30
bf16 = jnp.bfloat16
f32 = jnp.float32


def plain(left, right):
    return jnp.dot(left, right, preferred_element_type=f32)


def against(left, right):
    return lax.dot_general(left, right, (((1,), (1,)), ((), ())), preferred_element_type=f32)


def across(left, right):
    return lax.dot_general(left, right, (((0,), (0,)), ((), ())), preferred_element_type=f32)


def around(block, axis, distance):
    size = lax.axis_size(axis)
    return lax.ppermute(block, axis, [(i, (i + distance) % size) for i in range(size)])


def along(block, axis, distance):
    size = lax.axis_size(axis)
    route = [(i, i + distance) for i in range(size) if 0 <= i + distance < size]
    return lax.ppermute(block, axis, route)


def flipped(block, axis, bit):
    size = lax.axis_size(axis)
    return lax.ppermute(block, axis, [(i, i ^ bit) for i in range(size)])


def pick(table, index, size=1):
    return lax.dynamic_slice_in_dim(table, index, size, 0)


def norm_parts(value):
    centred = value - jnp.mean(value, axis=-1, keepdims=True)
    spread = lax.rsqrt(jnp.mean(centred * centred, axis=-1, keepdims=True) + epsilon)
    return centred * spread, spread


def norm_back(unit, spread, scaled):
    inner = jnp.mean(scaled * unit, axis=-1, keepdims=True)
    return spread * (scaled - jnp.mean(scaled, axis=-1, keepdims=True) - unit * inner)


def gelu_parts(value):
    rate = math.sqrt(2.0 / math.pi)
    square = value * value
    bend = jnp.tanh(rate * (value + 0.044715 * value * square))
    rising = 0.5 * (1.0 + bend)
    slope = rising + 0.5 * value * (1.0 - bend * bend) * (rate * (1.0 + 3 * 0.044715 * square))
    return value * rising, slope


def side_blocks(query_ref, group, head):
    begin = group * 4 * head
    return jnp.concatenate(
        [query_ref[:, begin + h * head : begin + (h + 1) * head] for h in range(4)], axis=0
    )


def put_blocks(out_ref, value, group, head):
    rows = value.shape[0] // 4
    for h in range(4):
        begin = (group * 4 + h) * head
        out_ref[:, begin : begin + head] = value[h * rows : (h + 1) * rows]


def table_copies(table_ref, buf, sem, layer, begin):
    ranks, chunks, _, width = buf.shape
    return [
        pltpu.make_async_copy(
            table_ref.at[x, y, layer, :, pl.ds(begin, width)], buf.at[x, y], sem.at[x, y]
        )
        for x in range(ranks)
        for y in range(chunks)
    ]


def query_kernel(layer, normed_ref, table_ref, bias_ref, eq_ref, sq_ref, out_ref, low_ref, buf, sem):
    ranks, chunks, rows, width = buf.shape
    copies = table_copies(table_ref, buf, sem, layer, 0)
    for copy in copies:
        copy.start()
    normed = normed_ref[...]
    low = against(normed, sq_ref[...]).astype(bf16)
    low_ref[...] = low
    for x in range(ranks):
        columns = pl.ds(x * width, width)
        total = bias_ref[:, columns] + plain(low, eq_ref[:, columns])
        for y in range(chunks):
            copies[x * chunks + y].wait()
            total = total + plain(normed[:, y * rows : (y + 1) * rows], buf[x, y])
        out_ref[:, columns] = total.astype(bf16)


def table_scratch(table, width):
    ranks, chunks, _, rows, _ = table.shape
    return [
        pltpu.VMEM((ranks, chunks, rows, width), bf16),
        pltpu.SemaphoreType.DMA((ranks, chunks)),
    ]


held = pl.BlockSpec(memory_space=pltpu.VMEM)
remote = pl.BlockSpec(memory_space=pl.ANY)


def project_queries(layer, normed, table, bias, eq, sq):
    rows, model = normed.shape
    rank = sq.shape[0]
    width = model // table.shape[0]
    return pl.pallas_call(
        lambda *refs: query_kernel(layer, *refs),
        in_specs=[held, remote, held, held, held],
        out_specs=[held] * 2,
        out_shape=[
            jax.ShapeDtypeStruct((rows, model), bf16),
            jax.ShapeDtypeStruct((rows, rank), bf16),
        ],
        scratch_shapes=table_scratch(table, width),
        compiler_params=pltpu.CompilerParams(vmem_limit_bytes=28 * 2**20),
        cost_estimate=pl.CostEstimate(
            flops=8 * rows * model * model, bytes_accessed=2 * model * model, transcendentals=0
        ),
        name="project_queries",
    )(normed, table, bias, eq, sq)


def attend_kernel(
    layer, head, query_ref, keyval_ref, bias_ref, table_ref, so_ref, eo_ref,
    prob_ref, mixed_ref, low_ref, out_ref, buf, sem,
):
    ranks, chunks, rows, width = buf.shape
    copies = table_copies(table_ref, buf, sem, layer, width)
    for copy in copies:
        copy.start()
    scale = 1.0 / math.sqrt(head)
    bias = jnp.concatenate([bias_ref[...].astype(f32)] * 4, axis=0)
    for g in range(prob_ref.shape[0]):
        queries = side_blocks(query_ref, g, head)
        scores = against(queries, keyval_ref[:, :head]) * scale + bias
        lifted = jnp.exp(scores - jnp.max(scores, axis=-1, keepdims=True))
        probs = (lifted * (1.0 / jnp.sum(lifted, axis=-1, keepdims=True))).astype(bf16)
        prob_ref[g] = probs
        put_blocks(mixed_ref, plain(probs, keyval_ref[:, head:]).astype(bf16), g, head)
    mixed = mixed_ref[...]
    low = against(mixed, so_ref[...]).astype(bf16)
    low_ref[...] = low
    for copy in copies:
        copy.wait()
    for y in range(chunks):
        columns = pl.ds(y * rows, rows)
        total = plain(low, eo_ref[:, columns])
        for x in range(ranks):
            total = total + against(mixed[:, x * width : (x + 1) * width], buf[x, y])
        out_ref[:, columns] = total


def attend(layer, queries, key_block, bias, table, so, eo, head):
    rows, model = queries.shape
    keys = key_block.shape[0]
    groups = model // head // 4
    rank = so.shape[0]
    return pl.pallas_call(
        lambda *refs: attend_kernel(layer, head, *refs),
        in_specs=[held, held, held, remote, held, held],
        out_specs=[held] * 4,
        out_shape=[
            jax.ShapeDtypeStruct((groups, 4 * rows, keys), bf16),
            jax.ShapeDtypeStruct((rows, model), bf16),
            jax.ShapeDtypeStruct((rows, rank), bf16),
            jax.ShapeDtypeStruct((rows, model), f32),
        ],
        scratch_shapes=table_scratch(table, model // table.shape[0]),
        compiler_params=pltpu.CompilerParams(vmem_limit_bytes=36 * 2**20),
        cost_estimate=pl.CostEstimate(
            flops=4 * rows * model * (keys + 2 * model),
            bytes_accessed=2 * model * model,
            transcendentals=groups * 4 * rows * keys,
        ),
        name="attend",
    )(queries, key_block, bias, table, so, eo)


def attend_back_kernel(
    layer, head, branch_ref, table_ref, so_ref, eo_ref, prob_ref, query_ref, keyval_ref, eq_ref, sq_ref,
    dq_ref, dkv_ref, inner_o_ref, inner_q_ref, part_ref,
    out_buf, out_sem, query_buf, query_sem, mixed_buf, key_sum, value_sum,
):
    ranks, chunks, rows, width = out_buf.shape
    out_copies = table_copies(table_ref, out_buf, out_sem, layer, width)
    query_copies = table_copies(table_ref, query_buf, query_sem, layer, 0)
    for copy in out_copies + query_copies:
        copy.start()
    scale = 1.0 / math.sqrt(head)
    branch = branch_ref[...]
    inner_o = against(branch, eo_ref[...]).astype(bf16)
    inner_o_ref[...] = inner_o
    for g in range(prob_ref.shape[0]):
        columns = pl.ds(g * width, width)
        total = plain(inner_o, so_ref[:, columns])
        for y in range(chunks):
            out_copies[g * chunks + y].wait()
            total = total + plain(branch[:, y * rows : (y + 1) * rows], out_buf[g, y])
        mixed_buf[:, columns] = total.astype(bf16)
        grad = side_blocks(mixed_buf, g, head)
        low_probs = prob_ref[g]
        probs = low_probs.astype(f32)
        grad_probs = against(grad, keyval_ref[:, head:])
        delta = jnp.sum(grad_probs * probs, axis=-1, keepdims=True)
        delta = delta / jnp.sum(probs, axis=-1, keepdims=True)
        grad_scores = (probs * (grad_probs - delta)).astype(bf16)
        put_blocks(dq_ref, (plain(grad_scores, keyval_ref[:, :head]) * scale).astype(bf16), g, head)
        keys = across(grad_scores, side_blocks(query_ref, g, head))
        values = across(low_probs, grad)
        if g == 0:
            key_sum[...] = keys
            value_sum[...] = values
        else:
            key_sum[...] += keys
            value_sum[...] += values
    dkv_ref[:, :head] = (key_sum[...] * scale).astype(bf16)
    dkv_ref[:, head:] = value_sum[...].astype(bf16)
    grad_q = dq_ref[...]
    inner_q = against(grad_q, eq_ref[...]).astype(bf16)
    inner_q_ref[...] = inner_q
    for copy in query_copies:
        copy.wait()
    for y in range(chunks):
        columns = pl.ds(y * rows, rows)
        total = plain(inner_q, sq_ref[:, columns])
        for x in range(ranks):
            total = total + against(grad_q[:, x * width : (x + 1) * width], query_buf[x, y])
        part_ref[:, columns] = total


def attend_back(layer, branch, table, so, eo, probs, queries, key_block, eq, sq, head):
    rows, model = queries.shape
    keys = key_block.shape[0]
    groups = probs.shape[0]
    rank = so.shape[0]
    width = model // table.shape[0]
    return pl.pallas_call(
        lambda *refs: attend_back_kernel(layer, head, *refs),
        in_specs=[held, remote] + [held] * 7,
        out_specs=[held] * 5,
        out_shape=[
            jax.ShapeDtypeStruct((rows, model), bf16),
            jax.ShapeDtypeStruct((keys, 2 * head), bf16),
            jax.ShapeDtypeStruct((rows, rank), bf16),
            jax.ShapeDtypeStruct((rows, rank), bf16),
            jax.ShapeDtypeStruct((rows, model), f32),
        ],
        scratch_shapes=table_scratch(table, width)
        + table_scratch(table, width)
        + [
            pltpu.VMEM((rows, model), bf16),
            pltpu.VMEM((keys, head), f32),
            pltpu.VMEM((keys, head), f32),
        ],
        compiler_params=pltpu.CompilerParams(vmem_limit_bytes=44 * 2**20),
        cost_estimate=pl.CostEstimate(
            flops=8 * rows * model * (keys + 2 * model),
            bytes_accessed=4 * model * model + 4 * groups * 4 * rows * keys,
            transcendentals=0,
        ),
        name="attend_back",
    )(branch, table, so, eo, probs, queries, key_block, eq, sq)


def feed_copies(table_ref, buf, sems):
    _, count, chunks, rows, tile = buf.shape
    half = count // 2 * tile
    copies = []
    for j in range(count):
        pair = []
        for k in range(2):
            columns = pl.ds(j * tile % half + k * half, tile)
            pair.append(
                pltpu.make_async_copy(
                    table_ref.at[:, j * tile // half, :, columns], buf.at[k, j], sems.at[k, j]
                )
            )
        copies.append(pair)
    return copies


def plain_chunks(left, buf, k, j):
    rows = buf.shape[3]
    return sum(plain(left[:, i * rows : (i + 1) * rows], buf[k, j, i]) for i in range(buf.shape[2]))


def against_chunk(left_ref, buf, k, i):
    tile = buf.shape[4]
    return sum(
        against(left_ref[:, j * tile : (j + 1) * tile], buf[k, j, i]) for j in range(buf.shape[1])
    )


def feed_pack(pack_ref, model, hidden):
    cuts = [model, 2 * model, 2 * model + hidden, 2 * model + 2 * hidden, 3 * model + 2 * hidden]
    return [pack_ref.at[:, a:b] for a, b in zip(cuts[:-1], cuts[1:])]


def feed_kernel(
    second_ref, table_ref, bias_ref, pack_ref,
    active_ref, slope_ref, low_u_ref, low_d_ref, out_ref, buf, sems,
):
    _, count, chunks, rows, tile = buf.shape
    su_ref, eu_ref, sd_ref, ed_ref = feed_pack(pack_ref, chunks * rows, count * tile)
    copies = feed_copies(table_ref, buf, sems)
    for up, _ in copies:
        up.start()
    for _, down in copies:
        down.start()
    second = second_ref[...]
    low_u = against(second, su_ref[...]).astype(bf16)
    low_u_ref[...] = low_u
    for j in range(count):
        columns = pl.ds(j * tile, tile)
        copies[j][0].wait()
        upward = plain_chunks(second, buf, 0, j)
        upward = upward + plain(low_u, eu_ref[:, columns]) + bias_ref[:, columns]
        active, slope = gelu_parts(upward)
        active_ref[:, columns] = active.astype(bf16)
        slope_ref[:, columns] = slope.astype(bf16)
    low_d = against(active_ref[...], sd_ref[...]).astype(bf16)
    low_d_ref[...] = low_d
    for _, down in copies:
        down.wait()
    for i in range(chunks):
        columns = pl.ds(i * rows, rows)
        out_ref[:, columns] = (
            against_chunk(active_ref, buf, 1, i) + plain(low_d, ed_ref[:, columns])
        ).astype(bf16)


def feed_back_kernel(
    branch_ref, table_ref, slope_ref, pack_ref,
    grad_up_ref, inner_d_ref, inner_u_ref, out_ref, buf, sems,
):
    _, count, chunks, rows, tile = buf.shape
    su_ref, eu_ref, sd_ref, ed_ref = feed_pack(pack_ref, chunks * rows, count * tile)
    copies = feed_copies(table_ref, buf, sems)
    for _, down in copies:
        down.start()
    for up, _ in copies:
        up.start()
    branch = branch_ref[...]
    inner_d = against(branch, ed_ref[...]).astype(bf16)
    inner_d_ref[...] = inner_d
    for j in range(count):
        columns = pl.ds(j * tile, tile)
        copies[j][1].wait()
        grad = plain_chunks(branch, buf, 1, j) + plain(inner_d, sd_ref[:, columns])
        grad_up_ref[:, columns] = (grad * slope_ref[:, columns].astype(f32)).astype(bf16)
    inner_u = against(grad_up_ref[...], eu_ref[...]).astype(bf16)
    inner_u_ref[...] = inner_u
    for up, _ in copies:
        up.wait()
    for i in range(chunks):
        columns = pl.ds(i * rows, rows)
        out_ref[:, columns] = (
            against_chunk(grad_up_ref, buf, 0, i) + plain(inner_u, su_ref[:, columns])
        ).astype(bf16)


def feed_both_kernel(
    second_ref, branch_ref, table_ref, bias_ref, pack_ref,
    active_ref, low_u_ref, low_d_ref, out_ref, grad_up_ref, inner_d_ref, inner_u_ref, back_ref,
    buf, sems,
):
    _, count, chunks, rows, tile = buf.shape
    su_ref, eu_ref, sd_ref, ed_ref = feed_pack(pack_ref, chunks * rows, count * tile)
    copies = feed_copies(table_ref, buf, sems)
    for up, down in copies:
        up.start()
        down.start()
    second = second_ref[...]
    branch = branch_ref[...]
    low_u = against(second, su_ref[...]).astype(bf16)
    low_u_ref[...] = low_u
    inner_d = against(branch, ed_ref[...]).astype(bf16)
    inner_d_ref[...] = inner_d
    for j in range(count):
        columns = pl.ds(j * tile, tile)
        copies[j][0].wait()
        upward = plain_chunks(second, buf, 0, j)
        upward = upward + plain(low_u, eu_ref[:, columns]) + bias_ref[:, columns]
        active, slope = gelu_parts(upward)
        active_ref[:, columns] = active.astype(bf16)
        copies[j][1].wait()
        grad = plain_chunks(branch, buf, 1, j) + plain(inner_d, sd_ref[:, columns])
        grad_up_ref[:, columns] = (grad * slope).astype(bf16)
    inner_u = against(grad_up_ref[...], eu_ref[...]).astype(bf16)
    inner_u_ref[...] = inner_u
    low_d = against(active_ref[...], sd_ref[...]).astype(bf16)
    low_d_ref[...] = low_d
    for i in range(chunks):
        columns = pl.ds(i * rows, rows)
        back_ref[:, columns] = (
            against_chunk(grad_up_ref, buf, 0, i) + plain(inner_u, su_ref[:, columns])
        ).astype(bf16)
        out_ref[:, columns] = (
            against_chunk(active_ref, buf, 1, i) + plain(low_d, ed_ref[:, columns])
        ).astype(bf16)


def feed_call(kernel, name, inputs, outputs, hidden, matmuls):
    table = [value for value in inputs if value.ndim == 4][0]
    rows, model = inputs[0].shape
    tile = 512
    chunks = table.shape[0]
    return pl.pallas_call(
        kernel,
        in_specs=[remote if value.ndim == 4 else held for value in inputs],
        out_specs=[held] * len(outputs),
        out_shape=[jax.ShapeDtypeStruct((rows, width), bf16) for width in outputs],
        scratch_shapes=[
            pltpu.VMEM((2, hidden // tile, chunks, model // chunks, tile), bf16),
            pltpu.SemaphoreType.DMA((2, hidden // tile)),
        ],
        compiler_params=pltpu.CompilerParams(vmem_limit_bytes=44 * 2**20),
        cost_estimate=pl.CostEstimate(
            flops=2 * matmuls * rows * model * hidden,
            bytes_accessed=4 * model * hidden,
            transcendentals=rows * hidden,
        ),
        name=name,
    )(*inputs)


def per_device(
    block_input,
    cotangent,
    doc_lengths,
    bank_choice,
    first_gain,
    first_shift,
    query_weight,
    query_bias,
    keyval_weight,
    value_bias,
    output_weight,
    output_bias,
    second_gain,
    second_shift,
    upward_weight,
    upward_bias,
    downward_weight,
    downward_bias,
    query_shrink,
    query_expand,
    keyval_shrink,
    keyval_expand,
    output_shrink,
    output_expand,
    upward_shrink,
    upward_expand,
    downward_shrink,
    downward_expand,
):
    section = lax.axis_index("section")
    data = lax.axis_index("dp")
    tensor = lax.axis_index("tensor")
    low_section = section == 0
    width = block_input.shape[2]
    rows = block_input.shape[1]
    ranks = lax.axis_size("tensor")
    span = rows * ranks
    head = value_bias.shape[1]
    local_q = query_bias.shape[1]
    local_f = upward_bias.shape[1]
    rank = query_expand.shape[2]
    banks = query_expand.shape[1]
    reach = WINDOW // span
    sides = [(0, 1), (1, 0)]

    def swap(value):
        return lax.ppermute(value, "section", sides)

    def by_layer(own, other):
        return jnp.where(low_section, own, other), jnp.where(low_section, other, own)

    def spread(block):
        parts = [block] + [around(block, "tensor", -j) for j in range(1, ranks)]
        return jnp.concatenate(parts, axis=0)

    def reduce_rows(partial):
        low = partial.astype(bf16)
        total = partial[:rows].astype(f32)
        for j in range(1, ranks):
            total = total + around(low[j * rows : (j + 1) * rows], "tensor", j).astype(f32)
        return total

    own_bank = lax.dynamic_index_in_dim(bank_choice, section, 0, keepdims=False)
    other_bank = lax.dynamic_index_in_dim(bank_choice, 1 - section, 0, keepdims=False)

    chips = lax.axis_size("dp") // 4
    both = ("section", "dp")
    every = ("section", "dp", "tensor")
    order = [
        side * 4 * chips + chip * 4 + near
        for chip in range(chips)
        for side in range(2)
        for near in range(4)
    ]
    order_all = [place * ranks + x for x in range(ranks) for place in order]

    def row_major(block):
        return with_layout_constraint(block, Layout(major_to_minor=(0, 1)))

    def gather(shard):
        table = lax.all_gather(row_major(shard), both, axis=0, tiled=True, axis_index_groups=[order])
        return row_major(table).reshape(chips, 2, -1, shard.shape[1])

    def gather_all(shard):
        table = lax.all_gather(
            row_major(shard), every, axis=0, tiled=True, axis_index_groups=[order_all]
        )
        return row_major(table).reshape(ranks, chips, 2, -1, shard.shape[1])

    def halves(shard):
        cut = shard.shape[1] // 2
        return shard[:, :cut], shard[:, cut:]

    keyval_half = jnp.where(tensor % 2 == 0, keyval_weight[0][:, :head], keyval_weight[0][:, head:])
    early_all = gather_all(
        jnp.concatenate([query_weight[0], row_major(output_weight[0].T), keyval_half], axis=1)
    )
    keyval_ws = [
        jnp.concatenate(
            [early_all[x, :, layer, :, 2 * local_q :].reshape(width, head) for x in range(2)], axis=1
        )
        for layer in range(2)
    ]

    vectors = jnp.concatenate(
        [
            first_gain,
            first_shift,
            jnp.zeros_like(value_bias),
            value_bias,
            output_bias,
            second_gain,
            second_shift,
            upward_bias,
            downward_bias,
        ],
        axis=1,
    )
    vector_sizes = [width, width, 2 * head, width, width, width, local_f, width]
    vector_layers = by_layer(vectors, swap(vectors))

    def chosen(table, bank, transpose):
        block = lax.dynamic_index_in_dim(table[0], bank, 0, keepdims=False)
        return block.T if transpose else block

    def pack(bank, parts):
        return jnp.concatenate([chosen(table, bank, flip) for table, flip in parts], axis=1)

    def exchanged(parts):
        return by_layer(pack(own_bank, parts), swap(pack(other_bank, parts)))

    def cut_pack(parts):
        own = jnp.concatenate([pack(own_bank, parts), query_rows], axis=1)
        other = jnp.concatenate([pack(other_bank, parts), query_rows], axis=1)
        return by_layer(own, swap(other))

    query_rows = jnp.broadcast_to(query_bias, (rank, local_q))
    cut_layers = jnp.stack(cut_pack([(query_expand, False), (output_shrink, True)]))
    cut_parts = jnp.stack(
        [cut_layers] + [around(cut_layers, "tensor", j) for j in range(1, ranks)]
    )
    cut_whole = jnp.stack(
        [
            lax.dynamic_index_in_dim(cut_parts, (tensor - r) % ranks, 0, keepdims=False)
            for r in range(ranks)
        ],
        axis=2,
    ).reshape(2, rank, ranks, 3, local_q)
    eq_all, so_all, query_bias_all = [
        cut_whole[:, :, :, k].reshape(2, rank, ranks * local_q) for k in range(3)
    ]
    early_layers = exchanged([(query_shrink, True), (keyval_shrink, True), (keyval_expand, False)])
    late_layers = exchanged(
        [
            (output_expand, False),
            (upward_shrink, True),
            (upward_expand, False),
            (downward_shrink, True),
            (downward_expand, False),
        ]
    )

    up_halves = halves(upward_weight[0])
    down_halves = halves(row_major(downward_weight[0].T))
    side = [jnp.concatenate([up_halves[h], down_halves[h]], axis=1) for h in range(2)]
    keep = jnp.where(low_section, side[0], side[1])
    gained = swap(jnp.where(low_section, side[1], side[0]))
    feed_tables = [gather(table) for table in by_layer(keep, gained)]

    def split(table, sizes):
        cuts = [0]
        for size in sizes:
            cuts.append(cuts[-1] + size)
        return [table[:, a:b] for a, b in zip(cuts[:-1], cuts[1:])]

    small = [
        [part.astype(f32) for part in split(vector_layers[layer], vector_sizes)]
        for layer in range(2)
    ]
    adapters = [
        split(early_layers[layer], [width, width, 2 * head]) + [late_layers[layer][:, :width]]
        for layer in range(2)
    ]

    inside = jnp.arange(rows, dtype=jnp.int32)
    query_place = data * span + tensor * rows + inside
    key_place = jnp.concatenate(
        [
            (data - back) * span + (tensor + j) % ranks * rows + inside
            for j in range(ranks)
            for back in range(reach, -1, -1)
        ]
    )
    lengths = lax.dynamic_index_in_dim(doc_lengths, section, 0, keepdims=False)
    ends = jnp.cumsum(lengths)
    query_doc = jnp.sum((query_place[:, None] >= ends[None, :]).astype(jnp.int32), axis=1)
    key_doc = jnp.sum((key_place[:, None] >= ends[None, :]).astype(jnp.int32), axis=1)
    distance = query_place[:, None] - key_place[None, :]
    allowed = (
        (key_place[None, :] >= 0)
        & (distance >= 0)
        & (distance < WINDOW)
        & (query_doc[:, None] == key_doc[None, :])
    )
    bias = jnp.where(allowed, 0.0, masked_score).astype(bf16)

    def forward_attend(layer, hidden):
        gain1, shift1, kv_bias, out_bias = small[layer][:4]
        sq, skv, ekv, eo = adapters[layer]
        unit1, rsd1 = norm_parts(hidden)
        normed = (unit1 * gain1 + shift1).astype(bf16)
        low_kv = against(normed, skv).astype(bf16)
        keyval = (plain(normed, keyval_ws[layer]) + kv_bias + plain(low_kv, ekv)).astype(bf16)
        pieces = [along(keyval, "dp", back) for back in range(reach, 0, -1)] + [keyval]
        key_block = spread(jnp.concatenate(pieces, axis=0))
        queries, low_q = project_queries(
            layer, normed, early_all, query_bias_all[layer, :1].astype(f32), eq_all[layer], sq
        )
        probs, mixed, low_o, attended = attend(
            layer, queries, key_block, bias, early_all, so_all[layer], eo, head
        )
        middle = hidden + (attended + out_bias)
        return middle, (unit1, rsd1, normed, low_q, low_kv, queries, key_block, probs, mixed, low_o)

    def feed_inputs(layer, middle):
        gain2, shift2, up_bias = small[layer][4:7]
        unit2, rsd2 = norm_parts(middle)
        second = spread((unit2 * gain2 + shift2).astype(bf16))
        return unit2, rsd2, second, up_bias

    def feed_result(layer, middle, partial):
        return middle + (reduce_rows(partial) + small[layer][7])

    def tiles(block):
        return block.reshape(rank, -1, 128).transpose(1, 0, 2)

    def flat(block):
        return block.transpose(1, 0, 2).reshape(rank, -1)

    turn, near = data // 4, data % 4

    def padded(pile, multiple):
        lack = -pile.shape[0] % multiple
        if not lack:
            return pile
        return jnp.concatenate([pile, jnp.zeros((lack,) + pile.shape[1:], pile.dtype)], axis=0)

    def piled(shared, quartered):
        pile = padded(jnp.concatenate([tiles(part) for part in shared], axis=0), ranks)
        return jnp.concatenate(
            [block.reshape((ranks, -1) + block.shape[1:]) for block in [pile] + [tiles(part) for part in quartered]],
            axis=1,
        ).astype(bf16)

    def owned_pile(mine, owned):
        pile = jnp.concatenate([mine] + [tiles(part) for part in owned], axis=0).astype(bf16)
        return padded(pile, lax.axis_size("dp"))

    def at(block, index, axis):
        return lax.dynamic_index_in_dim(block, index, axis, keepdims=False)

    def scattered_grads(layers):
        pile = jnp.stack([piled(shared, quartered) for shared, quartered, _ in layers], axis=1)
        mine = at(pile, tensor, 0).astype(f32)
        for j in range(1, ranks):
            mine = mine + around(at(pile, (tensor + j) % ranks, 0), "tensor", j).astype(f32)
        pile = jnp.stack([owned_pile(mine[i], layers[i][2]) for i in range(2)])
        pile = pile.reshape((2, chips, 4, -1) + pile.shape[2:])
        mine = at(pile, near, 2).astype(f32)
        for k in range(1, 4):
            mine = mine + flipped(at(pile, near ^ k, 2), "dp", k).astype(f32)
        pile = mine.astype(bf16)
        mine = at(pile, turn, 1).astype(f32)
        for k in range(1, chips):
            mine = mine + flipped(at(pile, turn ^ k, 1), "dp", 4 * k).astype(f32)
        return mine.astype(bf16)

    def crossed(block, mask):
        return lax.ppermute(block, both, [(i, i ^ mask) for i in range(8 * chips)])

    def spread_grads(zero, one, shared, quartered, owned):
        own = jnp.where(low_section, zero, one)
        away = jnp.where(low_section, one, zero)
        dp_size = 4 * chips
        home = jnp.stack([own, flipped(own, "dp", 2)])
        guest = jnp.stack([crossed(away, dp_size), crossed(away, dp_size + 2)])
        home, guest = [
            jnp.where(near // 2 == 0, block, block[::-1]) for block in (home, guest)
        ]
        pair = jnp.where(
            low_section, jnp.stack([home, guest], axis=1), jnp.stack([guest, home], axis=1)
        )
        parts = jnp.stack([pair] + [flipped(pair, "dp", 4 * k) for k in range(1, chips)])
        parts = jnp.stack([at(parts, turn ^ k, 0) for k in range(chips)])
        other = flipped(parts, "dp", 1)
        core = near % 2
        parts = jnp.stack(
            [jnp.where(core == 0, parts, other), jnp.where(core == 0, other, parts)], axis=2
        )
        pile = jnp.moveaxis(parts, 3, 0).reshape((2, -1) + parts.shape[5:])
        shared_sizes = [part.shape[1] // 128 for part in shared]
        quarter_sizes = [part.shape[1] // 128 // ranks for part in quartered]
        owned_sizes = [part.shape[1] // 128 for part in owned]
        each = -(-sum(shared_sizes) // ranks)
        own = pile[:, :each]
        parts = jnp.stack([own] + [around(own, "tensor", k) for k in range(1, ranks)])
        ordered = jnp.concatenate([at(parts, (tensor - r) % ranks, 0) for r in range(ranks)], axis=1)
        results = []
        for whole, begin, sizes in [
            (ordered, 0, shared_sizes),
            (pile, each, quarter_sizes + owned_sizes),
        ]:
            for count in sizes:
                results.append([flat(whole[m, begin : begin + count]) for m in range(2)])
                begin += count
        return results

    def feed_grads(layer, grad, unit2, rsd2, partial):
        return grad + norm_back(unit2, rsd2, reduce_rows(partial) * small[layer][4])

    def feed_adapters(second, branch, low_u, low_d, inner_u, inner_d, active, grad_up):
        shared = [across(inner_u, second), across(low_d, branch)]
        owned = [across(low_u, grad_up), across(inner_d, active)]
        return shared, owned

    def backward_attend(layer, kept, grad_middle):
        gain1 = small[layer][0]
        sq, skv, ekv, eo = adapters[layer]
        unit1, rsd1, normed, low_q, low_kv, queries, key_block, probs, mixed, low_o = kept
        branch = grad_middle.astype(bf16)
        grad_q, grad_block, inner_o, inner_q, partial = attend_back(
            layer, branch, early_all, so_all[layer], eo, probs, queries, key_block,
            eq_all[layer], sq, head,
        )
        count = (reach + 1) * rows
        blocks = grad_block[:count].astype(f32)
        for j in range(1, ranks):
            part = grad_block[j * count : (j + 1) * count]
            blocks = blocks + around(part, "tensor", j).astype(f32)
        own = blocks[reach * rows :]
        for back in range(1, reach + 1):
            begin = (reach - back) * rows
            own = own + along(blocks[begin : begin + rows].astype(bf16), "dp", -back).astype(f32)
        grad_kv = own.astype(bf16)
        inner_kv = against(grad_kv, ekv).astype(bf16)
        grad_normed = partial + against(grad_kv, keyval_ws[layer]) + plain(inner_kv, skv)
        grad_hidden = grad_middle + norm_back(unit1, rsd1, grad_normed * gain1)
        shared = [
            across(low_o, branch),
            across(inner_q, normed),
            across(inner_kv, normed),
            across(low_kv, grad_kv),
        ]
        quartered = [across(low_q, grad_q), across(inner_o, mixed)]
        return grad_hidden, shared, quartered

    fresh = lax.dynamic_index_in_dim(block_input, section, 0, keepdims=False).astype(f32)
    given = lax.dynamic_index_in_dim(cotangent, section, 0, keepdims=False).astype(f32)

    middle_zero, kept_zero = forward_attend(0, fresh)
    unit_zero, rsd_zero, second_zero, up_bias = feed_inputs(0, middle_zero)
    active_zero, slope_zero, low_u_zero, low_d_zero, partial = feed_call(
        feed_kernel,
        "feed",
        (second_zero, feed_tables[0], up_bias, late_layers[0]),
        (local_f, local_f, rank, rank, width),
        local_f,
        2,
    )
    passed = feed_result(0, middle_zero, partial).astype(bf16)

    middle_one, kept_one = forward_attend(1, passed.astype(f32))
    unit_one, rsd_one, second_one, up_bias = feed_inputs(1, middle_one)
    branch_one = spread(given.astype(bf16))
    active, low_u, low_d, partial, grad_up, inner_d, inner_u, partial_back = feed_call(
        feed_both_kernel,
        "feed_both",
        (second_one, branch_one, feed_tables[1], up_bias, late_layers[1]),
        (local_f, rank, rank, width, local_f, rank, rank, width),
        local_f,
        4,
    )
    grad_middle = feed_grads(1, given, unit_one, rsd_one, partial_back)
    shared, owned = feed_adapters(
        second_one, branch_one, low_u, low_d, inner_u, inner_d, active, grad_up
    )
    grad_one, more, quartered = backward_attend(1, kept_one, grad_middle)
    layer_one = (shared + more, quartered, owned)
    partial, _ = lax.optimization_barrier((partial, grad_middle))
    final = feed_result(1, middle_one, partial).astype(bf16)

    branch_zero = spread(grad_one.astype(bf16))
    grad_up, inner_d, inner_u, partial_back = feed_call(
        feed_back_kernel,
        "feed_back",
        (branch_zero, feed_tables[0], slope_zero, late_layers[0]),
        (local_f, rank, rank, width),
        local_f,
        2,
    )
    grad_middle_zero = feed_grads(0, grad_one, unit_zero, rsd_zero, partial_back)
    shared, owned = feed_adapters(
        second_zero,
        branch_zero,
        low_u_zero,
        low_d_zero,
        inner_u,
        inner_d,
        active_zero,
        grad_up,
    )
    grad_zero, more, quartered = backward_attend(0, kept_zero, grad_middle_zero)
    shared = shared + more
    mine = scattered_grads([(shared, quartered, owned), layer_one])
    grads = spread_grads(mine[0], mine[1], shared, quartered, owned)

    def both_micros(zero, one, kind):
        own = jnp.where(low_section, zero, one)
        received = swap(jnp.where(low_section, one, zero).astype(bf16)).astype(kind)
        return jnp.where(low_section, jnp.stack([own, received]), jnp.stack([received, own]))

    passed, final, _ = lax.optimization_barrier((passed, final, grad_middle_zero))
    section_outputs = both_micros(passed, final, bf16)
    input_grads = both_micros(grad_zero, grad_one, f32)
    onehot = (bank_choice[:, None] == jnp.arange(banks)[None, :]).astype(f32)

    def placed(pair, transpose):
        out = sum(
            onehot[m][:, None, None] * pair[m].astype(f32)[None] for m in range(2)
        )
        return (out.transpose(0, 2, 1) if transpose else out)[None]

    (
        up_shrink_grad,
        down_expand_grad,
        out_expand_grad,
        q_shrink_grad,
        kv_shrink_grad,
        kv_expand_grad,
        q_expand_grad,
        out_shrink_grad,
        up_expand_grad,
        down_shrink_grad,
    ) = grads
    return (
        section_outputs[None],
        input_grads[None],
        placed(q_shrink_grad, True),
        placed(q_expand_grad, False),
        placed(kv_shrink_grad, True),
        placed(kv_expand_grad, False),
        placed(out_shrink_grad, True),
        placed(out_expand_grad, False),
        placed(up_shrink_grad, True),
        placed(up_expand_grad, False),
        placed(down_shrink_grad, True),
        placed(down_expand_grad, False),
    )


def solution(mesh):
    return jax.shard_map(
        per_device,
        mesh=mesh,
        in_specs=(
            P(None, ("dp", "tensor"), None),
            P(None, ("dp", "tensor"), None),
            P(),
            P(),
            P("section", None),
            P("section", None),
            P("section", "dp", "tensor"),
            P("section", "tensor"),
            P("section", "dp", None),
            P("section", None),
            P("section", "tensor", "dp"),
            P("section", None),
            P("section", None),
            P("section", None),
            P("section", "dp", "tensor"),
            P("section", "tensor"),
            P("section", "tensor", "dp"),
            P("section", None),
            P("section", None, None, None),
            P("section", None, None, "tensor"),
            P("section", None, None, None),
            P("section", None, None, None),
            P("section", None, "tensor", None),
            P("section", None, None, None),
            P("section", None, None, None),
            P("section", None, None, "tensor"),
            P("section", None, "tensor", None),
            P("section", None, None, None),
        ),
        out_specs=(
            P("section", None, ("dp", "tensor"), None),
            P("section", None, ("dp", "tensor"), None),
            P("section", None, None, None),
            P("section", None, None, "tensor"),
            P("section", None, None, None),
            P("section", None, None, None),
            P("section", None, "tensor", None),
            P("section", None, None, None),
            P("section", None, None, None),
            P("section", None, None, "tensor"),
            P("section", None, "tensor", None),
            P("section", None, None, None),
        ),
        check_vma=False,
    )
```

```python
import math

import jax
import jax.numpy as jnp
from jax import lax
from jax.experimental import pallas as pl
from jax.experimental.layout import Layout, with_layout_constraint
from jax.experimental.pallas import tpu as pltpu
from jax.sharding import PartitionSpec as P

WINDOW = 1024
epsilon = 1e-05
masked_score = -1e30
bf16 = jnp.bfloat16
f32 = jnp.float32


def plain(left, right):
    return jnp.dot(left, right, preferred_element_type=f32)


def against(left, right):
    return lax.dot_general(left, right, (((1,), (1,)), ((), ())), preferred_element_type=f32)


def across(left, right):
    return lax.dot_general(left, right, (((0,), (0,)), ((), ())), preferred_element_type=f32)


def around(block, axis, distance):
    size = lax.axis_size(axis)
    return lax.ppermute(block, axis, [(i, (i + distance) % size) for i in range(size)])


def along(block, axis, distance):
    size = lax.axis_size(axis)
    route = [(i, i + distance) for i in range(size) if 0 <= i + distance < size]
    return lax.ppermute(block, axis, route)


def flipped(block, axis, bit):
    size = lax.axis_size(axis)
    return lax.ppermute(block, axis, [(i, i ^ bit) for i in range(size)])


def pick(table, index, size=1):
    return lax.dynamic_slice_in_dim(table, index, size, 0)


def norm_parts(value):
    centred = value - jnp.mean(value, axis=-1, keepdims=True)
    spread = lax.rsqrt(jnp.mean(centred * centred, axis=-1, keepdims=True) + epsilon)
    return centred * spread, spread


def norm_back(unit, spread, scaled):
    inner = jnp.mean(scaled * unit, axis=-1, keepdims=True)
    return spread * (scaled - jnp.mean(scaled, axis=-1, keepdims=True) - unit * inner)


def gelu_parts(value):
    rate = math.sqrt(2.0 / math.pi)
    square = value * value
    bend = jnp.tanh(rate * (value + 0.044715 * value * square))
    rising = 0.5 * (1.0 + bend)
    slope = rising + 0.5 * value * (1.0 - bend * bend) * (rate * (1.0 + 3 * 0.044715 * square))
    return value * rising, slope


def side_blocks(query_ref, group, head):
    begin = group * 4 * head
    return jnp.concatenate(
        [query_ref[:, begin + h * head : begin + (h + 1) * head] for h in range(4)], axis=0
    )


def put_blocks(out_ref, value, group, head):
    rows = value.shape[0] // 4
    for h in range(4):
        begin = (group * 4 + h) * head
        out_ref[:, begin : begin + head] = value[h * rows : (h + 1) * rows]


def table_copies(table_ref, buf, sem, layer, begin):
    ranks, chunks, _, width = buf.shape
    return [
        pltpu.make_async_copy(
            table_ref.at[x, y, layer, :, pl.ds(begin, width)], buf.at[x, y], sem.at[x, y]
        )
        for x in range(ranks)
        for y in range(chunks)
    ]


def query_kernel(layer, normed_ref, table_ref, bias_ref, eq_ref, sq_ref, out_ref, low_ref, buf, sem):
    ranks, chunks, rows, width = buf.shape
    copies = table_copies(table_ref, buf, sem, layer, 0)
    for copy in copies:
        copy.start()
    normed = normed_ref[...]
    low = against(normed, sq_ref[...]).astype(bf16)
    low_ref[...] = low
    for x in range(ranks):
        columns = pl.ds(x * width, width)
        total = bias_ref[:, columns] + plain(low, eq_ref[:, columns])
        for y in range(chunks):
            copies[x * chunks + y].wait()
            total = total + plain(normed[:, y * rows : (y + 1) * rows], buf[x, y])
        out_ref[:, columns] = total.astype(bf16)


def table_scratch(table, width):
    ranks, chunks, _, rows, _ = table.shape
    return [
        pltpu.VMEM((ranks, chunks, rows, width), bf16),
        pltpu.SemaphoreType.DMA((ranks, chunks)),
    ]


held = pl.BlockSpec(memory_space=pltpu.VMEM)
remote = pl.BlockSpec(memory_space=pl.ANY)


def project_queries(layer, normed, table, bias, eq, sq):
    rows, model = normed.shape
    rank = sq.shape[0]
    width = model // table.shape[0]
    return pl.pallas_call(
        lambda *refs: query_kernel(layer, *refs),
        in_specs=[held, remote, held, held, held],
        out_specs=[held] * 2,
        out_shape=[
            jax.ShapeDtypeStruct((rows, model), bf16),
            jax.ShapeDtypeStruct((rows, rank), bf16),
        ],
        scratch_shapes=table_scratch(table, width),
        compiler_params=pltpu.CompilerParams(vmem_limit_bytes=28 * 2**20),
        cost_estimate=pl.CostEstimate(
            flops=8 * rows * model * model, bytes_accessed=2 * model * model, transcendentals=0
        ),
        name="project_queries",
    )(normed, table, bias, eq, sq)


def attend_kernel(
    layer, head, query_ref, keyval_ref, bias_ref, table_ref, so_ref, eo_ref,
    prob_ref, mixed_ref, low_ref, out_ref, buf, sem,
):
    ranks, chunks, rows, width = buf.shape
    copies = table_copies(table_ref, buf, sem, layer, width)
    for copy in copies:
        copy.start()
    scale = 1.0 / math.sqrt(head)
    bias = jnp.concatenate([bias_ref[...].astype(f32)] * 4, axis=0)
    for g in range(prob_ref.shape[0]):
        queries = side_blocks(query_ref, g, head)
        scores = against(queries, keyval_ref[:, :head]) * scale + bias
        lifted = jnp.exp(scores - jnp.max(scores, axis=-1, keepdims=True))
        probs = (lifted * (1.0 / jnp.sum(lifted, axis=-1, keepdims=True))).astype(bf16)
        prob_ref[g] = probs
        put_blocks(mixed_ref, plain(probs, keyval_ref[:, head:]).astype(bf16), g, head)
    mixed = mixed_ref[...]
    low = against(mixed, so_ref[...]).astype(bf16)
    low_ref[...] = low
    for copy in copies:
        copy.wait()
    for y in range(chunks):
        columns = pl.ds(y * rows, rows)
        total = plain(low, eo_ref[:, columns])
        for x in range(ranks):
            total = total + against(mixed[:, x * width : (x + 1) * width], buf[x, y])
        out_ref[:, columns] = total


def attend(layer, queries, key_block, bias, table, so, eo, head):
    rows, model = queries.shape
    keys = key_block.shape[0]
    groups = model // head // 4
    rank = so.shape[0]
    return pl.pallas_call(
        lambda *refs: attend_kernel(layer, head, *refs),
        in_specs=[held, held, held, remote, held, held],
        out_specs=[held] * 4,
        out_shape=[
            jax.ShapeDtypeStruct((groups, 4 * rows, keys), bf16),
            jax.ShapeDtypeStruct((rows, model), bf16),
            jax.ShapeDtypeStruct((rows, rank), bf16),
            jax.ShapeDtypeStruct((rows, model), f32),
        ],
        scratch_shapes=table_scratch(table, model // table.shape[0]),
        compiler_params=pltpu.CompilerParams(vmem_limit_bytes=36 * 2**20),
        cost_estimate=pl.CostEstimate(
            flops=4 * rows * model * (keys + 2 * model),
            bytes_accessed=2 * model * model,
            transcendentals=groups * 4 * rows * keys,
        ),
        name="attend",
    )(queries, key_block, bias, table, so, eo)


def attend_back_kernel(
    layer, head, branch_ref, table_ref, so_ref, eo_ref, prob_ref, query_ref, keyval_ref, eq_ref, sq_ref,
    dq_ref, dkv_ref, inner_o_ref, inner_q_ref, part_ref,
    out_buf, out_sem, query_buf, query_sem, mixed_buf, key_sum, value_sum,
):
    ranks, chunks, rows, width = out_buf.shape
    out_copies = table_copies(table_ref, out_buf, out_sem, layer, width)
    query_copies = table_copies(table_ref, query_buf, query_sem, layer, 0)
    for copy in out_copies + query_copies:
        copy.start()
    scale = 1.0 / math.sqrt(head)
    branch = branch_ref[...]
    inner_o = against(branch, eo_ref[...]).astype(bf16)
    inner_o_ref[...] = inner_o
    for g in range(prob_ref.shape[0]):
        columns = pl.ds(g * width, width)
        total = plain(inner_o, so_ref[:, columns])
        for y in range(chunks):
            out_copies[g * chunks + y].wait()
            total = total + plain(branch[:, y * rows : (y + 1) * rows], out_buf[g, y])
        mixed_buf[:, columns] = total.astype(bf16)
        grad = side_blocks(mixed_buf, g, head)
        low_probs = prob_ref[g]
        probs = low_probs.astype(f32)
        grad_probs = against(grad, keyval_ref[:, head:])
        delta = jnp.sum(grad_probs * probs, axis=-1, keepdims=True)
        delta = delta / jnp.sum(probs, axis=-1, keepdims=True)
        grad_scores = (probs * (grad_probs - delta)).astype(bf16)
        put_blocks(dq_ref, (plain(grad_scores, keyval_ref[:, :head]) * scale).astype(bf16), g, head)
        keys = across(grad_scores, side_blocks(query_ref, g, head))
        values = across(low_probs, grad)
        if g == 0:
            key_sum[...] = keys
            value_sum[...] = values
        else:
            key_sum[...] += keys
            value_sum[...] += values
    dkv_ref[:, :head] = (key_sum[...] * scale).astype(bf16)
    dkv_ref[:, head:] = value_sum[...].astype(bf16)
    grad_q = dq_ref[...]
    inner_q = against(grad_q, eq_ref[...]).astype(bf16)
    inner_q_ref[...] = inner_q
    for copy in query_copies:
        copy.wait()
    for y in range(chunks):
        columns = pl.ds(y * rows, rows)
        total = plain(inner_q, sq_ref[:, columns])
        for x in range(ranks):
            total = total + against(grad_q[:, x * width : (x + 1) * width], query_buf[x, y])
        part_ref[:, columns] = total


def attend_back(layer, branch, table, so, eo, probs, queries, key_block, eq, sq, head):
    rows, model = queries.shape
    keys = key_block.shape[0]
    groups = probs.shape[0]
    rank = so.shape[0]
    width = model // table.shape[0]
    return pl.pallas_call(
        lambda *refs: attend_back_kernel(layer, head, *refs),
        in_specs=[held, remote] + [held] * 7,
        out_specs=[held] * 5,
        out_shape=[
            jax.ShapeDtypeStruct((rows, model), bf16),
            jax.ShapeDtypeStruct((keys, 2 * head), bf16),
            jax.ShapeDtypeStruct((rows, rank), bf16),
            jax.ShapeDtypeStruct((rows, rank), bf16),
            jax.ShapeDtypeStruct((rows, model), f32),
        ],
        scratch_shapes=table_scratch(table, width)
        + table_scratch(table, width)
        + [
            pltpu.VMEM((rows, model), bf16),
            pltpu.VMEM((keys, head), f32),
            pltpu.VMEM((keys, head), f32),
        ],
        compiler_params=pltpu.CompilerParams(vmem_limit_bytes=44 * 2**20),
        cost_estimate=pl.CostEstimate(
            flops=8 * rows * model * (keys + 2 * model),
            bytes_accessed=4 * model * model + 4 * groups * 4 * rows * keys,
            transcendentals=0,
        ),
        name="attend_back",
    )(branch, table, so, eo, probs, queries, key_block, eq, sq)


def feed_copies(table_ref, buf, sems):
    _, count, chunks, rows, tile = buf.shape
    half = count // 2 * tile
    copies = []
    for j in range(count):
        pair = []
        for k in range(2):
            columns = pl.ds(j * tile % half + k * half, tile)
            pair.append(
                pltpu.make_async_copy(
                    table_ref.at[:, j * tile // half, :, columns], buf.at[k, j], sems.at[k, j]
                )
            )
        copies.append(pair)
    return copies


def plain_chunks(left, buf, k, j):
    rows = buf.shape[3]
    return sum(plain(left[:, i * rows : (i + 1) * rows], buf[k, j, i]) for i in range(buf.shape[2]))


def against_chunk(left_ref, buf, k, i):
    tile = buf.shape[4]
    return sum(
        against(left_ref[:, j * tile : (j + 1) * tile], buf[k, j, i]) for j in range(buf.shape[1])
    )


def feed_pack(pack_ref, model, hidden):
    cuts = [0, model, model + hidden, model + 2 * hidden, 2 * model + 2 * hidden]
    return [pack_ref.at[:, a:b] for a, b in zip(cuts[:-1], cuts[1:])]


def feed_kernel(
    second_ref, table_ref, bias_ref, pack_ref,
    active_ref, slope_ref, low_u_ref, low_d_ref, out_ref, buf, sems,
):
    _, count, chunks, rows, tile = buf.shape
    su_ref, eu_ref, sd_ref, ed_ref = feed_pack(pack_ref, chunks * rows, count * tile)
    copies = feed_copies(table_ref, buf, sems)
    for up, _ in copies:
        up.start()
    for _, down in copies:
        down.start()
    second = second_ref[...]
    low_u = against(second, su_ref[...]).astype(bf16)
    low_u_ref[...] = low_u
    for j in range(count):
        columns = pl.ds(j * tile, tile)
        copies[j][0].wait()
        upward = plain_chunks(second, buf, 0, j)
        upward = upward + plain(low_u, eu_ref[:, columns]) + bias_ref[:, columns]
        active, slope = gelu_parts(upward)
        active_ref[:, columns] = active.astype(bf16)
        slope_ref[:, columns] = slope.astype(bf16)
    low_d = against(active_ref[...], sd_ref[...]).astype(bf16)
    low_d_ref[...] = low_d
    for _, down in copies:
        down.wait()
    for i in range(chunks):
        columns = pl.ds(i * rows, rows)
        out_ref[:, columns] = (
            against_chunk(active_ref, buf, 1, i) + plain(low_d, ed_ref[:, columns])
        ).astype(bf16)


def feed_back_kernel(
    branch_ref, table_ref, slope_ref, pack_ref,
    grad_up_ref, inner_d_ref, inner_u_ref, out_ref, buf, sems,
):
    _, count, chunks, rows, tile = buf.shape
    su_ref, eu_ref, sd_ref, ed_ref = feed_pack(pack_ref, chunks * rows, count * tile)
    copies = feed_copies(table_ref, buf, sems)
    for _, down in copies:
        down.start()
    for up, _ in copies:
        up.start()
    branch = branch_ref[...]
    inner_d = against(branch, ed_ref[...]).astype(bf16)
    inner_d_ref[...] = inner_d
    for j in range(count):
        columns = pl.ds(j * tile, tile)
        copies[j][1].wait()
        grad = plain_chunks(branch, buf, 1, j) + plain(inner_d, sd_ref[:, columns])
        grad_up_ref[:, columns] = (grad * slope_ref[:, columns].astype(f32)).astype(bf16)
    inner_u = against(grad_up_ref[...], eu_ref[...]).astype(bf16)
    inner_u_ref[...] = inner_u
    for up, _ in copies:
        up.wait()
    for i in range(chunks):
        columns = pl.ds(i * rows, rows)
        out_ref[:, columns] = (
            against_chunk(grad_up_ref, buf, 0, i) + plain(inner_u, su_ref[:, columns])
        ).astype(bf16)


def feed_both_kernel(
    second_ref, branch_ref, table_ref, bias_ref, pack_ref,
    active_ref, low_u_ref, low_d_ref, out_ref, grad_up_ref, inner_d_ref, inner_u_ref, back_ref,
    buf, sems,
):
    _, count, chunks, rows, tile = buf.shape
    su_ref, eu_ref, sd_ref, ed_ref = feed_pack(pack_ref, chunks * rows, count * tile)
    copies = feed_copies(table_ref, buf, sems)
    for up, down in copies:
        up.start()
        down.start()
    second = second_ref[...]
    branch = branch_ref[...]
    low_u = against(second, su_ref[...]).astype(bf16)
    low_u_ref[...] = low_u
    inner_d = against(branch, ed_ref[...]).astype(bf16)
    inner_d_ref[...] = inner_d
    for j in range(count):
        columns = pl.ds(j * tile, tile)
        copies[j][0].wait()
        upward = plain_chunks(second, buf, 0, j)
        upward = upward + plain(low_u, eu_ref[:, columns]) + bias_ref[:, columns]
        active, slope = gelu_parts(upward)
        active_ref[:, columns] = active.astype(bf16)
        copies[j][1].wait()
        grad = plain_chunks(branch, buf, 1, j) + plain(inner_d, sd_ref[:, columns])
        grad_up_ref[:, columns] = (grad * slope).astype(bf16)
    inner_u = against(grad_up_ref[...], eu_ref[...]).astype(bf16)
    inner_u_ref[...] = inner_u
    low_d = against(active_ref[...], sd_ref[...]).astype(bf16)
    low_d_ref[...] = low_d
    for i in range(chunks):
        columns = pl.ds(i * rows, rows)
        back_ref[:, columns] = (
            against_chunk(grad_up_ref, buf, 0, i) + plain(inner_u, su_ref[:, columns])
        ).astype(bf16)
        out_ref[:, columns] = (
            against_chunk(active_ref, buf, 1, i) + plain(low_d, ed_ref[:, columns])
        ).astype(bf16)


def feed_call(kernel, name, inputs, outputs, hidden, matmuls):
    table = [value for value in inputs if value.ndim == 4][0]
    rows, model = inputs[0].shape
    tile = 512
    chunks = table.shape[0]
    return pl.pallas_call(
        kernel,
        in_specs=[remote if value.ndim == 4 else held for value in inputs],
        out_specs=[held] * len(outputs),
        out_shape=[jax.ShapeDtypeStruct((rows, width), bf16) for width in outputs],
        scratch_shapes=[
            pltpu.VMEM((2, hidden // tile, chunks, model // chunks, tile), bf16),
            pltpu.SemaphoreType.DMA((2, hidden // tile)),
        ],
        compiler_params=pltpu.CompilerParams(vmem_limit_bytes=44 * 2**20),
        cost_estimate=pl.CostEstimate(
            flops=2 * matmuls * rows * model * hidden,
            bytes_accessed=4 * model * hidden,
            transcendentals=rows * hidden,
        ),
        name=name,
    )(*inputs)


def per_device(
    block_input,
    cotangent,
    doc_lengths,
    bank_choice,
    first_gain,
    first_shift,
    query_weight,
    query_bias,
    keyval_weight,
    value_bias,
    output_weight,
    output_bias,
    second_gain,
    second_shift,
    upward_weight,
    upward_bias,
    downward_weight,
    downward_bias,
    query_shrink,
    query_expand,
    keyval_shrink,
    keyval_expand,
    output_shrink,
    output_expand,
    upward_shrink,
    upward_expand,
    downward_shrink,
    downward_expand,
):
    section = lax.axis_index("section")
    data = lax.axis_index("dp")
    tensor = lax.axis_index("tensor")
    low_section = section == 0
    width = block_input.shape[2]
    rows = block_input.shape[1]
    ranks = lax.axis_size("tensor")
    span = rows * ranks
    head = value_bias.shape[1]
    local_q = query_bias.shape[1]
    local_f = upward_bias.shape[1]
    rank = query_expand.shape[2]
    banks = query_expand.shape[1]
    reach = WINDOW // span
    sides = [(0, 1), (1, 0)]

    def swap(value):
        return lax.ppermute(value, "section", sides)

    def by_layer(own, other):
        return jnp.where(low_section, own, other), jnp.where(low_section, other, own)

    def spread(block):
        parts = [block] + [around(block, "tensor", -j) for j in range(1, ranks)]
        return jnp.concatenate(parts, axis=0)

    def reduce_rows(partial):
        low = partial.astype(bf16)
        total = partial[:rows].astype(f32)
        for j in range(1, ranks):
            total = total + around(low[j * rows : (j + 1) * rows], "tensor", j).astype(f32)
        return total

    own_bank = lax.dynamic_index_in_dim(bank_choice, section, 0, keepdims=False)
    other_bank = lax.dynamic_index_in_dim(bank_choice, 1 - section, 0, keepdims=False)

    chips = lax.axis_size("dp") // 4
    both = ("section", "dp")
    every = ("section", "dp", "tensor")
    order = [
        side * 4 * chips + chip * 4 + near
        for chip in range(chips)
        for side in range(2)
        for near in range(4)
    ]
    order_all = [place * ranks + x for x in range(ranks) for place in order]

    def row_major(block):
        return with_layout_constraint(block, Layout(major_to_minor=(0, 1)))

    def gather(shard):
        table = lax.all_gather(row_major(shard), both, axis=0, tiled=True, axis_index_groups=[order])
        return row_major(table).reshape(chips, 2, -1, shard.shape[1])

    def gather_all(shard):
        table = lax.all_gather(
            row_major(shard), every, axis=0, tiled=True, axis_index_groups=[order_all]
        )
        return row_major(table).reshape(ranks, chips, 2, -1, shard.shape[1])

    def halves(shard):
        cut = shard.shape[1] // 2
        return shard[:, :cut], shard[:, cut:]

    keyval_half = jnp.where(tensor % 2 == 0, keyval_weight[0][:, :head], keyval_weight[0][:, head:])
    early_all = gather_all(
        jnp.concatenate([query_weight[0], row_major(output_weight[0].T), keyval_half], axis=1)
    )
    keyval_ws = [
        jnp.concatenate(
            [early_all[x, :, layer, :, 2 * local_q :].reshape(width, head) for x in range(2)], axis=1
        )
        for layer in range(2)
    ]

    vectors = jnp.concatenate(
        [
            first_gain,
            first_shift,
            jnp.zeros_like(value_bias),
            value_bias,
            output_bias,
            second_gain,
            second_shift,
            upward_bias,
            downward_bias,
        ],
        axis=1,
    )
    vector_sizes = [width, width, 2 * head, width, width, width, local_f, width]
    vector_layers = by_layer(vectors, swap(vectors))

    def chosen(table, bank, transpose):
        block = lax.dynamic_index_in_dim(table[0], bank, 0, keepdims=False)
        return block.T if transpose else block

    def pack(bank, parts):
        return jnp.concatenate([chosen(table, bank, flip) for table, flip in parts], axis=1)

    cut_parts = [(query_expand, False), (output_shrink, True)]
    whole_parts = [
        (query_shrink, True),
        (keyval_shrink, True),
        (keyval_expand, False),
        (output_expand, False),
        (upward_shrink, True),
        (upward_expand, False),
        (downward_shrink, True),
        (downward_expand, False),
    ]
    query_rows = jnp.broadcast_to(query_bias, (rank, local_q))

    def cut_pack(bank):
        return jnp.concatenate([pack(bank, cut_parts), query_rows], axis=1)

    shared_parts = [part for part in whole_parts if part[0] is not upward_expand and part[0] is not downward_shrink]
    split_parts = [(upward_expand, False), (downward_shrink, True)]
    shared_away = pack(other_bank, shared_parts)
    quarter = shared_away.shape[1] // ranks
    crossing = jnp.concatenate(
        [
            cut_pack(other_bank),
            lax.dynamic_slice_in_dim(shared_away, tensor * quarter, quarter, 1),
            pack(other_bank, split_parts),
        ],
        axis=1,
    )
    crossed_pack = swap(crossing)
    cut_width = 3 * local_q
    block = jnp.concatenate([cut_pack(own_bank), crossed_pack[:, : cut_width + quarter]], axis=1)
    blocks = jnp.stack([block] + [around(block, "tensor", j) for j in range(1, ranks)])
    blocks = [
        lax.dynamic_index_in_dim(blocks, (tensor - r) % ranks, 0, keepdims=False)
        for r in range(ranks)
    ]

    def joined(begin, size):
        return jnp.concatenate([block[:, begin : begin + size] for block in blocks], axis=1)

    cut_layers = [
        by_layer(joined(k * local_q, local_q), joined(cut_width + k * local_q, local_q))
        for k in range(3)
    ]
    eq_all, so_all, query_bias_all = cut_layers
    shared_layers = by_layer(pack(own_bank, shared_parts), joined(2 * cut_width, quarter))
    split_layers = by_layer(pack(own_bank, split_parts), crossed_pack[:, cut_width + quarter :])

    up_halves = halves(upward_weight[0])
    down_halves = halves(row_major(downward_weight[0].T))
    side = [jnp.concatenate([up_halves[h], down_halves[h]], axis=1) for h in range(2)]
    keep = jnp.where(low_section, side[0], side[1])
    gained = swap(jnp.where(low_section, side[1], side[0]))
    feed_tables = [gather(table) for table in by_layer(keep, gained)]

    def split(table, sizes):
        cuts = [0]
        for size in sizes:
            cuts.append(cuts[-1] + size)
        return [table[:, a:b] for a, b in zip(cuts[:-1], cuts[1:])]

    small = [
        [part.astype(f32) for part in split(vector_layers[layer], vector_sizes)]
        for layer in range(2)
    ]
    adapters = []
    feed_packs = []
    for layer in range(2):
        sq, skv, ekv, eo, su, ed = split(
            shared_layers[layer], [width, width, 2 * head, width, width, width]
        )
        eu, sd = split(split_layers[layer], [local_f, local_f])
        adapters.append((sq, skv, ekv, eo))
        feed_packs.append(jnp.concatenate([su, eu, sd, ed], axis=1))

    inside = jnp.arange(rows, dtype=jnp.int32)
    query_place = data * span + tensor * rows + inside
    key_place = jnp.concatenate(
        [
            (data - back) * span + (tensor + j) % ranks * rows + inside
            for j in range(ranks)
            for back in range(reach, -1, -1)
        ]
    )
    lengths = lax.dynamic_index_in_dim(doc_lengths, section, 0, keepdims=False)
    ends = jnp.cumsum(lengths)
    query_doc = jnp.sum((query_place[:, None] >= ends[None, :]).astype(jnp.int32), axis=1)
    key_doc = jnp.sum((key_place[:, None] >= ends[None, :]).astype(jnp.int32), axis=1)
    distance = query_place[:, None] - key_place[None, :]
    allowed = (
        (key_place[None, :] >= 0)
        & (distance >= 0)
        & (distance < WINDOW)
        & (query_doc[:, None] == key_doc[None, :])
    )
    bias = jnp.where(allowed, 0.0, masked_score).astype(bf16)

    def forward_attend(layer, hidden):
        gain1, shift1, kv_bias, out_bias = small[layer][:4]
        sq, skv, ekv, eo = adapters[layer]
        unit1, rsd1 = norm_parts(hidden)
        normed = (unit1 * gain1 + shift1).astype(bf16)
        low_kv = against(normed, skv).astype(bf16)
        keyval = (plain(normed, keyval_ws[layer]) + kv_bias + plain(low_kv, ekv)).astype(bf16)
        pieces = [along(keyval, "dp", back) for back in range(reach, 0, -1)] + [keyval]
        key_block = spread(jnp.concatenate(pieces, axis=0))
        queries, low_q = project_queries(
            layer, normed, early_all, query_bias_all[layer][:1].astype(f32), eq_all[layer], sq
        )
        probs, mixed, low_o, attended = attend(
            layer, queries, key_block, bias, early_all, so_all[layer], eo, head
        )
        middle = hidden + (attended + out_bias)
        return middle, (unit1, rsd1, normed, low_q, low_kv, queries, key_block, probs, mixed, low_o)

    def feed_inputs(layer, middle):
        gain2, shift2, up_bias = small[layer][4:7]
        unit2, rsd2 = norm_parts(middle)
        second = spread((unit2 * gain2 + shift2).astype(bf16))
        return unit2, rsd2, second, up_bias

    def feed_result(layer, middle, partial):
        return middle + (reduce_rows(partial) + small[layer][7])

    def tiles(block):
        return block.reshape(rank, -1, 128).transpose(1, 0, 2)

    def flat(block):
        return block.transpose(1, 0, 2).reshape(rank, -1)

    turn, near = data // 4, data % 4

    def padded(pile, multiple):
        lack = -pile.shape[0] % multiple
        if not lack:
            return pile
        return jnp.concatenate([pile, jnp.zeros((lack,) + pile.shape[1:], pile.dtype)], axis=0)

    def piled(*groups):
        piles = [
            padded(jnp.concatenate([tiles(part) for part in group], axis=0), ranks) for group in groups
        ]
        return jnp.concatenate(
            [pile.reshape((ranks, -1) + pile.shape[1:]) for pile in piles], axis=1
        ).astype(bf16)

    def at(block, index, axis):
        return lax.dynamic_index_in_dim(block, index, axis, keepdims=False)

    def summed_ranks(pile):
        total = at(pile, tensor, 0).astype(f32)
        for j in range(1, ranks):
            block = at(pile, (tensor + j) % ranks, 0)
            total = total + around(block, "tensor", j).astype(f32)
        return total

    def scattered_grads(layers):
        (shared, keyval, quartered, owned), other = layers
        groups = [other[0], other[1]] + [[part] for part in other[2]]
        early = summed_ranks(
            jnp.concatenate(
                [piled(*groups), piled(shared, *[[part] for part in quartered])], axis=1
            )
        )
        late = summed_ranks(piled(keyval))
        count = -(-sum(part.shape[1] // 128 for part in shared) // ranks)
        border = sum(-(-sum(part.shape[1] // 128 for part in group) // ranks) for group in groups)
        zero = early[border:]
        piles = [
            jnp.concatenate(
                [zero[:count], late, zero[count:]] + [tiles(part) for part in owned], axis=0
            ),
            jnp.concatenate([early[:border]] + [tiles(part) for part in other[3]], axis=0),
        ]
        pile = jnp.stack([padded(block.astype(bf16), lax.axis_size("dp")) for block in piles])
        pile = pile.reshape((2, 4, -1) + pile.shape[2:])
        mine = at(pile, near, 1).astype(f32)
        for k in range(1, 4):
            mine = mine + flipped(at(pile, near ^ k, 1), "dp", k).astype(f32)
        mine = mine.astype(bf16)
        parts = jnp.stack([mine] + [flipped(mine, "dp", 4 * k) for k in range(1, chips)])
        return sum(at(parts, turn ^ k, 0).astype(f32) for k in range(chips)).astype(bf16)

    def crossed(block, mask):
        return lax.ppermute(block, both, [(i, i ^ mask) for i in range(8 * chips)])

    def spread_grads(zero, one, shared, keyval, quartered, owned):
        own = jnp.where(low_section, zero, one)
        away = jnp.where(low_section, one, zero)
        dp_size = 4 * chips
        home = jnp.stack([own, flipped(own, "dp", 2)])
        guest = jnp.stack([crossed(away, dp_size), crossed(away, dp_size + 2)])
        home, guest = [
            jnp.where(near // 2 == 0, block, block[::-1]) for block in (home, guest)
        ]
        pair = jnp.where(
            low_section, jnp.stack([home, guest], axis=1), jnp.stack([guest, home], axis=1)
        )
        other = flipped(pair, "dp", 1)
        core = near % 2
        parts = jnp.stack(
            [jnp.where(core == 0, pair, other), jnp.where(core == 0, other, pair)], axis=1
        )
        pile = jnp.moveaxis(parts, 2, 0).reshape((2, -1) + parts.shape[4:])
        sizes = [[part.shape[1] // 128 for part in group] for group in (shared, keyval)]
        counts = [-(-sum(group) // ranks) for group in sizes]
        own = pile[:, : sum(counts)]
        parts = jnp.stack([own] + [around(own, "tensor", k) for k in range(1, ranks)])
        parts = [at(parts, (tensor - r) % ranks, 0) for r in range(ranks)]
        results = []

        def take(whole, begin, group):
            for count in group:
                results.append([flat(whole[m, begin : begin + count]) for m in range(2)])
                begin += count

        begin = 0
        for count, group in zip(counts, sizes):
            take(jnp.concatenate([part[:, begin : begin + count] for part in parts], axis=1), 0, group)
            begin += count
        rest = [part.shape[1] // 128 // ranks for part in quartered]
        take(pile, begin, rest + [part.shape[1] // 128 for part in owned])
        return results

    def feed_grads(layer, grad, unit2, rsd2, partial):
        return grad + norm_back(unit2, rsd2, reduce_rows(partial) * small[layer][4])

    def feed_adapters(second, branch, low_u, low_d, inner_u, inner_d, active, grad_up):
        shared = [across(inner_u, second), across(low_d, branch)]
        owned = [across(low_u, grad_up), across(inner_d, active)]
        return shared, owned

    def backward_attend(layer, kept, grad_middle):
        gain1 = small[layer][0]
        sq, skv, ekv, eo = adapters[layer]
        unit1, rsd1, normed, low_q, low_kv, queries, key_block, probs, mixed, low_o = kept
        branch = grad_middle.astype(bf16)
        grad_q, grad_block, inner_o, inner_q, partial = attend_back(
            layer, branch, early_all, so_all[layer], eo, probs, queries, key_block,
            eq_all[layer], sq, head,
        )
        count = (reach + 1) * rows
        blocks = grad_block[:count].astype(f32)
        for j in range(1, ranks):
            part = grad_block[j * count : (j + 1) * count]
            blocks = blocks + around(part, "tensor", j).astype(f32)
        own = blocks[reach * rows :]
        for back in range(1, reach + 1):
            begin = (reach - back) * rows
            own = own + along(blocks[begin : begin + rows].astype(bf16), "dp", -back).astype(f32)
        grad_kv = own.astype(bf16)
        inner_kv = against(grad_kv, ekv).astype(bf16)
        grad_normed = partial + against(grad_kv, keyval_ws[layer]) + plain(inner_kv, skv)
        grad_hidden = grad_middle + norm_back(unit1, rsd1, grad_normed * gain1)
        shared = [across(low_o, branch), across(inner_q, normed)]
        keyval = [across(inner_kv, normed), across(low_kv, grad_kv)]
        quartered = [across(low_q, grad_q), across(inner_o, mixed)]
        return grad_hidden, shared, keyval, quartered

    fresh = lax.dynamic_index_in_dim(block_input, section, 0, keepdims=False).astype(f32)
    given = lax.dynamic_index_in_dim(cotangent, section, 0, keepdims=False).astype(f32)
    branch_one = spread(given.astype(bf16))
    fresh, branch_one = lax.optimization_barrier((fresh, branch_one))

    middle_zero, kept_zero = forward_attend(0, fresh)
    unit_zero, rsd_zero, second_zero, up_bias = feed_inputs(0, middle_zero)
    active_zero, slope_zero, low_u_zero, low_d_zero, partial = feed_call(
        feed_kernel,
        "feed",
        (second_zero, feed_tables[0], up_bias, feed_packs[0]),
        (local_f, local_f, rank, rank, width),
        local_f,
        2,
    )
    passed = feed_result(0, middle_zero, partial).astype(bf16)

    middle_one, kept_one = forward_attend(1, passed.astype(f32))
    unit_one, rsd_one, second_one, up_bias = feed_inputs(1, middle_one)
    active, low_u, low_d, partial, grad_up, inner_d, inner_u, partial_back = feed_call(
        feed_both_kernel,
        "feed_both",
        (second_one, branch_one, feed_tables[1], up_bias, feed_packs[1]),
        (local_f, rank, rank, width, local_f, rank, rank, width),
        local_f,
        4,
    )
    grad_middle = feed_grads(1, given, unit_one, rsd_one, partial_back)
    shared, owned = feed_adapters(
        second_one, branch_one, low_u, low_d, inner_u, inner_d, active, grad_up
    )
    grad_one, more, keyval, quartered = backward_attend(1, kept_one, grad_middle)
    layer_one = (shared + more, keyval, quartered, owned)
    partial, _ = lax.optimization_barrier((partial, grad_middle))
    final = feed_result(1, middle_one, partial).astype(bf16)

    branch_zero = spread(grad_one.astype(bf16))
    grad_up, inner_d, inner_u, partial_back = feed_call(
        feed_back_kernel,
        "feed_back",
        (branch_zero, feed_tables[0], slope_zero, feed_packs[0]),
        (local_f, rank, rank, width),
        local_f,
        2,
    )
    grad_middle_zero = feed_grads(0, grad_one, unit_zero, rsd_zero, partial_back)
    shared, owned = feed_adapters(
        second_zero,
        branch_zero,
        low_u_zero,
        low_d_zero,
        inner_u,
        inner_d,
        active_zero,
        grad_up,
    )
    grad_zero, more, keyval, quartered = backward_attend(0, kept_zero, grad_middle_zero)
    layer_zero = (shared + more, keyval, quartered, owned)
    mine = scattered_grads([layer_zero, layer_one])
    grads = spread_grads(mine[0], mine[1], *layer_zero)

    def both_micros(zero, one, kind):
        own = jnp.where(low_section, zero, one)
        received = swap(jnp.where(low_section, one, zero).astype(bf16)).astype(kind)
        return jnp.where(low_section, jnp.stack([own, received]), jnp.stack([received, own]))

    passed, final, _ = lax.optimization_barrier((passed, final, grad_middle_zero))
    section_outputs = both_micros(passed, final, bf16)
    input_grads = both_micros(grad_zero, grad_one, f32)
    onehot = (bank_choice[:, None] == jnp.arange(banks)[None, :]).astype(f32)

    def placed(pair, transpose):
        out = sum(
            onehot[m][:, None, None] * pair[m].astype(f32)[None] for m in range(2)
        )
        return (out.transpose(0, 2, 1) if transpose else out)[None]

    (
        up_shrink_grad,
        down_expand_grad,
        out_expand_grad,
        q_shrink_grad,
        kv_shrink_grad,
        kv_expand_grad,
        q_expand_grad,
        out_shrink_grad,
        up_expand_grad,
        down_shrink_grad,
    ) = grads
    return (
        section_outputs[None],
        input_grads[None],
        placed(q_shrink_grad, True),
        placed(q_expand_grad, False),
        placed(kv_shrink_grad, True),
        placed(kv_expand_grad, False),
        placed(out_shrink_grad, True),
        placed(out_expand_grad, False),
        placed(up_shrink_grad, True),
        placed(up_expand_grad, False),
        placed(down_shrink_grad, True),
        placed(down_expand_grad, False),
    )


def solution(mesh):
    return jax.shard_map(
        per_device,
        mesh=mesh,
        in_specs=(
            P(None, ("dp", "tensor"), None),
            P(None, ("dp", "tensor"), None),
            P(),
            P(),
            P("section", None),
            P("section", None),
            P("section", "dp", "tensor"),
            P("section", "tensor"),
            P("section", "dp", None),
            P("section", None),
            P("section", "tensor", "dp"),
            P("section", None),
            P("section", None),
            P("section", None),
            P("section", "dp", "tensor"),
            P("section", "tensor"),
            P("section", "tensor", "dp"),
            P("section", None),
            P("section", None, None, None),
            P("section", None, None, "tensor"),
            P("section", None, None, None),
            P("section", None, None, None),
            P("section", None, "tensor", None),
            P("section", None, None, None),
            P("section", None, None, None),
            P("section", None, None, "tensor"),
            P("section", None, "tensor", None),
            P("section", None, None, None),
        ),
        out_specs=(
            P("section", None, ("dp", "tensor"), None),
            P("section", None, ("dp", "tensor"), None),
            P("section", None, None, None),
            P("section", None, None, "tensor"),
            P("section", None, None, None),
            P("section", None, None, None),
            P("section", None, "tensor", None),
            P("section", None, None, None),
            P("section", None, None, None),
            P("section", None, None, "tensor"),
            P("section", None, "tensor", None),
            P("section", None, None, None),
        ),
        check_vma=False,
    )
```

```python
import math

import jax
import jax.numpy as jnp
from jax import lax
from jax.experimental import pallas as pl
from jax.experimental.layout import Layout, with_layout_constraint
from jax.experimental.pallas import tpu as pltpu
from jax.sharding import PartitionSpec as P

WINDOW = 1024
epsilon = 1e-05
masked_score = -1e30
bf16 = jnp.bfloat16
f32 = jnp.float32


def plain(left, right):
    return jnp.dot(left, right, preferred_element_type=f32)


def against(left, right):
    return lax.dot_general(left, right, (((1,), (1,)), ((), ())), preferred_element_type=f32)


def across(left, right):
    return lax.dot_general(left, right, (((0,), (0,)), ((), ())), preferred_element_type=f32)


def around(block, axis, distance):
    size = lax.axis_size(axis)
    return lax.ppermute(block, axis, [(i, (i + distance) % size) for i in range(size)])


def along(block, axis, distance):
    size = lax.axis_size(axis)
    route = [(i, i + distance) for i in range(size) if 0 <= i + distance < size]
    return lax.ppermute(block, axis, route)


def flipped(block, axis, bit):
    size = lax.axis_size(axis)
    return lax.ppermute(block, axis, [(i, i ^ bit) for i in range(size)])


def pick(table, index, size=1):
    return lax.dynamic_slice_in_dim(table, index, size, 0)


def norm_parts(value):
    centred = value - jnp.mean(value, axis=-1, keepdims=True)
    spread = lax.rsqrt(jnp.mean(centred * centred, axis=-1, keepdims=True) + epsilon)
    return centred * spread, spread


def norm_back(unit, spread, scaled):
    inner = jnp.mean(scaled * unit, axis=-1, keepdims=True)
    return spread * (scaled - jnp.mean(scaled, axis=-1, keepdims=True) - unit * inner)


def gelu_parts(value):
    rate = math.sqrt(2.0 / math.pi)
    square = value * value
    bend = jnp.tanh(rate * (value + 0.044715 * value * square))
    rising = 0.5 * (1.0 + bend)
    slope = rising + 0.5 * value * (1.0 - bend * bend) * (rate * (1.0 + 3 * 0.044715 * square))
    return value * rising, slope


def side_blocks(query_ref, group, head):
    begin = group * 4 * head
    return jnp.concatenate(
        [query_ref[:, begin + h * head : begin + (h + 1) * head] for h in range(4)], axis=0
    )


def put_blocks(out_ref, value, group, head):
    rows = value.shape[0] // 4
    for h in range(4):
        begin = (group * 4 + h) * head
        out_ref[:, begin : begin + head] = value[h * rows : (h + 1) * rows]


def table_copies(table_ref, buf, sem, layer, begin):
    ranks, chunks, _, width = buf.shape
    return [
        pltpu.make_async_copy(
            table_ref.at[x, y, layer, :, pl.ds(begin, width)], buf.at[x, y], sem.at[x, y]
        )
        for x in range(ranks)
        for y in range(chunks)
    ]


def query_kernel(layer, normed_ref, table_ref, bias_ref, eq_ref, sq_ref, out_ref, low_ref, buf, sem):
    ranks, chunks, rows, width = buf.shape
    copies = table_copies(table_ref, buf, sem, layer, 0)
    for copy in copies:
        copy.start()
    normed = normed_ref[...]
    low = against(normed, sq_ref[...]).astype(bf16)
    low_ref[...] = low
    for x in range(ranks):
        columns = pl.ds(x * width, width)
        total = bias_ref[:, columns] + plain(low, eq_ref[:, columns])
        for y in range(chunks):
            copies[x * chunks + y].wait()
            total = total + plain(normed[:, y * rows : (y + 1) * rows], buf[x, y])
        out_ref[:, columns] = total.astype(bf16)


def table_scratch(table, width):
    ranks, chunks, _, rows, _ = table.shape
    return [
        pltpu.VMEM((ranks, chunks, rows, width), bf16),
        pltpu.SemaphoreType.DMA((ranks, chunks)),
    ]


held = pl.BlockSpec(memory_space=pltpu.VMEM)
remote = pl.BlockSpec(memory_space=pl.ANY)


def project_queries(layer, normed, table, bias, eq, sq):
    rows, model = normed.shape
    rank = sq.shape[0]
    width = model // table.shape[0]
    return pl.pallas_call(
        lambda *refs: query_kernel(layer, *refs),
        in_specs=[held, remote, held, held, held],
        out_specs=[held] * 2,
        out_shape=[
            jax.ShapeDtypeStruct((rows, model), bf16),
            jax.ShapeDtypeStruct((rows, rank), bf16),
        ],
        scratch_shapes=table_scratch(table, width),
        compiler_params=pltpu.CompilerParams(vmem_limit_bytes=28 * 2**20),
        cost_estimate=pl.CostEstimate(
            flops=8 * rows * model * model, bytes_accessed=2 * model * model, transcendentals=0
        ),
        name="project_queries",
    )(normed, table, bias, eq, sq)


def attend_kernel(
    layer, head, query_ref, keyval_ref, bias_ref, table_ref, so_ref, eo_ref,
    prob_ref, mixed_ref, low_ref, out_ref, buf, sem,
):
    ranks, chunks, rows, width = buf.shape
    copies = table_copies(table_ref, buf, sem, layer, width)
    for copy in copies:
        copy.start()
    scale = 1.0 / math.sqrt(head)
    bias = jnp.concatenate([bias_ref[...].astype(f32)] * 4, axis=0)
    for g in range(prob_ref.shape[0]):
        queries = side_blocks(query_ref, g, head)
        scores = against(queries, keyval_ref[:, :head]) * scale + bias
        lifted = jnp.exp(scores - jnp.max(scores, axis=-1, keepdims=True))
        probs = (lifted * (1.0 / jnp.sum(lifted, axis=-1, keepdims=True))).astype(bf16)
        prob_ref[g] = probs
        put_blocks(mixed_ref, plain(probs, keyval_ref[:, head:]).astype(bf16), g, head)
    mixed = mixed_ref[...]
    low = against(mixed, so_ref[...]).astype(bf16)
    low_ref[...] = low
    for copy in copies:
        copy.wait()
    for y in range(chunks):
        columns = pl.ds(y * rows, rows)
        total = plain(low, eo_ref[:, columns])
        for x in range(ranks):
            total = total + against(mixed[:, x * width : (x + 1) * width], buf[x, y])
        out_ref[:, columns] = total


def attend(layer, queries, key_block, bias, table, so, eo, head):
    rows, model = queries.shape
    keys = key_block.shape[0]
    groups = model // head // 4
    rank = so.shape[0]
    return pl.pallas_call(
        lambda *refs: attend_kernel(layer, head, *refs),
        in_specs=[held, held, held, remote, held, held],
        out_specs=[held] * 4,
        out_shape=[
            jax.ShapeDtypeStruct((groups, 4 * rows, keys), bf16),
            jax.ShapeDtypeStruct((rows, model), bf16),
            jax.ShapeDtypeStruct((rows, rank), bf16),
            jax.ShapeDtypeStruct((rows, model), f32),
        ],
        scratch_shapes=table_scratch(table, model // table.shape[0]),
        compiler_params=pltpu.CompilerParams(vmem_limit_bytes=36 * 2**20),
        cost_estimate=pl.CostEstimate(
            flops=4 * rows * model * (keys + 2 * model),
            bytes_accessed=2 * model * model,
            transcendentals=groups * 4 * rows * keys,
        ),
        name="attend",
    )(queries, key_block, bias, table, so, eo)


def attend_back_kernel(
    layer, head, branch_ref, table_ref, so_ref, eo_ref, prob_ref, query_ref, keyval_ref, eq_ref, sq_ref,
    dq_ref, dkv_ref, inner_o_ref, inner_q_ref, part_ref,
    out_buf, out_sem, query_buf, query_sem, mixed_buf, key_sum, value_sum,
):
    ranks, chunks, rows, width = out_buf.shape
    out_copies = table_copies(table_ref, out_buf, out_sem, layer, width)
    query_copies = table_copies(table_ref, query_buf, query_sem, layer, 0)
    for copy in out_copies + query_copies:
        copy.start()
    scale = 1.0 / math.sqrt(head)
    branch = branch_ref[...]
    inner_o = against(branch, eo_ref[...]).astype(bf16)
    inner_o_ref[...] = inner_o
    for g in range(prob_ref.shape[0]):
        columns = pl.ds(g * width, width)
        total = plain(inner_o, so_ref[:, columns])
        for y in range(chunks):
            out_copies[g * chunks + y].wait()
            total = total + plain(branch[:, y * rows : (y + 1) * rows], out_buf[g, y])
        mixed_buf[:, columns] = total.astype(bf16)
        grad = side_blocks(mixed_buf, g, head)
        low_probs = prob_ref[g]
        probs = low_probs.astype(f32)
        grad_probs = against(grad, keyval_ref[:, head:])
        delta = jnp.sum(grad_probs * probs, axis=-1, keepdims=True)
        delta = delta / jnp.sum(probs, axis=-1, keepdims=True)
        grad_scores = (probs * (grad_probs - delta)).astype(bf16)
        put_blocks(dq_ref, (plain(grad_scores, keyval_ref[:, :head]) * scale).astype(bf16), g, head)
        keys = across(grad_scores, side_blocks(query_ref, g, head))
        values = across(low_probs, grad)
        if g == 0:
            key_sum[...] = keys
            value_sum[...] = values
        else:
            key_sum[...] += keys
            value_sum[...] += values
    dkv_ref[:, :head] = (key_sum[...] * scale).astype(bf16)
    dkv_ref[:, head:] = value_sum[...].astype(bf16)
    grad_q = dq_ref[...]
    inner_q = against(grad_q, eq_ref[...]).astype(bf16)
    inner_q_ref[...] = inner_q
    for copy in query_copies:
        copy.wait()
    for y in range(chunks):
        columns = pl.ds(y * rows, rows)
        total = plain(inner_q, sq_ref[:, columns])
        for x in range(ranks):
            total = total + against(grad_q[:, x * width : (x + 1) * width], query_buf[x, y])
        part_ref[:, columns] = total


def attend_back(layer, branch, table, so, eo, probs, queries, key_block, eq, sq, head):
    rows, model = queries.shape
    keys = key_block.shape[0]
    groups = probs.shape[0]
    rank = so.shape[0]
    width = model // table.shape[0]
    return pl.pallas_call(
        lambda *refs: attend_back_kernel(layer, head, *refs),
        in_specs=[held, remote] + [held] * 7,
        out_specs=[held] * 5,
        out_shape=[
            jax.ShapeDtypeStruct((rows, model), bf16),
            jax.ShapeDtypeStruct((keys, 2 * head), bf16),
            jax.ShapeDtypeStruct((rows, rank), bf16),
            jax.ShapeDtypeStruct((rows, rank), bf16),
            jax.ShapeDtypeStruct((rows, model), f32),
        ],
        scratch_shapes=table_scratch(table, width)
        + table_scratch(table, width)
        + [
            pltpu.VMEM((rows, model), bf16),
            pltpu.VMEM((keys, head), f32),
            pltpu.VMEM((keys, head), f32),
        ],
        compiler_params=pltpu.CompilerParams(vmem_limit_bytes=44 * 2**20),
        cost_estimate=pl.CostEstimate(
            flops=8 * rows * model * (keys + 2 * model),
            bytes_accessed=4 * model * model + 4 * groups * 4 * rows * keys,
            transcendentals=0,
        ),
        name="attend_back",
    )(branch, table, so, eo, probs, queries, key_block, eq, sq)


def feed_copies(table_ref, buf, sems):
    _, count, chunks, rows, tile = buf.shape
    half = count // 2 * tile
    copies = []
    for j in range(count):
        pair = []
        for k in range(2):
            columns = pl.ds(j * tile % half + k * half, tile)
            pair.append(
                pltpu.make_async_copy(
                    table_ref.at[:, j * tile // half, :, columns], buf.at[k, j], sems.at[k, j]
                )
            )
        copies.append(pair)
    return copies


def plain_chunks(left, buf, k, j):
    rows = buf.shape[3]
    return sum(plain(left[:, i * rows : (i + 1) * rows], buf[k, j, i]) for i in range(buf.shape[2]))


def against_chunk(left_ref, buf, k, i):
    tile = buf.shape[4]
    return sum(
        against(left_ref[:, j * tile : (j + 1) * tile], buf[k, j, i]) for j in range(buf.shape[1])
    )


def own_copies(sources, buffers, sems):
    copies = [
        pltpu.make_async_copy(source, buffer, sems.at[i])
        for i, (source, buffer) in enumerate(zip(sources, buffers))
    ]
    for copy in copies:
        copy.start()
    return copies


def feed_pack(pack_ref, model, hidden):
    cuts = [0, model, model + hidden, model + 2 * hidden, 2 * model + 2 * hidden]
    return [pack_ref.at[:, a:b] for a, b in zip(cuts[:-1], cuts[1:])]


def feed_kernel(
    second_ref, table_ref, bias_ref, pack_ref,
    active_ref, slope_ref, low_u_ref, low_d_ref, out_ref, buf, sems, pack_buf, own_sems,
):
    _, count, chunks, rows, tile = buf.shape
    su_ref, eu_ref, sd_ref, ed_ref = feed_pack(pack_buf, chunks * rows, count * tile)
    copies = feed_copies(table_ref, buf, sems)
    own = own_copies([pack_ref], [pack_buf], own_sems)
    for up, _ in copies:
        up.start()
    for _, down in copies:
        down.start()
    second = second_ref[...]
    own[0].wait()
    low_u = against(second, su_ref[...]).astype(bf16)
    low_u_ref[...] = low_u
    for j in range(count):
        columns = pl.ds(j * tile, tile)
        copies[j][0].wait()
        upward = plain_chunks(second, buf, 0, j)
        upward = upward + plain(low_u, eu_ref[:, columns]) + bias_ref[:, columns]
        active, slope = gelu_parts(upward)
        active_ref[:, columns] = active.astype(bf16)
        slope_ref[:, columns] = slope.astype(bf16)
    low_d = against(active_ref[...], sd_ref[...]).astype(bf16)
    low_d_ref[...] = low_d
    for _, down in copies:
        down.wait()
    for i in range(chunks):
        columns = pl.ds(i * rows, rows)
        out_ref[:, columns] = (
            against_chunk(active_ref, buf, 1, i) + plain(low_d, ed_ref[:, columns])
        ).astype(bf16)


def feed_back_kernel(
    branch_ref, table_ref, slope_ref, pack_ref,
    grad_up_ref, inner_d_ref, inner_u_ref, out_ref, buf, sems, pack_buf, slope_buf, own_sems,
):
    _, count, chunks, rows, tile = buf.shape
    su_ref, eu_ref, sd_ref, ed_ref = feed_pack(pack_buf, chunks * rows, count * tile)
    copies = feed_copies(table_ref, buf, sems)
    own = own_copies([pack_ref, slope_ref], [pack_buf, slope_buf], own_sems)
    for _, down in copies:
        down.start()
    for up, _ in copies:
        up.start()
    branch = branch_ref[...]
    own[0].wait()
    inner_d = against(branch, ed_ref[...]).astype(bf16)
    inner_d_ref[...] = inner_d
    own[1].wait()
    for j in range(count):
        columns = pl.ds(j * tile, tile)
        copies[j][1].wait()
        grad = plain_chunks(branch, buf, 1, j) + plain(inner_d, sd_ref[:, columns])
        grad_up_ref[:, columns] = (grad * slope_buf[:, columns].astype(f32)).astype(bf16)
    inner_u = against(grad_up_ref[...], eu_ref[...]).astype(bf16)
    inner_u_ref[...] = inner_u
    for up, _ in copies:
        up.wait()
    for i in range(chunks):
        columns = pl.ds(i * rows, rows)
        out_ref[:, columns] = (
            against_chunk(grad_up_ref, buf, 0, i) + plain(inner_u, su_ref[:, columns])
        ).astype(bf16)


def feed_both_kernel(
    second_ref, branch_ref, table_ref, bias_ref, pack_ref,
    active_ref, low_u_ref, low_d_ref, out_ref, grad_up_ref, inner_d_ref, inner_u_ref, back_ref,
    buf, sems, pack_buf, branch_buf, own_sems,
):
    _, count, chunks, rows, tile = buf.shape
    su_ref, eu_ref, sd_ref, ed_ref = feed_pack(pack_buf, chunks * rows, count * tile)
    copies = feed_copies(table_ref, buf, sems)
    own = own_copies([pack_ref, branch_ref], [pack_buf, branch_buf], own_sems)
    for up, down in copies:
        up.start()
        down.start()
    second = second_ref[...]
    for copy in own:
        copy.wait()
    branch = branch_buf[...]
    low_u = against(second, su_ref[...]).astype(bf16)
    low_u_ref[...] = low_u
    inner_d = against(branch, ed_ref[...]).astype(bf16)
    inner_d_ref[...] = inner_d
    for j in range(count):
        columns = pl.ds(j * tile, tile)
        copies[j][0].wait()
        upward = plain_chunks(second, buf, 0, j)
        upward = upward + plain(low_u, eu_ref[:, columns]) + bias_ref[:, columns]
        active, slope = gelu_parts(upward)
        active_ref[:, columns] = active.astype(bf16)
        copies[j][1].wait()
        grad = plain_chunks(branch, buf, 1, j) + plain(inner_d, sd_ref[:, columns])
        grad_up_ref[:, columns] = (grad * slope).astype(bf16)
    inner_u = against(grad_up_ref[...], eu_ref[...]).astype(bf16)
    inner_u_ref[...] = inner_u
    low_d = against(active_ref[...], sd_ref[...]).astype(bf16)
    low_d_ref[...] = low_d
    for i in range(chunks):
        columns = pl.ds(i * rows, rows)
        back_ref[:, columns] = (
            against_chunk(grad_up_ref, buf, 0, i) + plain(inner_u, su_ref[:, columns])
        ).astype(bf16)
        out_ref[:, columns] = (
            against_chunk(active_ref, buf, 1, i) + plain(low_d, ed_ref[:, columns])
        ).astype(bf16)


def feed_call(kernel, name, inputs, copied, outputs, hidden, matmuls):
    table = [value for value in inputs if value.ndim == 4][0]
    rows, model = inputs[0].shape
    tile = 512
    chunks = table.shape[0]
    return pl.pallas_call(
        kernel,
        in_specs=[
            remote if value.ndim == 4 or i in copied else held for i, value in enumerate(inputs)
        ],
        out_specs=[held] * len(outputs),
        out_shape=[jax.ShapeDtypeStruct((rows, width), bf16) for width in outputs],
        scratch_shapes=[
            pltpu.VMEM((2, hidden // tile, chunks, model // chunks, tile), bf16),
            pltpu.SemaphoreType.DMA((2, hidden // tile)),
        ]
        + [pltpu.VMEM(inputs[i].shape, bf16) for i in copied]
        + [pltpu.SemaphoreType.DMA((len(copied),))],
        compiler_params=pltpu.CompilerParams(vmem_limit_bytes=44 * 2**20),
        cost_estimate=pl.CostEstimate(
            flops=2 * matmuls * rows * model * hidden,
            bytes_accessed=4 * model * hidden,
            transcendentals=rows * hidden,
        ),
        name=name,
    )(*inputs)


def per_device(
    block_input,
    cotangent,
    doc_lengths,
    bank_choice,
    first_gain,
    first_shift,
    query_weight,
    query_bias,
    keyval_weight,
    value_bias,
    output_weight,
    output_bias,
    second_gain,
    second_shift,
    upward_weight,
    upward_bias,
    downward_weight,
    downward_bias,
    query_shrink,
    query_expand,
    keyval_shrink,
    keyval_expand,
    output_shrink,
    output_expand,
    upward_shrink,
    upward_expand,
    downward_shrink,
    downward_expand,
):
    section = lax.axis_index("section")
    data = lax.axis_index("dp")
    tensor = lax.axis_index("tensor")
    low_section = section == 0
    width = block_input.shape[2]
    rows = block_input.shape[1]
    ranks = lax.axis_size("tensor")
    span = rows * ranks
    head = value_bias.shape[1]
    local_q = query_bias.shape[1]
    local_f = upward_bias.shape[1]
    rank = query_expand.shape[2]
    banks = query_expand.shape[1]
    reach = WINDOW // span
    sides = [(0, 1), (1, 0)]

    def swap(value):
        return lax.ppermute(value, "section", sides)

    def by_layer(own, other):
        return jnp.where(low_section, own, other), jnp.where(low_section, other, own)

    def spread(block):
        parts = [block] + [around(block, "tensor", -j) for j in range(1, ranks)]
        return jnp.concatenate(parts, axis=0)

    def reduce_rows(partial):
        low = partial.astype(bf16)
        total = partial[:rows].astype(f32)
        for j in range(1, ranks):
            total = total + around(low[j * rows : (j + 1) * rows], "tensor", j).astype(f32)
        return total

    own_bank = lax.dynamic_index_in_dim(bank_choice, section, 0, keepdims=False)
    other_bank = lax.dynamic_index_in_dim(bank_choice, 1 - section, 0, keepdims=False)

    chips = lax.axis_size("dp") // 4
    both = ("section", "dp")
    every = ("section", "dp", "tensor")
    order = [
        side * 4 * chips + chip * 4 + near
        for chip in range(chips)
        for side in range(2)
        for near in range(4)
    ]
    order_all = [place * ranks + x for x in range(ranks) for place in order]

    def row_major(block):
        return with_layout_constraint(block, Layout(major_to_minor=(0, 1)))

    def gather(shard):
        table = lax.all_gather(row_major(shard), both, axis=0, tiled=True, axis_index_groups=[order])
        return row_major(table).reshape(chips, 2, -1, shard.shape[1])

    def gather_all(shard):
        table = lax.all_gather(
            row_major(shard), every, axis=0, tiled=True, axis_index_groups=[order_all]
        )
        return row_major(table).reshape(ranks, chips, 2, -1, shard.shape[1])

    def halves(shard):
        cut = shard.shape[1] // 2
        return shard[:, :cut], shard[:, cut:]

    early_all = gather_all(
        jnp.concatenate([query_weight[0], row_major(output_weight[0].T)], axis=1)
    )

    def crossed(block, mask):
        return lax.ppermute(block, both, [(i, i ^ mask) for i in range(8 * chips)])

    shard = keyval_weight[0]
    pairs = by_layer(
        jnp.stack([shard, crossed(shard, 2)]),
        jnp.stack([crossed(shard, 4 * chips), crossed(shard, 4 * chips + 2)]),
    )
    quads = jnp.stack(pairs, axis=1)
    quads = jnp.stack([quads] + [crossed(quads, 4 * k) for k in range(1, chips)])
    blocks = jnp.stack([quads, crossed(quads, 1)], axis=2)
    blocks = blocks.reshape((4 * chips, 2) + shard.shape)
    keyval_all = jnp.take(blocks, jnp.arange(4 * chips, dtype=jnp.int32) ^ data, axis=0, mode="clip")
    keyval_ws = [keyval_all[:, layer].reshape(width, 2 * head) for layer in range(2)]

    vectors = jnp.concatenate(
        [
            first_gain,
            first_shift,
            jnp.zeros_like(value_bias),
            value_bias,
            output_bias,
            second_gain,
            second_shift,
            upward_bias,
            downward_bias,
        ],
        axis=1,
    )
    vector_sizes = [width, width, 2 * head, width, width, width, local_f, width]
    vector_layers = by_layer(vectors, swap(vectors))

    def chosen(table, bank, transpose):
        block = lax.dynamic_index_in_dim(table[0], bank, 0, keepdims=False)
        return block.T if transpose else block

    def pack(bank, parts):
        return jnp.concatenate([chosen(table, bank, flip) for table, flip in parts], axis=1)

    cut_parts = [(query_expand, False), (output_shrink, True)]
    whole_parts = [
        (query_shrink, True),
        (keyval_shrink, True),
        (keyval_expand, False),
        (output_expand, False),
        (upward_shrink, True),
        (upward_expand, False),
        (downward_shrink, True),
        (downward_expand, False),
    ]
    query_rows = jnp.broadcast_to(query_bias, (rank, local_q))

    def cut_pack(bank):
        return jnp.concatenate([pack(bank, cut_parts), query_rows], axis=1)

    shared_parts = [part for part in whole_parts if part[0] is not upward_expand and part[0] is not downward_shrink]
    split_parts = [(upward_expand, False), (downward_shrink, True)]
    shared_away = pack(other_bank, shared_parts)
    quarter = shared_away.shape[1] // ranks
    crossing = jnp.concatenate(
        [
            cut_pack(other_bank),
            lax.dynamic_slice_in_dim(shared_away, tensor * quarter, quarter, 1),
            pack(other_bank, split_parts),
        ],
        axis=1,
    )
    crossed_pack = swap(crossing)
    cut_width = 3 * local_q
    block = jnp.concatenate([cut_pack(own_bank), crossed_pack[:, : cut_width + quarter]], axis=1)
    blocks = jnp.stack([block] + [around(block, "tensor", j) for j in range(1, ranks)])
    blocks = [
        lax.dynamic_index_in_dim(blocks, (tensor - r) % ranks, 0, keepdims=False)
        for r in range(ranks)
    ]

    def joined(begin, size):
        return jnp.concatenate([block[:, begin : begin + size] for block in blocks], axis=1)

    cut_layers = [
        by_layer(joined(k * local_q, local_q), joined(cut_width + k * local_q, local_q))
        for k in range(3)
    ]
    eq_all, so_all, query_bias_all = cut_layers
    shared_layers = by_layer(pack(own_bank, shared_parts), joined(2 * cut_width, quarter))
    split_layers = by_layer(pack(own_bank, split_parts), crossed_pack[:, cut_width + quarter :])

    up_halves = halves(upward_weight[0])
    down_halves = halves(row_major(downward_weight[0].T))
    side = [jnp.concatenate([up_halves[h], down_halves[h]], axis=1) for h in range(2)]
    keep = jnp.where(low_section, side[0], side[1])
    gained = swap(jnp.where(low_section, side[1], side[0]))
    feed_tables = [gather(table) for table in by_layer(keep, gained)]

    def split(table, sizes):
        cuts = [0]
        for size in sizes:
            cuts.append(cuts[-1] + size)
        return [table[:, a:b] for a, b in zip(cuts[:-1], cuts[1:])]

    small = [
        [part.astype(f32) for part in split(vector_layers[layer], vector_sizes)]
        for layer in range(2)
    ]
    adapters = []
    feed_packs = []
    for layer in range(2):
        sq, skv, ekv, eo, su, ed = split(
            shared_layers[layer], [width, width, 2 * head, width, width, width]
        )
        eu, sd = split(split_layers[layer], [local_f, local_f])
        adapters.append((sq, skv, ekv, eo))
        feed_packs.append(jnp.concatenate([su, eu, sd, ed], axis=1))

    inside = jnp.arange(rows, dtype=jnp.int32)
    query_place = data * span + tensor * rows + inside
    key_place = jnp.concatenate(
        [
            (data - back) * span + (tensor + j) % ranks * rows + inside
            for j in range(ranks)
            for back in range(reach, -1, -1)
        ]
    )
    lengths = lax.dynamic_index_in_dim(doc_lengths, section, 0, keepdims=False)
    ends = jnp.cumsum(lengths)
    query_doc = jnp.sum((query_place[:, None] >= ends[None, :]).astype(jnp.int32), axis=1)
    key_doc = jnp.sum((key_place[:, None] >= ends[None, :]).astype(jnp.int32), axis=1)
    distance = query_place[:, None] - key_place[None, :]
    allowed = (
        (key_place[None, :] >= 0)
        & (distance >= 0)
        & (distance < WINDOW)
        & (query_doc[:, None] == key_doc[None, :])
    )
    bias = jnp.where(allowed, 0.0, masked_score).astype(bf16)

    def forward_attend(layer, hidden):
        gain1, shift1, kv_bias, out_bias = small[layer][:4]
        sq, skv, ekv, eo = adapters[layer]
        unit1, rsd1 = norm_parts(hidden)
        normed = (unit1 * gain1 + shift1).astype(bf16)
        low_kv = against(normed, skv).astype(bf16)
        keyval = (plain(normed, keyval_ws[layer]) + kv_bias + plain(low_kv, ekv)).astype(bf16)
        pieces = [along(keyval, "dp", back) for back in range(reach, 0, -1)] + [keyval]
        key_block = spread(jnp.concatenate(pieces, axis=0))
        queries, low_q = project_queries(
            layer, normed, early_all, query_bias_all[layer][:1].astype(f32), eq_all[layer], sq
        )
        probs, mixed, low_o, attended = attend(
            layer, queries, key_block, bias, early_all, so_all[layer], eo, head
        )
        middle = hidden + (attended + out_bias)
        return middle, (unit1, rsd1, normed, low_q, low_kv, queries, key_block, probs, mixed, low_o)

    def feed_inputs(layer, middle):
        gain2, shift2, up_bias = small[layer][4:7]
        unit2, rsd2 = norm_parts(middle)
        second = spread((unit2 * gain2 + shift2).astype(bf16))
        return unit2, rsd2, second, up_bias

    def feed_result(layer, middle, partial):
        return middle + (reduce_rows(partial) + small[layer][7])

    def tiles(block):
        return block.reshape(rank, -1, 128).transpose(1, 0, 2)

    def flat(block):
        return block.transpose(1, 0, 2).reshape(rank, -1)

    turn, near = data // 4, data % 4

    def padded(pile, multiple):
        lack = -pile.shape[0] % multiple
        if not lack:
            return pile
        return jnp.concatenate([pile, jnp.zeros((lack,) + pile.shape[1:], pile.dtype)], axis=0)

    def piled(shared, quartered):
        pile = padded(jnp.concatenate([tiles(part) for part in shared], axis=0), ranks)
        return jnp.concatenate(
            [block.reshape((ranks, -1) + block.shape[1:]) for block in [pile] + [tiles(part) for part in quartered]],
            axis=1,
        ).astype(bf16)

    def owned_pile(mine, owned):
        pile = jnp.concatenate([mine] + [tiles(part) for part in owned], axis=0).astype(bf16)
        return padded(pile, lax.axis_size("dp"))

    def at(block, index, axis):
        return lax.dynamic_index_in_dim(block, index, axis, keepdims=False)

    def scattered_grads(layers):
        pile = jnp.stack([piled(shared, quartered) for shared, quartered, _ in layers], axis=1)
        mine = at(pile, tensor, 0).astype(f32)
        for j in range(1, ranks):
            mine = mine + around(at(pile, (tensor + j) % ranks, 0), "tensor", j).astype(f32)
        pile = jnp.stack([owned_pile(mine[i], layers[i][2]) for i in range(2)])
        pile = pile.reshape((2, chips, 4, -1) + pile.shape[2:])
        mine = at(pile, near, 2).astype(f32)
        for k in range(1, 4):
            mine = mine + flipped(at(pile, near ^ k, 2), "dp", k).astype(f32)
        pile = mine.astype(bf16)
        mine = at(pile, turn, 1).astype(f32)
        for k in range(1, chips):
            mine = mine + flipped(at(pile, turn ^ k, 1), "dp", 4 * k).astype(f32)
        return mine.astype(bf16)

    def spread_grads(zero, one, shared, quartered, owned):
        own = jnp.where(low_section, zero, one)
        away = jnp.where(low_section, one, zero)
        dp_size = 4 * chips
        home = jnp.stack([own, flipped(own, "dp", 2)])
        guest = jnp.stack([crossed(away, dp_size), crossed(away, dp_size + 2)])
        home, guest = [
            jnp.where(near // 2 == 0, block, block[::-1]) for block in (home, guest)
        ]
        pair = jnp.where(
            low_section, jnp.stack([home, guest], axis=1), jnp.stack([guest, home], axis=1)
        )
        parts = jnp.stack([pair] + [flipped(pair, "dp", 4 * k) for k in range(1, chips)])
        parts = jnp.stack([at(parts, turn ^ k, 0) for k in range(chips)])
        other = flipped(parts, "dp", 1)
        core = near % 2
        parts = jnp.stack(
            [jnp.where(core == 0, parts, other), jnp.where(core == 0, other, parts)], axis=2
        )
        pile = jnp.moveaxis(parts, 3, 0).reshape((2, -1) + parts.shape[5:])
        shared_sizes = [part.shape[1] // 128 for part in shared]
        quarter_sizes = [part.shape[1] // 128 // ranks for part in quartered]
        owned_sizes = [part.shape[1] // 128 for part in owned]
        each = -(-sum(shared_sizes) // ranks)
        own = pile[:, :each]
        parts = jnp.stack([own] + [around(own, "tensor", k) for k in range(1, ranks)])
        ordered = jnp.concatenate([at(parts, (tensor - r) % ranks, 0) for r in range(ranks)], axis=1)
        results = []
        for whole, begin, sizes in [
            (ordered, 0, shared_sizes),
            (pile, each, quarter_sizes + owned_sizes),
        ]:
            for count in sizes:
                results.append([flat(whole[m, begin : begin + count]) for m in range(2)])
                begin += count
        return results

    def feed_grads(layer, grad, unit2, rsd2, partial):
        return grad + norm_back(unit2, rsd2, reduce_rows(partial) * small[layer][4])

    def feed_adapters(second, branch, low_u, low_d, inner_u, inner_d, active, grad_up):
        shared = [across(inner_u, second), across(low_d, branch)]
        owned = [across(low_u, grad_up), across(inner_d, active)]
        return shared, owned

    def backward_attend(layer, kept, grad_middle):
        gain1 = small[layer][0]
        sq, skv, ekv, eo = adapters[layer]
        unit1, rsd1, normed, low_q, low_kv, queries, key_block, probs, mixed, low_o = kept
        branch = grad_middle.astype(bf16)
        grad_q, grad_block, inner_o, inner_q, partial = attend_back(
            layer, branch, early_all, so_all[layer], eo, probs, queries, key_block,
            eq_all[layer], sq, head,
        )
        count = (reach + 1) * rows
        blocks = grad_block[:count].astype(f32)
        for j in range(1, ranks):
            part = grad_block[j * count : (j + 1) * count]
            blocks = blocks + around(part, "tensor", j).astype(f32)
        own = blocks[reach * rows :]
        for back in range(1, reach + 1):
            begin = (reach - back) * rows
            own = own + along(blocks[begin : begin + rows].astype(bf16), "dp", -back).astype(f32)
        grad_kv = own.astype(bf16)
        inner_kv = against(grad_kv, ekv).astype(bf16)
        grad_normed = partial + against(grad_kv, keyval_ws[layer]) + plain(inner_kv, skv)
        grad_hidden = grad_middle + norm_back(unit1, rsd1, grad_normed * gain1)
        shared = [
            across(low_o, branch),
            across(inner_q, normed),
            across(inner_kv, normed),
            across(low_kv, grad_kv),
        ]
        quartered = [across(low_q, grad_q), across(inner_o, mixed)]
        return grad_hidden, shared, quartered

    fresh = lax.dynamic_index_in_dim(block_input, section, 0, keepdims=False).astype(f32)
    given = lax.dynamic_index_in_dim(cotangent, section, 0, keepdims=False).astype(f32)
    branch_one = spread(given.astype(bf16))
    fresh, branch_one = lax.optimization_barrier((fresh, branch_one))

    middle_zero, kept_zero = forward_attend(0, fresh)
    unit_zero, rsd_zero, second_zero, up_bias = feed_inputs(0, middle_zero)
    active_zero, slope_zero, low_u_zero, low_d_zero, partial = feed_call(
        feed_kernel,
        "feed",
        (second_zero, feed_tables[0], up_bias, feed_packs[0]),
        (3,),
        (local_f, local_f, rank, rank, width),
        local_f,
        2,
    )
    passed = feed_result(0, middle_zero, partial).astype(bf16)

    middle_one, kept_one = forward_attend(1, passed.astype(f32))
    unit_one, rsd_one, second_one, up_bias = feed_inputs(1, middle_one)
    active, low_u, low_d, partial, grad_up, inner_d, inner_u, partial_back = feed_call(
        feed_both_kernel,
        "feed_both",
        (second_one, branch_one, feed_tables[1], up_bias, feed_packs[1]),
        (4, 1),
        (local_f, rank, rank, width, local_f, rank, rank, width),
        local_f,
        4,
    )
    grad_middle = feed_grads(1, given, unit_one, rsd_one, partial_back)
    shared, owned = feed_adapters(
        second_one, branch_one, low_u, low_d, inner_u, inner_d, active, grad_up
    )
    grad_one, more, quartered = backward_attend(1, kept_one, grad_middle)
    layer_one = (shared + more, quartered, owned)
    partial, _ = lax.optimization_barrier((partial, grad_middle))
    final = feed_result(1, middle_one, partial).astype(bf16)

    branch_zero = spread(grad_one.astype(bf16))
    grad_up, inner_d, inner_u, partial_back = feed_call(
        feed_back_kernel,
        "feed_back",
        (branch_zero, feed_tables[0], slope_zero, feed_packs[0]),
        (3, 2),
        (local_f, rank, rank, width),
        local_f,
        2,
    )
    grad_middle_zero = feed_grads(0, grad_one, unit_zero, rsd_zero, partial_back)
    shared, owned = feed_adapters(
        second_zero,
        branch_zero,
        low_u_zero,
        low_d_zero,
        inner_u,
        inner_d,
        active_zero,
        grad_up,
    )
    grad_zero, more, quartered = backward_attend(0, kept_zero, grad_middle_zero)
    layer_zero = (shared + more, quartered, owned)
    mine = scattered_grads([layer_zero, layer_one])
    grads = spread_grads(mine[0], mine[1], *layer_zero)

    def both_micros(zero, one, kind):
        own = jnp.where(low_section, zero, one)
        received = swap(jnp.where(low_section, one, zero).astype(bf16)).astype(kind)
        return jnp.where(low_section, jnp.stack([own, received]), jnp.stack([received, own]))

    passed, final, _ = lax.optimization_barrier((passed, final, grad_middle_zero))
    section_outputs = both_micros(passed, final, bf16)
    input_grads = both_micros(grad_zero, grad_one, f32)
    onehot = (bank_choice[:, None] == jnp.arange(banks)[None, :]).astype(f32)

    def placed(pair, transpose):
        out = sum(
            onehot[m][:, None, None] * pair[m].astype(f32)[None] for m in range(2)
        )
        return (out.transpose(0, 2, 1) if transpose else out)[None]

    (
        up_shrink_grad,
        down_expand_grad,
        out_expand_grad,
        q_shrink_grad,
        kv_shrink_grad,
        kv_expand_grad,
        q_expand_grad,
        out_shrink_grad,
        up_expand_grad,
        down_shrink_grad,
    ) = grads
    return (
        section_outputs[None],
        input_grads[None],
        placed(q_shrink_grad, True),
        placed(q_expand_grad, False),
        placed(kv_shrink_grad, True),
        placed(kv_expand_grad, False),
        placed(out_shrink_grad, True),
        placed(out_expand_grad, False),
        placed(up_shrink_grad, True),
        placed(up_expand_grad, False),
        placed(down_shrink_grad, True),
        placed(down_expand_grad, False),
    )


def solution(mesh):
    return jax.shard_map(
        per_device,
        mesh=mesh,
        in_specs=(
            P(None, ("dp", "tensor"), None),
            P(None, ("dp", "tensor"), None),
            P(),
            P(),
            P("section", None),
            P("section", None),
            P("section", "dp", "tensor"),
            P("section", "tensor"),
            P("section", "dp", None),
            P("section", None),
            P("section", "tensor", "dp"),
            P("section", None),
            P("section", None),
            P("section", None),
            P("section", "dp", "tensor"),
            P("section", "tensor"),
            P("section", "tensor", "dp"),
            P("section", None),
            P("section", None, None, None),
            P("section", None, None, "tensor"),
            P("section", None, None, None),
            P("section", None, None, None),
            P("section", None, "tensor", None),
            P("section", None, None, None),
            P("section", None, None, None),
            P("section", None, None, "tensor"),
            P("section", None, "tensor", None),
            P("section", None, None, None),
        ),
        out_specs=(
            P("section", None, ("dp", "tensor"), None),
            P("section", None, ("dp", "tensor"), None),
            P("section", None, None, None),
            P("section", None, None, "tensor"),
            P("section", None, None, None),
            P("section", None, None, None),
            P("section", None, "tensor", None),
            P("section", None, None, None),
            P("section", None, None, None),
            P("section", None, None, "tensor"),
            P("section", None, "tensor", None),
            P("section", None, None, None),
        ),
        check_vma=False,
    )
```

```python
import math

import jax
import jax.numpy as jnp
from jax import lax
from jax.experimental import pallas as pl
from jax.experimental.layout import Layout, with_layout_constraint
from jax.experimental.pallas import tpu as pltpu
from jax.sharding import PartitionSpec as P

WINDOW = 1024
epsilon = 1e-05
masked_score = -1e30
bf16 = jnp.bfloat16
f32 = jnp.float32


def plain(left, right):
    return jnp.dot(left, right, preferred_element_type=f32)


def against(left, right):
    return lax.dot_general(left, right, (((1,), (1,)), ((), ())), preferred_element_type=f32)


def across(left, right):
    return lax.dot_general(left, right, (((0,), (0,)), ((), ())), preferred_element_type=f32)


def around(block, axis, distance):
    size = lax.axis_size(axis)
    return lax.ppermute(block, axis, [(i, (i + distance) % size) for i in range(size)])


def along(block, axis, distance):
    size = lax.axis_size(axis)
    route = [(i, i + distance) for i in range(size) if 0 <= i + distance < size]
    return lax.ppermute(block, axis, route)


def flipped(block, axis, bit):
    size = lax.axis_size(axis)
    return lax.ppermute(block, axis, [(i, i ^ bit) for i in range(size)])


def pick(table, index, size=1):
    return lax.dynamic_slice_in_dim(table, index, size, 0)


def norm_parts(value):
    centred = value - jnp.mean(value, axis=-1, keepdims=True)
    spread = lax.rsqrt(jnp.mean(centred * centred, axis=-1, keepdims=True) + epsilon)
    return centred * spread, spread


def norm_back(unit, spread, scaled):
    inner = jnp.mean(scaled * unit, axis=-1, keepdims=True)
    return spread * (scaled - jnp.mean(scaled, axis=-1, keepdims=True) - unit * inner)


def gelu_parts(value):
    rate = math.sqrt(2.0 / math.pi)
    square = value * value
    bend = jnp.tanh(rate * (value + 0.044715 * value * square))
    rising = 0.5 * (1.0 + bend)
    slope = rising + 0.5 * value * (1.0 - bend * bend) * (rate * (1.0 + 3 * 0.044715 * square))
    return value * rising, slope


def side_blocks(query_ref, group, head):
    begin = group * 4 * head
    return jnp.concatenate(
        [query_ref[:, begin + h * head : begin + (h + 1) * head] for h in range(4)], axis=0
    )


def put_blocks(out_ref, value, group, head):
    rows = value.shape[0] // 4
    for h in range(4):
        begin = (group * 4 + h) * head
        out_ref[:, begin : begin + head] = value[h * rows : (h + 1) * rows]


def table_copies(table_ref, buf, sem, layer, begin):
    ranks, chunks, _, width = buf.shape
    return [
        pltpu.make_async_copy(
            table_ref.at[x, y, layer, :, pl.ds(begin, width)], buf.at[x, y], sem.at[x, y]
        )
        for x in range(ranks)
        for y in range(chunks)
    ]


def query_kernel(layer, normed_ref, table_ref, bias_ref, eq_ref, sq_ref, out_ref, low_ref, buf, sem):
    ranks, chunks, rows, width = buf.shape
    copies = table_copies(table_ref, buf, sem, layer, 0)
    for copy in copies:
        copy.start()
    normed = normed_ref[...]
    low = against(normed, sq_ref[...]).astype(bf16)
    low_ref[...] = low
    for x in range(ranks):
        columns = pl.ds(x * width, width)
        total = bias_ref[:, columns] + plain(low, eq_ref[:, columns])
        for y in range(chunks):
            copies[x * chunks + y].wait()
            total = total + plain(normed[:, y * rows : (y + 1) * rows], buf[x, y])
        out_ref[:, columns] = total.astype(bf16)


def table_scratch(table, width):
    ranks, chunks, _, rows, _ = table.shape
    return [
        pltpu.VMEM((ranks, chunks, rows, width), bf16),
        pltpu.SemaphoreType.DMA((ranks, chunks)),
    ]


held = pl.BlockSpec(memory_space=pltpu.VMEM)
remote = pl.BlockSpec(memory_space=pl.ANY)


def project_queries(layer, normed, table, bias, eq, sq):
    rows, model = normed.shape
    rank = sq.shape[0]
    width = model // table.shape[0]
    return pl.pallas_call(
        lambda *refs: query_kernel(layer, *refs),
        in_specs=[held, remote, held, held, held],
        out_specs=[held] * 2,
        out_shape=[
            jax.ShapeDtypeStruct((rows, model), bf16),
            jax.ShapeDtypeStruct((rows, rank), bf16),
        ],
        scratch_shapes=table_scratch(table, width),
        compiler_params=pltpu.CompilerParams(vmem_limit_bytes=28 * 2**20),
        cost_estimate=pl.CostEstimate(
            flops=8 * rows * model * model, bytes_accessed=2 * model * model, transcendentals=0
        ),
        name="project_queries",
    )(normed, table, bias, eq, sq)


def attend_kernel(
    layer, head, query_ref, keyval_ref, bias_ref, table_ref, so_ref, eo_ref,
    prob_ref, mixed_ref, low_ref, out_ref, buf, sem,
):
    ranks, chunks, rows, width = buf.shape
    copies = table_copies(table_ref, buf, sem, layer, width)
    for copy in copies:
        copy.start()
    scale = 1.0 / math.sqrt(head)
    bias = jnp.concatenate([bias_ref[...].astype(f32)] * 4, axis=0)
    for g in range(prob_ref.shape[0]):
        queries = side_blocks(query_ref, g, head)
        scores = against(queries, keyval_ref[:, :head]) * scale + bias
        lifted = jnp.exp(scores - jnp.max(scores, axis=-1, keepdims=True))
        probs = (lifted * (1.0 / jnp.sum(lifted, axis=-1, keepdims=True))).astype(bf16)
        prob_ref[g] = probs
        put_blocks(mixed_ref, plain(probs, keyval_ref[:, head:]).astype(bf16), g, head)
    mixed = mixed_ref[...]
    low = against(mixed, so_ref[...]).astype(bf16)
    low_ref[...] = low
    for copy in copies:
        copy.wait()
    for y in range(chunks):
        columns = pl.ds(y * rows, rows)
        total = plain(low, eo_ref[:, columns])
        for x in range(ranks):
            total = total + against(mixed[:, x * width : (x + 1) * width], buf[x, y])
        out_ref[:, columns] = total


def attend(layer, queries, key_block, bias, table, so, eo, head):
    rows, model = queries.shape
    keys = key_block.shape[0]
    groups = model // head // 4
    rank = so.shape[0]
    return pl.pallas_call(
        lambda *refs: attend_kernel(layer, head, *refs),
        in_specs=[held, held, held, remote, held, held],
        out_specs=[held] * 4,
        out_shape=[
            jax.ShapeDtypeStruct((groups, 4 * rows, keys), bf16),
            jax.ShapeDtypeStruct((rows, model), bf16),
            jax.ShapeDtypeStruct((rows, rank), bf16),
            jax.ShapeDtypeStruct((rows, model), f32),
        ],
        scratch_shapes=table_scratch(table, model // table.shape[0]),
        compiler_params=pltpu.CompilerParams(vmem_limit_bytes=36 * 2**20),
        cost_estimate=pl.CostEstimate(
            flops=4 * rows * model * (keys + 2 * model),
            bytes_accessed=2 * model * model,
            transcendentals=groups * 4 * rows * keys,
        ),
        name="attend",
    )(queries, key_block, bias, table, so, eo)


def attend_back_kernel(
    layer, head, branch_ref, table_ref, so_ref, eo_ref, prob_ref, query_ref, keyval_ref, eq_ref, sq_ref,
    dq_ref, dkv_ref, inner_o_ref, inner_q_ref, part_ref,
    out_buf, out_sem, query_buf, query_sem, mixed_buf, key_sum, value_sum,
):
    ranks, chunks, rows, width = out_buf.shape
    out_copies = table_copies(table_ref, out_buf, out_sem, layer, width)
    query_copies = table_copies(table_ref, query_buf, query_sem, layer, 0)
    for copy in out_copies + query_copies:
        copy.start()
    scale = 1.0 / math.sqrt(head)
    branch = branch_ref[...]
    inner_o = against(branch, eo_ref[...]).astype(bf16)
    inner_o_ref[...] = inner_o
    for g in range(prob_ref.shape[0]):
        columns = pl.ds(g * width, width)
        total = plain(inner_o, so_ref[:, columns])
        for y in range(chunks):
            out_copies[g * chunks + y].wait()
            total = total + plain(branch[:, y * rows : (y + 1) * rows], out_buf[g, y])
        mixed_buf[:, columns] = total.astype(bf16)
        grad = side_blocks(mixed_buf, g, head)
        low_probs = prob_ref[g]
        probs = low_probs.astype(f32)
        grad_probs = against(grad, keyval_ref[:, head:])
        delta = jnp.sum(grad_probs * probs, axis=-1, keepdims=True)
        delta = delta / jnp.sum(probs, axis=-1, keepdims=True)
        grad_scores = (probs * (grad_probs - delta)).astype(bf16)
        put_blocks(dq_ref, (plain(grad_scores, keyval_ref[:, :head]) * scale).astype(bf16), g, head)
        keys = across(grad_scores, side_blocks(query_ref, g, head))
        values = across(low_probs, grad)
        if g == 0:
            key_sum[...] = keys
            value_sum[...] = values
        else:
            key_sum[...] += keys
            value_sum[...] += values
    dkv_ref[:, :head] = (key_sum[...] * scale).astype(bf16)
    dkv_ref[:, head:] = value_sum[...].astype(bf16)
    grad_q = dq_ref[...]
    inner_q = against(grad_q, eq_ref[...]).astype(bf16)
    inner_q_ref[...] = inner_q
    for copy in query_copies:
        copy.wait()
    for y in range(chunks):
        columns = pl.ds(y * rows, rows)
        total = plain(inner_q, sq_ref[:, columns])
        for x in range(ranks):
            total = total + against(grad_q[:, x * width : (x + 1) * width], query_buf[x, y])
        part_ref[:, columns] = total


def attend_back(layer, branch, table, so, eo, probs, queries, key_block, eq, sq, head):
    rows, model = queries.shape
    keys = key_block.shape[0]
    groups = probs.shape[0]
    rank = so.shape[0]
    width = model // table.shape[0]
    return pl.pallas_call(
        lambda *refs: attend_back_kernel(layer, head, *refs),
        in_specs=[held, remote] + [held] * 7,
        out_specs=[held] * 5,
        out_shape=[
            jax.ShapeDtypeStruct((rows, model), bf16),
            jax.ShapeDtypeStruct((keys, 2 * head), bf16),
            jax.ShapeDtypeStruct((rows, rank), bf16),
            jax.ShapeDtypeStruct((rows, rank), bf16),
            jax.ShapeDtypeStruct((rows, model), f32),
        ],
        scratch_shapes=table_scratch(table, width)
        + table_scratch(table, width)
        + [
            pltpu.VMEM((rows, model), bf16),
            pltpu.VMEM((keys, head), f32),
            pltpu.VMEM((keys, head), f32),
        ],
        compiler_params=pltpu.CompilerParams(vmem_limit_bytes=44 * 2**20),
        cost_estimate=pl.CostEstimate(
            flops=8 * rows * model * (keys + 2 * model),
            bytes_accessed=4 * model * model + 4 * groups * 4 * rows * keys,
            transcendentals=0,
        ),
        name="attend_back",
    )(branch, table, so, eo, probs, queries, key_block, eq, sq)


def feed_copies(table_ref, buf, sems):
    _, count, chunks, rows, tile = buf.shape
    half = count // 2 * tile
    copies = []
    for j in range(count):
        pair = []
        for k in range(2):
            columns = pl.ds(j * tile % half + k * half, tile)
            pair.append(
                pltpu.make_async_copy(
                    table_ref.at[:, j * tile // half, :, columns], buf.at[k, j], sems.at[k, j]
                )
            )
        copies.append(pair)
    return copies


def plain_chunks(left, buf, k, j):
    rows = buf.shape[3]
    return sum(plain(left[:, i * rows : (i + 1) * rows], buf[k, j, i]) for i in range(buf.shape[2]))


def against_chunk(left_ref, buf, k, i):
    tile = buf.shape[4]
    return sum(
        against(left_ref[:, j * tile : (j + 1) * tile], buf[k, j, i]) for j in range(buf.shape[1])
    )


def own_copies(sources, buffers, sems):
    copies = [
        pltpu.make_async_copy(source, buffer, sems.at[i])
        for i, (source, buffer) in enumerate(zip(sources, buffers))
    ]
    for copy in copies:
        copy.start()
    return copies


def feed_pack(pack_ref, model, hidden):
    cuts = [0, model, model + hidden, model + 2 * hidden, 2 * model + 2 * hidden]
    return [pack_ref.at[:, a:b] for a, b in zip(cuts[:-1], cuts[1:])]


def feed_kernel(
    second_ref, table_ref, bias_ref, pack_ref,
    active_ref, slope_ref, low_u_ref, low_d_ref, out_ref, buf, sems, pack_buf, own_sems,
):
    _, count, chunks, rows, tile = buf.shape
    su_ref, eu_ref, sd_ref, ed_ref = feed_pack(pack_buf, chunks * rows, count * tile)
    copies = feed_copies(table_ref, buf, sems)
    own = own_copies([pack_ref], [pack_buf], own_sems)
    for up, _ in copies:
        up.start()
    for _, down in copies:
        down.start()
    second = second_ref[...]
    own[0].wait()
    low_u = against(second, su_ref[...]).astype(bf16)
    low_u_ref[...] = low_u
    for j in range(count):
        columns = pl.ds(j * tile, tile)
        copies[j][0].wait()
        upward = plain_chunks(second, buf, 0, j)
        upward = upward + plain(low_u, eu_ref[:, columns]) + bias_ref[:, columns]
        active, slope = gelu_parts(upward)
        active_ref[:, columns] = active.astype(bf16)
        slope_ref[:, columns] = slope.astype(bf16)
    low_d = against(active_ref[...], sd_ref[...]).astype(bf16)
    low_d_ref[...] = low_d
    for _, down in copies:
        down.wait()
    for i in range(chunks):
        columns = pl.ds(i * rows, rows)
        out_ref[:, columns] = (
            against_chunk(active_ref, buf, 1, i) + plain(low_d, ed_ref[:, columns])
        ).astype(bf16)


def feed_back_kernel(
    branch_ref, table_ref, slope_ref, pack_ref,
    grad_up_ref, inner_d_ref, inner_u_ref, out_ref, buf, sems, pack_buf, slope_buf, own_sems,
):
    _, count, chunks, rows, tile = buf.shape
    su_ref, eu_ref, sd_ref, ed_ref = feed_pack(pack_buf, chunks * rows, count * tile)
    copies = feed_copies(table_ref, buf, sems)
    own = own_copies([pack_ref, slope_ref], [pack_buf, slope_buf], own_sems)
    for _, down in copies:
        down.start()
    for up, _ in copies:
        up.start()
    branch = branch_ref[...]
    own[0].wait()
    inner_d = against(branch, ed_ref[...]).astype(bf16)
    inner_d_ref[...] = inner_d
    own[1].wait()
    for j in range(count):
        columns = pl.ds(j * tile, tile)
        copies[j][1].wait()
        grad = plain_chunks(branch, buf, 1, j) + plain(inner_d, sd_ref[:, columns])
        grad_up_ref[:, columns] = (grad * slope_buf[:, columns].astype(f32)).astype(bf16)
    inner_u = against(grad_up_ref[...], eu_ref[...]).astype(bf16)
    inner_u_ref[...] = inner_u
    for up, _ in copies:
        up.wait()
    for i in range(chunks):
        columns = pl.ds(i * rows, rows)
        out_ref[:, columns] = (
            against_chunk(grad_up_ref, buf, 0, i) + plain(inner_u, su_ref[:, columns])
        ).astype(bf16)


def feed_both_kernel(
    second_ref, branch_ref, table_ref, bias_ref, pack_ref,
    active_ref, low_u_ref, low_d_ref, out_ref, grad_up_ref, inner_d_ref, inner_u_ref, back_ref,
    buf, sems, pack_buf, branch_buf, own_sems,
):
    _, count, chunks, rows, tile = buf.shape
    su_ref, eu_ref, sd_ref, ed_ref = feed_pack(pack_buf, chunks * rows, count * tile)
    copies = feed_copies(table_ref, buf, sems)
    own = own_copies([pack_ref, branch_ref], [pack_buf, branch_buf], own_sems)
    for up, down in copies:
        up.start()
        down.start()
    second = second_ref[...]
    for copy in own:
        copy.wait()
    branch = branch_buf[...]
    low_u = against(second, su_ref[...]).astype(bf16)
    low_u_ref[...] = low_u
    inner_d = against(branch, ed_ref[...]).astype(bf16)
    inner_d_ref[...] = inner_d
    for j in range(count):
        columns = pl.ds(j * tile, tile)
        copies[j][0].wait()
        upward = plain_chunks(second, buf, 0, j)
        upward = upward + plain(low_u, eu_ref[:, columns]) + bias_ref[:, columns]
        active, slope = gelu_parts(upward)
        active_ref[:, columns] = active.astype(bf16)
        copies[j][1].wait()
        grad = plain_chunks(branch, buf, 1, j) + plain(inner_d, sd_ref[:, columns])
        grad_up_ref[:, columns] = (grad * slope).astype(bf16)
    inner_u = against(grad_up_ref[...], eu_ref[...]).astype(bf16)
    inner_u_ref[...] = inner_u
    low_d = against(active_ref[...], sd_ref[...]).astype(bf16)
    low_d_ref[...] = low_d
    for i in range(chunks):
        columns = pl.ds(i * rows, rows)
        back_ref[:, columns] = (
            against_chunk(grad_up_ref, buf, 0, i) + plain(inner_u, su_ref[:, columns])
        ).astype(bf16)
        out_ref[:, columns] = (
            against_chunk(active_ref, buf, 1, i) + plain(low_d, ed_ref[:, columns])
        ).astype(bf16)


def feed_call(kernel, name, inputs, copied, outputs, hidden, matmuls):
    table = [value for value in inputs if value.ndim == 4][0]
    rows, model = inputs[0].shape
    tile = 512
    chunks = table.shape[0]
    return pl.pallas_call(
        kernel,
        in_specs=[
            remote if value.ndim == 4 or i in copied else held for i, value in enumerate(inputs)
        ],
        out_specs=[held] * len(outputs),
        out_shape=[jax.ShapeDtypeStruct((rows, width), bf16) for width in outputs],
        scratch_shapes=[
            pltpu.VMEM((2, hidden // tile, chunks, model // chunks, tile), bf16),
            pltpu.SemaphoreType.DMA((2, hidden // tile)),
        ]
        + [pltpu.VMEM(inputs[i].shape, bf16) for i in copied]
        + [pltpu.SemaphoreType.DMA((len(copied),))],
        compiler_params=pltpu.CompilerParams(vmem_limit_bytes=44 * 2**20),
        cost_estimate=pl.CostEstimate(
            flops=2 * matmuls * rows * model * hidden,
            bytes_accessed=4 * model * hidden,
            transcendentals=rows * hidden,
        ),
        name=name,
    )(*inputs)


def per_device(
    block_input,
    cotangent,
    doc_lengths,
    bank_choice,
    first_gain,
    first_shift,
    query_weight,
    query_bias,
    keyval_weight,
    value_bias,
    output_weight,
    output_bias,
    second_gain,
    second_shift,
    upward_weight,
    upward_bias,
    downward_weight,
    downward_bias,
    query_shrink,
    query_expand,
    keyval_shrink,
    keyval_expand,
    output_shrink,
    output_expand,
    upward_shrink,
    upward_expand,
    downward_shrink,
    downward_expand,
):
    section = lax.axis_index("section")
    data = lax.axis_index("dp")
    tensor = lax.axis_index("tensor")
    low_section = section == 0
    width = block_input.shape[2]
    rows = block_input.shape[1]
    ranks = lax.axis_size("tensor")
    span = rows * ranks
    head = value_bias.shape[1]
    local_q = query_bias.shape[1]
    local_f = upward_bias.shape[1]
    rank = query_expand.shape[2]
    banks = query_expand.shape[1]
    reach = WINDOW // span
    sides = [(0, 1), (1, 0)]

    def swap(value):
        return lax.ppermute(value, "section", sides)

    def by_layer(own, other):
        return jnp.where(low_section, own, other), jnp.where(low_section, other, own)

    def spread(block):
        parts = [block] + [around(block, "tensor", -j) for j in range(1, ranks)]
        return jnp.concatenate(parts, axis=0)

    def reduce_rows(partial):
        low = partial.astype(bf16)
        total = partial[:rows].astype(f32)
        for j in range(1, ranks):
            total = total + around(low[j * rows : (j + 1) * rows], "tensor", j).astype(f32)
        return total

    own_bank = lax.dynamic_index_in_dim(bank_choice, section, 0, keepdims=False)
    other_bank = lax.dynamic_index_in_dim(bank_choice, 1 - section, 0, keepdims=False)

    chips = lax.axis_size("dp") // 4
    both = ("section", "dp")
    every = ("section", "dp", "tensor")
    order = [
        side * 4 * chips + chip * 4 + near
        for chip in range(chips)
        for side in range(2)
        for near in range(4)
    ]
    order_all = [place * ranks + x for x in range(ranks) for place in order]

    def row_major(block):
        return with_layout_constraint(block, Layout(major_to_minor=(0, 1)))

    def gather(shard):
        table = lax.all_gather(row_major(shard), both, axis=0, tiled=True, axis_index_groups=[order])
        return row_major(table).reshape(chips, 2, -1, shard.shape[1])

    def gather_all(shard):
        table = lax.all_gather(
            row_major(shard), every, axis=0, tiled=True, axis_index_groups=[order_all]
        )
        return row_major(table).reshape(ranks, chips, 2, -1, shard.shape[1])

    def halves(shard):
        cut = shard.shape[1] // 2
        return shard[:, :cut], shard[:, cut:]

    keyval_half = jnp.where(tensor % 2 == 0, keyval_weight[0][:, :head], keyval_weight[0][:, head:])
    early_all = gather_all(
        jnp.concatenate([query_weight[0], row_major(output_weight[0].T), keyval_half], axis=1)
    )
    keyval_ws = [
        jnp.concatenate(
            [early_all[x, :, layer, :, 2 * local_q :].reshape(width, head) for x in range(2)], axis=1
        )
        for layer in range(2)
    ]

    def crossed(block, mask):
        return lax.ppermute(block, both, [(i, i ^ mask) for i in range(8 * chips)])

    vectors = jnp.concatenate(
        [
            first_gain,
            first_shift,
            jnp.zeros_like(value_bias),
            value_bias,
            output_bias,
            second_gain,
            second_shift,
            upward_bias,
            downward_bias,
        ],
        axis=1,
    )
    vector_sizes = [width, width, 2 * head, width, width, width, local_f, width]
    vector_layers = by_layer(vectors, swap(vectors))

    def chosen(table, bank, transpose):
        block = lax.dynamic_index_in_dim(table[0], bank, 0, keepdims=False)
        return block.T if transpose else block

    def pack(bank, parts):
        return jnp.concatenate([chosen(table, bank, flip) for table, flip in parts], axis=1)

    cut_parts = [(query_expand, False), (output_shrink, True)]
    whole_parts = [
        (query_shrink, True),
        (keyval_shrink, True),
        (keyval_expand, False),
        (output_expand, False),
        (upward_shrink, True),
        (upward_expand, False),
        (downward_shrink, True),
        (downward_expand, False),
    ]
    query_rows = jnp.broadcast_to(query_bias, (rank, local_q))

    def cut_pack(bank):
        return jnp.concatenate([pack(bank, cut_parts), query_rows], axis=1)

    shared_parts = [part for part in whole_parts if part[0] is not upward_expand and part[0] is not downward_shrink]
    split_parts = [(upward_expand, False), (downward_shrink, True)]
    shared_away = pack(other_bank, shared_parts)
    quarter = shared_away.shape[1] // ranks
    crossing = jnp.concatenate(
        [
            cut_pack(other_bank),
            lax.dynamic_slice_in_dim(shared_away, tensor * quarter, quarter, 1),
            pack(other_bank, split_parts),
        ],
        axis=1,
    )
    crossed_pack = swap(crossing)
    cut_width = 3 * local_q
    block = jnp.concatenate([cut_pack(own_bank), crossed_pack[:, : cut_width + quarter]], axis=1)
    blocks = jnp.stack([block] + [around(block, "tensor", j) for j in range(1, ranks)])
    blocks = [
        lax.dynamic_index_in_dim(blocks, (tensor - r) % ranks, 0, keepdims=False)
        for r in range(ranks)
    ]

    def joined(begin, size):
        return jnp.concatenate([block[:, begin : begin + size] for block in blocks], axis=1)

    cut_layers = [
        by_layer(joined(k * local_q, local_q), joined(cut_width + k * local_q, local_q))
        for k in range(3)
    ]
    eq_all, so_all, query_bias_all = cut_layers
    shared_layers = by_layer(pack(own_bank, shared_parts), joined(2 * cut_width, quarter))
    split_layers = by_layer(pack(own_bank, split_parts), crossed_pack[:, cut_width + quarter :])

    up_halves = halves(upward_weight[0])
    down_halves = halves(row_major(downward_weight[0].T))
    side = [jnp.concatenate([up_halves[h], down_halves[h]], axis=1) for h in range(2)]
    keep = jnp.where(low_section, side[0], side[1])
    gained = swap(jnp.where(low_section, side[1], side[0]))
    feed_tables = [gather(table) for table in by_layer(keep, gained)]

    def split(table, sizes):
        cuts = [0]
        for size in sizes:
            cuts.append(cuts[-1] + size)
        return [table[:, a:b] for a, b in zip(cuts[:-1], cuts[1:])]

    small = [
        [part.astype(f32) for part in split(vector_layers[layer], vector_sizes)]
        for layer in range(2)
    ]
    adapters = []
    feed_packs = []
    for layer in range(2):
        sq, skv, ekv, eo, su, ed = split(
            shared_layers[layer], [width, width, 2 * head, width, width, width]
        )
        eu, sd = split(split_layers[layer], [local_f, local_f])
        adapters.append((sq, skv, ekv, eo))
        feed_packs.append(jnp.concatenate([su, eu, sd, ed], axis=1))

    inside = jnp.arange(rows, dtype=jnp.int32)
    query_place = data * span + tensor * rows + inside
    key_place = jnp.concatenate(
        [
            (data - back) * span + (tensor + j) % ranks * rows + inside
            for j in range(ranks)
            for back in range(reach, -1, -1)
        ]
    )
    lengths = lax.dynamic_index_in_dim(doc_lengths, section, 0, keepdims=False)
    ends = jnp.cumsum(lengths)
    query_doc = jnp.sum((query_place[:, None] >= ends[None, :]).astype(jnp.int32), axis=1)
    key_doc = jnp.sum((key_place[:, None] >= ends[None, :]).astype(jnp.int32), axis=1)
    distance = query_place[:, None] - key_place[None, :]
    allowed = (
        (key_place[None, :] >= 0)
        & (distance >= 0)
        & (distance < WINDOW)
        & (query_doc[:, None] == key_doc[None, :])
    )
    bias = jnp.where(allowed, 0.0, masked_score).astype(bf16)

    def forward_attend(layer, hidden):
        gain1, shift1, kv_bias, out_bias = small[layer][:4]
        sq, skv, ekv, eo = adapters[layer]
        unit1, rsd1 = norm_parts(hidden)
        normed = (unit1 * gain1 + shift1).astype(bf16)
        low_kv = against(normed, skv).astype(bf16)
        keyval = (plain(normed, keyval_ws[layer]) + kv_bias + plain(low_kv, ekv)).astype(bf16)
        pieces = [along(keyval, "dp", back) for back in range(reach, 0, -1)] + [keyval]
        key_block = spread(jnp.concatenate(pieces, axis=0))
        queries, low_q = project_queries(
            layer, normed, early_all, query_bias_all[layer][:1].astype(f32), eq_all[layer], sq
        )
        probs, mixed, low_o, attended = attend(
            layer, queries, key_block, bias, early_all, so_all[layer], eo, head
        )
        middle = hidden + (attended + out_bias)
        return middle, (unit1, rsd1, normed, low_q, low_kv, queries, key_block, probs, mixed, low_o)

    def feed_inputs(layer, middle):
        gain2, shift2, up_bias = small[layer][4:7]
        unit2, rsd2 = norm_parts(middle)
        second = spread((unit2 * gain2 + shift2).astype(bf16))
        return unit2, rsd2, second, up_bias

    def feed_result(layer, middle, partial):
        return middle + (reduce_rows(partial) + small[layer][7])

    def tiles(block):
        return block.reshape(rank, -1, 128).transpose(1, 0, 2)

    def flat(block):
        return block.transpose(1, 0, 2).reshape(rank, -1)

    turn, near = data // 4, data % 4

    def padded(pile, multiple):
        lack = -pile.shape[0] % multiple
        if not lack:
            return pile
        return jnp.concatenate([pile, jnp.zeros((lack,) + pile.shape[1:], pile.dtype)], axis=0)

    def piled(*groups):
        piles = [
            padded(jnp.concatenate([tiles(part) for part in group], axis=0), ranks) for group in groups
        ]
        return jnp.concatenate(
            [pile.reshape((ranks, -1) + pile.shape[1:]) for pile in piles], axis=1
        ).astype(bf16)

    def at(block, index, axis):
        return lax.dynamic_index_in_dim(block, index, axis, keepdims=False)

    def summed_ranks(pile):
        total = at(pile, tensor, 0).astype(f32)
        for j in range(1, ranks):
            block = at(pile, (tensor + j) % ranks, 0)
            total = total + around(block, "tensor", j).astype(f32)
        return total

    def scattered_grads(layers):
        piles = [
            jnp.concatenate([mine] + [tiles(part) for part in keyval + owned], axis=0).astype(bf16)
            for mine, keyval, owned in layers
        ]
        pile = jnp.stack([padded(block, lax.axis_size("dp")) for block in piles])
        pile = pile.reshape((2, chips, 4, -1) + pile.shape[2:])
        mine = at(pile, near, 2).astype(f32)
        for k in range(1, 4):
            mine = mine + flipped(at(pile, near ^ k, 2), "dp", k).astype(f32)
        pile = mine.astype(bf16)
        mine = at(pile, turn, 1).astype(f32)
        for k in range(1, chips):
            mine = mine + flipped(at(pile, turn ^ k, 1), "dp", 4 * k).astype(f32)
        return mine.astype(bf16)

    def spread_grads(zero, one, shared, keyval, quartered, owned):
        own = jnp.where(low_section, zero, one)
        away = jnp.where(low_section, one, zero)
        dp_size = 4 * chips
        home = jnp.stack([own, flipped(own, "dp", 2)])
        guest = jnp.stack([crossed(away, dp_size), crossed(away, dp_size + 2)])
        home, guest = [
            jnp.where(near // 2 == 0, block, block[::-1]) for block in (home, guest)
        ]
        pair = jnp.where(
            low_section, jnp.stack([home, guest], axis=1), jnp.stack([guest, home], axis=1)
        )
        parts = jnp.stack([pair] + [flipped(pair, "dp", 4 * k) for k in range(1, chips)])
        parts = jnp.stack([at(parts, turn ^ k, 0) for k in range(chips)])
        other = flipped(parts, "dp", 1)
        core = near % 2
        parts = jnp.stack(
            [jnp.where(core == 0, parts, other), jnp.where(core == 0, other, parts)], axis=2
        )
        pile = jnp.moveaxis(parts, 3, 0).reshape((2, -1) + parts.shape[5:])
        shared_sizes, keyval_sizes, quarter_sizes, owned_sizes = [
            [part.shape[1] // 128 // cut for part in group]
            for group, cut in [(shared, 1), (keyval, 1), (quartered, ranks), (owned, 1)]
        ]
        each = sum(shared_sizes) // ranks
        border = each + sum(quarter_sizes)
        own = jnp.concatenate([pile[:, :each], pile[:, border : border + sum(keyval_sizes)]], axis=1)
        parts = jnp.stack([own] + [around(own, "tensor", k) for k in range(1, ranks)])
        parts = [at(parts, (tensor - r) % ranks, 0) for r in range(ranks)]
        ordered = jnp.concatenate([part[:, :each] for part in parts], axis=1)
        total = sum(part[:, each:].astype(f32) for part in parts)
        results = []
        for whole, begin, sizes in [
            (ordered, 0, shared_sizes),
            (total, 0, keyval_sizes),
            (pile, each, quarter_sizes),
            (pile, border + sum(keyval_sizes), owned_sizes),
        ]:
            for count in sizes:
                results.append([flat(whole[m, begin : begin + count]) for m in range(2)])
                begin += count
        return results

    def feed_grads(layer, grad, unit2, rsd2, partial):
        return grad + norm_back(unit2, rsd2, reduce_rows(partial) * small[layer][4])

    def feed_adapters(second, branch, low_u, low_d, inner_u, inner_d, active, grad_up):
        shared = [across(inner_u, second), across(low_d, branch)]
        owned = [across(low_u, grad_up), across(inner_d, active)]
        return shared, owned

    def backward_attend(layer, kept, grad_middle, shared, others):
        gain1 = small[layer][0]
        sq, skv, ekv, eo = adapters[layer]
        unit1, rsd1, normed, low_q, low_kv, queries, key_block, probs, mixed, low_o = kept
        branch = grad_middle.astype(bf16)
        grad_q, grad_block, inner_o, inner_q, partial = attend_back(
            layer, branch, early_all, so_all[layer], eo, probs, queries, key_block,
            eq_all[layer], sq, head,
        )
        shared = shared + [across(low_o, branch), across(inner_q, normed)]
        quartered = [across(low_q, grad_q), across(inner_o, mixed)]
        count = (reach + 1) * rows
        pile = piled(shared, *[[part] for part in quartered])
        if others is None:
            blocks = grad_block[:count].astype(f32)
            for j in range(1, ranks):
                part = grad_block[j * count : (j + 1) * count]
                blocks = blocks + around(part, "tensor", j).astype(f32)
        else:
            turned = jnp.stack(
                [at(pile, (tensor + j) % ranks, 0) for j in range(ranks)]
            )
            turned_others = jnp.stack(
                [at(others, (tensor + j) % ranks, 0) for j in range(ranks)]
            )
            keys = grad_block.reshape(ranks, count // rank, rank, 2, head).transpose(0, 1, 3, 2, 4)
            keys = keys.reshape(ranks, -1, rank, head)
            message = jnp.concatenate([keys, turned, turned_others], axis=1)
            total = message[0].astype(f32)
            for j in range(1, ranks):
                total = total + around(message[j], "tensor", j).astype(f32)
            places = count // rank * 2
            blocks = total[:places].reshape(count // rank, 2, rank, head).transpose(0, 2, 1, 3)
            blocks = blocks.reshape(count, 2 * head)
            pile = total[places:]
        own = blocks[reach * rows :]
        for back in range(1, reach + 1):
            begin = (reach - back) * rows
            own = own + along(blocks[begin : begin + rows].astype(bf16), "dp", -back).astype(f32)
        grad_kv = own.astype(bf16)
        inner_kv = against(grad_kv, ekv).astype(bf16)
        grad_normed = partial + against(grad_kv, keyval_ws[layer]) + plain(inner_kv, skv)
        grad_hidden = grad_middle + norm_back(unit1, rsd1, grad_normed * gain1)
        keyval = [across(inner_kv, normed), across(low_kv, grad_kv)]
        return grad_hidden, pile, shared, keyval, quartered

    fresh = lax.dynamic_index_in_dim(block_input, section, 0, keepdims=False).astype(f32)
    given = lax.dynamic_index_in_dim(cotangent, section, 0, keepdims=False).astype(f32)
    middle_zero, kept_zero = forward_attend(0, fresh)
    unit_zero, rsd_zero, second_zero, up_bias = feed_inputs(0, middle_zero)
    own_rows, second_zero = lax.optimization_barrier((given.astype(bf16), second_zero))
    branch_one = spread(own_rows)
    second_zero, branch_one = lax.optimization_barrier((second_zero, branch_one))
    active_zero, slope_zero, low_u_zero, low_d_zero, partial = feed_call(
        feed_kernel,
        "feed",
        (second_zero, feed_tables[0], up_bias, feed_packs[0]),
        (3,),
        (local_f, local_f, rank, rank, width),
        local_f,
        2,
    )
    passed = feed_result(0, middle_zero, partial).astype(bf16)

    middle_one, kept_one = forward_attend(1, passed.astype(f32))
    unit_one, rsd_one, second_one, up_bias = feed_inputs(1, middle_one)
    active, low_u, low_d, partial, grad_up, inner_d, inner_u, partial_back = feed_call(
        feed_both_kernel,
        "feed_both",
        (second_one, branch_one, feed_tables[1], up_bias, feed_packs[1]),
        (4, 1),
        (local_f, rank, rank, width, local_f, rank, rank, width),
        local_f,
        4,
    )
    grad_middle = feed_grads(1, given, unit_one, rsd_one, partial_back)
    shared, owned = feed_adapters(
        second_one, branch_one, low_u, low_d, inner_u, inner_d, active, grad_up
    )
    grad_one, pile_one, _, keyval_one, _ = backward_attend(1, kept_one, grad_middle, shared, None)
    owned_one = owned
    partial, _ = lax.optimization_barrier((partial, grad_middle))
    final = feed_result(1, middle_one, partial).astype(bf16)

    branch_zero = spread(grad_one.astype(bf16))
    grad_up, inner_d, inner_u, partial_back = feed_call(
        feed_back_kernel,
        "feed_back",
        (branch_zero, feed_tables[0], slope_zero, feed_packs[0]),
        (3, 2),
        (local_f, rank, rank, width),
        local_f,
        2,
    )
    grad_middle_zero = feed_grads(0, grad_one, unit_zero, rsd_zero, partial_back)
    shared, owned = feed_adapters(
        second_zero,
        branch_zero,
        low_u_zero,
        low_d_zero,
        inner_u,
        inner_d,
        active_zero,
        grad_up,
    )
    grad_zero, pile, shared, keyval, quartered = backward_attend(
        0, kept_zero, grad_middle_zero, shared, pile_one
    )
    half_pile = pile.shape[0] // 2
    mine = scattered_grads(
        [(pile[:half_pile], keyval, owned), (pile[half_pile:], keyval_one, owned_one)]
    )
    grads = spread_grads(mine[0], mine[1], shared, keyval, quartered, owned)

    def both_micros(zero, one, kind):
        own = jnp.where(low_section, zero, one)
        received = swap(jnp.where(low_section, one, zero).astype(bf16)).astype(kind)
        return jnp.where(low_section, jnp.stack([own, received]), jnp.stack([received, own]))

    passed, final, _ = lax.optimization_barrier((passed, final, grad_middle_zero))
    section_outputs = both_micros(passed, final, bf16)
    input_grads = both_micros(grad_zero, grad_one, f32)
    onehot = (bank_choice[:, None] == jnp.arange(banks)[None, :]).astype(f32)

    def placed(pair, transpose):
        out = sum(
            onehot[m][:, None, None] * pair[m].astype(f32)[None] for m in range(2)
        )
        return (out.transpose(0, 2, 1) if transpose else out)[None]

    (
        up_shrink_grad,
        down_expand_grad,
        out_expand_grad,
        q_shrink_grad,
        kv_shrink_grad,
        kv_expand_grad,
        q_expand_grad,
        out_shrink_grad,
        up_expand_grad,
        down_shrink_grad,
    ) = grads
    return (
        section_outputs[None],
        input_grads[None],
        placed(q_shrink_grad, True),
        placed(q_expand_grad, False),
        placed(kv_shrink_grad, True),
        placed(kv_expand_grad, False),
        placed(out_shrink_grad, True),
        placed(out_expand_grad, False),
        placed(up_shrink_grad, True),
        placed(up_expand_grad, False),
        placed(down_shrink_grad, True),
        placed(down_expand_grad, False),
    )


def solution(mesh):
    return jax.shard_map(
        per_device,
        mesh=mesh,
        in_specs=(
            P(None, ("dp", "tensor"), None),
            P(None, ("dp", "tensor"), None),
            P(),
            P(),
            P("section", None),
            P("section", None),
            P("section", "dp", "tensor"),
            P("section", "tensor"),
            P("section", "dp", None),
            P("section", None),
            P("section", "tensor", "dp"),
            P("section", None),
            P("section", None),
            P("section", None),
            P("section", "dp", "tensor"),
            P("section", "tensor"),
            P("section", "tensor", "dp"),
            P("section", None),
            P("section", None, None, None),
            P("section", None, None, "tensor"),
            P("section", None, None, None),
            P("section", None, None, None),
            P("section", None, "tensor", None),
            P("section", None, None, None),
            P("section", None, None, None),
            P("section", None, None, "tensor"),
            P("section", None, "tensor", None),
            P("section", None, None, None),
        ),
        out_specs=(
            P("section", None, ("dp", "tensor"), None),
            P("section", None, ("dp", "tensor"), None),
            P("section", None, None, None),
            P("section", None, None, "tensor"),
            P("section", None, None, None),
            P("section", None, None, None),
            P("section", None, "tensor", None),
            P("section", None, None, None),
            P("section", None, None, None),
            P("section", None, None, "tensor"),
            P("section", None, "tensor", None),
            P("section", None, None, None),
        ),
        check_vma=False,
    )
```

```python
import math

import jax
import jax.numpy as jnp
from jax import lax
from jax.experimental import pallas as pl
from jax.experimental.layout import Layout, with_layout_constraint
from jax.experimental.pallas import tpu as pltpu
from jax.sharding import PartitionSpec as P

WINDOW = 1024
epsilon = 1e-05
masked_score = -1e30
bf16 = jnp.bfloat16
f32 = jnp.float32


def plain(left, right):
    return jnp.dot(left, right, preferred_element_type=f32)


def against(left, right):
    return lax.dot_general(left, right, (((1,), (1,)), ((), ())), preferred_element_type=f32)


def across(left, right):
    return lax.dot_general(left, right, (((0,), (0,)), ((), ())), preferred_element_type=f32)


def around(block, axis, distance):
    size = lax.axis_size(axis)
    return lax.ppermute(block, axis, [(i, (i + distance) % size) for i in range(size)])


def along(block, axis, distance):
    size = lax.axis_size(axis)
    route = [(i, i + distance) for i in range(size) if 0 <= i + distance < size]
    return lax.ppermute(block, axis, route)


def flipped(block, axis, bit):
    size = lax.axis_size(axis)
    return lax.ppermute(block, axis, [(i, i ^ bit) for i in range(size)])


def pick(table, index, size=1):
    return lax.dynamic_slice_in_dim(table, index, size, 0)


def norm_parts(value):
    centred = value - jnp.mean(value, axis=-1, keepdims=True)
    spread = lax.rsqrt(jnp.mean(centred * centred, axis=-1, keepdims=True) + epsilon)
    return centred * spread, spread


def norm_back(unit, spread, scaled):
    inner = jnp.mean(scaled * unit, axis=-1, keepdims=True)
    return spread * (scaled - jnp.mean(scaled, axis=-1, keepdims=True) - unit * inner)


def gelu_parts(value):
    rate = math.sqrt(2.0 / math.pi)
    square = value * value
    bend = jnp.tanh(rate * (value + 0.044715 * value * square))
    rising = 0.5 * (1.0 + bend)
    slope = rising + 0.5 * value * (1.0 - bend * bend) * (rate * (1.0 + 3 * 0.044715 * square))
    return value * rising, slope


def side_blocks(query_ref, group, head):
    begin = group * 4 * head
    return jnp.concatenate(
        [query_ref[:, begin + h * head : begin + (h + 1) * head] for h in range(4)], axis=0
    )


def put_blocks(out_ref, value, group, head):
    rows = value.shape[0] // 4
    for h in range(4):
        begin = (group * 4 + h) * head
        out_ref[:, begin : begin + head] = value[h * rows : (h + 1) * rows]


def table_copies(table_ref, buf, sem, layer, begin):
    ranks, chunks, _, width = buf.shape
    return [
        pltpu.make_async_copy(
            table_ref.at[x, y, layer, :, pl.ds(begin, width)], buf.at[x, y], sem.at[x, y]
        )
        for x in range(ranks)
        for y in range(chunks)
    ]


def query_kernel(layer, normed_ref, table_ref, bias_ref, eq_ref, sq_ref, out_ref, low_ref, buf, sem):
    ranks, chunks, rows, width = buf.shape
    copies = table_copies(table_ref, buf, sem, layer, 0)
    for copy in copies:
        copy.start()
    normed = normed_ref[...]
    low = against(normed, sq_ref[...]).astype(bf16)
    low_ref[...] = low
    for x in range(ranks):
        columns = pl.ds(x * width, width)
        total = bias_ref[:, columns] + plain(low, eq_ref[:, columns])
        for y in range(chunks):
            copies[x * chunks + y].wait()
            total = total + plain(normed[:, y * rows : (y + 1) * rows], buf[x, y])
        out_ref[:, columns] = total.astype(bf16)


def table_scratch(table, width):
    ranks, chunks, _, rows, _ = table.shape
    return [
        pltpu.VMEM((ranks, chunks, rows, width), bf16),
        pltpu.SemaphoreType.DMA((ranks, chunks)),
    ]


held = pl.BlockSpec(memory_space=pltpu.VMEM)
remote = pl.BlockSpec(memory_space=pl.ANY)


def project_queries(layer, normed, table, bias, eq, sq):
    rows, model = normed.shape
    rank = sq.shape[0]
    width = model // table.shape[0]
    return pl.pallas_call(
        lambda *refs: query_kernel(layer, *refs),
        in_specs=[held, remote, held, held, held],
        out_specs=[held] * 2,
        out_shape=[
            jax.ShapeDtypeStruct((rows, model), bf16),
            jax.ShapeDtypeStruct((rows, rank), bf16),
        ],
        scratch_shapes=table_scratch(table, width),
        compiler_params=pltpu.CompilerParams(vmem_limit_bytes=28 * 2**20),
        cost_estimate=pl.CostEstimate(
            flops=8 * rows * model * model, bytes_accessed=2 * model * model, transcendentals=0
        ),
        name="project_queries",
    )(normed, table, bias, eq, sq)


def attend_kernel(
    layer, head, query_ref, keyval_ref, bias_ref, table_ref, so_ref, eo_ref,
    prob_ref, mixed_ref, low_ref, out_ref, buf, sem,
):
    ranks, chunks, rows, width = buf.shape
    copies = table_copies(table_ref, buf, sem, layer, width)
    for copy in copies:
        copy.start()
    scale = 1.0 / math.sqrt(head)
    bias = jnp.concatenate([bias_ref[...].astype(f32)] * 4, axis=0)
    for g in range(prob_ref.shape[0]):
        queries = side_blocks(query_ref, g, head)
        scores = against(queries, keyval_ref[:, :head]) * scale + bias
        lifted = jnp.exp(scores - jnp.max(scores, axis=-1, keepdims=True))
        probs = (lifted * (1.0 / jnp.sum(lifted, axis=-1, keepdims=True))).astype(bf16)
        prob_ref[g] = probs
        put_blocks(mixed_ref, plain(probs, keyval_ref[:, head:]).astype(bf16), g, head)
    mixed = mixed_ref[...]
    low = against(mixed, so_ref[...]).astype(bf16)
    low_ref[...] = low
    for copy in copies:
        copy.wait()
    for y in range(chunks):
        columns = pl.ds(y * rows, rows)
        total = plain(low, eo_ref[:, columns])
        for x in range(ranks):
            total = total + against(mixed[:, x * width : (x + 1) * width], buf[x, y])
        out_ref[:, columns] = total


def attend(layer, queries, key_block, bias, table, so, eo, head):
    rows, model = queries.shape
    keys = key_block.shape[0]
    groups = model // head // 4
    rank = so.shape[0]
    return pl.pallas_call(
        lambda *refs: attend_kernel(layer, head, *refs),
        in_specs=[held, held, held, remote, held, held],
        out_specs=[held] * 4,
        out_shape=[
            jax.ShapeDtypeStruct((groups, 4 * rows, keys), bf16),
            jax.ShapeDtypeStruct((rows, model), bf16),
            jax.ShapeDtypeStruct((rows, rank), bf16),
            jax.ShapeDtypeStruct((rows, model), f32),
        ],
        scratch_shapes=table_scratch(table, model // table.shape[0]),
        compiler_params=pltpu.CompilerParams(vmem_limit_bytes=36 * 2**20),
        cost_estimate=pl.CostEstimate(
            flops=4 * rows * model * (keys + 2 * model),
            bytes_accessed=2 * model * model,
            transcendentals=groups * 4 * rows * keys,
        ),
        name="attend",
    )(queries, key_block, bias, table, so, eo)


def attend_back_kernel(
    layer, head, branch_ref, table_ref, so_ref, eo_ref, prob_ref, query_ref, keyval_ref, eq_ref, sq_ref,
    dq_ref, dkv_ref, inner_o_ref, inner_q_ref, part_ref,
    out_buf, out_sem, query_buf, query_sem, mixed_buf, key_sum, value_sum,
):
    ranks, chunks, rows, width = out_buf.shape
    out_copies = table_copies(table_ref, out_buf, out_sem, layer, width)
    query_copies = table_copies(table_ref, query_buf, query_sem, layer, 0)
    for copy in out_copies + query_copies:
        copy.start()
    scale = 1.0 / math.sqrt(head)
    branch = branch_ref[...]
    inner_o = against(branch, eo_ref[...]).astype(bf16)
    inner_o_ref[...] = inner_o
    for g in range(prob_ref.shape[0]):
        columns = pl.ds(g * width, width)
        total = plain(inner_o, so_ref[:, columns])
        for y in range(chunks):
            out_copies[g * chunks + y].wait()
            total = total + plain(branch[:, y * rows : (y + 1) * rows], out_buf[g, y])
        mixed_buf[:, columns] = total.astype(bf16)
        grad = side_blocks(mixed_buf, g, head)
        low_probs = prob_ref[g]
        probs = low_probs.astype(f32)
        grad_probs = against(grad, keyval_ref[:, head:])
        delta = jnp.sum(grad_probs * probs, axis=-1, keepdims=True)
        delta = delta / jnp.sum(probs, axis=-1, keepdims=True)
        grad_scores = (probs * (grad_probs - delta)).astype(bf16)
        put_blocks(dq_ref, (plain(grad_scores, keyval_ref[:, :head]) * scale).astype(bf16), g, head)
        keys = across(grad_scores, side_blocks(query_ref, g, head))
        values = across(low_probs, grad)
        if g == 0:
            key_sum[...] = keys
            value_sum[...] = values
        else:
            key_sum[...] += keys
            value_sum[...] += values
    dkv_ref[:, :head] = (key_sum[...] * scale).astype(bf16)
    dkv_ref[:, head:] = value_sum[...].astype(bf16)
    grad_q = dq_ref[...]
    inner_q = against(grad_q, eq_ref[...]).astype(bf16)
    inner_q_ref[...] = inner_q
    for copy in query_copies:
        copy.wait()
    for y in range(chunks):
        columns = pl.ds(y * rows, rows)
        total = plain(inner_q, sq_ref[:, columns])
        for x in range(ranks):
            total = total + against(grad_q[:, x * width : (x + 1) * width], query_buf[x, y])
        part_ref[:, columns] = total


def attend_back(layer, branch, table, so, eo, probs, queries, key_block, eq, sq, head):
    rows, model = queries.shape
    keys = key_block.shape[0]
    groups = probs.shape[0]
    rank = so.shape[0]
    width = model // table.shape[0]
    return pl.pallas_call(
        lambda *refs: attend_back_kernel(layer, head, *refs),
        in_specs=[held, remote] + [held] * 7,
        out_specs=[held] * 5,
        out_shape=[
            jax.ShapeDtypeStruct((rows, model), bf16),
            jax.ShapeDtypeStruct((keys, 2 * head), bf16),
            jax.ShapeDtypeStruct((rows, rank), bf16),
            jax.ShapeDtypeStruct((rows, rank), bf16),
            jax.ShapeDtypeStruct((rows, model), f32),
        ],
        scratch_shapes=table_scratch(table, width)
        + table_scratch(table, width)
        + [
            pltpu.VMEM((rows, model), bf16),
            pltpu.VMEM((keys, head), f32),
            pltpu.VMEM((keys, head), f32),
        ],
        compiler_params=pltpu.CompilerParams(vmem_limit_bytes=44 * 2**20),
        cost_estimate=pl.CostEstimate(
            flops=8 * rows * model * (keys + 2 * model),
            bytes_accessed=4 * model * model + 4 * groups * 4 * rows * keys,
            transcendentals=0,
        ),
        name="attend_back",
    )(branch, table, so, eo, probs, queries, key_block, eq, sq)


def feed_copies(table_ref, buf, sems):
    _, count, chunks, rows, tile = buf.shape
    half = count // 2 * tile
    copies = []
    for j in range(count):
        pair = []
        for k in range(2):
            columns = pl.ds(j * tile % half + k * half, tile)
            pair.append(
                pltpu.make_async_copy(
                    table_ref.at[:, j * tile // half, :, columns], buf.at[k, j], sems.at[k, j]
                )
            )
        copies.append(pair)
    return copies


def plain_chunks(left, buf, k, j):
    rows = buf.shape[3]
    return sum(plain(left[:, i * rows : (i + 1) * rows], buf[k, j, i]) for i in range(buf.shape[2]))


def against_chunk(left_ref, buf, k, i):
    tile = buf.shape[4]
    return sum(
        against(left_ref[:, j * tile : (j + 1) * tile], buf[k, j, i]) for j in range(buf.shape[1])
    )


def own_copies(sources, buffers, sems):
    copies = [
        pltpu.make_async_copy(source, buffer, sems.at[i])
        for i, (source, buffer) in enumerate(zip(sources, buffers))
    ]
    for copy in copies:
        copy.start()
    return copies


def feed_pack(pack_ref, model, hidden):
    cuts = [0, model, model + hidden, model + 2 * hidden, 2 * model + 2 * hidden]
    return [pack_ref.at[:, a:b] for a, b in zip(cuts[:-1], cuts[1:])]


def feed_kernel(
    second_ref, table_ref, bias_ref, pack_ref,
    active_ref, slope_ref, low_u_ref, low_d_ref, out_ref, buf, sems, pack_buf, own_sems,
):
    _, count, chunks, rows, tile = buf.shape
    su_ref, eu_ref, sd_ref, ed_ref = feed_pack(pack_buf, chunks * rows, count * tile)
    copies = feed_copies(table_ref, buf, sems)
    own = own_copies([pack_ref], [pack_buf], own_sems)
    for up, _ in copies:
        up.start()
    for _, down in copies:
        down.start()
    second = second_ref[...]
    own[0].wait()
    low_u = against(second, su_ref[...]).astype(bf16)
    low_u_ref[...] = low_u
    for j in range(count):
        columns = pl.ds(j * tile, tile)
        copies[j][0].wait()
        upward = plain_chunks(second, buf, 0, j)
        upward = upward + plain(low_u, eu_ref[:, columns]) + bias_ref[:, columns]
        active, slope = gelu_parts(upward)
        active_ref[:, columns] = active.astype(bf16)
        slope_ref[:, columns] = slope.astype(bf16)
    low_d = against(active_ref[...], sd_ref[...]).astype(bf16)
    low_d_ref[...] = low_d
    for _, down in copies:
        down.wait()
    for i in range(chunks):
        columns = pl.ds(i * rows, rows)
        out_ref[:, columns] = (
            against_chunk(active_ref, buf, 1, i) + plain(low_d, ed_ref[:, columns])
        ).astype(bf16)


def feed_back_kernel(
    branch_ref, table_ref, slope_ref, pack_ref,
    grad_up_ref, inner_d_ref, inner_u_ref, out_ref, buf, sems, pack_buf, slope_buf, own_sems,
):
    _, count, chunks, rows, tile = buf.shape
    su_ref, eu_ref, sd_ref, ed_ref = feed_pack(pack_buf, chunks * rows, count * tile)
    copies = feed_copies(table_ref, buf, sems)
    own = own_copies([pack_ref, slope_ref], [pack_buf, slope_buf], own_sems)
    for _, down in copies:
        down.start()
    for up, _ in copies:
        up.start()
    branch = branch_ref[...]
    own[0].wait()
    inner_d = against(branch, ed_ref[...]).astype(bf16)
    inner_d_ref[...] = inner_d
    own[1].wait()
    for j in range(count):
        columns = pl.ds(j * tile, tile)
        copies[j][1].wait()
        grad = plain_chunks(branch, buf, 1, j) + plain(inner_d, sd_ref[:, columns])
        grad_up_ref[:, columns] = (grad * slope_buf[:, columns].astype(f32)).astype(bf16)
    inner_u = against(grad_up_ref[...], eu_ref[...]).astype(bf16)
    inner_u_ref[...] = inner_u
    for up, _ in copies:
        up.wait()
    for i in range(chunks):
        columns = pl.ds(i * rows, rows)
        out_ref[:, columns] = (
            against_chunk(grad_up_ref, buf, 0, i) + plain(inner_u, su_ref[:, columns])
        ).astype(bf16)


def feed_both_kernel(
    second_ref, branch_ref, table_ref, bias_ref, pack_ref,
    active_ref, low_u_ref, low_d_ref, out_ref, grad_up_ref, inner_d_ref, inner_u_ref, back_ref,
    buf, sems, pack_buf, branch_buf, own_sems,
):
    _, count, chunks, rows, tile = buf.shape
    su_ref, eu_ref, sd_ref, ed_ref = feed_pack(pack_buf, chunks * rows, count * tile)
    copies = feed_copies(table_ref, buf, sems)
    own = own_copies([pack_ref, branch_ref], [pack_buf, branch_buf], own_sems)
    for up, down in copies:
        up.start()
        down.start()
    second = second_ref[...]
    for copy in own:
        copy.wait()
    branch = branch_buf[...]
    low_u = against(second, su_ref[...]).astype(bf16)
    low_u_ref[...] = low_u
    inner_d = against(branch, ed_ref[...]).astype(bf16)
    inner_d_ref[...] = inner_d
    for j in range(count):
        columns = pl.ds(j * tile, tile)
        copies[j][0].wait()
        upward = plain_chunks(second, buf, 0, j)
        upward = upward + plain(low_u, eu_ref[:, columns]) + bias_ref[:, columns]
        active, slope = gelu_parts(upward)
        active_ref[:, columns] = active.astype(bf16)
        copies[j][1].wait()
        grad = plain_chunks(branch, buf, 1, j) + plain(inner_d, sd_ref[:, columns])
        grad_up_ref[:, columns] = (grad * slope).astype(bf16)
    inner_u = against(grad_up_ref[...], eu_ref[...]).astype(bf16)
    inner_u_ref[...] = inner_u
    low_d = against(active_ref[...], sd_ref[...]).astype(bf16)
    low_d_ref[...] = low_d
    for i in range(chunks):
        columns = pl.ds(i * rows, rows)
        back_ref[:, columns] = (
            against_chunk(grad_up_ref, buf, 0, i) + plain(inner_u, su_ref[:, columns])
        ).astype(bf16)
        out_ref[:, columns] = (
            against_chunk(active_ref, buf, 1, i) + plain(low_d, ed_ref[:, columns])
        ).astype(bf16)


def feed_call(kernel, name, inputs, copied, outputs, hidden, matmuls):
    table = [value for value in inputs if value.ndim == 4][0]
    rows, model = inputs[0].shape
    tile = 512
    chunks = table.shape[0]
    return pl.pallas_call(
        kernel,
        in_specs=[
            remote if value.ndim == 4 or i in copied else held for i, value in enumerate(inputs)
        ],
        out_specs=[held] * len(outputs),
        out_shape=[jax.ShapeDtypeStruct((rows, width), bf16) for width in outputs],
        scratch_shapes=[
            pltpu.VMEM((2, hidden // tile, chunks, model // chunks, tile), bf16),
            pltpu.SemaphoreType.DMA((2, hidden // tile)),
        ]
        + [pltpu.VMEM(inputs[i].shape, bf16) for i in copied]
        + [pltpu.SemaphoreType.DMA((len(copied),))],
        compiler_params=pltpu.CompilerParams(vmem_limit_bytes=44 * 2**20),
        cost_estimate=pl.CostEstimate(
            flops=2 * matmuls * rows * model * hidden,
            bytes_accessed=4 * model * hidden,
            transcendentals=rows * hidden,
        ),
        name=name,
    )(*inputs)


def per_device(
    block_input,
    cotangent,
    doc_lengths,
    bank_choice,
    first_gain,
    first_shift,
    query_weight,
    query_bias,
    keyval_weight,
    value_bias,
    output_weight,
    output_bias,
    second_gain,
    second_shift,
    upward_weight,
    upward_bias,
    downward_weight,
    downward_bias,
    query_shrink,
    query_expand,
    keyval_shrink,
    keyval_expand,
    output_shrink,
    output_expand,
    upward_shrink,
    upward_expand,
    downward_shrink,
    downward_expand,
):
    section = lax.axis_index("section")
    data = lax.axis_index("dp")
    tensor = lax.axis_index("tensor")
    low_section = section == 0
    width = block_input.shape[2]
    rows = block_input.shape[1]
    ranks = lax.axis_size("tensor")
    span = rows * ranks
    head = value_bias.shape[1]
    local_q = query_bias.shape[1]
    local_f = upward_bias.shape[1]
    rank = query_expand.shape[2]
    banks = query_expand.shape[1]
    reach = WINDOW // span
    sides = [(0, 1), (1, 0)]

    def swap(value):
        return lax.ppermute(value, "section", sides)

    def by_layer(own, other):
        return jnp.where(low_section, own, other), jnp.where(low_section, other, own)

    def spread(block):
        parts = [block] + [around(block, "tensor", -j) for j in range(1, ranks)]
        return jnp.concatenate(parts, axis=0)

    def reduce_rows(partial):
        low = partial.astype(bf16)
        total = partial[:rows].astype(f32)
        for j in range(1, ranks):
            total = total + around(low[j * rows : (j + 1) * rows], "tensor", j).astype(f32)
        return total

    own_bank = lax.dynamic_index_in_dim(bank_choice, section, 0, keepdims=False)
    other_bank = lax.dynamic_index_in_dim(bank_choice, 1 - section, 0, keepdims=False)

    chips = lax.axis_size("dp") // 4
    both = ("section", "dp")
    every = ("section", "dp", "tensor")
    order = [
        side * 4 * chips + chip * 4 + near
        for chip in range(chips)
        for side in range(2)
        for near in range(4)
    ]
    order_all = [place * ranks + x for x in range(ranks) for place in order]

    def row_major(block):
        return with_layout_constraint(block, Layout(major_to_minor=(0, 1)))

    def gather(shard):
        table = lax.all_gather(row_major(shard), both, axis=0, tiled=True, axis_index_groups=[order])
        return row_major(table).reshape(chips, 2, -1, shard.shape[1])

    def gather_all(shard):
        table = lax.all_gather(
            row_major(shard), every, axis=0, tiled=True, axis_index_groups=[order_all]
        )
        return row_major(table).reshape(ranks, chips, 2, -1, shard.shape[1])

    def halves(shard):
        cut = shard.shape[1] // 2
        return shard[:, :cut], shard[:, cut:]

    keyval_half = jnp.where(tensor % 2 == 0, keyval_weight[0][:, :head], keyval_weight[0][:, head:])
    early_all = gather_all(
        jnp.concatenate([query_weight[0], row_major(output_weight[0].T), keyval_half], axis=1)
    )
    keyval_ws = [
        jnp.concatenate(
            [early_all[x, :, layer, :, 2 * local_q :].reshape(width, head) for x in range(2)], axis=1
        )
        for layer in range(2)
    ]

    def crossed(block, mask):
        return lax.ppermute(block, both, [(i, i ^ mask) for i in range(8 * chips)])

    vectors = jnp.concatenate(
        [
            first_gain,
            first_shift,
            jnp.zeros_like(value_bias),
            value_bias,
            output_bias,
            second_gain,
            second_shift,
            upward_bias,
            downward_bias,
        ],
        axis=1,
    )
    vector_sizes = [width, width, 2 * head, width, width, width, local_f, width]
    vector_layers = by_layer(vectors, swap(vectors))

    def chosen(table, bank, transpose):
        block = lax.dynamic_index_in_dim(table[0], bank, 0, keepdims=False)
        return block.T if transpose else block

    def pack(bank, parts):
        return jnp.concatenate([chosen(table, bank, flip) for table, flip in parts], axis=1)

    cut_parts = [(query_expand, False), (output_shrink, True)]
    whole_parts = [
        (query_shrink, True),
        (keyval_shrink, True),
        (keyval_expand, False),
        (output_expand, False),
        (upward_shrink, True),
        (upward_expand, False),
        (downward_shrink, True),
        (downward_expand, False),
    ]
    query_rows = jnp.broadcast_to(query_bias, (rank, local_q))

    def cut_pack(bank):
        return jnp.concatenate([pack(bank, cut_parts), query_rows], axis=1)

    shared_parts = [part for part in whole_parts if part[0] is not upward_expand and part[0] is not downward_shrink]
    split_parts = [(upward_expand, False), (downward_shrink, True)]
    shared_away = pack(other_bank, shared_parts)
    quarter = shared_away.shape[1] // ranks
    crossing = jnp.concatenate(
        [
            cut_pack(other_bank),
            lax.dynamic_slice_in_dim(shared_away, tensor * quarter, quarter, 1),
            pack(other_bank, split_parts),
        ],
        axis=1,
    )
    crossed_pack = swap(crossing)
    cut_width = 3 * local_q
    block = jnp.concatenate([cut_pack(own_bank), crossed_pack[:, : cut_width + quarter]], axis=1)
    blocks = jnp.stack([block] + [around(block, "tensor", j) for j in range(1, ranks)])
    blocks = [
        lax.dynamic_index_in_dim(blocks, (tensor - r) % ranks, 0, keepdims=False)
        for r in range(ranks)
    ]

    def joined(begin, size):
        return jnp.concatenate([block[:, begin : begin + size] for block in blocks], axis=1)

    cut_layers = [
        by_layer(joined(k * local_q, local_q), joined(cut_width + k * local_q, local_q))
        for k in range(3)
    ]
    eq_all, so_all, query_bias_all = cut_layers
    shared_layers = by_layer(pack(own_bank, shared_parts), joined(2 * cut_width, quarter))
    split_layers = by_layer(pack(own_bank, split_parts), crossed_pack[:, cut_width + quarter :])

    up_halves = halves(upward_weight[0])
    down_halves = halves(row_major(downward_weight[0].T))
    side = [jnp.concatenate([up_halves[h], down_halves[h]], axis=1) for h in range(2)]
    keep = jnp.where(low_section, side[0], side[1])
    gained = swap(jnp.where(low_section, side[1], side[0]))
    feed_tables = [gather(table) for table in by_layer(keep, gained)]

    def split(table, sizes):
        cuts = [0]
        for size in sizes:
            cuts.append(cuts[-1] + size)
        return [table[:, a:b] for a, b in zip(cuts[:-1], cuts[1:])]

    small = [
        [part.astype(f32) for part in split(vector_layers[layer], vector_sizes)]
        for layer in range(2)
    ]
    adapters = []
    feed_packs = []
    for layer in range(2):
        sq, skv, ekv, eo, su, ed = split(
            shared_layers[layer], [width, width, 2 * head, width, width, width]
        )
        eu, sd = split(split_layers[layer], [local_f, local_f])
        adapters.append((sq, skv, ekv, eo))
        feed_packs.append(jnp.concatenate([su, eu, sd, ed], axis=1))

    inside = jnp.arange(rows, dtype=jnp.int32)
    query_place = data * span + tensor * rows + inside
    key_place = jnp.concatenate(
        [
            (data - back) * span + (tensor + j) % ranks * rows + inside
            for j in range(ranks)
            for back in range(reach, -1, -1)
        ]
    )
    lengths = lax.dynamic_index_in_dim(doc_lengths, section, 0, keepdims=False)
    ends = jnp.cumsum(lengths)
    query_doc = jnp.sum((query_place[:, None] >= ends[None, :]).astype(jnp.int32), axis=1)
    key_doc = jnp.sum((key_place[:, None] >= ends[None, :]).astype(jnp.int32), axis=1)
    distance = query_place[:, None] - key_place[None, :]
    allowed = (
        (key_place[None, :] >= 0)
        & (distance >= 0)
        & (distance < WINDOW)
        & (query_doc[:, None] == key_doc[None, :])
    )
    bias = jnp.where(allowed, 0.0, masked_score).astype(bf16)

    def forward_attend(layer, hidden):
        gain1, shift1, kv_bias, out_bias = small[layer][:4]
        sq, skv, ekv, eo = adapters[layer]
        unit1, rsd1 = norm_parts(hidden)
        normed = (unit1 * gain1 + shift1).astype(bf16)
        low_kv = against(normed, skv).astype(bf16)
        keyval = (plain(normed, keyval_ws[layer]) + kv_bias + plain(low_kv, ekv)).astype(bf16)
        pieces = [along(keyval, "dp", back) for back in range(reach, 0, -1)] + [keyval]
        key_block = spread(jnp.concatenate(pieces, axis=0))
        queries, low_q = project_queries(
            layer, normed, early_all, query_bias_all[layer][:1].astype(f32), eq_all[layer], sq
        )
        probs, mixed, low_o, attended = attend(
            layer, queries, key_block, bias, early_all, so_all[layer], eo, head
        )
        middle = hidden + (attended + out_bias)
        return middle, (unit1, rsd1, normed, low_q, low_kv, queries, key_block, probs, mixed, low_o)

    def feed_inputs(layer, middle):
        gain2, shift2, up_bias = small[layer][4:7]
        unit2, rsd2 = norm_parts(middle)
        second = spread((unit2 * gain2 + shift2).astype(bf16))
        return unit2, rsd2, second, up_bias

    def feed_result(layer, middle, partial):
        return middle + (reduce_rows(partial) + small[layer][7])

    def tiles(block):
        return block.reshape(rank, -1, 128).transpose(1, 0, 2)

    def flat(block):
        return block.transpose(1, 0, 2).reshape(rank, -1)

    turn, near = data // 4, data % 4

    def padded(pile, multiple):
        lack = -pile.shape[0] % multiple
        if not lack:
            return pile
        return jnp.concatenate([pile, jnp.zeros((lack,) + pile.shape[1:], pile.dtype)], axis=0)

    def piled(*groups):
        piles = [
            padded(jnp.concatenate([tiles(part) for part in group], axis=0), ranks) for group in groups
        ]
        return jnp.concatenate(
            [pile.reshape((ranks, -1) + pile.shape[1:]) for pile in piles], axis=1
        ).astype(bf16)

    def at(block, index, axis):
        return lax.dynamic_index_in_dim(block, index, axis, keepdims=False)

    def summed_ranks(pile):
        total = at(pile, tensor, 0).astype(f32)
        for j in range(1, ranks):
            block = at(pile, (tensor + j) % ranks, 0)
            total = total + around(block, "tensor", j).astype(f32)
        return total.astype(bf16)

    def summed_beside(pile):
        flat_pile = pile.reshape((-1,) + pile.shape[2:])
        return lax.psum_scatter(flat_pile, "tensor", scatter_dimension=0, tiled=True)

    def scattered_grads(layers):
        piles = [
            jnp.concatenate(mine + [tiles(part).astype(bf16) for part in owned], axis=0)
            for mine, owned in layers
        ]
        pile = jnp.stack([padded(block, lax.axis_size("dp")) for block in piles])
        pile = pile.reshape((2, chips, 4, -1) + pile.shape[2:])
        mine = at(pile, near, 2).astype(f32)
        for k in range(1, 4):
            mine = mine + flipped(at(pile, near ^ k, 2), "dp", k).astype(f32)
        pile = mine.astype(bf16)
        mine = at(pile, turn, 1).astype(f32)
        for k in range(1, chips):
            mine = mine + flipped(at(pile, turn ^ k, 1), "dp", 4 * k).astype(f32)
        return mine.astype(bf16)

    def spread_grads(zero, one, fed, attended, quartered, owned):
        own = jnp.where(low_section, zero, one)
        away = jnp.where(low_section, one, zero)
        dp_size = 4 * chips
        home = jnp.stack([own, flipped(own, "dp", 2)])
        guest = jnp.stack([crossed(away, dp_size), crossed(away, dp_size + 2)])
        home, guest = [
            jnp.where(near // 2 == 0, block, block[::-1]) for block in (home, guest)
        ]
        pair = jnp.where(
            low_section, jnp.stack([home, guest], axis=1), jnp.stack([guest, home], axis=1)
        )
        parts = jnp.stack([pair] + [flipped(pair, "dp", 4 * k) for k in range(1, chips)])
        parts = jnp.stack([at(parts, turn ^ k, 0) for k in range(chips)])
        other = flipped(parts, "dp", 1)
        core = near % 2
        parts = jnp.stack(
            [jnp.where(core == 0, parts, other), jnp.where(core == 0, other, parts)], axis=2
        )
        pile = jnp.moveaxis(parts, 3, 0).reshape((2, -1) + parts.shape[5:])
        fed_sizes, attended_sizes, quarter_sizes, owned_sizes = [
            [part.shape[1] // 128 // cut for part in group]
            for group, cut in [(fed, 1), (attended, 1), (quartered, ranks), (owned, 1)]
        ]
        counts = [-(-sum(sizes) // ranks) for sizes in (fed_sizes, attended_sizes)]
        each = sum(counts)
        own = pile[:, :each]
        parts = jnp.stack([own] + [around(own, "tensor", k) for k in range(1, ranks)])
        parts = [at(parts, (tensor - r) % ranks, 0) for r in range(ranks)]
        results = []
        for whole, begin, sizes in [
            (jnp.concatenate([part[:, : counts[0]] for part in parts], axis=1), 0, fed_sizes),
            (jnp.concatenate([part[:, counts[0] :] for part in parts], axis=1), 0, attended_sizes),
            (pile, each, quarter_sizes + owned_sizes),
        ]:
            for count in sizes:
                results.append([flat(whole[m, begin : begin + count]) for m in range(2)])
                begin += count
        return results

    def feed_grads(layer, grad, unit2, rsd2, partial):
        return grad + norm_back(unit2, rsd2, reduce_rows(partial) * small[layer][4])

    def feed_adapters(second, branch, low_u, low_d, inner_u, inner_d, active, grad_up):
        shared = [across(inner_u, second), across(low_d, branch)]
        owned = [across(low_u, grad_up), across(inner_d, active)]
        return shared, owned

    def backward_attend(layer, kept, grad_middle):
        gain1 = small[layer][0]
        sq, skv, ekv, eo = adapters[layer]
        unit1, rsd1, normed, low_q, low_kv, queries, key_block, probs, mixed, low_o = kept
        branch = grad_middle.astype(bf16)
        grad_q, grad_block, inner_o, inner_q, partial = attend_back(
            layer, branch, early_all, so_all[layer], eo, probs, queries, key_block,
            eq_all[layer], sq, head,
        )
        count = (reach + 1) * rows
        blocks = grad_block[:count].astype(f32)
        for j in range(1, ranks):
            part = grad_block[j * count : (j + 1) * count]
            blocks = blocks + around(part, "tensor", j).astype(f32)
        own = blocks[reach * rows :]
        for back in range(1, reach + 1):
            begin = (reach - back) * rows
            own = own + along(blocks[begin : begin + rows].astype(bf16), "dp", -back).astype(f32)
        grad_kv = own.astype(bf16)
        inner_kv = against(grad_kv, ekv).astype(bf16)
        grad_normed = partial + against(grad_kv, keyval_ws[layer]) + plain(inner_kv, skv)
        grad_hidden = grad_middle + norm_back(unit1, rsd1, grad_normed * gain1)
        shared = [
            across(low_o, branch),
            across(inner_q, normed),
            across(inner_kv, normed),
            across(low_kv, grad_kv),
        ]
        quartered = [across(low_q, grad_q), across(inner_o, mixed)]
        return grad_hidden, shared, quartered

    fresh = lax.dynamic_index_in_dim(block_input, section, 0, keepdims=False).astype(f32)
    given = lax.dynamic_index_in_dim(cotangent, section, 0, keepdims=False).astype(f32)
    middle_zero, kept_zero = forward_attend(0, fresh)
    unit_zero, rsd_zero, second_zero, up_bias = feed_inputs(0, middle_zero)
    own_rows, second_zero = lax.optimization_barrier((given.astype(bf16), second_zero))
    branch_one = spread(own_rows)
    second_zero, branch_one = lax.optimization_barrier((second_zero, branch_one))
    active_zero, slope_zero, low_u_zero, low_d_zero, partial = feed_call(
        feed_kernel,
        "feed",
        (second_zero, feed_tables[0], up_bias, feed_packs[0]),
        (3,),
        (local_f, local_f, rank, rank, width),
        local_f,
        2,
    )
    passed = feed_result(0, middle_zero, partial).astype(bf16)

    middle_one, kept_one = forward_attend(1, passed.astype(f32))
    unit_one, rsd_one, second_one, up_bias = feed_inputs(1, middle_one)
    active, low_u, low_d, partial, grad_up, inner_d, inner_u, partial_back = feed_call(
        feed_both_kernel,
        "feed_both",
        (second_one, branch_one, feed_tables[1], up_bias, feed_packs[1]),
        (4, 1),
        (local_f, rank, rank, width, local_f, rank, rank, width),
        local_f,
        4,
    )
    grad_middle = feed_grads(1, given, unit_one, rsd_one, partial_back)
    shared, owned = feed_adapters(
        second_one, branch_one, low_u, low_d, inner_u, inner_d, active, grad_up
    )
    grad_one, attended, quartered = backward_attend(1, kept_one, grad_middle)
    pile = piled(shared, attended, *[[part] for part in quartered])
    layer_one = ([summed_beside(pile)], owned)
    partial, _ = lax.optimization_barrier((partial, grad_middle))
    final = feed_result(1, middle_one, partial).astype(bf16)

    branch_zero = spread(grad_one.astype(bf16))
    grad_up, inner_d, inner_u, partial_back = feed_call(
        feed_back_kernel,
        "feed_back",
        (branch_zero, feed_tables[0], slope_zero, feed_packs[0]),
        (3, 2),
        (local_f, rank, rank, width),
        local_f,
        2,
    )
    grad_middle_zero = feed_grads(0, grad_one, unit_zero, rsd_zero, partial_back)
    shared, owned = feed_adapters(
        second_zero,
        branch_zero,
        low_u_zero,
        low_d_zero,
        inner_u,
        inner_d,
        active_zero,
        grad_up,
    )
    fed_mine = summed_beside(piled(shared))
    grad_zero, attended, quartered = backward_attend(0, kept_zero, grad_middle_zero)
    mine = summed_ranks(piled(attended, *[[part] for part in quartered]))
    mine = scattered_grads([([fed_mine, mine], owned), layer_one])
    grads = spread_grads(mine[0], mine[1], shared, attended, quartered, owned)

    def both_micros(zero, one, kind):
        own = jnp.where(low_section, zero, one)
        received = swap(jnp.where(low_section, one, zero).astype(bf16)).astype(kind)
        return jnp.where(low_section, jnp.stack([own, received]), jnp.stack([received, own]))

    passed, final, _ = lax.optimization_barrier((passed, final, grad_middle_zero))
    section_outputs = both_micros(passed, final, bf16)
    input_grads = both_micros(grad_zero, grad_one, f32)
    onehot = (bank_choice[:, None] == jnp.arange(banks)[None, :]).astype(f32)

    def placed(pair, transpose):
        out = sum(
            onehot[m][:, None, None] * pair[m].astype(f32)[None] for m in range(2)
        )
        return (out.transpose(0, 2, 1) if transpose else out)[None]

    (
        up_shrink_grad,
        down_expand_grad,
        out_expand_grad,
        q_shrink_grad,
        kv_shrink_grad,
        kv_expand_grad,
        q_expand_grad,
        out_shrink_grad,
        up_expand_grad,
        down_shrink_grad,
    ) = grads
    return (
        section_outputs[None],
        input_grads[None],
        placed(q_shrink_grad, True),
        placed(q_expand_grad, False),
        placed(kv_shrink_grad, True),
        placed(kv_expand_grad, False),
        placed(out_shrink_grad, True),
        placed(out_expand_grad, False),
        placed(up_shrink_grad, True),
        placed(up_expand_grad, False),
        placed(down_shrink_grad, True),
        placed(down_expand_grad, False),
    )


def solution(mesh):
    return jax.shard_map(
        per_device,
        mesh=mesh,
        in_specs=(
            P(None, ("dp", "tensor"), None),
            P(None, ("dp", "tensor"), None),
            P(),
            P(),
            P("section", None),
            P("section", None),
            P("section", "dp", "tensor"),
            P("section", "tensor"),
            P("section", "dp", None),
            P("section", None),
            P("section", "tensor", "dp"),
            P("section", None),
            P("section", None),
            P("section", None),
            P("section", "dp", "tensor"),
            P("section", "tensor"),
            P("section", "tensor", "dp"),
            P("section", None),
            P("section", None, None, None),
            P("section", None, None, "tensor"),
            P("section", None, None, None),
            P("section", None, None, None),
            P("section", None, "tensor", None),
            P("section", None, None, None),
            P("section", None, None, None),
            P("section", None, None, "tensor"),
            P("section", None, "tensor", None),
            P("section", None, None, None),
        ),
        out_specs=(
            P("section", None, ("dp", "tensor"), None),
            P("section", None, ("dp", "tensor"), None),
            P("section", None, None, None),
            P("section", None, None, "tensor"),
            P("section", None, None, None),
            P("section", None, None, None),
            P("section", None, "tensor", None),
            P("section", None, None, None),
            P("section", None, None, None),
            P("section", None, None, "tensor"),
            P("section", None, "tensor", None),
            P("section", None, None, None),
        ),
        check_vma=False,
    )
```

```python
import math

import jax
import jax.numpy as jnp
from jax import lax
from jax.experimental import pallas as pl
from jax.experimental.layout import Layout, with_layout_constraint
from jax.experimental.pallas import tpu as pltpu
from jax.sharding import PartitionSpec as P

WINDOW = 1024
epsilon = 1e-05
masked_score = -1e30
bf16 = jnp.bfloat16
f32 = jnp.float32


def plain(left, right):
    return jnp.dot(left, right, preferred_element_type=f32)


def against(left, right):
    return lax.dot_general(left, right, (((1,), (1,)), ((), ())), preferred_element_type=f32)


def across(left, right):
    return lax.dot_general(left, right, (((0,), (0,)), ((), ())), preferred_element_type=f32)


def around(block, axis, distance):
    size = lax.axis_size(axis)
    return lax.ppermute(block, axis, [(i, (i + distance) % size) for i in range(size)])


def along(block, axis, distance):
    size = lax.axis_size(axis)
    route = [(i, i + distance) for i in range(size) if 0 <= i + distance < size]
    return lax.ppermute(block, axis, route)


def flipped(block, axis, bit):
    size = lax.axis_size(axis)
    return lax.ppermute(block, axis, [(i, i ^ bit) for i in range(size)])


def pick(table, index, size=1):
    return lax.dynamic_slice_in_dim(table, index, size, 0)


def norm_parts(value):
    centred = value - jnp.mean(value, axis=-1, keepdims=True)
    spread = lax.rsqrt(jnp.mean(centred * centred, axis=-1, keepdims=True) + epsilon)
    return centred * spread, spread


def norm_back(unit, spread, scaled):
    inner = jnp.mean(scaled * unit, axis=-1, keepdims=True)
    return spread * (scaled - jnp.mean(scaled, axis=-1, keepdims=True) - unit * inner)


def gelu_parts(value):
    rate = math.sqrt(2.0 / math.pi)
    square = value * value
    bend = jnp.tanh(rate * (value + 0.044715 * value * square))
    rising = 0.5 * (1.0 + bend)
    slope = rising + 0.5 * value * (1.0 - bend * bend) * (rate * (1.0 + 3 * 0.044715 * square))
    return value * rising, slope


def side_blocks(query_ref, group, head):
    begin = group * 4 * head
    return jnp.concatenate(
        [query_ref[:, begin + h * head : begin + (h + 1) * head] for h in range(4)], axis=0
    )


def put_blocks(out_ref, value, group, head):
    rows = value.shape[0] // 4
    for h in range(4):
        begin = (group * 4 + h) * head
        out_ref[:, begin : begin + head] = value[h * rows : (h + 1) * rows]


def table_copies(table_ref, buf, sem, layer, begin):
    ranks, chunks, _, width = buf.shape
    return [
        pltpu.make_async_copy(
            table_ref.at[x, y, layer, :, pl.ds(begin, width)], buf.at[x, y], sem.at[x, y]
        )
        for x in range(ranks)
        for y in range(chunks)
    ]


def query_kernel(layer, normed_ref, table_ref, bias_ref, eq_ref, sq_ref, out_ref, low_ref, buf, sem):
    ranks, chunks, rows, width = buf.shape
    copies = table_copies(table_ref, buf, sem, layer, 0)
    for copy in copies:
        copy.start()
    normed = normed_ref[...]
    low = against(normed, sq_ref[...]).astype(bf16)
    low_ref[...] = low
    for x in range(ranks):
        columns = pl.ds(x * width, width)
        total = bias_ref[:, columns] + plain(low, eq_ref[:, columns])
        for y in range(chunks):
            copies[x * chunks + y].wait()
            total = total + plain(normed[:, y * rows : (y + 1) * rows], buf[x, y])
        out_ref[:, columns] = total.astype(bf16)


def table_scratch(table, width):
    ranks, chunks, _, rows, _ = table.shape
    return [
        pltpu.VMEM((ranks, chunks, rows, width), bf16),
        pltpu.SemaphoreType.DMA((ranks, chunks)),
    ]


held = pl.BlockSpec(memory_space=pltpu.VMEM)
remote = pl.BlockSpec(memory_space=pl.ANY)


def project_queries(layer, normed, table, bias, eq, sq):
    rows, model = normed.shape
    rank = sq.shape[0]
    width = model // table.shape[0]
    return pl.pallas_call(
        lambda *refs: query_kernel(layer, *refs),
        in_specs=[held, remote, held, held, held],
        out_specs=[held] * 2,
        out_shape=[
            jax.ShapeDtypeStruct((rows, model), bf16),
            jax.ShapeDtypeStruct((rows, rank), bf16),
        ],
        scratch_shapes=table_scratch(table, width),
        compiler_params=pltpu.CompilerParams(vmem_limit_bytes=28 * 2**20),
        cost_estimate=pl.CostEstimate(
            flops=8 * rows * model * model, bytes_accessed=2 * model * model, transcendentals=0
        ),
        name="project_queries",
    )(normed, table, bias, eq, sq)


def attend_kernel(
    layer, head, query_ref, keyval_ref, bias_ref, table_ref, so_ref, eo_ref,
    prob_ref, mixed_ref, low_ref, out_ref, buf, sem,
):
    ranks, chunks, rows, width = buf.shape
    copies = table_copies(table_ref, buf, sem, layer, width)
    for copy in copies:
        copy.start()
    scale = 1.0 / math.sqrt(head)
    bias = jnp.concatenate([bias_ref[...].astype(f32)] * 4, axis=0)
    for g in range(prob_ref.shape[0]):
        queries = side_blocks(query_ref, g, head)
        scores = against(queries, keyval_ref[:, :head]) * scale + bias
        lifted = jnp.exp(scores - jnp.max(scores, axis=-1, keepdims=True))
        probs = (lifted * (1.0 / jnp.sum(lifted, axis=-1, keepdims=True))).astype(bf16)
        prob_ref[g] = probs
        put_blocks(mixed_ref, plain(probs, keyval_ref[:, head:]).astype(bf16), g, head)
    mixed = mixed_ref[...]
    low = against(mixed, so_ref[...]).astype(bf16)
    low_ref[...] = low
    for copy in copies:
        copy.wait()
    for y in range(chunks):
        columns = pl.ds(y * rows, rows)
        total = plain(low, eo_ref[:, columns])
        for x in range(ranks):
            total = total + against(mixed[:, x * width : (x + 1) * width], buf[x, y])
        out_ref[:, columns] = total


def attend(layer, queries, key_block, bias, table, so, eo, head):
    rows, model = queries.shape
    keys = key_block.shape[0]
    groups = model // head // 4
    rank = so.shape[0]
    return pl.pallas_call(
        lambda *refs: attend_kernel(layer, head, *refs),
        in_specs=[held, held, held, remote, held, held],
        out_specs=[held] * 4,
        out_shape=[
            jax.ShapeDtypeStruct((groups, 4 * rows, keys), bf16),
            jax.ShapeDtypeStruct((rows, model), bf16),
            jax.ShapeDtypeStruct((rows, rank), bf16),
            jax.ShapeDtypeStruct((rows, model), f32),
        ],
        scratch_shapes=table_scratch(table, model // table.shape[0]),
        compiler_params=pltpu.CompilerParams(vmem_limit_bytes=36 * 2**20),
        cost_estimate=pl.CostEstimate(
            flops=4 * rows * model * (keys + 2 * model),
            bytes_accessed=2 * model * model,
            transcendentals=groups * 4 * rows * keys,
        ),
        name="attend",
    )(queries, key_block, bias, table, so, eo)


def attend_back_kernel(
    layer, head, branch_ref, table_ref, so_ref, eo_ref, prob_ref, query_ref, keyval_ref, eq_ref, sq_ref,
    dq_ref, dkv_ref, inner_o_ref, inner_q_ref, part_ref,
    out_buf, out_sem, query_buf, query_sem, mixed_buf, key_sum, value_sum,
):
    ranks, chunks, rows, width = out_buf.shape
    out_copies = table_copies(table_ref, out_buf, out_sem, layer, width)
    query_copies = table_copies(table_ref, query_buf, query_sem, layer, 0)
    for copy in out_copies + query_copies:
        copy.start()
    scale = 1.0 / math.sqrt(head)
    branch = branch_ref[...]
    inner_o = against(branch, eo_ref[...]).astype(bf16)
    inner_o_ref[...] = inner_o
    for g in range(prob_ref.shape[0]):
        columns = pl.ds(g * width, width)
        total = plain(inner_o, so_ref[:, columns])
        for y in range(chunks):
            out_copies[g * chunks + y].wait()
            total = total + plain(branch[:, y * rows : (y + 1) * rows], out_buf[g, y])
        mixed_buf[:, columns] = total.astype(bf16)
        grad = side_blocks(mixed_buf, g, head)
        low_probs = prob_ref[g]
        probs = low_probs.astype(f32)
        grad_probs = against(grad, keyval_ref[:, head:])
        delta = jnp.sum(grad_probs * probs, axis=-1, keepdims=True)
        delta = delta / jnp.sum(probs, axis=-1, keepdims=True)
        grad_scores = (probs * (grad_probs - delta)).astype(bf16)
        put_blocks(dq_ref, (plain(grad_scores, keyval_ref[:, :head]) * scale).astype(bf16), g, head)
        keys = across(grad_scores, side_blocks(query_ref, g, head))
        values = across(low_probs, grad)
        if g == 0:
            key_sum[...] = keys
            value_sum[...] = values
        else:
            key_sum[...] += keys
            value_sum[...] += values
    dkv_ref[:, :head] = (key_sum[...] * scale).astype(bf16)
    dkv_ref[:, head:] = value_sum[...].astype(bf16)
    grad_q = dq_ref[...]
    inner_q = against(grad_q, eq_ref[...]).astype(bf16)
    inner_q_ref[...] = inner_q
    for copy in query_copies:
        copy.wait()
    for y in range(chunks):
        columns = pl.ds(y * rows, rows)
        total = plain(inner_q, sq_ref[:, columns])
        for x in range(ranks):
            total = total + against(grad_q[:, x * width : (x + 1) * width], query_buf[x, y])
        part_ref[:, columns] = total


def attend_back(layer, branch, table, so, eo, probs, queries, key_block, eq, sq, head):
    rows, model = queries.shape
    keys = key_block.shape[0]
    groups = probs.shape[0]
    rank = so.shape[0]
    width = model // table.shape[0]
    return pl.pallas_call(
        lambda *refs: attend_back_kernel(layer, head, *refs),
        in_specs=[held, remote] + [held] * 7,
        out_specs=[held] * 5,
        out_shape=[
            jax.ShapeDtypeStruct((rows, model), bf16),
            jax.ShapeDtypeStruct((keys, 2 * head), bf16),
            jax.ShapeDtypeStruct((rows, rank), bf16),
            jax.ShapeDtypeStruct((rows, rank), bf16),
            jax.ShapeDtypeStruct((rows, model), f32),
        ],
        scratch_shapes=table_scratch(table, width)
        + table_scratch(table, width)
        + [
            pltpu.VMEM((rows, model), bf16),
            pltpu.VMEM((keys, head), f32),
            pltpu.VMEM((keys, head), f32),
        ],
        compiler_params=pltpu.CompilerParams(vmem_limit_bytes=44 * 2**20),
        cost_estimate=pl.CostEstimate(
            flops=8 * rows * model * (keys + 2 * model),
            bytes_accessed=4 * model * model + 4 * groups * 4 * rows * keys,
            transcendentals=0,
        ),
        name="attend_back",
    )(branch, table, so, eo, probs, queries, key_block, eq, sq)


def feed_copies(table_ref, buf, sems):
    _, count, chunks, rows, tile = buf.shape
    half = count // 2 * tile
    copies = []
    for j in range(count):
        pair = []
        for k in range(2):
            columns = pl.ds(j * tile % half + k * half, tile)
            pair.append(
                pltpu.make_async_copy(
                    table_ref.at[:, j * tile // half, :, columns], buf.at[k, j], sems.at[k, j]
                )
            )
        copies.append(pair)
    return copies


def plain_chunks(left, buf, k, j):
    rows = buf.shape[3]
    return sum(plain(left[:, i * rows : (i + 1) * rows], buf[k, j, i]) for i in range(buf.shape[2]))


def against_chunk(left_ref, buf, k, i):
    tile = buf.shape[4]
    return sum(
        against(left_ref[:, j * tile : (j + 1) * tile], buf[k, j, i]) for j in range(buf.shape[1])
    )


def own_copies(sources, buffers, sems):
    copies = [
        pltpu.make_async_copy(source, buffer, sems.at[i])
        for i, (source, buffer) in enumerate(zip(sources, buffers))
    ]
    for copy in copies:
        copy.start()
    return copies


def feed_pack(pack_ref, model, hidden):
    cuts = [0, model, model + hidden, model + 2 * hidden, 2 * model + 2 * hidden]
    return [pack_ref.at[:, a:b] for a, b in zip(cuts[:-1], cuts[1:])]


def feed_kernel(
    second_ref, table_ref, bias_ref, pack_ref,
    active_ref, slope_ref, low_u_ref, low_d_ref, out_ref, buf, sems, pack_buf, own_sems,
):
    _, count, chunks, rows, tile = buf.shape
    su_ref, eu_ref, sd_ref, ed_ref = feed_pack(pack_buf, chunks * rows, count * tile)
    copies = feed_copies(table_ref, buf, sems)
    own = own_copies([pack_ref], [pack_buf], own_sems)
    for up, _ in copies:
        up.start()
    for _, down in copies:
        down.start()
    second = second_ref[...]
    own[0].wait()
    low_u = against(second, su_ref[...]).astype(bf16)
    low_u_ref[...] = low_u
    for j in range(count):
        columns = pl.ds(j * tile, tile)
        copies[j][0].wait()
        upward = plain_chunks(second, buf, 0, j)
        upward = upward + plain(low_u, eu_ref[:, columns]) + bias_ref[:, columns]
        active, slope = gelu_parts(upward)
        active_ref[:, columns] = active.astype(bf16)
        slope_ref[:, columns] = slope.astype(bf16)
    low_d = against(active_ref[...], sd_ref[...]).astype(bf16)
    low_d_ref[...] = low_d
    for _, down in copies:
        down.wait()
    for i in range(chunks):
        columns = pl.ds(i * rows, rows)
        out_ref[:, columns] = (
            against_chunk(active_ref, buf, 1, i) + plain(low_d, ed_ref[:, columns])
        ).astype(bf16)


def feed_back_kernel(
    branch_ref, table_ref, slope_ref, pack_ref,
    grad_up_ref, inner_d_ref, inner_u_ref, out_ref, buf, sems, pack_buf, slope_buf, own_sems,
):
    _, count, chunks, rows, tile = buf.shape
    su_ref, eu_ref, sd_ref, ed_ref = feed_pack(pack_buf, chunks * rows, count * tile)
    copies = feed_copies(table_ref, buf, sems)
    own = own_copies([pack_ref, slope_ref], [pack_buf, slope_buf], own_sems)
    for _, down in copies:
        down.start()
    for up, _ in copies:
        up.start()
    branch = branch_ref[...]
    own[0].wait()
    inner_d = against(branch, ed_ref[...]).astype(bf16)
    inner_d_ref[...] = inner_d
    own[1].wait()
    for j in range(count):
        columns = pl.ds(j * tile, tile)
        copies[j][1].wait()
        grad = plain_chunks(branch, buf, 1, j) + plain(inner_d, sd_ref[:, columns])
        grad_up_ref[:, columns] = (grad * slope_buf[:, columns].astype(f32)).astype(bf16)
    inner_u = against(grad_up_ref[...], eu_ref[...]).astype(bf16)
    inner_u_ref[...] = inner_u
    for up, _ in copies:
        up.wait()
    for i in range(chunks):
        columns = pl.ds(i * rows, rows)
        out_ref[:, columns] = (
            against_chunk(grad_up_ref, buf, 0, i) + plain(inner_u, su_ref[:, columns])
        ).astype(bf16)


def feed_both_kernel(
    second_ref, branch_ref, table_ref, bias_ref, pack_ref,
    active_ref, low_u_ref, low_d_ref, out_ref, grad_up_ref, inner_d_ref, inner_u_ref, back_ref,
    buf, sems, pack_buf, branch_buf, own_sems,
):
    _, count, chunks, rows, tile = buf.shape
    su_ref, eu_ref, sd_ref, ed_ref = feed_pack(pack_buf, chunks * rows, count * tile)
    copies = feed_copies(table_ref, buf, sems)
    own = own_copies([pack_ref, branch_ref], [pack_buf, branch_buf], own_sems)
    for up, down in copies:
        up.start()
        down.start()
    second = second_ref[...]
    for copy in own:
        copy.wait()
    branch = branch_buf[...]
    low_u = against(second, su_ref[...]).astype(bf16)
    low_u_ref[...] = low_u
    inner_d = against(branch, ed_ref[...]).astype(bf16)
    inner_d_ref[...] = inner_d
    for j in range(count):
        columns = pl.ds(j * tile, tile)
        copies[j][0].wait()
        upward = plain_chunks(second, buf, 0, j)
        upward = upward + plain(low_u, eu_ref[:, columns]) + bias_ref[:, columns]
        active, slope = gelu_parts(upward)
        active_ref[:, columns] = active.astype(bf16)
        copies[j][1].wait()
        grad = plain_chunks(branch, buf, 1, j) + plain(inner_d, sd_ref[:, columns])
        grad_up_ref[:, columns] = (grad * slope).astype(bf16)
    inner_u = against(grad_up_ref[...], eu_ref[...]).astype(bf16)
    inner_u_ref[...] = inner_u
    low_d = against(active_ref[...], sd_ref[...]).astype(bf16)
    low_d_ref[...] = low_d
    for i in range(chunks):
        columns = pl.ds(i * rows, rows)
        back_ref[:, columns] = (
            against_chunk(grad_up_ref, buf, 0, i) + plain(inner_u, su_ref[:, columns])
        ).astype(bf16)
        out_ref[:, columns] = (
            against_chunk(active_ref, buf, 1, i) + plain(low_d, ed_ref[:, columns])
        ).astype(bf16)


def feed_call(kernel, name, inputs, copied, outputs, hidden, matmuls):
    table = [value for value in inputs if value.ndim == 4][0]
    rows, model = inputs[0].shape
    tile = 512
    chunks = table.shape[0]
    return pl.pallas_call(
        kernel,
        in_specs=[
            remote if value.ndim == 4 or i in copied else held for i, value in enumerate(inputs)
        ],
        out_specs=[held] * len(outputs),
        out_shape=[jax.ShapeDtypeStruct((rows, width), bf16) for width in outputs],
        scratch_shapes=[
            pltpu.VMEM((2, hidden // tile, chunks, model // chunks, tile), bf16),
            pltpu.SemaphoreType.DMA((2, hidden // tile)),
        ]
        + [pltpu.VMEM(inputs[i].shape, bf16) for i in copied]
        + [pltpu.SemaphoreType.DMA((len(copied),))],
        compiler_params=pltpu.CompilerParams(vmem_limit_bytes=44 * 2**20),
        cost_estimate=pl.CostEstimate(
            flops=2 * matmuls * rows * model * hidden,
            bytes_accessed=4 * model * hidden,
            transcendentals=rows * hidden,
        ),
        name=name,
    )(*inputs)


def per_device(
    block_input,
    cotangent,
    doc_lengths,
    bank_choice,
    first_gain,
    first_shift,
    query_weight,
    query_bias,
    keyval_weight,
    value_bias,
    output_weight,
    output_bias,
    second_gain,
    second_shift,
    upward_weight,
    upward_bias,
    downward_weight,
    downward_bias,
    query_shrink,
    query_expand,
    keyval_shrink,
    keyval_expand,
    output_shrink,
    output_expand,
    upward_shrink,
    upward_expand,
    downward_shrink,
    downward_expand,
):
    section = lax.axis_index("section")
    data = lax.axis_index("dp")
    tensor = lax.axis_index("tensor")
    low_section = section == 0
    width = block_input.shape[2]
    rows = block_input.shape[1]
    ranks = lax.axis_size("tensor")
    span = rows * ranks
    head = value_bias.shape[1]
    local_q = query_bias.shape[1]
    local_f = upward_bias.shape[1]
    rank = query_expand.shape[2]
    banks = query_expand.shape[1]
    reach = WINDOW // span
    sides = [(0, 1), (1, 0)]

    def swap(value):
        return lax.ppermute(value, "section", sides)

    def by_layer(own, other):
        return jnp.where(low_section, own, other), jnp.where(low_section, other, own)

    def spread(block):
        parts = [block] + [around(block, "tensor", -j) for j in range(1, ranks)]
        return jnp.concatenate(parts, axis=0)

    def reduce_rows(partial):
        low = partial.astype(bf16)
        total = partial[:rows].astype(f32)
        for j in range(1, ranks):
            total = total + around(low[j * rows : (j + 1) * rows], "tensor", j).astype(f32)
        return total

    own_bank = lax.dynamic_index_in_dim(bank_choice, section, 0, keepdims=False)
    other_bank = lax.dynamic_index_in_dim(bank_choice, 1 - section, 0, keepdims=False)

    chips = lax.axis_size("dp") // 4
    both = ("section", "dp")
    every = ("section", "dp", "tensor")
    order = [
        side * 4 * chips + chip * 4 + near
        for chip in range(chips)
        for side in range(2)
        for near in range(4)
    ]
    order_all = [place * ranks + x for x in range(ranks) for place in order]

    def row_major(block):
        return with_layout_constraint(block, Layout(major_to_minor=(0, 1)))

    def gather(shard):
        table = lax.all_gather(row_major(shard), both, axis=0, tiled=True, axis_index_groups=[order])
        return row_major(table).reshape(chips, 2, -1, shard.shape[1])

    def gather_all(shard):
        table = lax.all_gather(
            row_major(shard), every, axis=0, tiled=True, axis_index_groups=[order_all]
        )
        return row_major(table).reshape(ranks, chips, 2, -1, shard.shape[1])

    def halves(shard):
        cut = shard.shape[1] // 2
        return shard[:, :cut], shard[:, cut:]

    keyval_half = jnp.where(tensor % 2 == 0, keyval_weight[0][:, :head], keyval_weight[0][:, head:])
    early_all = gather_all(
        jnp.concatenate([query_weight[0], row_major(output_weight[0].T), keyval_half], axis=1)
    )
    keyval_ws = [
        jnp.concatenate(
            [early_all[x, :, layer, :, 2 * local_q :].reshape(width, head) for x in range(2)], axis=1
        )
        for layer in range(2)
    ]

    def crossed(block, mask):
        return lax.ppermute(block, both, [(i, i ^ mask) for i in range(8 * chips)])

    vectors = jnp.concatenate(
        [
            first_gain,
            first_shift,
            jnp.zeros_like(value_bias),
            value_bias,
            output_bias,
            second_gain,
            second_shift,
            upward_bias,
            downward_bias,
        ],
        axis=1,
    )
    vector_sizes = [width, width, 2 * head, width, width, width, local_f, width]
    vector_layers = by_layer(vectors, swap(vectors))

    def chosen(table, bank, transpose):
        block = lax.dynamic_index_in_dim(table[0], bank, 0, keepdims=False)
        return block.T if transpose else block

    def pack(bank, parts):
        return jnp.concatenate([chosen(table, bank, flip) for table, flip in parts], axis=1)

    cut_parts = [(query_expand, False), (output_shrink, True)]
    whole_parts = [
        (query_shrink, True),
        (keyval_shrink, True),
        (keyval_expand, False),
        (output_expand, False),
        (upward_shrink, True),
        (upward_expand, False),
        (downward_shrink, True),
        (downward_expand, False),
    ]
    query_rows = jnp.broadcast_to(query_bias, (rank, local_q))

    def cut_pack(bank):
        return jnp.concatenate([pack(bank, cut_parts), query_rows], axis=1)

    shared_parts = [part for part in whole_parts if part[0] is not upward_expand and part[0] is not downward_shrink]
    split_parts = [(upward_expand, False), (downward_shrink, True)]
    shared_away = pack(other_bank, shared_parts)
    quarter = shared_away.shape[1] // ranks
    crossing = jnp.concatenate(
        [
            cut_pack(other_bank),
            lax.dynamic_slice_in_dim(shared_away, tensor * quarter, quarter, 1),
            pack(other_bank, split_parts),
        ],
        axis=1,
    )
    crossed_pack = swap(crossing)
    cut_width = 3 * local_q
    block = jnp.concatenate([cut_pack(own_bank), crossed_pack[:, : cut_width + quarter]], axis=1)
    blocks = jnp.stack([block] + [around(block, "tensor", j) for j in range(1, ranks)])
    blocks = [
        lax.dynamic_index_in_dim(blocks, (tensor - r) % ranks, 0, keepdims=False)
        for r in range(ranks)
    ]

    def joined(begin, size):
        return jnp.concatenate([block[:, begin : begin + size] for block in blocks], axis=1)

    cut_layers = [
        by_layer(joined(k * local_q, local_q), joined(cut_width + k * local_q, local_q))
        for k in range(3)
    ]
    eq_all, so_all, query_bias_all = cut_layers
    shared_layers = by_layer(pack(own_bank, shared_parts), joined(2 * cut_width, quarter))
    split_layers = by_layer(pack(own_bank, split_parts), crossed_pack[:, cut_width + quarter :])

    up_halves = halves(upward_weight[0])
    down_halves = halves(row_major(downward_weight[0].T))
    side = [jnp.concatenate([up_halves[h], down_halves[h]], axis=1) for h in range(2)]
    keep = jnp.where(low_section, side[0], side[1])
    gained = swap(jnp.where(low_section, side[1], side[0]))
    feed_tables = [gather(table) for table in by_layer(keep, gained)]

    def split(table, sizes):
        cuts = [0]
        for size in sizes:
            cuts.append(cuts[-1] + size)
        return [table[:, a:b] for a, b in zip(cuts[:-1], cuts[1:])]

    small = [
        [part.astype(f32) for part in split(vector_layers[layer], vector_sizes)]
        for layer in range(2)
    ]
    adapters = []
    feed_packs = []
    for layer in range(2):
        sq, skv, ekv, eo, su, ed = split(
            shared_layers[layer], [width, width, 2 * head, width, width, width]
        )
        eu, sd = split(split_layers[layer], [local_f, local_f])
        adapters.append((sq, skv, ekv, eo))
        feed_packs.append(jnp.concatenate([su, eu, sd, ed], axis=1))

    inside = jnp.arange(rows, dtype=jnp.int32)
    query_place = data * span + tensor * rows + inside
    key_place = jnp.concatenate(
        [
            (data - back) * span + (tensor + j) % ranks * rows + inside
            for j in range(ranks)
            for back in range(reach, -1, -1)
        ]
    )
    lengths = lax.dynamic_index_in_dim(doc_lengths, section, 0, keepdims=False)
    ends = jnp.cumsum(lengths)
    query_doc = jnp.sum((query_place[:, None] >= ends[None, :]).astype(jnp.int32), axis=1)
    key_doc = jnp.sum((key_place[:, None] >= ends[None, :]).astype(jnp.int32), axis=1)
    distance = query_place[:, None] - key_place[None, :]
    allowed = (
        (key_place[None, :] >= 0)
        & (distance >= 0)
        & (distance < WINDOW)
        & (query_doc[:, None] == key_doc[None, :])
    )
    bias = jnp.where(allowed, 0.0, masked_score).astype(bf16)

    def forward_attend(layer, hidden):
        gain1, shift1, kv_bias, out_bias = small[layer][:4]
        sq, skv, ekv, eo = adapters[layer]
        unit1, rsd1 = norm_parts(hidden)
        normed = (unit1 * gain1 + shift1).astype(bf16)
        low_kv = against(normed, skv).astype(bf16)
        keyval = (plain(normed, keyval_ws[layer]) + kv_bias + plain(low_kv, ekv)).astype(bf16)
        pieces = [along(keyval, "dp", back) for back in range(reach, 0, -1)] + [keyval]
        key_block = spread(jnp.concatenate(pieces, axis=0))
        queries, low_q = project_queries(
            layer, normed, early_all, query_bias_all[layer][:1].astype(f32), eq_all[layer], sq
        )
        probs, mixed, low_o, attended = attend(
            layer, queries, key_block, bias, early_all, so_all[layer], eo, head
        )
        middle = hidden + (attended + out_bias)
        return middle, (unit1, rsd1, normed, low_q, low_kv, queries, key_block, probs, mixed, low_o)

    def feed_inputs(layer, middle):
        gain2, shift2, up_bias = small[layer][4:7]
        unit2, rsd2 = norm_parts(middle)
        second = spread((unit2 * gain2 + shift2).astype(bf16))
        return unit2, rsd2, second, up_bias

    def feed_result(layer, middle, partial):
        return middle + (reduce_rows(partial) + small[layer][7])

    def tiles(block):
        return block.reshape(rank, -1, 128).transpose(1, 0, 2)

    def flat(block):
        return block.transpose(1, 0, 2).reshape(rank, -1)

    turn, near = data // 4, data % 4

    def padded(pile, multiple):
        lack = -pile.shape[0] % multiple
        if not lack:
            return pile
        return jnp.concatenate([pile, jnp.zeros((lack,) + pile.shape[1:], pile.dtype)], axis=0)

    def piled(shared, quartered):
        pile = padded(jnp.concatenate([tiles(part) for part in shared], axis=0), ranks)
        return jnp.concatenate(
            [block.reshape((ranks, -1) + block.shape[1:]) for block in [pile] + [tiles(part) for part in quartered]],
            axis=1,
        ).astype(bf16)

    def owned_pile(mine, owned):
        pile = jnp.concatenate([mine] + [tiles(part) for part in owned], axis=0).astype(bf16)
        return padded(pile, lax.axis_size("dp"))

    def at(block, index, axis):
        return lax.dynamic_index_in_dim(block, index, axis, keepdims=False)

    def scattered_grads(layers):
        pile = jnp.stack([piled(shared, quartered) for shared, quartered, _ in layers], axis=1)
        mine = at(pile, tensor, 0).astype(f32)
        for j in range(1, ranks):
            mine = mine + around(at(pile, (tensor + j) % ranks, 0), "tensor", j).astype(f32)
        pile = jnp.stack([owned_pile(mine[i], layers[i][2]) for i in range(2)])
        pile = pile.reshape((2, chips, 4, -1) + pile.shape[2:])
        mine = at(pile, near, 2).astype(f32)
        for k in range(1, 4):
            mine = mine + flipped(at(pile, near ^ k, 2), "dp", k).astype(f32)
        pile = mine.astype(bf16)
        mine = at(pile, turn, 1).astype(f32)
        for k in range(1, chips):
            mine = mine + flipped(at(pile, turn ^ k, 1), "dp", 4 * k).astype(f32)
        return mine.astype(bf16)

    def spread_grads(zero, one, shared, quartered, owned):
        own = jnp.where(low_section, zero, one)
        away = jnp.where(low_section, one, zero)
        dp_size = 4 * chips
        home = jnp.stack([own, flipped(own, "dp", 2)])
        guest = jnp.stack([crossed(away, dp_size), crossed(away, dp_size + 2)])
        home, guest = [
            jnp.where(near // 2 == 0, block, block[::-1]) for block in (home, guest)
        ]
        pair = jnp.where(
            low_section, jnp.stack([home, guest], axis=1), jnp.stack([guest, home], axis=1)
        )
        parts = jnp.stack([pair] + [flipped(pair, "dp", 4 * k) for k in range(1, chips)])
        parts = jnp.stack([at(parts, turn ^ k, 0) for k in range(chips)])
        other = flipped(parts, "dp", 1)
        core = near % 2
        parts = jnp.stack(
            [jnp.where(core == 0, parts, other), jnp.where(core == 0, other, parts)], axis=2
        )
        pile = jnp.moveaxis(parts, 3, 0).reshape((2, -1) + parts.shape[5:])
        shared_sizes = [part.shape[1] // 128 for part in shared]
        quarter_sizes = [part.shape[1] // 128 // ranks for part in quartered]
        owned_sizes = [part.shape[1] // 128 for part in owned]
        each = -(-sum(shared_sizes) // ranks)
        own = pile[:, :each]
        parts = jnp.stack([own] + [around(own, "tensor", k) for k in range(1, ranks)])
        ordered = jnp.concatenate([at(parts, (tensor - r) % ranks, 0) for r in range(ranks)], axis=1)
        results = []
        for whole, begin, sizes in [
            (ordered, 0, shared_sizes),
            (pile, each, quarter_sizes + owned_sizes),
        ]:
            for count in sizes:
                results.append([flat(whole[m, begin : begin + count]) for m in range(2)])
                begin += count
        return results

    def feed_grads(layer, grad, unit2, rsd2, partial):
        return grad + norm_back(unit2, rsd2, reduce_rows(partial) * small[layer][4])

    def feed_adapters(second, branch, low_u, low_d, inner_u, inner_d, active, grad_up):
        shared = [across(inner_u, second), across(low_d, branch)]
        owned = [across(low_u, grad_up), across(inner_d, active)]
        return shared, owned

    def backward_attend(layer, kept, grad_middle):
        gain1 = small[layer][0]
        sq, skv, ekv, eo = adapters[layer]
        unit1, rsd1, normed, low_q, low_kv, queries, key_block, probs, mixed, low_o = kept
        branch = grad_middle.astype(bf16)
        grad_q, grad_block, inner_o, inner_q, partial = attend_back(
            layer, branch, early_all, so_all[layer], eo, probs, queries, key_block,
            eq_all[layer], sq, head,
        )
        count = (reach + 1) * rows
        blocks = grad_block[:count].astype(f32)
        for j in range(1, ranks):
            part = grad_block[j * count : (j + 1) * count]
            blocks = blocks + around(part, "tensor", j).astype(f32)
        own = blocks[reach * rows :]
        for back in range(1, reach + 1):
            begin = (reach - back) * rows
            own = own + along(blocks[begin : begin + rows].astype(bf16), "dp", -back).astype(f32)
        grad_kv = own.astype(bf16)
        inner_kv = against(grad_kv, ekv).astype(bf16)
        grad_normed = partial + against(grad_kv, keyval_ws[layer]) + plain(inner_kv, skv)
        grad_hidden = grad_middle + norm_back(unit1, rsd1, grad_normed * gain1)
        shared = [
            across(low_o, branch),
            across(inner_q, normed),
            across(inner_kv, normed),
            across(low_kv, grad_kv),
        ]
        quartered = [across(low_q, grad_q), across(inner_o, mixed)]
        return grad_hidden, shared, quartered

    fresh = lax.dynamic_index_in_dim(block_input, section, 0, keepdims=False).astype(f32)
    given = lax.dynamic_index_in_dim(cotangent, section, 0, keepdims=False).astype(f32)
    middle_zero, kept_zero = forward_attend(0, fresh)
    unit_zero, rsd_zero, second_zero, up_bias = feed_inputs(0, middle_zero)
    own_rows, second_zero = lax.optimization_barrier((given.astype(bf16), second_zero))
    branch_one = spread(own_rows)
    second_zero, branch_one = lax.optimization_barrier((second_zero, branch_one))
    active_zero, slope_zero, low_u_zero, low_d_zero, partial = feed_call(
        feed_kernel,
        "feed",
        (second_zero, feed_tables[0], up_bias, feed_packs[0]),
        (3,),
        (local_f, local_f, rank, rank, width),
        local_f,
        2,
    )
    passed = feed_result(0, middle_zero, partial).astype(bf16)

    middle_one, kept_one = forward_attend(1, passed.astype(f32))
    unit_one, rsd_one, second_one, up_bias = feed_inputs(1, middle_one)
    active, low_u, low_d, partial, grad_up, inner_d, inner_u, partial_back = feed_call(
        feed_both_kernel,
        "feed_both",
        (second_one, branch_one, feed_tables[1], up_bias, feed_packs[1]),
        (4, 1),
        (local_f, rank, rank, width, local_f, rank, rank, width),
        local_f,
        4,
    )
    grad_middle = feed_grads(1, given, unit_one, rsd_one, partial_back)
    shared, owned = feed_adapters(
        second_one, branch_one, low_u, low_d, inner_u, inner_d, active, grad_up
    )
    grad_one, more, quartered = backward_attend(1, kept_one, grad_middle)
    layer_one = (shared + more, quartered, owned)
    partial, _ = lax.optimization_barrier((partial, grad_middle))
    final = feed_result(1, middle_one, partial).astype(bf16)

    branch_zero = spread(grad_one.astype(bf16))
    grad_up, inner_d, inner_u, partial_back = feed_call(
        feed_back_kernel,
        "feed_back",
        (branch_zero, feed_tables[0], slope_zero, feed_packs[0]),
        (3, 2),
        (local_f, rank, rank, width),
        local_f,
        2,
    )
    grad_middle_zero = feed_grads(0, grad_one, unit_zero, rsd_zero, partial_back)
    shared, owned = feed_adapters(
        second_zero,
        branch_zero,
        low_u_zero,
        low_d_zero,
        inner_u,
        inner_d,
        active_zero,
        grad_up,
    )
    grad_zero, more, quartered = backward_attend(0, kept_zero, grad_middle_zero)
    layer_zero = (shared + more, quartered, owned)
    mine = scattered_grads([layer_zero, layer_one])
    grads = spread_grads(mine[0], mine[1], *layer_zero)

    def both_micros(zero, one, kind):
        own = jnp.where(low_section, zero, one)
        received = swap(jnp.where(low_section, one, zero).astype(bf16)).astype(kind)
        return jnp.where(low_section, jnp.stack([own, received]), jnp.stack([received, own]))

    passed, final, _ = lax.optimization_barrier((passed, final, grad_middle_zero))
    section_outputs = both_micros(passed, final, bf16)
    input_grads = both_micros(grad_zero, grad_one, f32)
    onehot = (bank_choice[:, None] == jnp.arange(banks)[None, :]).astype(f32)

    def placed(pair, transpose):
        out = sum(
            onehot[m][:, None, None] * pair[m].astype(f32)[None] for m in range(2)
        )
        return (out.transpose(0, 2, 1) if transpose else out)[None]

    (
        up_shrink_grad,
        down_expand_grad,
        out_expand_grad,
        q_shrink_grad,
        kv_shrink_grad,
        kv_expand_grad,
        q_expand_grad,
        out_shrink_grad,
        up_expand_grad,
        down_shrink_grad,
    ) = grads
    return (
        section_outputs[None],
        input_grads[None],
        placed(q_shrink_grad, True),
        placed(q_expand_grad, False),
        placed(kv_shrink_grad, True),
        placed(kv_expand_grad, False),
        placed(out_shrink_grad, True),
        placed(out_expand_grad, False),
        placed(up_shrink_grad, True),
        placed(up_expand_grad, False),
        placed(down_shrink_grad, True),
        placed(down_expand_grad, False),
    )


def solution(mesh):
    return jax.shard_map(
        per_device,
        mesh=mesh,
        in_specs=(
            P(None, ("dp", "tensor"), None),
            P(None, ("dp", "tensor"), None),
            P(),
            P(),
            P("section", None),
            P("section", None),
            P("section", "dp", "tensor"),
            P("section", "tensor"),
            P("section", "dp", None),
            P("section", None),
            P("section", "tensor", "dp"),
            P("section", None),
            P("section", None),
            P("section", None),
            P("section", "dp", "tensor"),
            P("section", "tensor"),
            P("section", "tensor", "dp"),
            P("section", None),
            P("section", None, None, None),
            P("section", None, None, "tensor"),
            P("section", None, None, None),
            P("section", None, None, None),
            P("section", None, "tensor", None),
            P("section", None, None, None),
            P("section", None, None, None),
            P("section", None, None, "tensor"),
            P("section", None, "tensor", None),
            P("section", None, None, None),
        ),
        out_specs=(
            P("section", None, ("dp", "tensor"), None),
            P("section", None, ("dp", "tensor"), None),
            P("section", None, None, None),
            P("section", None, None, "tensor"),
            P("section", None, None, None),
            P("section", None, None, None),
            P("section", None, "tensor", None),
            P("section", None, None, None),
            P("section", None, None, None),
            P("section", None, None, "tensor"),
            P("section", None, "tensor", None),
            P("section", None, None, None),
        ),
        check_vma=False,
    )
```

```python
import math

import jax
import jax.numpy as jnp
from jax import lax
from jax.experimental import pallas as pl
from jax.experimental.layout import Layout, with_layout_constraint
from jax.experimental.pallas import tpu as pltpu
from jax.sharding import PartitionSpec as P

WINDOW = 1024
epsilon = 1e-05
masked_score = -1e30
bf16 = jnp.bfloat16
f32 = jnp.float32


def plain(left, right):
    return jnp.dot(left, right, preferred_element_type=f32)


def against(left, right):
    return lax.dot_general(left, right, (((1,), (1,)), ((), ())), preferred_element_type=f32)


def across(left, right):
    return lax.dot_general(left, right, (((0,), (0,)), ((), ())), preferred_element_type=f32)


def around(block, axis, distance):
    size = lax.axis_size(axis)
    return lax.ppermute(block, axis, [(i, (i + distance) % size) for i in range(size)])


def along(block, axis, distance):
    size = lax.axis_size(axis)
    route = [(i, i + distance) for i in range(size) if 0 <= i + distance < size]
    return lax.ppermute(block, axis, route)


def flipped(block, axis, bit):
    size = lax.axis_size(axis)
    return lax.ppermute(block, axis, [(i, i ^ bit) for i in range(size)])


def pick(table, index, size=1):
    return lax.dynamic_slice_in_dim(table, index, size, 0)


def norm_parts(value):
    centred = value - jnp.mean(value, axis=-1, keepdims=True)
    spread = lax.rsqrt(jnp.mean(centred * centred, axis=-1, keepdims=True) + epsilon)
    return centred * spread, spread


def norm_back(unit, spread, scaled):
    inner = jnp.mean(scaled * unit, axis=-1, keepdims=True)
    return spread * (scaled - jnp.mean(scaled, axis=-1, keepdims=True) - unit * inner)


def gelu_parts(value):
    rate = math.sqrt(2.0 / math.pi)
    square = value * value
    bend = jnp.tanh(rate * (value + 0.044715 * value * square))
    rising = 0.5 * (1.0 + bend)
    slope = rising + 0.5 * value * (1.0 - bend * bend) * (rate * (1.0 + 3 * 0.044715 * square))
    return value * rising, slope


def side_blocks(query_ref, group, head):
    begin = group * 4 * head
    return jnp.concatenate(
        [query_ref[:, begin + h * head : begin + (h + 1) * head] for h in range(4)], axis=0
    )


def put_blocks(out_ref, value, group, head):
    rows = value.shape[0] // 4
    for h in range(4):
        begin = (group * 4 + h) * head
        out_ref[:, begin : begin + head] = value[h * rows : (h + 1) * rows]


def table_copies(table_ref, buf, sem, layer, begin):
    ranks, chunks, _, width = buf.shape
    return [
        pltpu.make_async_copy(
            table_ref.at[x, y, layer, :, pl.ds(begin, width)], buf.at[x, y], sem.at[x, y]
        )
        for x in range(ranks)
        for y in range(chunks)
    ]


def query_kernel(layer, normed_ref, table_ref, bias_ref, eq_ref, sq_ref, out_ref, low_ref, buf, sem):
    ranks, chunks, rows, width = buf.shape
    copies = table_copies(table_ref, buf, sem, layer, 0)
    for copy in copies:
        copy.start()
    normed = normed_ref[...]
    low = against(normed, sq_ref[...]).astype(bf16)
    low_ref[...] = low
    for x in range(ranks):
        columns = pl.ds(x * width, width)
        total = bias_ref[:, columns] + plain(low, eq_ref[:, columns])
        for y in range(chunks):
            copies[x * chunks + y].wait()
            total = total + plain(normed[:, y * rows : (y + 1) * rows], buf[x, y])
        out_ref[:, columns] = total.astype(bf16)


def table_scratch(table, width):
    ranks, chunks, _, rows, _ = table.shape
    return [
        pltpu.VMEM((ranks, chunks, rows, width), bf16),
        pltpu.SemaphoreType.DMA((ranks, chunks)),
    ]


held = pl.BlockSpec(memory_space=pltpu.VMEM)
remote = pl.BlockSpec(memory_space=pl.ANY)


def project_queries(layer, normed, table, bias, eq, sq):
    rows, model = normed.shape
    rank = sq.shape[0]
    width = model // table.shape[0]
    return pl.pallas_call(
        lambda *refs: query_kernel(layer, *refs),
        in_specs=[held, remote, held, held, held],
        out_specs=[held] * 2,
        out_shape=[
            jax.ShapeDtypeStruct((rows, model), bf16),
            jax.ShapeDtypeStruct((rows, rank), bf16),
        ],
        scratch_shapes=table_scratch(table, width),
        compiler_params=pltpu.CompilerParams(vmem_limit_bytes=28 * 2**20),
        cost_estimate=pl.CostEstimate(
            flops=8 * rows * model * model, bytes_accessed=2 * model * model, transcendentals=0
        ),
        name="project_queries",
    )(normed, table, bias, eq, sq)


def attend_kernel(
    layer, head, query_ref, keyval_ref, bias_ref, table_ref, so_ref, eo_ref,
    prob_ref, mixed_ref, low_ref, out_ref, buf, sem,
):
    ranks, chunks, rows, width = buf.shape
    copies = table_copies(table_ref, buf, sem, layer, width)
    for copy in copies:
        copy.start()
    scale = 1.0 / math.sqrt(head)
    bias = jnp.concatenate([bias_ref[...].astype(f32)] * 4, axis=0)
    for g in range(prob_ref.shape[0]):
        queries = side_blocks(query_ref, g, head)
        scores = against(queries, keyval_ref[:, :head]) * scale + bias
        lifted = jnp.exp(scores - jnp.max(scores, axis=-1, keepdims=True))
        probs = (lifted * (1.0 / jnp.sum(lifted, axis=-1, keepdims=True))).astype(bf16)
        prob_ref[g] = probs
        put_blocks(mixed_ref, plain(probs, keyval_ref[:, head:]).astype(bf16), g, head)
    mixed = mixed_ref[...]
    low = against(mixed, so_ref[...]).astype(bf16)
    low_ref[...] = low
    for copy in copies:
        copy.wait()
    for y in range(chunks):
        columns = pl.ds(y * rows, rows)
        total = plain(low, eo_ref[:, columns])
        for x in range(ranks):
            total = total + against(mixed[:, x * width : (x + 1) * width], buf[x, y])
        out_ref[:, columns] = total


def attend(layer, queries, key_block, bias, table, so, eo, head):
    rows, model = queries.shape
    keys = key_block.shape[0]
    groups = model // head // 4
    rank = so.shape[0]
    return pl.pallas_call(
        lambda *refs: attend_kernel(layer, head, *refs),
        in_specs=[held, held, held, remote, held, held],
        out_specs=[held] * 4,
        out_shape=[
            jax.ShapeDtypeStruct((groups, 4 * rows, keys), bf16),
            jax.ShapeDtypeStruct((rows, model), bf16),
            jax.ShapeDtypeStruct((rows, rank), bf16),
            jax.ShapeDtypeStruct((rows, model), f32),
        ],
        scratch_shapes=table_scratch(table, model // table.shape[0]),
        compiler_params=pltpu.CompilerParams(vmem_limit_bytes=36 * 2**20),
        cost_estimate=pl.CostEstimate(
            flops=4 * rows * model * (keys + 2 * model),
            bytes_accessed=2 * model * model,
            transcendentals=groups * 4 * rows * keys,
        ),
        name="attend",
    )(queries, key_block, bias, table, so, eo)


def attend_back_kernel(
    layer, head, branch_ref, table_ref, so_ref, eo_ref, prob_ref, query_ref, keyval_ref,
    dq_ref, dkv_ref, inner_o_ref, out_buf, out_sem, mixed_buf, key_sum, value_sum,
):
    ranks, chunks, rows, width = out_buf.shape
    out_copies = table_copies(table_ref, out_buf, out_sem, layer, width)
    for copy in out_copies:
        copy.start()
    scale = 1.0 / math.sqrt(head)
    branch = branch_ref[...]
    inner_o = against(branch, eo_ref[...]).astype(bf16)
    inner_o_ref[...] = inner_o
    for g in range(prob_ref.shape[0]):
        columns = pl.ds(g * width, width)
        total = plain(inner_o, so_ref[:, columns])
        for y in range(chunks):
            out_copies[g * chunks + y].wait()
            total = total + plain(branch[:, y * rows : (y + 1) * rows], out_buf[g, y])
        mixed_buf[:, columns] = total.astype(bf16)
        grad = side_blocks(mixed_buf, g, head)
        low_probs = prob_ref[g]
        probs = low_probs.astype(f32)
        grad_probs = against(grad, keyval_ref[:, head:])
        delta = jnp.sum(grad_probs * probs, axis=-1, keepdims=True)
        delta = delta / jnp.sum(probs, axis=-1, keepdims=True)
        grad_scores = (probs * (grad_probs - delta)).astype(bf16)
        put_blocks(dq_ref, (plain(grad_scores, keyval_ref[:, :head]) * scale).astype(bf16), g, head)
        keys = across(grad_scores, side_blocks(query_ref, g, head))
        values = across(low_probs, grad)
        if g == 0:
            key_sum[...] = keys
            value_sum[...] = values
        else:
            key_sum[...] += keys
            value_sum[...] += values
    dkv_ref[:, :head] = (key_sum[...] * scale).astype(bf16)
    dkv_ref[:, head:] = value_sum[...].astype(bf16)


def query_back_kernel(layer, grad_ref, table_ref, eq_ref, sq_ref, inner_ref, part_ref, buf, sem):
    ranks, chunks, rows, width = buf.shape
    copies = table_copies(table_ref, buf, sem, layer, 0)
    for copy in copies:
        copy.start()
    grad = grad_ref[...]
    inner = against(grad, eq_ref[...]).astype(bf16)
    inner_ref[...] = inner
    for copy in copies:
        copy.wait()
    for y in range(chunks):
        columns = pl.ds(y * rows, rows)
        total = plain(inner, sq_ref[:, columns])
        for x in range(ranks):
            total = total + against(grad[:, x * width : (x + 1) * width], buf[x, y])
        part_ref[:, columns] = total


def query_back(layer, grad, table, eq, sq):
    rows, model = grad.shape
    rank = sq.shape[0]
    return pl.pallas_call(
        lambda *refs: query_back_kernel(layer, *refs),
        in_specs=[held, remote, held, held],
        out_specs=[held] * 2,
        out_shape=[
            jax.ShapeDtypeStruct((rows, rank), bf16),
            jax.ShapeDtypeStruct((rows, model), f32),
        ],
        scratch_shapes=table_scratch(table, model // table.shape[0]),
        compiler_params=pltpu.CompilerParams(vmem_limit_bytes=28 * 2**20),
        cost_estimate=pl.CostEstimate(
            flops=8 * rows * model * model, bytes_accessed=2 * model * model, transcendentals=0
        ),
        name="query_back",
    )(grad, table, eq, sq)


def attend_back(layer, branch, table, so, eo, probs, queries, key_block, head):
    rows, model = queries.shape
    keys = key_block.shape[0]
    groups = probs.shape[0]
    rank = so.shape[0]
    width = model // table.shape[0]
    return pl.pallas_call(
        lambda *refs: attend_back_kernel(layer, head, *refs),
        in_specs=[held, remote] + [held] * 5,
        out_specs=[held] * 3,
        out_shape=[
            jax.ShapeDtypeStruct((rows, model), bf16),
            jax.ShapeDtypeStruct((keys, 2 * head), bf16),
            jax.ShapeDtypeStruct((rows, rank), bf16),
        ],
        scratch_shapes=table_scratch(table, width)
        + [
            pltpu.VMEM((rows, model), bf16),
            pltpu.VMEM((keys, head), f32),
            pltpu.VMEM((keys, head), f32),
        ],
        compiler_params=pltpu.CompilerParams(vmem_limit_bytes=44 * 2**20),
        cost_estimate=pl.CostEstimate(
            flops=8 * rows * model * (keys + model),
            bytes_accessed=2 * model * model + 4 * groups * 4 * rows * keys,
            transcendentals=0,
        ),
        name="attend_back",
    )(branch, table, so, eo, probs, queries, key_block)


def feed_copies(table_ref, buf, sems):
    _, count, chunks, rows, tile = buf.shape
    half = count // 2 * tile
    copies = []
    for j in range(count):
        pair = []
        for k in range(2):
            columns = pl.ds(j * tile % half + k * half, tile)
            pair.append(
                pltpu.make_async_copy(
                    table_ref.at[:, j * tile // half, :, columns], buf.at[k, j], sems.at[k, j]
                )
            )
        copies.append(pair)
    return copies


def plain_chunks(left, buf, k, j):
    rows = buf.shape[3]
    return sum(plain(left[:, i * rows : (i + 1) * rows], buf[k, j, i]) for i in range(buf.shape[2]))


def against_chunk(left_ref, buf, k, i):
    tile = buf.shape[4]
    return sum(
        against(left_ref[:, j * tile : (j + 1) * tile], buf[k, j, i]) for j in range(buf.shape[1])
    )


def own_copies(sources, buffers, sems):
    copies = [
        pltpu.make_async_copy(source, buffer, sems.at[i])
        for i, (source, buffer) in enumerate(zip(sources, buffers))
    ]
    for copy in copies:
        copy.start()
    return copies


def feed_pack(pack_ref, model, hidden):
    cuts = [0, model, model + hidden, model + 2 * hidden, 2 * model + 2 * hidden]
    return [pack_ref.at[:, a:b] for a, b in zip(cuts[:-1], cuts[1:])]


def feed_kernel(
    second_ref, table_ref, bias_ref, pack_ref,
    active_ref, slope_ref, low_u_ref, low_d_ref, out_ref, buf, sems, pack_buf, own_sems,
):
    _, count, chunks, rows, tile = buf.shape
    su_ref, eu_ref, sd_ref, ed_ref = feed_pack(pack_buf, chunks * rows, count * tile)
    copies = feed_copies(table_ref, buf, sems)
    own = own_copies([pack_ref], [pack_buf], own_sems)
    for up, _ in copies:
        up.start()
    for _, down in copies:
        down.start()
    second = second_ref[...]
    own[0].wait()
    low_u = against(second, su_ref[...]).astype(bf16)
    low_u_ref[...] = low_u
    for j in range(count):
        columns = pl.ds(j * tile, tile)
        copies[j][0].wait()
        upward = plain_chunks(second, buf, 0, j)
        upward = upward + plain(low_u, eu_ref[:, columns]) + bias_ref[:, columns]
        active, slope = gelu_parts(upward)
        active_ref[:, columns] = active.astype(bf16)
        slope_ref[:, columns] = slope.astype(bf16)
    low_d = against(active_ref[...], sd_ref[...]).astype(bf16)
    low_d_ref[...] = low_d
    for _, down in copies:
        down.wait()
    for i in range(chunks):
        columns = pl.ds(i * rows, rows)
        out_ref[:, columns] = (
            against_chunk(active_ref, buf, 1, i) + plain(low_d, ed_ref[:, columns])
        ).astype(bf16)


def feed_back_kernel(
    branch_ref, table_ref, slope_ref, pack_ref,
    grad_up_ref, inner_d_ref, inner_u_ref, out_ref, buf, sems, pack_buf, slope_buf, own_sems,
):
    _, count, chunks, rows, tile = buf.shape
    su_ref, eu_ref, sd_ref, ed_ref = feed_pack(pack_buf, chunks * rows, count * tile)
    copies = feed_copies(table_ref, buf, sems)
    own = own_copies([pack_ref, slope_ref], [pack_buf, slope_buf], own_sems)
    for _, down in copies:
        down.start()
    for up, _ in copies:
        up.start()
    branch = branch_ref[...]
    own[0].wait()
    inner_d = against(branch, ed_ref[...]).astype(bf16)
    inner_d_ref[...] = inner_d
    own[1].wait()
    for j in range(count):
        columns = pl.ds(j * tile, tile)
        copies[j][1].wait()
        grad = plain_chunks(branch, buf, 1, j) + plain(inner_d, sd_ref[:, columns])
        grad_up_ref[:, columns] = (grad * slope_buf[:, columns].astype(f32)).astype(bf16)
    inner_u = against(grad_up_ref[...], eu_ref[...]).astype(bf16)
    inner_u_ref[...] = inner_u
    for up, _ in copies:
        up.wait()
    for i in range(chunks):
        columns = pl.ds(i * rows, rows)
        out_ref[:, columns] = (
            against_chunk(grad_up_ref, buf, 0, i) + plain(inner_u, su_ref[:, columns])
        ).astype(bf16)


def feed_both_kernel(
    second_ref, branch_ref, table_ref, bias_ref, pack_ref,
    active_ref, low_u_ref, low_d_ref, out_ref, grad_up_ref, inner_d_ref, inner_u_ref, back_ref,
    buf, sems, pack_buf, branch_buf, own_sems,
):
    _, count, chunks, rows, tile = buf.shape
    su_ref, eu_ref, sd_ref, ed_ref = feed_pack(pack_buf, chunks * rows, count * tile)
    copies = feed_copies(table_ref, buf, sems)
    own = own_copies([pack_ref, branch_ref], [pack_buf, branch_buf], own_sems)
    for up, down in copies:
        up.start()
        down.start()
    second = second_ref[...]
    for copy in own:
        copy.wait()
    branch = branch_buf[...]
    low_u = against(second, su_ref[...]).astype(bf16)
    low_u_ref[...] = low_u
    inner_d = against(branch, ed_ref[...]).astype(bf16)
    inner_d_ref[...] = inner_d
    for j in range(count):
        columns = pl.ds(j * tile, tile)
        copies[j][0].wait()
        upward = plain_chunks(second, buf, 0, j)
        upward = upward + plain(low_u, eu_ref[:, columns]) + bias_ref[:, columns]
        active, slope = gelu_parts(upward)
        active_ref[:, columns] = active.astype(bf16)
        copies[j][1].wait()
        grad = plain_chunks(branch, buf, 1, j) + plain(inner_d, sd_ref[:, columns])
        grad_up_ref[:, columns] = (grad * slope).astype(bf16)
    inner_u = against(grad_up_ref[...], eu_ref[...]).astype(bf16)
    inner_u_ref[...] = inner_u
    low_d = against(active_ref[...], sd_ref[...]).astype(bf16)
    low_d_ref[...] = low_d
    for i in range(chunks):
        columns = pl.ds(i * rows, rows)
        back_ref[:, columns] = (
            against_chunk(grad_up_ref, buf, 0, i) + plain(inner_u, su_ref[:, columns])
        ).astype(bf16)
        out_ref[:, columns] = (
            against_chunk(active_ref, buf, 1, i) + plain(low_d, ed_ref[:, columns])
        ).astype(bf16)


def feed_call(kernel, name, inputs, copied, outputs, hidden, matmuls):
    table = [value for value in inputs if value.ndim == 4][0]
    rows, model = inputs[0].shape
    tile = 512
    chunks = table.shape[0]
    return pl.pallas_call(
        kernel,
        in_specs=[
            remote if value.ndim == 4 or i in copied else held for i, value in enumerate(inputs)
        ],
        out_specs=[held] * len(outputs),
        out_shape=[jax.ShapeDtypeStruct((rows, width), bf16) for width in outputs],
        scratch_shapes=[
            pltpu.VMEM((2, hidden // tile, chunks, model // chunks, tile), bf16),
            pltpu.SemaphoreType.DMA((2, hidden // tile)),
        ]
        + [pltpu.VMEM(inputs[i].shape, bf16) for i in copied]
        + [pltpu.SemaphoreType.DMA((len(copied),))],
        compiler_params=pltpu.CompilerParams(vmem_limit_bytes=44 * 2**20),
        cost_estimate=pl.CostEstimate(
            flops=2 * matmuls * rows * model * hidden,
            bytes_accessed=4 * model * hidden,
            transcendentals=rows * hidden,
        ),
        name=name,
    )(*inputs)


def per_device(
    block_input,
    cotangent,
    doc_lengths,
    bank_choice,
    first_gain,
    first_shift,
    query_weight,
    query_bias,
    keyval_weight,
    value_bias,
    output_weight,
    output_bias,
    second_gain,
    second_shift,
    upward_weight,
    upward_bias,
    downward_weight,
    downward_bias,
    query_shrink,
    query_expand,
    keyval_shrink,
    keyval_expand,
    output_shrink,
    output_expand,
    upward_shrink,
    upward_expand,
    downward_shrink,
    downward_expand,
):
    section = lax.axis_index("section")
    data = lax.axis_index("dp")
    tensor = lax.axis_index("tensor")
    low_section = section == 0
    width = block_input.shape[2]
    rows = block_input.shape[1]
    ranks = lax.axis_size("tensor")
    span = rows * ranks
    head = value_bias.shape[1]
    local_q = query_bias.shape[1]
    local_f = upward_bias.shape[1]
    rank = query_expand.shape[2]
    banks = query_expand.shape[1]
    reach = WINDOW // span
    sides = [(0, 1), (1, 0)]

    def swap(value):
        return lax.ppermute(value, "section", sides)

    def by_layer(own, other):
        return jnp.where(low_section, own, other), jnp.where(low_section, other, own)

    def spread(block):
        parts = [block] + [around(block, "tensor", -j) for j in range(1, ranks)]
        return jnp.concatenate(parts, axis=0)

    def reduce_rows(partial):
        low = partial.astype(bf16)
        total = partial[:rows].astype(f32)
        for j in range(1, ranks):
            total = total + around(low[j * rows : (j + 1) * rows], "tensor", j).astype(f32)
        return total

    own_bank = lax.dynamic_index_in_dim(bank_choice, section, 0, keepdims=False)
    other_bank = lax.dynamic_index_in_dim(bank_choice, 1 - section, 0, keepdims=False)

    chips = lax.axis_size("dp") // 4
    both = ("section", "dp")
    every = ("section", "dp", "tensor")
    order = [
        side * 4 * chips + chip * 4 + near
        for chip in range(chips)
        for side in range(2)
        for near in range(4)
    ]
    order_all = [place * ranks + x for x in range(ranks) for place in order]

    def row_major(block):
        return with_layout_constraint(block, Layout(major_to_minor=(0, 1)))

    def gather(shard):
        table = lax.all_gather(row_major(shard), both, axis=0, tiled=True, axis_index_groups=[order])
        return row_major(table).reshape(chips, 2, -1, shard.shape[1])

    def gather_all(shard):
        table = lax.all_gather(
            row_major(shard), every, axis=0, tiled=True, axis_index_groups=[order_all]
        )
        return row_major(table).reshape(ranks, chips, 2, -1, shard.shape[1])

    def halves(shard):
        cut = shard.shape[1] // 2
        return shard[:, :cut], shard[:, cut:]

    keyval_half = jnp.where(tensor % 2 == 0, keyval_weight[0][:, :head], keyval_weight[0][:, head:])
    early_all = gather_all(
        jnp.concatenate([query_weight[0], row_major(output_weight[0].T), keyval_half], axis=1)
    )
    keyval_ws = [
        jnp.concatenate(
            [early_all[x, :, layer, :, 2 * local_q :].reshape(width, head) for x in range(2)], axis=1
        )
        for layer in range(2)
    ]

    def crossed(block, mask):
        return lax.ppermute(block, both, [(i, i ^ mask) for i in range(8 * chips)])

    vectors = jnp.concatenate(
        [
            first_gain,
            first_shift,
            jnp.zeros_like(value_bias),
            value_bias,
            output_bias,
            second_gain,
            second_shift,
            upward_bias,
            downward_bias,
        ],
        axis=1,
    )
    vector_sizes = [width, width, 2 * head, width, width, width, local_f, width]
    vector_layers = by_layer(vectors, swap(vectors))

    def chosen(table, bank, transpose):
        block = lax.dynamic_index_in_dim(table[0], bank, 0, keepdims=False)
        return block.T if transpose else block

    def pack(bank, parts):
        return jnp.concatenate([chosen(table, bank, flip) for table, flip in parts], axis=1)

    cut_parts = [(query_expand, False), (output_shrink, True)]
    whole_parts = [
        (query_shrink, True),
        (keyval_shrink, True),
        (keyval_expand, False),
        (output_expand, False),
        (upward_shrink, True),
        (upward_expand, False),
        (downward_shrink, True),
        (downward_expand, False),
    ]
    query_rows = jnp.broadcast_to(query_bias, (rank, local_q))

    def cut_pack(bank):
        return jnp.concatenate([pack(bank, cut_parts), query_rows], axis=1)

    shared_parts = [part for part in whole_parts if part[0] is not upward_expand and part[0] is not downward_shrink]
    split_parts = [(upward_expand, False), (downward_shrink, True)]
    shared_away = pack(other_bank, shared_parts)
    quarter = shared_away.shape[1] // ranks
    crossing = jnp.concatenate(
        [
            cut_pack(other_bank),
            lax.dynamic_slice_in_dim(shared_away, tensor * quarter, quarter, 1),
            pack(other_bank, split_parts),
        ],
        axis=1,
    )
    crossed_pack = swap(crossing)
    cut_width = 3 * local_q
    block = jnp.concatenate([cut_pack(own_bank), crossed_pack[:, : cut_width + quarter]], axis=1)
    blocks = jnp.stack([block] + [around(block, "tensor", j) for j in range(1, ranks)])
    blocks = [
        lax.dynamic_index_in_dim(blocks, (tensor - r) % ranks, 0, keepdims=False)
        for r in range(ranks)
    ]

    def joined(begin, size):
        return jnp.concatenate([block[:, begin : begin + size] for block in blocks], axis=1)

    cut_layers = [
        by_layer(joined(k * local_q, local_q), joined(cut_width + k * local_q, local_q))
        for k in range(3)
    ]
    eq_all, so_all, query_bias_all = cut_layers
    shared_layers = by_layer(pack(own_bank, shared_parts), joined(2 * cut_width, quarter))
    split_layers = by_layer(pack(own_bank, split_parts), crossed_pack[:, cut_width + quarter :])

    up_halves = halves(upward_weight[0])
    down_halves = halves(row_major(downward_weight[0].T))
    side = [jnp.concatenate([up_halves[h], down_halves[h]], axis=1) for h in range(2)]
    keep = jnp.where(low_section, side[0], side[1])
    gained = swap(jnp.where(low_section, side[1], side[0]))
    feed_tables = [gather(table) for table in by_layer(keep, gained)]

    def split(table, sizes):
        cuts = [0]
        for size in sizes:
            cuts.append(cuts[-1] + size)
        return [table[:, a:b] for a, b in zip(cuts[:-1], cuts[1:])]

    small = [
        [part.astype(f32) for part in split(vector_layers[layer], vector_sizes)]
        for layer in range(2)
    ]
    adapters = []
    feed_packs = []
    for layer in range(2):
        sq, skv, ekv, eo, su, ed = split(
            shared_layers[layer], [width, width, 2 * head, width, width, width]
        )
        eu, sd = split(split_layers[layer], [local_f, local_f])
        adapters.append((sq, skv, ekv, eo))
        feed_packs.append(jnp.concatenate([su, eu, sd, ed], axis=1))

    inside = jnp.arange(rows, dtype=jnp.int32)
    query_place = data * span + tensor * rows + inside
    key_place = jnp.concatenate(
        [
            (data - back) * span + (tensor + j) % ranks * rows + inside
            for j in range(ranks)
            for back in range(reach, -1, -1)
        ]
    )
    lengths = lax.dynamic_index_in_dim(doc_lengths, section, 0, keepdims=False)
    ends = jnp.cumsum(lengths)
    query_doc = jnp.sum((query_place[:, None] >= ends[None, :]).astype(jnp.int32), axis=1)
    key_doc = jnp.sum((key_place[:, None] >= ends[None, :]).astype(jnp.int32), axis=1)
    distance = query_place[:, None] - key_place[None, :]
    allowed = (
        (key_place[None, :] >= 0)
        & (distance >= 0)
        & (distance < WINDOW)
        & (query_doc[:, None] == key_doc[None, :])
    )
    bias = jnp.where(allowed, 0.0, masked_score).astype(bf16)

    def forward_attend(layer, hidden):
        gain1, shift1, kv_bias, out_bias = small[layer][:4]
        sq, skv, ekv, eo = adapters[layer]
        unit1, rsd1 = norm_parts(hidden)
        normed = (unit1 * gain1 + shift1).astype(bf16)
        low_kv = against(normed, skv).astype(bf16)
        keyval = (plain(normed, keyval_ws[layer]) + kv_bias + plain(low_kv, ekv)).astype(bf16)
        pieces = [along(keyval, "dp", back) for back in range(reach, 0, -1)] + [keyval]
        own_keys = jnp.concatenate(pieces, axis=0)
        blocks = [own_keys] + [around(own_keys, "tensor", -j) for j in range(1, ranks)]
        query_rows, blocks[1] = lax.optimization_barrier((normed, blocks[1]))
        key_block = jnp.concatenate(blocks, axis=0)
        queries, low_q = project_queries(
            layer, query_rows, early_all, query_bias_all[layer][:1].astype(f32), eq_all[layer], sq
        )
        probs, mixed, low_o, attended = attend(
            layer, queries, key_block, bias, early_all, so_all[layer], eo, head
        )
        middle = hidden + (attended + out_bias)
        return middle, (unit1, rsd1, normed, low_q, low_kv, queries, key_block, probs, mixed, low_o)

    def feed_inputs(layer, middle):
        gain2, shift2, up_bias = small[layer][4:7]
        unit2, rsd2 = norm_parts(middle)
        second = spread((unit2 * gain2 + shift2).astype(bf16))
        return unit2, rsd2, second, up_bias

    def feed_result(layer, middle, partial):
        return middle + (reduce_rows(partial) + small[layer][7])

    def tiles(block):
        return block.reshape(rank, -1, 128).transpose(1, 0, 2)

    def flat(block):
        return block.transpose(1, 0, 2).reshape(rank, -1)

    turn, near = data // 4, data % 4

    def padded(pile, multiple):
        lack = -pile.shape[0] % multiple
        if not lack:
            return pile
        return jnp.concatenate([pile, jnp.zeros((lack,) + pile.shape[1:], pile.dtype)], axis=0)

    def piled(shared, quartered):
        pile = padded(jnp.concatenate([tiles(part) for part in shared], axis=0), ranks)
        return jnp.concatenate(
            [block.reshape((ranks, -1) + block.shape[1:]) for block in [pile] + [tiles(part) for part in quartered]],
            axis=1,
        ).astype(bf16)

    def owned_pile(mine, owned):
        pile = jnp.concatenate([mine] + [tiles(part) for part in owned], axis=0).astype(bf16)
        return padded(pile, lax.axis_size("dp"))

    def at(block, index, axis):
        return lax.dynamic_index_in_dim(block, index, axis, keepdims=False)

    def scattered_grads(layers, late):
        pile = jnp.stack([piled(shared, quartered) for shared, quartered, _ in layers], axis=1)
        mine = at(pile, tensor, 0).astype(f32)
        for j in range(1, ranks):
            mine = mine + around(at(pile, (tensor + j) % ranks, 0), "tensor", j).astype(f32)
        pile = jnp.stack([owned_pile(mine[i], layers[i][2]) for i in range(2)])
        pile = pile.reshape((2, chips, 4, -1) + pile.shape[2:])
        mine = at(pile, near, 2).astype(f32)
        for k in range(1, 4):
            mine = mine + flipped(at(pile, near ^ k, 2), "dp", k).astype(f32)
        pile, late = lax.optimization_barrier((mine.astype(bf16), late))
        mine = at(pile, turn, 1).astype(f32)
        for k in range(1, chips):
            mine = mine + flipped(at(pile, turn ^ k, 1), "dp", 4 * k).astype(f32)
        return mine.astype(bf16), late

    def spread_grads(zero, one, shared, quartered, owned):
        own = jnp.where(low_section, zero, one)
        away = jnp.where(low_section, one, zero)
        dp_size = 4 * chips
        home = jnp.stack([own, flipped(own, "dp", 2)])
        guest = jnp.stack([crossed(away, dp_size), crossed(away, dp_size + 2)])
        home, guest = [
            jnp.where(near // 2 == 0, block, block[::-1]) for block in (home, guest)
        ]
        pair = jnp.where(
            low_section, jnp.stack([home, guest], axis=1), jnp.stack([guest, home], axis=1)
        )
        parts = jnp.stack([pair] + [flipped(pair, "dp", 4 * k) for k in range(1, chips)])
        parts = jnp.stack([at(parts, turn ^ k, 0) for k in range(chips)])
        other = flipped(parts, "dp", 1)
        core = near % 2
        parts = jnp.stack(
            [jnp.where(core == 0, parts, other), jnp.where(core == 0, other, parts)], axis=2
        )
        pile = jnp.moveaxis(parts, 3, 0).reshape((2, -1) + parts.shape[5:])
        shared_sizes = [part.shape[1] // 128 for part in shared]
        quarter_sizes = [part.shape[1] // 128 // ranks for part in quartered]
        owned_sizes = [part.shape[1] // 128 for part in owned]
        each = -(-sum(shared_sizes) // ranks)
        own = pile[:, :each]
        parts = jnp.stack([own] + [around(own, "tensor", k) for k in range(1, ranks)])
        ordered = jnp.concatenate([at(parts, (tensor - r) % ranks, 0) for r in range(ranks)], axis=1)
        results = []
        for whole, begin, sizes in [
            (ordered, 0, shared_sizes),
            (pile, each, quarter_sizes + owned_sizes),
        ]:
            for count in sizes:
                results.append([flat(whole[m, begin : begin + count]) for m in range(2)])
                begin += count
        return results

    def feed_grads(layer, grad, unit2, rsd2, partial):
        return grad + norm_back(unit2, rsd2, reduce_rows(partial) * small[layer][4])

    def feed_adapters(second, branch, low_u, low_d, inner_u, inner_d, active, grad_up):
        shared = [across(inner_u, second), across(low_d, branch)]
        owned = [across(low_u, grad_up), across(inner_d, active)]
        return shared, owned

    def backward_attend(layer, kept, grad_middle):
        gain1 = small[layer][0]
        sq, skv, ekv, eo = adapters[layer]
        unit1, rsd1, normed, low_q, low_kv, queries, key_block, probs, mixed, low_o = kept
        branch = grad_middle.astype(bf16)
        grad_q, grad_block, inner_o = attend_back(
            layer, branch, early_all, so_all[layer], eo, probs, queries, key_block, head
        )
        inner_q, partial = query_back(layer, grad_q, early_all, eq_all[layer], sq)
        count = (reach + 1) * rows
        blocks = grad_block[:count].astype(f32)
        for j in range(1, ranks):
            part = grad_block[j * count : (j + 1) * count]
            blocks = blocks + around(part, "tensor", j).astype(f32)
        own = blocks[reach * rows :]
        for back in range(1, reach + 1):
            begin = (reach - back) * rows
            own = own + along(blocks[begin : begin + rows].astype(bf16), "dp", -back).astype(f32)
        grad_kv = own.astype(bf16)
        inner_kv = against(grad_kv, ekv).astype(bf16)
        grad_normed = partial + against(grad_kv, keyval_ws[layer]) + plain(inner_kv, skv)
        grad_hidden = grad_middle + norm_back(unit1, rsd1, grad_normed * gain1)
        shared = [
            across(low_o, branch),
            across(inner_q, normed),
            across(inner_kv, normed),
            across(low_kv, grad_kv),
        ]
        quartered = [across(low_q, grad_q), across(inner_o, mixed)]
        return grad_hidden, shared, quartered

    fresh = lax.dynamic_index_in_dim(block_input, section, 0, keepdims=False).astype(f32)
    given = lax.dynamic_index_in_dim(cotangent, section, 0, keepdims=False).astype(f32)
    middle_zero, kept_zero = forward_attend(0, fresh)
    unit_zero, rsd_zero, second_zero, up_bias = feed_inputs(0, middle_zero)
    own_rows, second_zero = lax.optimization_barrier((given.astype(bf16), second_zero))
    branch_one = spread(own_rows)
    second_zero, branch_one = lax.optimization_barrier((second_zero, branch_one))
    active_zero, slope_zero, low_u_zero, low_d_zero, partial = feed_call(
        feed_kernel,
        "feed",
        (second_zero, feed_tables[0], up_bias, feed_packs[0]),
        (3,),
        (local_f, local_f, rank, rank, width),
        local_f,
        2,
    )
    passed = feed_result(0, middle_zero, partial).astype(bf16)

    middle_one, kept_one = forward_attend(1, passed.astype(f32))
    unit_one, rsd_one, second_one, up_bias = feed_inputs(1, middle_one)
    active, low_u, low_d, partial, grad_up, inner_d, inner_u, partial_back = feed_call(
        feed_both_kernel,
        "feed_both",
        (second_one, branch_one, feed_tables[1], up_bias, feed_packs[1]),
        (4, 1),
        (local_f, rank, rank, width, local_f, rank, rank, width),
        local_f,
        4,
    )
    grad_middle = feed_grads(1, given, unit_one, rsd_one, partial_back)
    shared, owned = feed_adapters(
        second_one, branch_one, low_u, low_d, inner_u, inner_d, active, grad_up
    )
    grad_one, more, quartered = backward_attend(1, kept_one, grad_middle)
    layer_one = (shared + more, quartered, owned)
    partial_one = partial

    branch_zero = spread(grad_one.astype(bf16))
    grad_up, inner_d, inner_u, partial_back = feed_call(
        feed_back_kernel,
        "feed_back",
        (branch_zero, feed_tables[0], slope_zero, feed_packs[0]),
        (3, 2),
        (local_f, rank, rank, width),
        local_f,
        2,
    )
    grad_middle_zero = feed_grads(0, grad_one, unit_zero, rsd_zero, partial_back)
    shared, owned = feed_adapters(
        second_zero,
        branch_zero,
        low_u_zero,
        low_d_zero,
        inner_u,
        inner_d,
        active_zero,
        grad_up,
    )
    grad_zero, more, quartered = backward_attend(0, kept_zero, grad_middle_zero)
    layer_zero = (shared + more, quartered, owned)
    mine, partial_one = scattered_grads([layer_zero, layer_one], partial_one)
    final = feed_result(1, middle_one, partial_one).astype(bf16)
    grads = spread_grads(mine[0], mine[1], *layer_zero)

    def both_micros(zero, one, kind):
        own = jnp.where(low_section, zero, one)
        received = swap(jnp.where(low_section, one, zero).astype(bf16)).astype(kind)
        return jnp.where(low_section, jnp.stack([own, received]), jnp.stack([received, own]))

    section_outputs = both_micros(passed, final, bf16)
    input_grads = both_micros(grad_zero, grad_one, f32)
    onehot = (bank_choice[:, None] == jnp.arange(banks)[None, :]).astype(f32)

    def placed(pair, transpose):
        out = sum(
            onehot[m][:, None, None] * pair[m].astype(f32)[None] for m in range(2)
        )
        return (out.transpose(0, 2, 1) if transpose else out)[None]

    (
        up_shrink_grad,
        down_expand_grad,
        out_expand_grad,
        q_shrink_grad,
        kv_shrink_grad,
        kv_expand_grad,
        q_expand_grad,
        out_shrink_grad,
        up_expand_grad,
        down_shrink_grad,
    ) = grads
    return (
        section_outputs[None],
        input_grads[None],
        placed(q_shrink_grad, True),
        placed(q_expand_grad, False),
        placed(kv_shrink_grad, True),
        placed(kv_expand_grad, False),
        placed(out_shrink_grad, True),
        placed(out_expand_grad, False),
        placed(up_shrink_grad, True),
        placed(up_expand_grad, False),
        placed(down_shrink_grad, True),
        placed(down_expand_grad, False),
    )


def solution(mesh):
    return jax.shard_map(
        per_device,
        mesh=mesh,
        in_specs=(
            P(None, ("dp", "tensor"), None),
            P(None, ("dp", "tensor"), None),
            P(),
            P(),
            P("section", None),
            P("section", None),
            P("section", "dp", "tensor"),
            P("section", "tensor"),
            P("section", "dp", None),
            P("section", None),
            P("section", "tensor", "dp"),
            P("section", None),
            P("section", None),
            P("section", None),
            P("section", "dp", "tensor"),
            P("section", "tensor"),
            P("section", "tensor", "dp"),
            P("section", None),
            P("section", None, None, None),
            P("section", None, None, "tensor"),
            P("section", None, None, None),
            P("section", None, None, None),
            P("section", None, "tensor", None),
            P("section", None, None, None),
            P("section", None, None, None),
            P("section", None, None, "tensor"),
            P("section", None, "tensor", None),
            P("section", None, None, None),
        ),
        out_specs=(
            P("section", None, ("dp", "tensor"), None),
            P("section", None, ("dp", "tensor"), None),
            P("section", None, None, None),
            P("section", None, None, "tensor"),
            P("section", None, None, None),
            P("section", None, None, None),
            P("section", None, "tensor", None),
            P("section", None, None, None),
            P("section", None, None, None),
            P("section", None, None, "tensor"),
            P("section", None, "tensor", None),
            P("section", None, None, None),
        ),
        check_vma=False,
    )
```

```python
import math

import jax
import jax.numpy as jnp
from jax import lax
from jax.experimental import pallas as pl
from jax.experimental.layout import Layout, with_layout_constraint
from jax.experimental.pallas import tpu as pltpu
from jax.sharding import PartitionSpec as P

WINDOW = 1024
epsilon = 1e-05
masked_score = -1e30
bf16 = jnp.bfloat16
f32 = jnp.float32


def plain(left, right):
    return jnp.dot(left, right, preferred_element_type=f32)


def against(left, right):
    return lax.dot_general(left, right, (((1,), (1,)), ((), ())), preferred_element_type=f32)


def across(left, right):
    return lax.dot_general(left, right, (((0,), (0,)), ((), ())), preferred_element_type=f32)


def around(block, axis, distance):
    size = lax.axis_size(axis)
    return lax.ppermute(block, axis, [(i, (i + distance) % size) for i in range(size)])


def along(block, axis, distance):
    size = lax.axis_size(axis)
    route = [(i, i + distance) for i in range(size) if 0 <= i + distance < size]
    return lax.ppermute(block, axis, route)


def flipped(block, axis, bit):
    size = lax.axis_size(axis)
    return lax.ppermute(block, axis, [(i, i ^ bit) for i in range(size)])


def pick(table, index, size=1):
    return lax.dynamic_slice_in_dim(table, index, size, 0)


def norm_parts(value):
    centred = value - jnp.mean(value, axis=-1, keepdims=True)
    spread = lax.rsqrt(jnp.mean(centred * centred, axis=-1, keepdims=True) + epsilon)
    return centred * spread, spread


def norm_back(unit, spread, scaled):
    inner = jnp.mean(scaled * unit, axis=-1, keepdims=True)
    return spread * (scaled - jnp.mean(scaled, axis=-1, keepdims=True) - unit * inner)


def gelu_parts(value):
    rate = math.sqrt(2.0 / math.pi)
    square = value * value
    bend = jnp.tanh(rate * (value + 0.044715 * value * square))
    rising = 0.5 * (1.0 + bend)
    slope = rising + 0.5 * value * (1.0 - bend * bend) * (rate * (1.0 + 3 * 0.044715 * square))
    return value * rising, slope


def side_blocks(query_ref, group, head):
    begin = group * 4 * head
    return jnp.concatenate(
        [query_ref[:, begin + h * head : begin + (h + 1) * head] for h in range(4)], axis=0
    )


def put_blocks(out_ref, value, group, head):
    rows = value.shape[0] // 4
    for h in range(4):
        begin = (group * 4 + h) * head
        out_ref[:, begin : begin + head] = value[h * rows : (h + 1) * rows]


def table_copies(table_ref, buf, sem, layer, begin):
    ranks, chunks, _, width = buf.shape
    return [
        pltpu.make_async_copy(
            table_ref.at[x, y, layer, :, pl.ds(begin, width)], buf.at[x, y], sem.at[x, y]
        )
        for x in range(ranks)
        for y in range(chunks)
    ]


def query_kernel(layer, normed_ref, table_ref, bias_ref, eq_ref, sq_ref, out_ref, low_ref, buf, sem):
    ranks, chunks, rows, width = buf.shape
    copies = table_copies(table_ref, buf, sem, layer, 0)
    for copy in copies:
        copy.start()
    normed = normed_ref[...]
    low = against(normed, sq_ref[...]).astype(bf16)
    low_ref[...] = low
    for x in range(ranks):
        columns = pl.ds(x * width, width)
        total = bias_ref[:, columns] + plain(low, eq_ref[:, columns])
        for y in range(chunks):
            copies[x * chunks + y].wait()
            total = total + plain(normed[:, y * rows : (y + 1) * rows], buf[x, y])
        out_ref[:, columns] = total.astype(bf16)


def table_scratch(table, width):
    ranks, chunks, _, rows, _ = table.shape
    return [
        pltpu.VMEM((ranks, chunks, rows, width), bf16),
        pltpu.SemaphoreType.DMA((ranks, chunks)),
    ]


held = pl.BlockSpec(memory_space=pltpu.VMEM)
remote = pl.BlockSpec(memory_space=pl.ANY)


def project_queries(layer, normed, table, bias, eq, sq):
    rows, model = normed.shape
    rank = sq.shape[0]
    width = model // table.shape[0]
    return pl.pallas_call(
        lambda *refs: query_kernel(layer, *refs),
        in_specs=[held, remote, held, held, held],
        out_specs=[held] * 2,
        out_shape=[
            jax.ShapeDtypeStruct((rows, model), bf16),
            jax.ShapeDtypeStruct((rows, rank), bf16),
        ],
        scratch_shapes=table_scratch(table, width),
        compiler_params=pltpu.CompilerParams(vmem_limit_bytes=28 * 2**20),
        cost_estimate=pl.CostEstimate(
            flops=8 * rows * model * model, bytes_accessed=2 * model * model, transcendentals=0
        ),
        name="project_queries",
    )(normed, table, bias, eq, sq)


def attend_kernel(
    layer, head, query_ref, keyval_ref, bias_ref, table_ref, so_ref, eo_ref,
    prob_ref, mixed_ref, low_ref, out_ref, buf, sem,
):
    ranks, chunks, rows, width = buf.shape
    copies = table_copies(table_ref, buf, sem, layer, width)
    for copy in copies:
        copy.start()
    scale = 1.0 / math.sqrt(head)
    bias = jnp.concatenate([bias_ref[...].astype(f32)] * 4, axis=0)
    for g in range(prob_ref.shape[0]):
        queries = side_blocks(query_ref, g, head)
        scores = against(queries, keyval_ref[:, :head]) * scale + bias
        lifted = jnp.exp(scores - jnp.max(scores, axis=-1, keepdims=True))
        probs = (lifted * (1.0 / jnp.sum(lifted, axis=-1, keepdims=True))).astype(bf16)
        prob_ref[g] = probs
        put_blocks(mixed_ref, plain(probs, keyval_ref[:, head:]).astype(bf16), g, head)
    mixed = mixed_ref[...]
    low = against(mixed, so_ref[...]).astype(bf16)
    low_ref[...] = low
    for copy in copies:
        copy.wait()
    for y in range(chunks):
        columns = pl.ds(y * rows, rows)
        total = plain(low, eo_ref[:, columns])
        for x in range(ranks):
            total = total + against(mixed[:, x * width : (x + 1) * width], buf[x, y])
        out_ref[:, columns] = total


def attend(layer, queries, key_block, bias, table, so, eo, head):
    rows, model = queries.shape
    keys = key_block.shape[0]
    groups = model // head // 4
    rank = so.shape[0]
    return pl.pallas_call(
        lambda *refs: attend_kernel(layer, head, *refs),
        in_specs=[held, held, held, remote, held, held],
        out_specs=[held] * 4,
        out_shape=[
            jax.ShapeDtypeStruct((groups, 4 * rows, keys), bf16),
            jax.ShapeDtypeStruct((rows, model), bf16),
            jax.ShapeDtypeStruct((rows, rank), bf16),
            jax.ShapeDtypeStruct((rows, model), f32),
        ],
        scratch_shapes=table_scratch(table, model // table.shape[0]),
        compiler_params=pltpu.CompilerParams(vmem_limit_bytes=36 * 2**20),
        cost_estimate=pl.CostEstimate(
            flops=4 * rows * model * (keys + 2 * model),
            bytes_accessed=2 * model * model,
            transcendentals=groups * 4 * rows * keys,
        ),
        name="attend",
    )(queries, key_block, bias, table, so, eo)


def attend_back_kernel(
    layer, head, branch_ref, table_ref, so_ref, eo_ref, prob_ref, query_ref, keyval_ref,
    dq_ref, dkv_ref, inner_o_ref, out_buf, out_sem, mixed_buf, key_sum, value_sum,
):
    ranks, chunks, rows, width = out_buf.shape
    out_copies = table_copies(table_ref, out_buf, out_sem, layer, width)
    for copy in out_copies:
        copy.start()
    scale = 1.0 / math.sqrt(head)
    branch = branch_ref[...]
    inner_o = against(branch, eo_ref[...]).astype(bf16)
    inner_o_ref[...] = inner_o
    for g in range(prob_ref.shape[0]):
        columns = pl.ds(g * width, width)
        total = plain(inner_o, so_ref[:, columns])
        for y in range(chunks):
            out_copies[g * chunks + y].wait()
            total = total + plain(branch[:, y * rows : (y + 1) * rows], out_buf[g, y])
        mixed_buf[:, columns] = total.astype(bf16)
        grad = side_blocks(mixed_buf, g, head)
        low_probs = prob_ref[g]
        probs = low_probs.astype(f32)
        grad_probs = against(grad, keyval_ref[:, head:])
        delta = jnp.sum(grad_probs * probs, axis=-1, keepdims=True)
        delta = delta / jnp.sum(probs, axis=-1, keepdims=True)
        grad_scores = (probs * (grad_probs - delta)).astype(bf16)
        put_blocks(dq_ref, (plain(grad_scores, keyval_ref[:, :head]) * scale).astype(bf16), g, head)
        keys = across(grad_scores, side_blocks(query_ref, g, head))
        values = across(low_probs, grad)
        if g == 0:
            key_sum[...] = keys
            value_sum[...] = values
        else:
            key_sum[...] += keys
            value_sum[...] += values
    dkv_ref[:, :head] = (key_sum[...] * scale).astype(bf16)
    dkv_ref[:, head:] = value_sum[...].astype(bf16)


def query_back_kernel(layer, grad_ref, table_ref, eq_ref, sq_ref, inner_ref, part_ref, buf, sem):
    ranks, chunks, rows, width = buf.shape
    copies = table_copies(table_ref, buf, sem, layer, 0)
    for copy in copies:
        copy.start()
    grad = grad_ref[...]
    inner = against(grad, eq_ref[...]).astype(bf16)
    inner_ref[...] = inner
    for copy in copies:
        copy.wait()
    for y in range(chunks):
        columns = pl.ds(y * rows, rows)
        total = plain(inner, sq_ref[:, columns])
        for x in range(ranks):
            total = total + against(grad[:, x * width : (x + 1) * width], buf[x, y])
        part_ref[:, columns] = total


def query_back(layer, grad, table, eq, sq):
    rows, model = grad.shape
    rank = sq.shape[0]
    return pl.pallas_call(
        lambda *refs: query_back_kernel(layer, *refs),
        in_specs=[held, remote, held, held],
        out_specs=[held] * 2,
        out_shape=[
            jax.ShapeDtypeStruct((rows, rank), bf16),
            jax.ShapeDtypeStruct((rows, model), f32),
        ],
        scratch_shapes=table_scratch(table, model // table.shape[0]),
        compiler_params=pltpu.CompilerParams(vmem_limit_bytes=28 * 2**20),
        cost_estimate=pl.CostEstimate(
            flops=8 * rows * model * model, bytes_accessed=2 * model * model, transcendentals=0
        ),
        name="query_back",
    )(grad, table, eq, sq)


def attend_back(layer, branch, table, so, eo, probs, queries, key_block, head):
    rows, model = queries.shape
    keys = key_block.shape[0]
    groups = probs.shape[0]
    rank = so.shape[0]
    width = model // table.shape[0]
    return pl.pallas_call(
        lambda *refs: attend_back_kernel(layer, head, *refs),
        in_specs=[held, remote] + [held] * 5,
        out_specs=[held] * 3,
        out_shape=[
            jax.ShapeDtypeStruct((rows, model), bf16),
            jax.ShapeDtypeStruct((keys, 2 * head), bf16),
            jax.ShapeDtypeStruct((rows, rank), bf16),
        ],
        scratch_shapes=table_scratch(table, width)
        + [
            pltpu.VMEM((rows, model), bf16),
            pltpu.VMEM((keys, head), f32),
            pltpu.VMEM((keys, head), f32),
        ],
        compiler_params=pltpu.CompilerParams(vmem_limit_bytes=44 * 2**20),
        cost_estimate=pl.CostEstimate(
            flops=8 * rows * model * (keys + model),
            bytes_accessed=2 * model * model + 4 * groups * 4 * rows * keys,
            transcendentals=0,
        ),
        name="attend_back",
    )(branch, table, so, eo, probs, queries, key_block)


def feed_copies(table_ref, buf, sems):
    _, count, chunks, rows, tile = buf.shape
    half = count // 2 * tile
    copies = []
    for j in range(count):
        pair = []
        for k in range(2):
            columns = pl.ds(j * tile % half + k * half, tile)
            pair.append(
                pltpu.make_async_copy(
                    table_ref.at[:, j * tile // half, :, columns], buf.at[k, j], sems.at[k, j]
                )
            )
        copies.append(pair)
    return copies


def plain_chunks(left, buf, k, j):
    rows = buf.shape[3]
    return sum(plain(left[:, i * rows : (i + 1) * rows], buf[k, j, i]) for i in range(buf.shape[2]))


def against_chunk(left_ref, buf, k, i):
    tile = buf.shape[4]
    return sum(
        against(left_ref[:, j * tile : (j + 1) * tile], buf[k, j, i]) for j in range(buf.shape[1])
    )


def own_copies(sources, buffers, sems):
    copies = [
        pltpu.make_async_copy(source, buffer, sems.at[i])
        for i, (source, buffer) in enumerate(zip(sources, buffers))
    ]
    for copy in copies:
        copy.start()
    return copies


def feed_pack(pack_ref, model, hidden):
    cuts = [0, model, model + hidden, model + 2 * hidden, 2 * model + 2 * hidden]
    return [pack_ref.at[:, a:b] for a, b in zip(cuts[:-1], cuts[1:])]


def feed_kernel(
    second_ref, table_ref, bias_ref, pack_ref,
    active_ref, slope_ref, low_u_ref, low_d_ref, out_ref, buf, sems, pack_buf, own_sems,
):
    _, count, chunks, rows, tile = buf.shape
    su_ref, eu_ref, sd_ref, ed_ref = feed_pack(pack_buf, chunks * rows, count * tile)
    copies = feed_copies(table_ref, buf, sems)
    own = own_copies([pack_ref], [pack_buf], own_sems)
    for up, _ in copies:
        up.start()
    for _, down in copies:
        down.start()
    second = second_ref[...]
    own[0].wait()
    low_u = against(second, su_ref[...]).astype(bf16)
    low_u_ref[...] = low_u
    for j in range(count):
        columns = pl.ds(j * tile, tile)
        copies[j][0].wait()
        upward = plain_chunks(second, buf, 0, j)
        upward = upward + plain(low_u, eu_ref[:, columns]) + bias_ref[:, columns]
        active, slope = gelu_parts(upward)
        active_ref[:, columns] = active.astype(bf16)
        slope_ref[:, columns] = slope.astype(bf16)
    low_d = against(active_ref[...], sd_ref[...]).astype(bf16)
    low_d_ref[...] = low_d
    for _, down in copies:
        down.wait()
    for i in range(chunks):
        columns = pl.ds(i * rows, rows)
        out_ref[:, columns] = (
            against_chunk(active_ref, buf, 1, i) + plain(low_d, ed_ref[:, columns])
        ).astype(bf16)


def feed_back_kernel(
    branch_ref, table_ref, slope_ref, pack_ref,
    grad_up_ref, inner_d_ref, inner_u_ref, out_ref, buf, sems, pack_buf, slope_buf, own_sems,
):
    _, count, chunks, rows, tile = buf.shape
    su_ref, eu_ref, sd_ref, ed_ref = feed_pack(pack_buf, chunks * rows, count * tile)
    copies = feed_copies(table_ref, buf, sems)
    own = own_copies([pack_ref, slope_ref], [pack_buf, slope_buf], own_sems)
    for _, down in copies:
        down.start()
    for up, _ in copies:
        up.start()
    branch = branch_ref[...]
    own[0].wait()
    inner_d = against(branch, ed_ref[...]).astype(bf16)
    inner_d_ref[...] = inner_d
    own[1].wait()
    for j in range(count):
        columns = pl.ds(j * tile, tile)
        copies[j][1].wait()
        grad = plain_chunks(branch, buf, 1, j) + plain(inner_d, sd_ref[:, columns])
        grad_up_ref[:, columns] = (grad * slope_buf[:, columns].astype(f32)).astype(bf16)
    inner_u = against(grad_up_ref[...], eu_ref[...]).astype(bf16)
    inner_u_ref[...] = inner_u
    for up, _ in copies:
        up.wait()
    for i in range(chunks):
        columns = pl.ds(i * rows, rows)
        out_ref[:, columns] = (
            against_chunk(grad_up_ref, buf, 0, i) + plain(inner_u, su_ref[:, columns])
        ).astype(bf16)


def feed_both_kernel(
    second_ref, branch_ref, table_ref, bias_ref, pack_ref,
    active_ref, low_u_ref, low_d_ref, out_ref, grad_up_ref, inner_d_ref, inner_u_ref, back_ref,
    buf, sems, pack_buf, branch_buf, own_sems,
):
    _, count, chunks, rows, tile = buf.shape
    su_ref, eu_ref, sd_ref, ed_ref = feed_pack(pack_buf, chunks * rows, count * tile)
    copies = feed_copies(table_ref, buf, sems)
    own = own_copies([pack_ref, branch_ref], [pack_buf, branch_buf], own_sems)
    for up, down in copies:
        up.start()
        down.start()
    second = second_ref[...]
    for copy in own:
        copy.wait()
    branch = branch_buf[...]
    low_u = against(second, su_ref[...]).astype(bf16)
    low_u_ref[...] = low_u
    inner_d = against(branch, ed_ref[...]).astype(bf16)
    inner_d_ref[...] = inner_d
    for j in range(count):
        columns = pl.ds(j * tile, tile)
        copies[j][0].wait()
        upward = plain_chunks(second, buf, 0, j)
        upward = upward + plain(low_u, eu_ref[:, columns]) + bias_ref[:, columns]
        active, slope = gelu_parts(upward)
        active_ref[:, columns] = active.astype(bf16)
        copies[j][1].wait()
        grad = plain_chunks(branch, buf, 1, j) + plain(inner_d, sd_ref[:, columns])
        grad_up_ref[:, columns] = (grad * slope).astype(bf16)
    inner_u = against(grad_up_ref[...], eu_ref[...]).astype(bf16)
    inner_u_ref[...] = inner_u
    low_d = against(active_ref[...], sd_ref[...]).astype(bf16)
    low_d_ref[...] = low_d
    for i in range(chunks):
        columns = pl.ds(i * rows, rows)
        back_ref[:, columns] = (
            against_chunk(grad_up_ref, buf, 0, i) + plain(inner_u, su_ref[:, columns])
        ).astype(bf16)
        out_ref[:, columns] = (
            against_chunk(active_ref, buf, 1, i) + plain(low_d, ed_ref[:, columns])
        ).astype(bf16)


def feed_call(kernel, name, inputs, copied, outputs, hidden, matmuls):
    table = [value for value in inputs if value.ndim == 4][0]
    rows, model = inputs[0].shape
    tile = 512
    chunks = table.shape[0]
    return pl.pallas_call(
        kernel,
        in_specs=[
            remote if value.ndim == 4 or i in copied else held for i, value in enumerate(inputs)
        ],
        out_specs=[held] * len(outputs),
        out_shape=[jax.ShapeDtypeStruct((rows, width), bf16) for width in outputs],
        scratch_shapes=[
            pltpu.VMEM((2, hidden // tile, chunks, model // chunks, tile), bf16),
            pltpu.SemaphoreType.DMA((2, hidden // tile)),
        ]
        + [pltpu.VMEM(inputs[i].shape, bf16) for i in copied]
        + [pltpu.SemaphoreType.DMA((len(copied),))],
        compiler_params=pltpu.CompilerParams(vmem_limit_bytes=44 * 2**20),
        cost_estimate=pl.CostEstimate(
            flops=2 * matmuls * rows * model * hidden,
            bytes_accessed=4 * model * hidden,
            transcendentals=rows * hidden,
        ),
        name=name,
    )(*inputs)


def per_device(
    block_input,
    cotangent,
    doc_lengths,
    bank_choice,
    first_gain,
    first_shift,
    query_weight,
    query_bias,
    keyval_weight,
    value_bias,
    output_weight,
    output_bias,
    second_gain,
    second_shift,
    upward_weight,
    upward_bias,
    downward_weight,
    downward_bias,
    query_shrink,
    query_expand,
    keyval_shrink,
    keyval_expand,
    output_shrink,
    output_expand,
    upward_shrink,
    upward_expand,
    downward_shrink,
    downward_expand,
):
    section = lax.axis_index("section")
    data = lax.axis_index("dp")
    tensor = lax.axis_index("tensor")
    low_section = section == 0
    width = block_input.shape[2]
    rows = block_input.shape[1]
    ranks = lax.axis_size("tensor")
    span = rows * ranks
    head = value_bias.shape[1]
    local_q = query_bias.shape[1]
    local_f = upward_bias.shape[1]
    rank = query_expand.shape[2]
    banks = query_expand.shape[1]
    reach = WINDOW // span
    sides = [(0, 1), (1, 0)]

    def swap(value):
        return lax.ppermute(value, "section", sides)

    def by_layer(own, other):
        return jnp.where(low_section, own, other), jnp.where(low_section, other, own)

    def spread(block):
        parts = [block] + [around(block, "tensor", -j) for j in range(1, ranks)]
        return jnp.concatenate(parts, axis=0)

    def reduce_rows(partial):
        low = partial.astype(bf16)
        total = partial[:rows].astype(f32)
        for j in range(1, ranks):
            total = total + around(low[j * rows : (j + 1) * rows], "tensor", j).astype(f32)
        return total

    own_bank = lax.dynamic_index_in_dim(bank_choice, section, 0, keepdims=False)
    other_bank = lax.dynamic_index_in_dim(bank_choice, 1 - section, 0, keepdims=False)

    chips = lax.axis_size("dp") // 4
    both = ("section", "dp")
    every = ("section", "dp", "tensor")
    order = [
        side * 4 * chips + chip * 4 + near
        for chip in range(chips)
        for side in range(2)
        for near in range(4)
    ]
    order_all = [place * ranks + x for x in range(ranks) for place in order]

    def row_major(block):
        return with_layout_constraint(block, Layout(major_to_minor=(0, 1)))

    def gather(shard):
        table = lax.all_gather(row_major(shard), both, axis=0, tiled=True, axis_index_groups=[order])
        return row_major(table).reshape(chips, 2, -1, shard.shape[1])

    def gather_all(shard):
        table = lax.all_gather(
            row_major(shard), every, axis=0, tiled=True, axis_index_groups=[order_all]
        )
        return row_major(table).reshape(ranks, chips, 2, -1, shard.shape[1])

    def halves(shard):
        cut = shard.shape[1] // 2
        return shard[:, :cut], shard[:, cut:]

    keyval_half = jnp.where(tensor % 2 == 0, keyval_weight[0][:, :head], keyval_weight[0][:, head:])
    early_all = gather_all(
        jnp.concatenate([query_weight[0], row_major(output_weight[0].T), keyval_half], axis=1)
    )
    keyval_ws = [
        jnp.concatenate(
            [early_all[x, :, layer, :, 2 * local_q :].reshape(width, head) for x in range(2)], axis=1
        )
        for layer in range(2)
    ]

    def crossed(block, mask):
        return lax.ppermute(block, both, [(i, i ^ mask) for i in range(8 * chips)])

    vectors = jnp.concatenate(
        [
            first_gain,
            first_shift,
            jnp.zeros_like(value_bias),
            value_bias,
            output_bias,
            second_gain,
            second_shift,
            upward_bias,
            downward_bias,
        ],
        axis=1,
    )
    vector_sizes = [width, width, 2 * head, width, width, width, local_f, width]
    vector_layers = by_layer(vectors, swap(vectors))

    def chosen(table, bank, transpose):
        block = lax.dynamic_index_in_dim(table[0], bank, 0, keepdims=False)
        return block.T if transpose else block

    def pack(bank, parts):
        return jnp.concatenate([chosen(table, bank, flip) for table, flip in parts], axis=1)

    cut_parts = [(query_expand, False), (output_shrink, True)]
    whole_parts = [
        (query_shrink, True),
        (keyval_shrink, True),
        (keyval_expand, False),
        (output_expand, False),
        (upward_shrink, True),
        (upward_expand, False),
        (downward_shrink, True),
        (downward_expand, False),
    ]
    query_rows = jnp.broadcast_to(query_bias, (rank, local_q))

    def cut_pack(bank):
        return jnp.concatenate([pack(bank, cut_parts), query_rows], axis=1)

    shared_parts = [part for part in whole_parts if part[0] is not upward_expand and part[0] is not downward_shrink]
    split_parts = [(upward_expand, False), (downward_shrink, True)]
    shared_away = pack(other_bank, shared_parts)
    quarter = shared_away.shape[1] // ranks
    crossing = jnp.concatenate(
        [
            cut_pack(other_bank),
            lax.dynamic_slice_in_dim(shared_away, tensor * quarter, quarter, 1),
            pack(other_bank, split_parts),
        ],
        axis=1,
    )
    crossed_pack = swap(crossing)
    cut_width = 3 * local_q
    block = jnp.concatenate([cut_pack(own_bank), crossed_pack[:, : cut_width + quarter]], axis=1)
    blocks = jnp.stack([block] + [around(block, "tensor", j) for j in range(1, ranks)])
    blocks = [
        lax.dynamic_index_in_dim(blocks, (tensor - r) % ranks, 0, keepdims=False)
        for r in range(ranks)
    ]

    def joined(begin, size):
        return jnp.concatenate([block[:, begin : begin + size] for block in blocks], axis=1)

    cut_layers = [
        by_layer(joined(k * local_q, local_q), joined(cut_width + k * local_q, local_q))
        for k in range(3)
    ]
    eq_all, so_all, query_bias_all = cut_layers
    shared_layers = by_layer(pack(own_bank, shared_parts), joined(2 * cut_width, quarter))
    split_layers = by_layer(pack(own_bank, split_parts), crossed_pack[:, cut_width + quarter :])

    up_halves = halves(upward_weight[0])
    down_halves = halves(row_major(downward_weight[0].T))
    side = [jnp.concatenate([up_halves[h], down_halves[h]], axis=1) for h in range(2)]
    keep = jnp.where(low_section, side[0], side[1])
    gained = swap(jnp.where(low_section, side[1], side[0]))
    feed_tables = [gather(table) for table in by_layer(keep, gained)]

    def split(table, sizes):
        cuts = [0]
        for size in sizes:
            cuts.append(cuts[-1] + size)
        return [table[:, a:b] for a, b in zip(cuts[:-1], cuts[1:])]

    small = [
        [part.astype(f32) for part in split(vector_layers[layer], vector_sizes)]
        for layer in range(2)
    ]
    adapters = []
    feed_packs = []
    for layer in range(2):
        sq, skv, ekv, eo, su, ed = split(
            shared_layers[layer], [width, width, 2 * head, width, width, width]
        )
        eu, sd = split(split_layers[layer], [local_f, local_f])
        adapters.append((sq, skv, ekv, eo))
        feed_packs.append(jnp.concatenate([su, eu, sd, ed], axis=1))

    inside = jnp.arange(rows, dtype=jnp.int32)
    query_place = data * span + tensor * rows + inside
    key_place = jnp.concatenate(
        [
            (data - back) * span + (tensor + j) % ranks * rows + inside
            for j in range(ranks)
            for back in range(reach, -1, -1)
        ]
    )
    lengths = lax.dynamic_index_in_dim(doc_lengths, section, 0, keepdims=False)
    ends = jnp.cumsum(lengths)
    query_doc = jnp.sum((query_place[:, None] >= ends[None, :]).astype(jnp.int32), axis=1)
    key_doc = jnp.sum((key_place[:, None] >= ends[None, :]).astype(jnp.int32), axis=1)
    distance = query_place[:, None] - key_place[None, :]
    allowed = (
        (key_place[None, :] >= 0)
        & (distance >= 0)
        & (distance < WINDOW)
        & (query_doc[:, None] == key_doc[None, :])
    )
    bias = jnp.where(allowed, 0.0, masked_score).astype(bf16)

    def forward_attend(layer, hidden):
        gain1, shift1, kv_bias, out_bias = small[layer][:4]
        sq, skv, ekv, eo = adapters[layer]
        unit1, rsd1 = norm_parts(hidden)
        normed = (unit1 * gain1 + shift1).astype(bf16)
        low_kv = against(normed, skv).astype(bf16)
        keyval = (plain(normed, keyval_ws[layer]) + kv_bias + plain(low_kv, ekv)).astype(bf16)
        pieces = [along(keyval, "dp", back) for back in range(reach, 0, -1)] + [keyval]
        key_block = spread(jnp.concatenate(pieces, axis=0))
        queries, low_q = project_queries(
            layer, normed, early_all, query_bias_all[layer][:1].astype(f32), eq_all[layer], sq
        )
        probs, mixed, low_o, attended = attend(
            layer, queries, key_block, bias, early_all, so_all[layer], eo, head
        )
        middle = hidden + (attended + out_bias)
        return middle, (unit1, rsd1, normed, low_q, low_kv, queries, key_block, probs, mixed, low_o)

    def feed_inputs(layer, middle):
        gain2, shift2, up_bias = small[layer][4:7]
        unit2, rsd2 = norm_parts(middle)
        second = spread((unit2 * gain2 + shift2).astype(bf16))
        return unit2, rsd2, second, up_bias

    def feed_result(layer, middle, partial):
        return middle + (reduce_rows(partial) + small[layer][7])

    def tiles(block):
        return block.reshape(rank, -1, 128).transpose(1, 0, 2)

    def flat(block):
        return block.transpose(1, 0, 2).reshape(rank, -1)

    turn, near = data // 4, data % 4

    def padded(pile, multiple):
        lack = -pile.shape[0] % multiple
        if not lack:
            return pile
        return jnp.concatenate([pile, jnp.zeros((lack,) + pile.shape[1:], pile.dtype)], axis=0)

    def piled(shared, quartered):
        pile = padded(jnp.concatenate([tiles(part) for part in shared], axis=0), ranks)
        return jnp.concatenate(
            [block.reshape((ranks, -1) + block.shape[1:]) for block in [pile] + [tiles(part) for part in quartered]],
            axis=1,
        ).astype(bf16)

    def owned_pile(mine, owned):
        pile = jnp.concatenate([mine] + [tiles(part) for part in owned], axis=0).astype(bf16)
        return padded(pile, lax.axis_size("dp"))

    def at(block, index, axis):
        return lax.dynamic_index_in_dim(block, index, axis, keepdims=False)

    def scattered_grads(layers, late):
        pile = jnp.stack([piled(shared, quartered) for shared, quartered, _ in layers], axis=1)
        mine = at(pile, tensor, 0).astype(f32)
        for j in range(1, ranks):
            mine = mine + around(at(pile, (tensor + j) % ranks, 0), "tensor", j).astype(f32)
        pile = jnp.stack([owned_pile(mine[i], layers[i][2]) for i in range(2)])
        pile = pile.reshape((2, chips, 4, -1) + pile.shape[2:])
        mine = at(pile, near, 2).astype(f32)
        for k in range(1, 4):
            mine = mine + flipped(at(pile, near ^ k, 2), "dp", k).astype(f32)
        pile, late = lax.optimization_barrier((mine.astype(bf16), late))
        mine = at(pile, turn, 1).astype(f32)
        for k in range(1, chips):
            mine = mine + flipped(at(pile, turn ^ k, 1), "dp", 4 * k).astype(f32)
        return mine.astype(bf16), late

    def spread_grads(zero, one, shared, quartered, owned):
        own = jnp.where(low_section, zero, one)
        away = jnp.where(low_section, one, zero)
        dp_size = 4 * chips
        home = jnp.stack([own, flipped(own, "dp", 2)])
        guest = jnp.stack([crossed(away, dp_size), crossed(away, dp_size + 2)])
        home, guest = [
            jnp.where(near // 2 == 0, block, block[::-1]) for block in (home, guest)
        ]
        pair = jnp.where(
            low_section, jnp.stack([home, guest], axis=1), jnp.stack([guest, home], axis=1)
        )
        parts = jnp.stack([pair] + [flipped(pair, "dp", 4 * k) for k in range(1, chips)])
        parts = jnp.stack([at(parts, turn ^ k, 0) for k in range(chips)])
        other = flipped(parts, "dp", 1)
        core = near % 2
        parts = jnp.stack(
            [jnp.where(core == 0, parts, other), jnp.where(core == 0, other, parts)], axis=2
        )
        pile = jnp.moveaxis(parts, 3, 0).reshape((2, -1) + parts.shape[5:])
        shared_sizes = [part.shape[1] // 128 for part in shared]
        quarter_sizes = [part.shape[1] // 128 // ranks for part in quartered]
        owned_sizes = [part.shape[1] // 128 for part in owned]
        each = -(-sum(shared_sizes) // ranks)
        own = pile[:, :each]
        parts = jnp.stack([own] + [around(own, "tensor", k) for k in range(1, ranks)])
        ordered = jnp.concatenate([at(parts, (tensor - r) % ranks, 0) for r in range(ranks)], axis=1)
        results = []
        for whole, begin, sizes in [
            (ordered, 0, shared_sizes),
            (pile, each, quarter_sizes + owned_sizes),
        ]:
            for count in sizes:
                results.append([flat(whole[m, begin : begin + count]) for m in range(2)])
                begin += count
        return results

    def feed_grads(layer, grad, unit2, rsd2, partial):
        return grad + norm_back(unit2, rsd2, reduce_rows(partial) * small[layer][4])

    def feed_adapters(second, branch, low_u, low_d, inner_u, inner_d, active, grad_up):
        shared = [across(inner_u, second), across(low_d, branch)]
        owned = [across(low_u, grad_up), across(inner_d, active)]
        return shared, owned

    def backward_attend(layer, kept, grad_middle):
        gain1 = small[layer][0]
        sq, skv, ekv, eo = adapters[layer]
        unit1, rsd1, normed, low_q, low_kv, queries, key_block, probs, mixed, low_o = kept
        branch = grad_middle.astype(bf16)
        grad_q, grad_block, inner_o = attend_back(
            layer, branch, early_all, so_all[layer], eo, probs, queries, key_block, head
        )
        inner_q, partial = query_back(layer, grad_q, early_all, eq_all[layer], sq)
        count = (reach + 1) * rows
        blocks = grad_block[:count].astype(f32)
        for j in range(1, ranks):
            part = grad_block[j * count : (j + 1) * count]
            blocks = blocks + around(part, "tensor", j).astype(f32)
        own = blocks[reach * rows :]
        for back in range(1, reach + 1):
            begin = (reach - back) * rows
            own = own + along(blocks[begin : begin + rows].astype(bf16), "dp", -back).astype(f32)
        grad_kv = own.astype(bf16)
        inner_kv = against(grad_kv, ekv).astype(bf16)
        grad_normed = partial + against(grad_kv, keyval_ws[layer]) + plain(inner_kv, skv)
        grad_hidden = grad_middle + norm_back(unit1, rsd1, grad_normed * gain1)
        shared = [
            across(low_o, branch),
            across(inner_q, normed),
            across(inner_kv, normed),
            across(low_kv, grad_kv),
        ]
        quartered = [across(low_q, grad_q), across(inner_o, mixed)]
        return grad_hidden, shared, quartered

    fresh = lax.dynamic_index_in_dim(block_input, section, 0, keepdims=False).astype(f32)
    given = lax.dynamic_index_in_dim(cotangent, section, 0, keepdims=False).astype(f32)
    middle_zero, kept_zero = forward_attend(0, fresh)
    unit_zero, rsd_zero, second_zero, up_bias = feed_inputs(0, middle_zero)
    own_rows, second_zero = lax.optimization_barrier((given.astype(bf16), second_zero))
    branch_one = spread(own_rows)
    second_zero, branch_one = lax.optimization_barrier((second_zero, branch_one))
    active_zero, slope_zero, low_u_zero, low_d_zero, partial = feed_call(
        feed_kernel,
        "feed",
        (second_zero, feed_tables[0], up_bias, feed_packs[0]),
        (3,),
        (local_f, local_f, rank, rank, width),
        local_f,
        2,
    )
    passed = feed_result(0, middle_zero, partial).astype(bf16)

    middle_one, kept_one = forward_attend(1, passed.astype(f32))
    unit_one, rsd_one, second_one, up_bias = feed_inputs(1, middle_one)
    active, low_u, low_d, partial, grad_up, inner_d, inner_u, partial_back = feed_call(
        feed_both_kernel,
        "feed_both",
        (second_one, branch_one, feed_tables[1], up_bias, feed_packs[1]),
        (4, 1),
        (local_f, rank, rank, width, local_f, rank, rank, width),
        local_f,
        4,
    )
    grad_middle = feed_grads(1, given, unit_one, rsd_one, partial_back)
    shared, owned = feed_adapters(
        second_one, branch_one, low_u, low_d, inner_u, inner_d, active, grad_up
    )
    grad_one, more, quartered = backward_attend(1, kept_one, grad_middle)
    layer_one = (shared + more, quartered, owned)
    partial_one = partial

    branch_zero = spread(grad_one.astype(bf16))
    grad_up, inner_d, inner_u, partial_back = feed_call(
        feed_back_kernel,
        "feed_back",
        (branch_zero, feed_tables[0], slope_zero, feed_packs[0]),
        (3, 2),
        (local_f, rank, rank, width),
        local_f,
        2,
    )
    grad_middle_zero = feed_grads(0, grad_one, unit_zero, rsd_zero, partial_back)
    shared, owned = feed_adapters(
        second_zero,
        branch_zero,
        low_u_zero,
        low_d_zero,
        inner_u,
        inner_d,
        active_zero,
        grad_up,
    )
    grad_zero, more, quartered = backward_attend(0, kept_zero, grad_middle_zero)
    layer_zero = (shared + more, quartered, owned)
    mine, partial_one = scattered_grads([layer_zero, layer_one], partial_one)
    final = feed_result(1, middle_one, partial_one).astype(bf16)
    grads = spread_grads(mine[0], mine[1], *layer_zero)

    def both_micros(zero, one, kind):
        own = jnp.where(low_section, zero, one)
        received = swap(jnp.where(low_section, one, zero).astype(bf16)).astype(kind)
        return jnp.where(low_section, jnp.stack([own, received]), jnp.stack([received, own]))

    section_outputs = both_micros(passed, final, bf16)
    input_grads = both_micros(grad_zero, grad_one, f32)
    onehot = (bank_choice[:, None] == jnp.arange(banks)[None, :]).astype(f32)

    def placed(pair, transpose):
        out = sum(
            onehot[m][:, None, None] * pair[m].astype(f32)[None] for m in range(2)
        )
        return (out.transpose(0, 2, 1) if transpose else out)[None]

    (
        up_shrink_grad,
        down_expand_grad,
        out_expand_grad,
        q_shrink_grad,
        kv_shrink_grad,
        kv_expand_grad,
        q_expand_grad,
        out_shrink_grad,
        up_expand_grad,
        down_shrink_grad,
    ) = grads
    return (
        section_outputs[None],
        input_grads[None],
        placed(q_shrink_grad, True),
        placed(q_expand_grad, False),
        placed(kv_shrink_grad, True),
        placed(kv_expand_grad, False),
        placed(out_shrink_grad, True),
        placed(out_expand_grad, False),
        placed(up_shrink_grad, True),
        placed(up_expand_grad, False),
        placed(down_shrink_grad, True),
        placed(down_expand_grad, False),
    )


def solution(mesh):
    return jax.shard_map(
        per_device,
        mesh=mesh,
        in_specs=(
            P(None, ("dp", "tensor"), None),
            P(None, ("dp", "tensor"), None),
            P(),
            P(),
            P("section", None),
            P("section", None),
            P("section", "dp", "tensor"),
            P("section", "tensor"),
            P("section", "dp", None),
            P("section", None),
            P("section", "tensor", "dp"),
            P("section", None),
            P("section", None),
            P("section", None),
            P("section", "dp", "tensor"),
            P("section", "tensor"),
            P("section", "tensor", "dp"),
            P("section", None),
            P("section", None, None, None),
            P("section", None, None, "tensor"),
            P("section", None, None, None),
            P("section", None, None, None),
            P("section", None, "tensor", None),
            P("section", None, None, None),
            P("section", None, None, None),
            P("section", None, None, "tensor"),
            P("section", None, "tensor", None),
            P("section", None, None, None),
        ),
        out_specs=(
            P("section", None, ("dp", "tensor"), None),
            P("section", None, ("dp", "tensor"), None),
            P("section", None, None, None),
            P("section", None, None, "tensor"),
            P("section", None, None, None),
            P("section", None, None, None),
            P("section", None, "tensor", None),
            P("section", None, None, None),
            P("section", None, None, None),
            P("section", None, None, "tensor"),
            P("section", None, "tensor", None),
            P("section", None, None, None),
        ),
        check_vma=False,
    )
```

```python
import math

import jax
import jax.numpy as jnp
from jax import lax
from jax.experimental import pallas as pl
from jax.experimental.layout import Layout, with_layout_constraint
from jax.experimental.pallas import tpu as pltpu
from jax.sharding import PartitionSpec as P

WINDOW = 1024
epsilon = 1e-05
masked_score = -1e30
bf16 = jnp.bfloat16
f32 = jnp.float32


def plain(left, right):
    return jnp.dot(left, right, preferred_element_type=f32)


def against(left, right):
    return lax.dot_general(left, right, (((1,), (1,)), ((), ())), preferred_element_type=f32)


def across(left, right):
    return lax.dot_general(left, right, (((0,), (0,)), ((), ())), preferred_element_type=f32)


def around(block, axis, distance):
    size = lax.axis_size(axis)
    return lax.ppermute(block, axis, [(i, (i + distance) % size) for i in range(size)])


def along(block, axis, distance):
    size = lax.axis_size(axis)
    route = [(i, i + distance) for i in range(size) if 0 <= i + distance < size]
    return lax.ppermute(block, axis, route)


def flipped(block, axis, bit):
    size = lax.axis_size(axis)
    return lax.ppermute(block, axis, [(i, i ^ bit) for i in range(size)])


def pick(table, index, size=1):
    return lax.dynamic_slice_in_dim(table, index, size, 0)


def norm_parts(value):
    centred = value - jnp.mean(value, axis=-1, keepdims=True)
    spread = lax.rsqrt(jnp.mean(centred * centred, axis=-1, keepdims=True) + epsilon)
    return centred * spread, spread


def norm_back(unit, spread, scaled):
    inner = jnp.mean(scaled * unit, axis=-1, keepdims=True)
    return spread * (scaled - jnp.mean(scaled, axis=-1, keepdims=True) - unit * inner)


def gelu_parts(value):
    rate = math.sqrt(2.0 / math.pi)
    square = value * value
    bend = jnp.tanh(rate * (value + 0.044715 * value * square))
    rising = 0.5 * (1.0 + bend)
    slope = rising + 0.5 * value * (1.0 - bend * bend) * (rate * (1.0 + 3 * 0.044715 * square))
    return value * rising, slope


def side_blocks(query_ref, group, head):
    begin = group * 4 * head
    return jnp.concatenate(
        [query_ref[:, begin + h * head : begin + (h + 1) * head] for h in range(4)], axis=0
    )


def put_blocks(out_ref, value, group, head):
    rows = value.shape[0] // 4
    for h in range(4):
        begin = (group * 4 + h) * head
        out_ref[:, begin : begin + head] = value[h * rows : (h + 1) * rows]


def table_copies(table_ref, buf, sem, layer, begin):
    ranks, chunks, _, width = buf.shape
    return [
        pltpu.make_async_copy(
            table_ref.at[x, y, layer, :, pl.ds(begin, width)], buf.at[x, y], sem.at[x, y]
        )
        for x in range(ranks)
        for y in range(chunks)
    ]


def query_kernel(layer, normed_ref, table_ref, bias_ref, eq_ref, sq_ref, out_ref, low_ref, buf, sem):
    ranks, chunks, rows, width = buf.shape
    copies = table_copies(table_ref, buf, sem, layer, 0)
    for copy in copies:
        copy.start()
    normed = normed_ref[...]
    low = against(normed, sq_ref[...]).astype(bf16)
    low_ref[...] = low
    for x in range(ranks):
        columns = pl.ds(x * width, width)
        total = bias_ref[:, columns] + plain(low, eq_ref[:, columns])
        for y in range(chunks):
            copies[x * chunks + y].wait()
            total = total + plain(normed[:, y * rows : (y + 1) * rows], buf[x, y])
        out_ref[:, columns] = total.astype(bf16)


def table_scratch(table, width):
    ranks, chunks, _, rows, _ = table.shape
    return [
        pltpu.VMEM((ranks, chunks, rows, width), bf16),
        pltpu.SemaphoreType.DMA((ranks, chunks)),
    ]


held = pl.BlockSpec(memory_space=pltpu.VMEM)
remote = pl.BlockSpec(memory_space=pl.ANY)


def project_queries(layer, normed, table, bias, eq, sq):
    rows, model = normed.shape
    rank = sq.shape[0]
    width = model // table.shape[0]
    return pl.pallas_call(
        lambda *refs: query_kernel(layer, *refs),
        in_specs=[held, remote, held, held, held],
        out_specs=[held] * 2,
        out_shape=[
            jax.ShapeDtypeStruct((rows, model), bf16),
            jax.ShapeDtypeStruct((rows, rank), bf16),
        ],
        scratch_shapes=table_scratch(table, width),
        compiler_params=pltpu.CompilerParams(vmem_limit_bytes=28 * 2**20),
        cost_estimate=pl.CostEstimate(
            flops=8 * rows * model * model, bytes_accessed=2 * model * model, transcendentals=0
        ),
        name="project_queries",
    )(normed, table, bias, eq, sq)


def attend_kernel(
    layer, head, query_ref, keyval_ref, bias_ref, table_ref, so_ref, eo_ref,
    prob_ref, mixed_ref, low_ref, out_ref, buf, sem,
):
    ranks, chunks, rows, width = buf.shape
    copies = table_copies(table_ref, buf, sem, layer, width)
    for copy in copies:
        copy.start()
    scale = 1.0 / math.sqrt(head)
    bias = jnp.concatenate([bias_ref[...].astype(f32)] * 4, axis=0)
    for g in range(prob_ref.shape[0]):
        queries = side_blocks(query_ref, g, head)
        scores = against(queries, keyval_ref[:, :head]) * scale + bias
        lifted = jnp.exp(scores - jnp.max(scores, axis=-1, keepdims=True))
        probs = (lifted * (1.0 / jnp.sum(lifted, axis=-1, keepdims=True))).astype(bf16)
        prob_ref[g] = probs
        put_blocks(mixed_ref, plain(probs, keyval_ref[:, head:]).astype(bf16), g, head)
    mixed = mixed_ref[...]
    low = against(mixed, so_ref[...]).astype(bf16)
    low_ref[...] = low
    for copy in copies:
        copy.wait()
    for y in range(chunks):
        columns = pl.ds(y * rows, rows)
        total = plain(low, eo_ref[:, columns])
        for x in range(ranks):
            total = total + against(mixed[:, x * width : (x + 1) * width], buf[x, y])
        out_ref[:, columns] = total


def attend(layer, queries, key_block, bias, table, so, eo, head):
    rows, model = queries.shape
    keys = key_block.shape[0]
    groups = model // head // 4
    rank = so.shape[0]
    return pl.pallas_call(
        lambda *refs: attend_kernel(layer, head, *refs),
        in_specs=[held, held, held, remote, held, held],
        out_specs=[held] * 4,
        out_shape=[
            jax.ShapeDtypeStruct((groups, 4 * rows, keys), bf16),
            jax.ShapeDtypeStruct((rows, model), bf16),
            jax.ShapeDtypeStruct((rows, rank), bf16),
            jax.ShapeDtypeStruct((rows, model), f32),
        ],
        scratch_shapes=table_scratch(table, model // table.shape[0]),
        compiler_params=pltpu.CompilerParams(vmem_limit_bytes=36 * 2**20),
        cost_estimate=pl.CostEstimate(
            flops=4 * rows * model * (keys + 2 * model),
            bytes_accessed=2 * model * model,
            transcendentals=groups * 4 * rows * keys,
        ),
        name="attend",
    )(queries, key_block, bias, table, so, eo)


def attend_back_kernel(
    layer, head, branch_ref, table_ref, so_ref, eo_ref, prob_ref, query_ref, keyval_ref,
    dq_ref, dkv_ref, inner_o_ref, out_buf, out_sem, mixed_buf, key_sum, value_sum,
):
    ranks, chunks, rows, width = out_buf.shape
    out_copies = table_copies(table_ref, out_buf, out_sem, layer, width)
    for copy in out_copies:
        copy.start()
    scale = 1.0 / math.sqrt(head)
    branch = branch_ref[...]
    inner_o = against(branch, eo_ref[...]).astype(bf16)
    inner_o_ref[...] = inner_o
    for g in range(prob_ref.shape[0]):
        columns = pl.ds(g * width, width)
        total = plain(inner_o, so_ref[:, columns])
        for y in range(chunks):
            out_copies[g * chunks + y].wait()
            total = total + plain(branch[:, y * rows : (y + 1) * rows], out_buf[g, y])
        mixed_buf[:, columns] = total.astype(bf16)
        grad = side_blocks(mixed_buf, g, head)
        low_probs = prob_ref[g]
        probs = low_probs.astype(f32)
        grad_probs = against(grad, keyval_ref[:, head:])
        delta = jnp.sum(grad_probs * probs, axis=-1, keepdims=True)
        delta = delta / jnp.sum(probs, axis=-1, keepdims=True)
        grad_scores = (probs * (grad_probs - delta)).astype(bf16)
        put_blocks(dq_ref, (plain(grad_scores, keyval_ref[:, :head]) * scale).astype(bf16), g, head)
        keys = across(grad_scores, side_blocks(query_ref, g, head))
        values = across(low_probs, grad)
        if g == 0:
            key_sum[...] = keys
            value_sum[...] = values
        else:
            key_sum[...] += keys
            value_sum[...] += values
    dkv_ref[:, :head] = (key_sum[...] * scale).astype(bf16)
    dkv_ref[:, head:] = value_sum[...].astype(bf16)


def query_back_kernel(layer, grad_ref, table_ref, eq_ref, sq_ref, inner_ref, part_ref, buf, sem):
    ranks, chunks, rows, width = buf.shape
    copies = table_copies(table_ref, buf, sem, layer, 0)
    for copy in copies:
        copy.start()
    grad = grad_ref[...]
    inner = against(grad, eq_ref[...]).astype(bf16)
    inner_ref[...] = inner
    for copy in copies:
        copy.wait()
    for y in range(chunks):
        columns = pl.ds(y * rows, rows)
        total = plain(inner, sq_ref[:, columns])
        for x in range(ranks):
            total = total + against(grad[:, x * width : (x + 1) * width], buf[x, y])
        part_ref[:, columns] = total


def query_back(layer, grad, table, eq, sq):
    rows, model = grad.shape
    rank = sq.shape[0]
    return pl.pallas_call(
        lambda *refs: query_back_kernel(layer, *refs),
        in_specs=[held, remote, held, held],
        out_specs=[held] * 2,
        out_shape=[
            jax.ShapeDtypeStruct((rows, rank), bf16),
            jax.ShapeDtypeStruct((rows, model), f32),
        ],
        scratch_shapes=table_scratch(table, model // table.shape[0]),
        compiler_params=pltpu.CompilerParams(vmem_limit_bytes=28 * 2**20),
        cost_estimate=pl.CostEstimate(
            flops=8 * rows * model * model, bytes_accessed=2 * model * model, transcendentals=0
        ),
        name="query_back",
    )(grad, table, eq, sq)


def attend_back(layer, branch, table, so, eo, probs, queries, key_block, head):
    rows, model = queries.shape
    keys = key_block.shape[0]
    groups = probs.shape[0]
    rank = so.shape[0]
    width = model // table.shape[0]
    return pl.pallas_call(
        lambda *refs: attend_back_kernel(layer, head, *refs),
        in_specs=[held, remote] + [held] * 5,
        out_specs=[held] * 3,
        out_shape=[
            jax.ShapeDtypeStruct((rows, model), bf16),
            jax.ShapeDtypeStruct((keys, 2 * head), bf16),
            jax.ShapeDtypeStruct((rows, rank), bf16),
        ],
        scratch_shapes=table_scratch(table, width)
        + [
            pltpu.VMEM((rows, model), bf16),
            pltpu.VMEM((keys, head), f32),
            pltpu.VMEM((keys, head), f32),
        ],
        compiler_params=pltpu.CompilerParams(vmem_limit_bytes=44 * 2**20),
        cost_estimate=pl.CostEstimate(
            flops=8 * rows * model * (keys + model),
            bytes_accessed=2 * model * model + 4 * groups * 4 * rows * keys,
            transcendentals=0,
        ),
        name="attend_back",
    )(branch, table, so, eo, probs, queries, key_block)


def feed_copies(table_ref, buf, sems):
    _, count, chunks, rows, tile = buf.shape
    half = count // 2 * tile
    copies = []
    for j in range(count):
        pair = []
        for k in range(2):
            columns = pl.ds(j * tile % half + k * half, tile)
            pair.append(
                pltpu.make_async_copy(
                    table_ref.at[:, j * tile // half, :, columns], buf.at[k, j], sems.at[k, j]
                )
            )
        copies.append(pair)
    return copies


def plain_chunks(left, buf, k, j):
    rows = buf.shape[3]
    return sum(plain(left[:, i * rows : (i + 1) * rows], buf[k, j, i]) for i in range(buf.shape[2]))


def against_chunk(left_ref, buf, k, i):
    tile = buf.shape[4]
    return sum(
        against(left_ref[:, j * tile : (j + 1) * tile], buf[k, j, i]) for j in range(buf.shape[1])
    )


def own_copies(sources, buffers, sems):
    copies = [
        pltpu.make_async_copy(source, buffer, sems.at[i])
        for i, (source, buffer) in enumerate(zip(sources, buffers))
    ]
    for copy in copies:
        copy.start()
    return copies


def feed_pack(pack_ref, model, hidden):
    cuts = [0, model, model + hidden, model + 2 * hidden, 2 * model + 2 * hidden]
    return [pack_ref.at[:, a:b] for a, b in zip(cuts[:-1], cuts[1:])]


def feed_kernel(
    second_ref, table_ref, bias_ref, pack_ref,
    active_ref, slope_ref, low_u_ref, low_d_ref, out_ref, buf, sems, pack_buf, own_sems,
):
    _, count, chunks, rows, tile = buf.shape
    su_ref, eu_ref, sd_ref, ed_ref = feed_pack(pack_buf, chunks * rows, count * tile)
    copies = feed_copies(table_ref, buf, sems)
    own = own_copies([pack_ref], [pack_buf], own_sems)
    for up, _ in copies:
        up.start()
    for _, down in copies:
        down.start()
    second = second_ref[...]
    own[0].wait()
    low_u = against(second, su_ref[...]).astype(bf16)
    low_u_ref[...] = low_u
    for j in range(count):
        columns = pl.ds(j * tile, tile)
        copies[j][0].wait()
        upward = plain_chunks(second, buf, 0, j)
        upward = upward + plain(low_u, eu_ref[:, columns]) + bias_ref[:, columns]
        active, slope = gelu_parts(upward)
        active_ref[:, columns] = active.astype(bf16)
        slope_ref[:, columns] = slope.astype(bf16)
    low_d = against(active_ref[...], sd_ref[...]).astype(bf16)
    low_d_ref[...] = low_d
    for _, down in copies:
        down.wait()
    for i in range(chunks):
        columns = pl.ds(i * rows, rows)
        out_ref[:, columns] = (
            against_chunk(active_ref, buf, 1, i) + plain(low_d, ed_ref[:, columns])
        ).astype(bf16)


def feed_back_kernel(
    branch_ref, table_ref, slope_ref, pack_ref,
    grad_up_ref, inner_d_ref, inner_u_ref, out_ref, buf, sems, pack_buf, slope_buf, own_sems,
):
    _, count, chunks, rows, tile = buf.shape
    su_ref, eu_ref, sd_ref, ed_ref = feed_pack(pack_buf, chunks * rows, count * tile)
    copies = feed_copies(table_ref, buf, sems)
    own = own_copies([pack_ref, slope_ref], [pack_buf, slope_buf], own_sems)
    for _, down in copies:
        down.start()
    for up, _ in copies:
        up.start()
    branch = branch_ref[...]
    own[0].wait()
    inner_d = against(branch, ed_ref[...]).astype(bf16)
    inner_d_ref[...] = inner_d
    own[1].wait()
    for j in range(count):
        columns = pl.ds(j * tile, tile)
        copies[j][1].wait()
        grad = plain_chunks(branch, buf, 1, j) + plain(inner_d, sd_ref[:, columns])
        grad_up_ref[:, columns] = (grad * slope_buf[:, columns].astype(f32)).astype(bf16)
    inner_u = against(grad_up_ref[...], eu_ref[...]).astype(bf16)
    inner_u_ref[...] = inner_u
    for up, _ in copies:
        up.wait()
    for i in range(chunks):
        columns = pl.ds(i * rows, rows)
        out_ref[:, columns] = (
            against_chunk(grad_up_ref, buf, 0, i) + plain(inner_u, su_ref[:, columns])
        ).astype(bf16)


def feed_both_kernel(
    second_ref, branch_ref, table_ref, bias_ref, pack_ref,
    active_ref, low_u_ref, grad_up_ref, inner_d_ref, inner_u_ref, back_ref,
    buf, sems, pack_buf, branch_buf, own_sems,
):
    _, count, chunks, rows, tile = buf.shape
    su_ref, eu_ref, sd_ref, ed_ref = feed_pack(pack_buf, chunks * rows, count * tile)
    copies = feed_copies(table_ref, buf, sems)
    own = own_copies([pack_ref, branch_ref], [pack_buf, branch_buf], own_sems)
    for up, down in copies:
        up.start()
        down.start()
    second = second_ref[...]
    for copy in own:
        copy.wait()
    branch = branch_buf[...]
    low_u = against(second, su_ref[...]).astype(bf16)
    low_u_ref[...] = low_u
    inner_d = against(branch, ed_ref[...]).astype(bf16)
    inner_d_ref[...] = inner_d
    for j in range(count):
        columns = pl.ds(j * tile, tile)
        copies[j][0].wait()
        upward = plain_chunks(second, buf, 0, j)
        upward = upward + plain(low_u, eu_ref[:, columns]) + bias_ref[:, columns]
        active, slope = gelu_parts(upward)
        active_ref[:, columns] = active.astype(bf16)
        copies[j][1].wait()
        grad = plain_chunks(branch, buf, 1, j) + plain(inner_d, sd_ref[:, columns])
        grad_up_ref[:, columns] = (grad * slope).astype(bf16)
    inner_u = against(grad_up_ref[...], eu_ref[...]).astype(bf16)
    inner_u_ref[...] = inner_u
    for i in range(chunks):
        columns = pl.ds(i * rows, rows)
        back_ref[:, columns] = (
            against_chunk(grad_up_ref, buf, 0, i) + plain(inner_u, su_ref[:, columns])
        ).astype(bf16)


def feed_down_kernel(
    active_ref, table_ref, pack_ref, low_d_ref, out_ref, buf, sems, pack_buf, own_sems
):
    _, count, chunks, rows, tile = buf.shape
    _, _, sd_ref, ed_ref = feed_pack(pack_buf, chunks * rows, count * tile)
    copies = feed_copies(table_ref, buf, sems)
    own = own_copies([pack_ref], [pack_buf], own_sems)
    for _, down in copies:
        down.start()
    own[0].wait()
    low_d = against(active_ref[...], sd_ref[...]).astype(bf16)
    low_d_ref[...] = low_d
    for _, down in copies:
        down.wait()
    for i in range(chunks):
        columns = pl.ds(i * rows, rows)
        out_ref[:, columns] = (
            against_chunk(active_ref, buf, 1, i) + plain(low_d, ed_ref[:, columns])
        ).astype(bf16)


def feed_call(kernel, name, inputs, copied, outputs, hidden, matmuls):
    table = [value for value in inputs if value.ndim == 4][0]
    rows, model = inputs[0].shape
    tile = 512
    chunks = table.shape[0]
    return pl.pallas_call(
        kernel,
        in_specs=[
            remote if value.ndim == 4 or i in copied else held for i, value in enumerate(inputs)
        ],
        out_specs=[held] * len(outputs),
        out_shape=[jax.ShapeDtypeStruct((rows, width), bf16) for width in outputs],
        scratch_shapes=[
            pltpu.VMEM((2, hidden // tile, chunks, model // chunks, tile), bf16),
            pltpu.SemaphoreType.DMA((2, hidden // tile)),
        ]
        + [pltpu.VMEM(inputs[i].shape, bf16) for i in copied]
        + [pltpu.SemaphoreType.DMA((len(copied),))],
        compiler_params=pltpu.CompilerParams(vmem_limit_bytes=44 * 2**20),
        cost_estimate=pl.CostEstimate(
            flops=2 * matmuls * rows * model * hidden,
            bytes_accessed=4 * model * hidden,
            transcendentals=rows * hidden,
        ),
        name=name,
    )(*inputs)


def per_device(
    block_input,
    cotangent,
    doc_lengths,
    bank_choice,
    first_gain,
    first_shift,
    query_weight,
    query_bias,
    keyval_weight,
    value_bias,
    output_weight,
    output_bias,
    second_gain,
    second_shift,
    upward_weight,
    upward_bias,
    downward_weight,
    downward_bias,
    query_shrink,
    query_expand,
    keyval_shrink,
    keyval_expand,
    output_shrink,
    output_expand,
    upward_shrink,
    upward_expand,
    downward_shrink,
    downward_expand,
):
    section = lax.axis_index("section")
    data = lax.axis_index("dp")
    tensor = lax.axis_index("tensor")
    low_section = section == 0
    width = block_input.shape[2]
    rows = block_input.shape[1]
    ranks = lax.axis_size("tensor")
    span = rows * ranks
    head = value_bias.shape[1]
    local_q = query_bias.shape[1]
    local_f = upward_bias.shape[1]
    rank = query_expand.shape[2]
    banks = query_expand.shape[1]
    reach = WINDOW // span
    sides = [(0, 1), (1, 0)]

    def swap(value):
        return lax.ppermute(value, "section", sides)

    def by_layer(own, other):
        return jnp.where(low_section, own, other), jnp.where(low_section, other, own)

    def spread(block):
        parts = [block] + [around(block, "tensor", -j) for j in range(1, ranks)]
        return jnp.concatenate(parts, axis=0)

    def reduce_rows(partial):
        low = partial.astype(bf16)
        total = partial[:rows].astype(f32)
        for j in range(1, ranks):
            total = total + around(low[j * rows : (j + 1) * rows], "tensor", j).astype(f32)
        return total

    own_bank = lax.dynamic_index_in_dim(bank_choice, section, 0, keepdims=False)
    other_bank = lax.dynamic_index_in_dim(bank_choice, 1 - section, 0, keepdims=False)

    chips = lax.axis_size("dp") // 4
    both = ("section", "dp")
    every = ("section", "dp", "tensor")
    order = [
        side * 4 * chips + chip * 4 + near
        for chip in range(chips)
        for side in range(2)
        for near in range(4)
    ]
    order_all = [place * ranks + x for x in range(ranks) for place in order]

    def row_major(block):
        return with_layout_constraint(block, Layout(major_to_minor=(0, 1)))

    def gather(shard):
        table = lax.all_gather(row_major(shard), both, axis=0, tiled=True, axis_index_groups=[order])
        return row_major(table).reshape(chips, 2, -1, shard.shape[1])

    def gather_all(shard):
        table = lax.all_gather(
            row_major(shard), every, axis=0, tiled=True, axis_index_groups=[order_all]
        )
        return row_major(table).reshape(ranks, chips, 2, -1, shard.shape[1])

    def halves(shard):
        cut = shard.shape[1] // 2
        return shard[:, :cut], shard[:, cut:]

    keyval_half = jnp.where(tensor % 2 == 0, keyval_weight[0][:, :head], keyval_weight[0][:, head:])
    early_all = gather_all(
        jnp.concatenate([query_weight[0], row_major(output_weight[0].T), keyval_half], axis=1)
    )
    keyval_ws = [
        jnp.concatenate(
            [early_all[x, :, layer, :, 2 * local_q :].reshape(width, head) for x in range(2)], axis=1
        )
        for layer in range(2)
    ]

    def crossed(block, mask):
        return lax.ppermute(block, both, [(i, i ^ mask) for i in range(8 * chips)])

    vectors = jnp.concatenate(
        [
            first_gain,
            first_shift,
            jnp.zeros_like(value_bias),
            value_bias,
            output_bias,
            second_gain,
            second_shift,
            upward_bias,
            downward_bias,
        ],
        axis=1,
    )
    vector_sizes = [width, width, 2 * head, width, width, width, local_f, width]
    vector_layers = by_layer(vectors, swap(vectors))

    def chosen(table, bank, transpose):
        block = lax.dynamic_index_in_dim(table[0], bank, 0, keepdims=False)
        return block.T if transpose else block

    def pack(bank, parts):
        return jnp.concatenate([chosen(table, bank, flip) for table, flip in parts], axis=1)

    cut_parts = [(query_expand, False), (output_shrink, True)]
    whole_parts = [
        (query_shrink, True),
        (keyval_shrink, True),
        (keyval_expand, False),
        (output_expand, False),
        (upward_shrink, True),
        (upward_expand, False),
        (downward_shrink, True),
        (downward_expand, False),
    ]
    query_rows = jnp.broadcast_to(query_bias, (rank, local_q))

    def cut_pack(bank):
        return jnp.concatenate([pack(bank, cut_parts), query_rows], axis=1)

    shared_parts = [part for part in whole_parts if part[0] is not upward_expand and part[0] is not downward_shrink]
    split_parts = [(upward_expand, False), (downward_shrink, True)]
    shared_away = pack(other_bank, shared_parts)
    quarter = shared_away.shape[1] // ranks
    crossing = jnp.concatenate(
        [
            cut_pack(other_bank),
            lax.dynamic_slice_in_dim(shared_away, tensor * quarter, quarter, 1),
            pack(other_bank, split_parts),
        ],
        axis=1,
    )
    crossed_pack = swap(crossing)
    cut_width = 3 * local_q
    block = jnp.concatenate([cut_pack(own_bank), crossed_pack[:, : cut_width + quarter]], axis=1)
    blocks = jnp.stack([block] + [around(block, "tensor", j) for j in range(1, ranks)])
    blocks = [
        lax.dynamic_index_in_dim(blocks, (tensor - r) % ranks, 0, keepdims=False)
        for r in range(ranks)
    ]

    def joined(begin, size):
        return jnp.concatenate([block[:, begin : begin + size] for block in blocks], axis=1)

    cut_layers = [
        by_layer(joined(k * local_q, local_q), joined(cut_width + k * local_q, local_q))
        for k in range(3)
    ]
    eq_all, so_all, query_bias_all = cut_layers
    shared_layers = by_layer(pack(own_bank, shared_parts), joined(2 * cut_width, quarter))
    split_layers = by_layer(pack(own_bank, split_parts), crossed_pack[:, cut_width + quarter :])

    up_halves = halves(upward_weight[0])
    down_halves = halves(row_major(downward_weight[0].T))
    side = [jnp.concatenate([up_halves[h], down_halves[h]], axis=1) for h in range(2)]
    keep = jnp.where(low_section, side[0], side[1])
    gained = swap(jnp.where(low_section, side[1], side[0]))
    feed_tables = [gather(table) for table in by_layer(keep, gained)]

    def split(table, sizes):
        cuts = [0]
        for size in sizes:
            cuts.append(cuts[-1] + size)
        return [table[:, a:b] for a, b in zip(cuts[:-1], cuts[1:])]

    small = [
        [part.astype(f32) for part in split(vector_layers[layer], vector_sizes)]
        for layer in range(2)
    ]
    adapters = []
    feed_packs = []
    for layer in range(2):
        sq, skv, ekv, eo, su, ed = split(
            shared_layers[layer], [width, width, 2 * head, width, width, width]
        )
        eu, sd = split(split_layers[layer], [local_f, local_f])
        adapters.append((sq, skv, ekv, eo))
        feed_packs.append(jnp.concatenate([su, eu, sd, ed], axis=1))

    inside = jnp.arange(rows, dtype=jnp.int32)
    query_place = data * span + tensor * rows + inside
    key_place = jnp.concatenate(
        [
            (data - back) * span + (tensor + j) % ranks * rows + inside
            for j in range(ranks)
            for back in range(reach, -1, -1)
        ]
    )
    lengths = lax.dynamic_index_in_dim(doc_lengths, section, 0, keepdims=False)
    ends = jnp.cumsum(lengths)
    query_doc = jnp.sum((query_place[:, None] >= ends[None, :]).astype(jnp.int32), axis=1)
    key_doc = jnp.sum((key_place[:, None] >= ends[None, :]).astype(jnp.int32), axis=1)
    distance = query_place[:, None] - key_place[None, :]
    allowed = (
        (key_place[None, :] >= 0)
        & (distance >= 0)
        & (distance < WINDOW)
        & (query_doc[:, None] == key_doc[None, :])
    )
    bias = jnp.where(allowed, 0.0, masked_score).astype(bf16)

    def forward_attend(layer, hidden):
        gain1, shift1, kv_bias, out_bias = small[layer][:4]
        sq, skv, ekv, eo = adapters[layer]
        unit1, rsd1 = norm_parts(hidden)
        normed = (unit1 * gain1 + shift1).astype(bf16)
        low_kv = against(normed, skv).astype(bf16)
        keyval = (plain(normed, keyval_ws[layer]) + kv_bias + plain(low_kv, ekv)).astype(bf16)
        pieces = [along(keyval, "dp", back) for back in range(reach, 0, -1)] + [keyval]
        key_block = spread(jnp.concatenate(pieces, axis=0))
        queries, low_q = project_queries(
            layer, normed, early_all, query_bias_all[layer][:1].astype(f32), eq_all[layer], sq
        )
        probs, mixed, low_o, attended = attend(
            layer, queries, key_block, bias, early_all, so_all[layer], eo, head
        )
        middle = hidden + (attended + out_bias)
        return middle, (unit1, rsd1, normed, low_q, low_kv, queries, key_block, probs, mixed, low_o)

    def feed_inputs(layer, middle):
        gain2, shift2, up_bias = small[layer][4:7]
        unit2, rsd2 = norm_parts(middle)
        second = spread((unit2 * gain2 + shift2).astype(bf16))
        return unit2, rsd2, second, up_bias

    def feed_result(layer, middle, partial):
        return middle + (reduce_rows(partial) + small[layer][7])

    def tiles(block):
        return block.reshape(rank, -1, 128).transpose(1, 0, 2)

    def flat(block):
        return block.transpose(1, 0, 2).reshape(rank, -1)

    turn, near = data // 4, data % 4

    def padded(pile, multiple):
        lack = -pile.shape[0] % multiple
        if not lack:
            return pile
        return jnp.concatenate([pile, jnp.zeros((lack,) + pile.shape[1:], pile.dtype)], axis=0)

    def piled(shared, quartered):
        pile = padded(jnp.concatenate([tiles(part) for part in shared], axis=0), ranks)
        return jnp.concatenate(
            [block.reshape((ranks, -1) + block.shape[1:]) for block in [pile] + [tiles(part) for part in quartered]],
            axis=1,
        ).astype(bf16)

    def owned_pile(mine, owned):
        pile = jnp.concatenate([mine] + [tiles(part) for part in owned], axis=0).astype(bf16)
        return padded(pile, lax.axis_size("dp"))

    def at(block, index, axis):
        return lax.dynamic_index_in_dim(block, index, axis, keepdims=False)

    def scattered_grads(layers, late):
        pile = jnp.stack([piled(shared, quartered) for shared, quartered, _ in layers], axis=1)
        mine = at(pile, tensor, 0).astype(f32)
        for j in range(1, ranks):
            mine = mine + around(at(pile, (tensor + j) % ranks, 0), "tensor", j).astype(f32)
        pile = jnp.stack([owned_pile(mine[i], layers[i][2]) for i in range(2)])
        pile = pile.reshape((2, chips, 4, -1) + pile.shape[2:])
        mine = at(pile, near, 2).astype(f32)
        for k in range(1, 4):
            mine = mine + flipped(at(pile, near ^ k, 2), "dp", k).astype(f32)
        pile, late = lax.optimization_barrier((mine.astype(bf16), late))
        mine = at(pile, turn, 1).astype(f32)
        for k in range(1, chips):
            mine = mine + flipped(at(pile, turn ^ k, 1), "dp", 4 * k).astype(f32)
        return mine.astype(bf16), late

    def spread_grads(zero, one, shared, quartered, owned):
        own = jnp.where(low_section, zero, one)
        away = jnp.where(low_section, one, zero)
        dp_size = 4 * chips
        home = jnp.stack([own, flipped(own, "dp", 2)])
        guest = jnp.stack([crossed(away, dp_size), crossed(away, dp_size + 2)])
        home, guest = [
            jnp.where(near // 2 == 0, block, block[::-1]) for block in (home, guest)
        ]
        pair = jnp.where(
            low_section, jnp.stack([home, guest], axis=1), jnp.stack([guest, home], axis=1)
        )
        parts = jnp.stack([pair] + [flipped(pair, "dp", 4 * k) for k in range(1, chips)])
        parts = jnp.stack([at(parts, turn ^ k, 0) for k in range(chips)])
        other = flipped(parts, "dp", 1)
        core = near % 2
        parts = jnp.stack(
            [jnp.where(core == 0, parts, other), jnp.where(core == 0, other, parts)], axis=2
        )
        pile = jnp.moveaxis(parts, 3, 0).reshape((2, -1) + parts.shape[5:])
        shared_sizes = [part.shape[1] // 128 for part in shared]
        quarter_sizes = [part.shape[1] // 128 // ranks for part in quartered]
        owned_sizes = [part.shape[1] // 128 for part in owned]
        each = -(-sum(shared_sizes) // ranks)
        own = pile[:, :each]
        parts = jnp.stack([own] + [around(own, "tensor", k) for k in range(1, ranks)])
        ordered = jnp.concatenate([at(parts, (tensor - r) % ranks, 0) for r in range(ranks)], axis=1)
        results = []
        for whole, begin, sizes in [
            (ordered, 0, shared_sizes),
            (pile, each, quarter_sizes + owned_sizes),
        ]:
            for count in sizes:
                results.append([flat(whole[m, begin : begin + count]) for m in range(2)])
                begin += count
        return results

    def feed_grads(layer, grad, unit2, rsd2, partial):
        return grad + norm_back(unit2, rsd2, reduce_rows(partial) * small[layer][4])

    def feed_adapters(second, branch, low_u, low_d, inner_u, inner_d, active, grad_up):
        shared = [across(inner_u, second), across(low_d, branch)]
        owned = [across(low_u, grad_up), across(inner_d, active)]
        return shared, owned

    def backward_attend(layer, kept, grad_middle):
        gain1 = small[layer][0]
        sq, skv, ekv, eo = adapters[layer]
        unit1, rsd1, normed, low_q, low_kv, queries, key_block, probs, mixed, low_o = kept
        branch = grad_middle.astype(bf16)
        grad_q, grad_block, inner_o = attend_back(
            layer, branch, early_all, so_all[layer], eo, probs, queries, key_block, head
        )
        inner_q, partial = query_back(layer, grad_q, early_all, eq_all[layer], sq)
        count = (reach + 1) * rows
        blocks = grad_block[:count].astype(f32)
        for j in range(1, ranks):
            part = grad_block[j * count : (j + 1) * count]
            blocks = blocks + around(part, "tensor", j).astype(f32)
        own = blocks[reach * rows :]
        for back in range(1, reach + 1):
            begin = (reach - back) * rows
            own = own + along(blocks[begin : begin + rows].astype(bf16), "dp", -back).astype(f32)
        grad_kv = own.astype(bf16)
        inner_kv = against(grad_kv, ekv).astype(bf16)
        grad_normed = partial + against(grad_kv, keyval_ws[layer]) + plain(inner_kv, skv)
        grad_hidden = grad_middle + norm_back(unit1, rsd1, grad_normed * gain1)
        shared = [
            across(low_o, branch),
            across(inner_q, normed),
            across(inner_kv, normed),
            across(low_kv, grad_kv),
        ]
        quartered = [across(low_q, grad_q), across(inner_o, mixed)]
        return grad_hidden, shared, quartered

    fresh = lax.dynamic_index_in_dim(block_input, section, 0, keepdims=False).astype(f32)
    given = lax.dynamic_index_in_dim(cotangent, section, 0, keepdims=False).astype(f32)
    middle_zero, kept_zero = forward_attend(0, fresh)
    unit_zero, rsd_zero, second_zero, up_bias = feed_inputs(0, middle_zero)
    own_rows, second_zero = lax.optimization_barrier((given.astype(bf16), second_zero))
    branch_one = spread(own_rows)
    second_zero, branch_one = lax.optimization_barrier((second_zero, branch_one))
    active_zero, slope_zero, low_u_zero, low_d_zero, partial = feed_call(
        feed_kernel,
        "feed",
        (second_zero, feed_tables[0], up_bias, feed_packs[0]),
        (3,),
        (local_f, local_f, rank, rank, width),
        local_f,
        2,
    )
    passed = feed_result(0, middle_zero, partial).astype(bf16)

    middle_one, kept_one = forward_attend(1, passed.astype(f32))
    unit_one, rsd_one, second_one, up_bias = feed_inputs(1, middle_one)
    active, low_u, grad_up, inner_d, inner_u, partial_back = feed_call(
        feed_both_kernel,
        "feed_both",
        (second_one, branch_one, feed_tables[1], up_bias, feed_packs[1]),
        (4, 1),
        (local_f, rank, local_f, rank, rank, width),
        local_f,
        3,
    )
    low_d, partial = feed_call(
        feed_down_kernel,
        "feed_down",
        (active, feed_tables[1], feed_packs[1]),
        (2,),
        (rank, width),
        local_f,
        1,
    )
    grad_middle = feed_grads(1, given, unit_one, rsd_one, partial_back)
    shared, owned = feed_adapters(
        second_one, branch_one, low_u, low_d, inner_u, inner_d, active, grad_up
    )
    grad_one, more, quartered = backward_attend(1, kept_one, grad_middle)
    layer_one = (shared + more, quartered, owned)
    partial_one = partial

    branch_zero = spread(grad_one.astype(bf16))
    grad_up, inner_d, inner_u, partial_back = feed_call(
        feed_back_kernel,
        "feed_back",
        (branch_zero, feed_tables[0], slope_zero, feed_packs[0]),
        (3, 2),
        (local_f, rank, rank, width),
        local_f,
        2,
    )
    grad_middle_zero = feed_grads(0, grad_one, unit_zero, rsd_zero, partial_back)
    shared, owned = feed_adapters(
        second_zero,
        branch_zero,
        low_u_zero,
        low_d_zero,
        inner_u,
        inner_d,
        active_zero,
        grad_up,
    )
    grad_zero, more, quartered = backward_attend(0, kept_zero, grad_middle_zero)
    layer_zero = (shared + more, quartered, owned)
    mine, partial_one = scattered_grads([layer_zero, layer_one], partial_one)
    final = feed_result(1, middle_one, partial_one).astype(bf16)
    grads = spread_grads(mine[0], mine[1], *layer_zero)

    def both_micros(zero, one, kind):
        own = jnp.where(low_section, zero, one)
        received = swap(jnp.where(low_section, one, zero).astype(bf16)).astype(kind)
        return jnp.where(low_section, jnp.stack([own, received]), jnp.stack([received, own]))

    section_outputs = both_micros(passed, final, bf16)
    input_grads = both_micros(grad_zero, grad_one, f32)
    onehot = (bank_choice[:, None] == jnp.arange(banks)[None, :]).astype(f32)

    def placed(pair, transpose):
        out = sum(
            onehot[m][:, None, None] * pair[m].astype(f32)[None] for m in range(2)
        )
        return (out.transpose(0, 2, 1) if transpose else out)[None]

    (
        up_shrink_grad,
        down_expand_grad,
        out_expand_grad,
        q_shrink_grad,
        kv_shrink_grad,
        kv_expand_grad,
        q_expand_grad,
        out_shrink_grad,
        up_expand_grad,
        down_shrink_grad,
    ) = grads
    return (
        section_outputs[None],
        input_grads[None],
        placed(q_shrink_grad, True),
        placed(q_expand_grad, False),
        placed(kv_shrink_grad, True),
        placed(kv_expand_grad, False),
        placed(out_shrink_grad, True),
        placed(out_expand_grad, False),
        placed(up_shrink_grad, True),
        placed(up_expand_grad, False),
        placed(down_shrink_grad, True),
        placed(down_expand_grad, False),
    )


def solution(mesh):
    return jax.shard_map(
        per_device,
        mesh=mesh,
        in_specs=(
            P(None, ("dp", "tensor"), None),
            P(None, ("dp", "tensor"), None),
            P(),
            P(),
            P("section", None),
            P("section", None),
            P("section", "dp", "tensor"),
            P("section", "tensor"),
            P("section", "dp", None),
            P("section", None),
            P("section", "tensor", "dp"),
            P("section", None),
            P("section", None),
            P("section", None),
            P("section", "dp", "tensor"),
            P("section", "tensor"),
            P("section", "tensor", "dp"),
            P("section", None),
            P("section", None, None, None),
            P("section", None, None, "tensor"),
            P("section", None, None, None),
            P("section", None, None, None),
            P("section", None, "tensor", None),
            P("section", None, None, None),
            P("section", None, None, None),
            P("section", None, None, "tensor"),
            P("section", None, "tensor", None),
            P("section", None, None, None),
        ),
        out_specs=(
            P("section", None, ("dp", "tensor"), None),
            P("section", None, ("dp", "tensor"), None),
            P("section", None, None, None),
            P("section", None, None, "tensor"),
            P("section", None, None, None),
            P("section", None, None, None),
            P("section", None, "tensor", None),
            P("section", None, None, None),
            P("section", None, None, None),
            P("section", None, None, "tensor"),
            P("section", None, "tensor", None),
            P("section", None, None, None),
        ),
        check_vma=False,
    )
```
